32 devices in a mesh: shot: 8 (over z, y), depth: 4 (over x, core).
Axes of the slice: x: 2, y: 2, z: 4, core: 2. Of those that a mesh axis runs over, the one named last changes fastest.
Arguments:
- courant_sq: float32 [32, 64, 128], P('depth'), may hold values from 0.03 to 0.245
- momentum: float32 [32, 64, 128], P('depth'), may hold values from -6 to 6
- fwd_prev: float32 [16, 32, 64, 128], P('shot', 'depth'), may hold values from -6 to 6
- fwd_cur: float32 [16, 32, 64, 128], P('shot', 'depth'), may hold values from -6 to 6
- adj_next: float32 [16, 32, 64, 128], P('shot', 'depth'), may hold values from -6 to 6
- adj_cur: float32 [16, 32, 64, 128], P('shot', 'depth'), may hold values from -6 to 6
- observed: float32 [16, 8, 512], P('shot'), may hold values from -24 to 24
- src_cells: int32 [16], P('shot'), may hold values from 0 to 262143
- rec_cells: int32 [16, 512], P('shot'), may hold values from 0 to 262143
- ckpt_step: int32 [], replicated, may hold values from 0 to 999999
Outputs:
- momentum_half: float32 [32, 64, 128], P('depth')
- kinetic: float32 [], replicated
The draws below stay inside these ranges and needn't reach their ends.
Inputs may be any that keep to these rules, and one draw needn't show every extreme that they name: `src_cells`: cell indices as defined in the reference program. `rec_cells`: cell indices as defined in the reference program.
All inputs are finite; a program needn't handle non-finite values.
Results may differ from the reference program's by a relative error of at most 0.0003.
Values sent between devices are 32-bit elements; how exact they have to be, the bound alone decides.
No kernel may reach another device: no remote copies, remote signals or barrier semaphores. Data moves between devices by JAX's collectives and lax.ppermute only.
A program may use at most 64 MiB of HBM per device.

```python
import math
import jax
import jax.numpy as jnp
from jax import lax

NX = 64
NY = 128
STEPS = 8
NREC = 512
NZ = 32
SHOTS = 16


def draw_courant_sq(key, part):
    key = jax.random.fold_in(key, 11)
    shape = (NZ, NX, NY)
    unit = jax.random.uniform(key, shape, jnp.float32)
    return jnp.exp(math.log(0.03) + unit * (math.log(0.24) - math.log(0.03)))


def place_ends(entries, rng, least, high):
    index_at = [jax.random.randint(jax.random.fold_in(rng, axis), (), 0, length) for axis, length in enumerate(entries.shape)]
    longest = entries.shape.index(max(entries.shape))
    beside = index_at[:longest] + [(index_at[longest] + 1) % entries.shape[longest]] + index_at[longest + 1:]
    return entries.at[tuple(index_at)].set(least).at[tuple(beside)].set(high)


def level_of(rng, dims, pieces, least, high):
    loudness, own = 1.0, jax.random.fold_in(rng, 6)
    for position, blocks in pieces:
        steps = jnp.exp(jax.random.uniform(jax.random.fold_in(own, position), (blocks,), jnp.float32, least / len(pieces), high / len(pieces)))
        loudness = loudness * jnp.repeat(steps, dims[position] // blocks).reshape([-1 if axis == position else 1 for axis in range(len(dims))])
    return loudness


def noise(own_key, dims, deviation, most, split=(), held_as=jnp.bfloat16):
    array = deviation * jax.random.normal(own_key, dims, jnp.float32)
    if split:
        array = array * level_of(own_key, dims, split, -0.22, 0.18)
    return jnp.clip(array, -most, most).astype(held_as)


def setup_inputs(seed: int = 0) -> dict:
    key_of = jax.random.split(jax.random.key(seed), 11)
    courant_sq = draw_courant_sq(jax.random.fold_in(key_of[10], 71), 0)
    momentum = noise(key_of[1], (NZ, NX, NY), 1.0, 6.0, ((0, 4),), jnp.float32)
    fwd_prev = noise(key_of[2], (SHOTS, NZ, NX, NY), 1.0, 6.0, ((0, 8), (1, 4)), jnp.float32)
    fwd_cur = noise(key_of[3], (SHOTS, NZ, NX, NY), 1.0, 6.0, ((0, 8), (1, 4)), jnp.float32)
    adj_next = noise(key_of[4], (SHOTS, NZ, NX, NY), 1.0, 6.0, ((0, 8), (1, 4)), jnp.float32)
    adj_cur = noise(key_of[5], (SHOTS, NZ, NX, NY), 1.0, 6.0, ((0, 8), (1, 4)), jnp.float32)
    observed = noise(key_of[6], (SHOTS, STEPS, NREC), 4.0, 24.0, ((0, 8),), jnp.float32)
    src_cells = place_ends(jax.random.randint(key_of[7], (SHOTS,), 0, NZ * NX * NY), jax.random.fold_in(key_of[7], 1), 0, (NZ * NX * NY) - 1).astype(jnp.int32)
    rec_cells = place_ends(jax.random.randint(key_of[8], (SHOTS, NREC), 0, NZ * NX * NY), jax.random.fold_in(key_of[8], 1), 0, (NZ * NX * NY) - 1).astype(jnp.int32)
    ckpt_step = jax.random.randint(key_of[9], (), 0, 1000000).astype(jnp.int32)
    return dict(courant_sq=courant_sq, momentum=momentum, fwd_prev=fwd_prev, fwd_cur=fwd_cur, adj_next=adj_next, adj_cur=adj_cur, observed=observed, src_cells=src_cells, rec_cells=rec_cells, ckpt_step=ckpt_step)


CENTER = -2.5
NEAR = 4.0 / 3.0
FAR = -1.0 / 12.0
AMPLITUDE = 100.0
EPSILON = 1e-06

def laplace(padded):
    lateral = jnp.pad(padded[:, 2:-2], ((0, 0), (0, 0), (2, 2), (2, 2)))
    center = padded[:, 2:-2]
    along_z = NEAR * (padded[:, 1:-3] + padded[:, 3:-1]) + FAR * (padded[:, :-4] + padded[:, 4:])
    along_x = NEAR * (lateral[:, :, 1:-3, 2:-2] + lateral[:, :, 3:-1, 2:-2]) + FAR * (lateral[:, :, :-4, 2:-2] + lateral[:, :, 4:, 2:-2])
    along_y = NEAR * (lateral[:, :, 2:-2, 1:-3] + lateral[:, :, 2:-2, 3:-1]) + FAR * (lateral[:, :, 2:-2, :-4] + lateral[:, :, 2:-2, 4:])
    return 3.0 * CENTER * center + along_z + along_x + along_y

def locate(field, cell_ids, first_plane):
    shot_count, planes, rows_x, rows_y = field.shape
    plane_cells = rows_x * rows_y
    local_index = cell_ids - first_plane * plane_cells
    inside = (local_index >= 0) & (local_index < planes * plane_cells)
    target = jnp.where(inside, local_index, 0).astype(jnp.int32)
    return (inside, target)

def inject(field, cell_ids, values, first_plane):
    shot_count = field.shape[0]
    inside, target = locate(field, cell_ids, first_plane)
    amount = jnp.where(inside, values, jnp.zeros_like(values))
    flattened = field.reshape(shot_count, -1)
    lanes = jnp.arange(shot_count)[:, None]
    flattened = flattened.at[lanes, target].add(amount)
    return flattened.reshape(field.shape)

def sample(field, cell_ids, first_plane):
    shot_count = field.shape[0]
    inside, target = locate(field, cell_ids, first_plane)
    values = jnp.take_along_axis(field.reshape(shot_count, -1), target, axis=1)
    return jnp.where(inside, values, jnp.zeros_like(values))

def wave_value(start, step):
    cycle = jnp.mod(start.astype(jnp.int32) + jnp.int32(step), jnp.int32(48))
    phase = (cycle.astype(jnp.float32) - 24.0) / 12.0
    return AMPLITUDE * (1.0 - 2.0 * phase * phase) * jnp.exp(-phase * phase)

def depth_pad(field):
    return jnp.pad(field, ((0, 0), (2, 2), (0, 0), (0, 0)))

def reference(courant_sq, momentum, fwd_prev, fwd_cur, adj_next, adj_cur, observed, src_cells, rec_cells, ckpt_step):

    def one_shot(grand_total, per_shot):
        older, current, adj_later, adj_now, traces, source, receivers = per_shot
        older = older[None]
        current = current[None]
        adj_later = adj_later[None]
        adj_now = adj_now[None]
        source = source.reshape(1, 1)
        receivers = receivers[None]
        laplacians = []
        misfits = []
        for step in range(STEPS):
            laplacian = laplace(depth_pad(current))
            strength = jnp.full((1, 1), wave_value(ckpt_step, step), jnp.float32)
            laplacian = inject(laplacian, source, strength, 0)
            newer = 2.0 * current - older + courant_sq * laplacian
            misfits.append(sample(newer, receivers, 0) - traces[None, step])
            laplacians.append(laplacian)
            older, current = (current, newer)
        for step in reversed(range(STEPS)):
            adj_new = 2.0 * adj_now - adj_later + laplace(depth_pad(courant_sq * adj_now))
            adj_new = inject(adj_new, receivers, misfits[step], 0)
            grand_total = grand_total + lax.optimization_barrier(jnp.sum(adj_new * laplacians[step], axis=0))
            adj_later, adj_now = (adj_now, adj_new)
        return (grand_total, None)
    start_total = jnp.zeros((NZ, NX, NY), jnp.float32)
    gradient, _ = lax.scan(one_shot, start_total, (fwd_prev, fwd_cur, adj_next, adj_cur, observed, src_cells, rec_cells))
    depths = jnp.arange(NZ).astype(jnp.float32)
    weight = (1.0 + 2.0 * depths / (NZ - 1))[:, None, None]
    scaled = weight * gradient
    inv_scale = lax.rsqrt(jnp.mean(scaled * scaled) + EPSILON)
    momentum_half = momentum - 0.5 * inv_scale * scaled
    kinetic = 0.5 * jnp.mean(weight * momentum_half * momentum_half)
    return (momentum_half, kinetic)
```

```python
import functools

import jax
import jax.numpy as jnp
from jax import lax
from jax.experimental import pallas as pl
from jax.experimental.pallas import tpu as pltpu
from jax.sharding import Mesh
from jax.sharding import PartitionSpec as P

CENTER = -2.5
NEAR = 4.0 / 3.0
FAR = -1.0 / 12.0
AMPLITUDE = 100.0
EPSILON = 1e-06


def with_halo(value, sides, width):
    for axis, dim in sides:
        size, length = (lax.axis_size(axis), value.shape[dim])
        up = [(i, (i + 1) % size) for i in range(size - 1)]
        down = [(j, i) for i, j in up]
        last = lax.slice_in_dim(value, length - width, length, axis=dim)
        leading = lax.slice_in_dim(value, 0, width, axis=dim)
        before = lax.ppermute(last, axis, up)
        after = lax.ppermute(leading, axis, down)
        value = jnp.concatenate([before, value, after], axis=dim)
    return value


def laplace(padded):
    lateral = jnp.pad(padded[:, 2:-2], ((0, 0), (0, 0), (2, 2), (2, 2)))
    center = padded[:, 2:-2]
    along_z = NEAR * (padded[:, 1:-3] + padded[:, 3:-1]) + FAR * (padded[:, :-4] + padded[:, 4:])
    along_x = NEAR * (lateral[:, :, 1:-3, 2:-2] + lateral[:, :, 3:-1, 2:-2]) + FAR * (
        lateral[:, :, :-4, 2:-2] + lateral[:, :, 4:, 2:-2]
    )
    along_y = NEAR * (lateral[:, :, 2:-2, 1:-3] + lateral[:, :, 2:-2, 3:-1]) + FAR * (
        lateral[:, :, 2:-2, :-4] + lateral[:, :, 2:-2, 4:]
    )
    return 3.0 * CENTER * center + along_z + along_x + along_y


def locate(field, cell_ids, first_plane):
    shot_count, planes, rows_x, rows_y = field.shape
    plane_cells = rows_x * rows_y
    local_index = cell_ids - first_plane * plane_cells
    inside = (local_index >= 0) & (local_index < planes * plane_cells)
    target = jnp.where(inside, local_index, 0)
    return (inside, target)


def inject(field, cell_ids, values, first_plane):
    shot_count = field.shape[0]
    inside, target = locate(field, cell_ids, first_plane)
    amount = jnp.where(inside, values, jnp.zeros_like(values))
    flattened = field.reshape(shot_count, -1)
    lanes = jnp.arange(shot_count)[:, None]
    flattened = flattened.at[lanes, target].add(amount)
    return flattened.reshape(field.shape)


def sample(field, cell_ids, first_plane):
    shot_count = field.shape[0]
    inside, target = locate(field, cell_ids, first_plane)
    values = jnp.take_along_axis(field.reshape(shot_count, -1), target, axis=1)
    return jnp.where(inside, values, jnp.zeros_like(values))


def wave_value(start, step):
    cycle = jnp.mod(start + jnp.int32(step), jnp.int32(48))
    phase = (cycle.astype(jnp.float32) - 24.0) / 12.0
    return AMPLITUDE * (1.0 - 2.0 * phase * phase) * jnp.exp(-phase * phase)


def statistics(scaled, moment, weight, cells_all):
    grand_total = lax.psum(jnp.sum(scaled * scaled), ("shot", "depth"))
    factor = lax.rsqrt(grand_total / cells_all + EPSILON)
    halfway = moment - 0.5 * factor * scaled
    energy = lax.psum(jnp.sum(weight * halfway * halfway), ("shot", "depth"))
    return (factor, 0.5 * energy / cells_all)


def slab_shards(
    courant_sq,
    momentum,
    fwd_prev,
    fwd_cur,
    adj_next,
    adj_cur,
    observed,
    src_cells,
    rec_cells,
    ckpt_step,
):
    shot_count, planes, rows_x, rows_y = fwd_cur.shape
    steps_all = observed.shape[1]
    first_plane = lax.axis_index("depth") * planes
    total_planes = planes * lax.axis_size("depth")
    cells_all = total_planes * rows_x * rows_y
    sources = src_cells[:, None]
    older, current = (fwd_prev, fwd_cur)
    laplacians = []
    misfits = []
    for step in range(steps_all):
        padded = with_halo(current, (("depth", 1),), 2)
        strength = jnp.full(sources.shape, wave_value(ckpt_step, step), jnp.float32)
        laplacian = inject(laplace(padded), sources, strength, first_plane)
        newer = 2.0 * current - older + courant_sq * laplacian
        misfits.append(sample(newer, rec_cells, first_plane) - observed[:, step, :])
        laplacians.append(laplacian)
        older, current = (current, newer)
    adj_later, adj_now = (adj_next, adj_cur)
    gradient = jnp.zeros((planes, rows_x, rows_y), jnp.float32)
    for step in reversed(range(steps_all)):
        padded = with_halo(courant_sq * adj_now, (("depth", 1),), 2)
        adj_new = 2.0 * adj_now - adj_later + laplace(padded)
        adj_new = inject(adj_new, rec_cells, misfits[step], first_plane)
        gradient = gradient + jnp.sum(adj_new * laplacians[step], axis=0)
        adj_later, adj_now = (adj_now, adj_new)
    depths = (first_plane + jnp.arange(planes)).astype(jnp.float32)
    weight = (1.0 + 2.0 * depths / (total_planes - 1))[:, None, None]
    share_rows = rows_x // lax.axis_size("shot")
    offset = lax.axis_index("shot") * share_rows
    moment_share = lax.dynamic_slice_in_dim(momentum, offset, share_rows, 1)
    gradient = lax.psum(gradient, "shot")
    scaled = weight * gradient
    scaled_share = lax.dynamic_slice_in_dim(scaled, offset, share_rows, 1)
    factor, kinetic = statistics(scaled_share, moment_share, weight, cells_all)
    momentum_half = momentum - 0.5 * factor * scaled
    return (momentum_half, kinetic)


def interleave(dst, dst_at, src, src_at, rows, factor=None):
    groups = rows // 8
    for i in range(groups):
        value = src[(*src_at, pl.ds(i, 8, stride=groups), slice(None))]
        if factor is not None:
            value = value * factor
        dst[(*dst_at, pl.ds(i * 8, 8), slice(None))] = value


def lap12(field, slot, z):
    center = field[slot, z + 2]
    rows, lanes = center.shape
    sub = lax.broadcasted_iota(jnp.int32, (8, lanes), 0)
    lane = lax.broadcasted_iota(jnp.int32, (rows, lanes), 1)

    def later(block):
        return jnp.where(sub < 7, pltpu.roll(block, 7, 0), 0.0)

    def earlier(block):
        return jnp.where(sub > 0, pltpu.roll(block, 1, 0), 0.0)

    first, second = center[0:8], center[8:16]
    last, before = center[rows - 8 :], center[rows - 16 : rows - 8]
    late = later(first)
    early = earlier(last)
    near = jnp.concatenate([center[8:], late], 0) + jnp.concatenate([early, center[:-8]], 0)
    far = jnp.concatenate([center[16:], late, later(second)], 0) + jnp.concatenate(
        [earlier(before), early, center[:-16]], 0
    )
    near = near + (field[slot, z + 1] + field[slot, z + 3])
    far = far + (field[slot, z] + field[slot, z + 4])
    near = near + jnp.where(lane >= 1, pltpu.roll(center, 1, 1), 0.0)
    near = near + jnp.where(lane < lanes - 1, pltpu.roll(center, lanes - 1, 1), 0.0)
    far = far + jnp.where(lane >= 2, pltpu.roll(center, 2, 1), 0.0)
    far = far + jnp.where(lane < lanes - 2, pltpu.roll(center, lanes - 2, 1), 0.0)
    return center, 16.0 * near - far - 90.0 * center


def scatter_kernel(row_ref, y_ref, obs_ref, out_ref, spread):
    receivers, steps = obs_ref.shape
    lanes = out_ref.shape[2]
    tile = out_ref.shape[1]

    @pl.when(pl.program_id(0) == 0)
    def _():
        lane = lax.broadcasted_iota(jnp.int32, (receivers, lanes), 1)
        at = lane == y_ref[...]
        for k in range(steps):
            column = obs_ref[:, k : k + 1]
            high = column.astype(jnp.bfloat16).astype(jnp.float32)
            low = column - high
            cols = pl.ds(k * lanes, lanes)
            spread[0, :, cols] = jnp.where(at, high, 0.0).astype(jnp.bfloat16)
            spread[1, :, cols] = jnp.where(at, low, 0.0).astype(jnp.bfloat16)
        cols = pl.ds(steps * lanes, lanes)
        spread[0, :, cols] = jnp.where(at, 1.0, 0.0).astype(jnp.bfloat16)
        spread[1, :, cols] = jnp.zeros((receivers, lanes), jnp.bfloat16)

    ids = lax.broadcasted_iota(jnp.int32, (tile, receivers), 0) + pl.program_id(0) * tile
    chosen = jnp.where(ids == row_ref[...], 1.0, 0.0).astype(jnp.bfloat16)
    total = jnp.dot(chosen, spread[0], preferred_element_type=jnp.float32)
    total = total + jnp.dot(chosen, spread[1], preferred_element_type=jnp.float32)
    for k in range(steps + 1):
        out_ref[k] = total[:, k * lanes : (k + 1) * lanes]


def scatter(cells, observed, planes_all, rows_x, rows_y):
    steps, receivers = observed.shape
    groups = rows_x // 8
    x = (cells // rows_y) % rows_x
    row = (cells // (rows_x * rows_y)) * rows_x + (x % groups) * 8 + x // groups
    lanes = cells % rows_y
    rows_all = planes_all * rows_x
    tile = 256
    return pl.pallas_call(
        scatter_kernel,
        grid=(rows_all // tile,),
        in_specs=[
            pl.BlockSpec((1, receivers), lambda t: (0, 0)),
            pl.BlockSpec((receivers, 1), lambda t: (0, 0)),
            pl.BlockSpec((receivers, steps), lambda t: (0, 0)),
        ],
        out_specs=pl.BlockSpec((steps + 1, tile, rows_y), lambda t: (0, t, 0)),
        out_shape=jax.ShapeDtypeStruct((steps + 1, rows_all, rows_y), jnp.float32),
        scratch_shapes=[pltpu.VMEM((2, receivers, (steps + 1) * rows_y), jnp.bfloat16)],
        compiler_params=pltpu.CompilerParams(vmem_limit_bytes=32 * 2**20),
        cost_estimate=pl.CostEstimate(
            flops=4 * rows_all * receivers * (steps + 1) * rows_y,
            bytes_accessed=4 * (steps + 1) * rows_all * rows_y,
            transcendentals=0,
        ),
        name="receiver_scatter",
    )(row[None, :], lanes[:, None], observed.T)


def load_blocks(meta, blocks, field, planes, rows):
    ends = field.shape[1]
    for slot in range(2):
        for z in (0, 1, ends - 2, ends - 1):
            field[slot, z] = jnp.zeros(field.shape[2:], jnp.float32)
    for b, block in enumerate(blocks):

        @pl.loop(0, planes)
        def _(p):
            z = meta[b] + p + 2
            interleave(field, (1, z), block, (0, p), rows)
            interleave(field, (0, z), block, (1, p), rows)


def for_owned(meta, planes, body):
    for owned in (True, False):
        core = meta[4] if owned else 1 - meta[4]

        @pl.loop(0, 2 * planes)
        def _(index):
            chip, p = index // planes, index % planes
            z = (2 * chip + core) * planes + p
            body(z, chip if owned else None, p)


def forward_kernel(meta, wave, own, mate, over, far, c0, c1, c2, c3, obs, count, lap_ref, inject_ref, cour_ref, field):
    step = pl.program_id(0)
    planes, rows, lanes = c0.shape

    @pl.when(step == 0)
    def _():
        load_blocks(meta, (own, mate, over, far), field, planes, rows)
        for b, block in enumerate((c0, c1, c2, c3)):

            @pl.loop(0, planes)
            def _(p):
                interleave(cour_ref, (meta[b] + p,), block, (p,), rows, 1.0 / 12.0)

    now = lax.rem(step, 2)
    then = 1 - now

    def body(z, chip, p):
        center, lap = lap12(field, now, z)
        if chip is not None:
            lap_ref[0, p, chip] = lap
        newer = 2.0 * center - field[then, z + 2] + cour_ref[z] * lap
        field[then, z + 2] = newer
        inject_ref[0, z] = obs[0, z] - count[0, z] * newer

    for_owned(meta, planes, body)

    z, row, lane = meta[5], pl.multiple_of(meta[6], 8), meta[8]
    here = (lax.broadcasted_iota(jnp.int32, (8, lanes), 0) == meta[7]) & (
        lax.broadcasted_iota(jnp.int32, (8, lanes), 1) == lane
    )
    strength = jnp.where(here, 12.0 * wave[step], 0.0)
    tile = pl.ds(row, 8)
    slab, p = z // planes, lax.rem(z, planes)

    @pl.when(lax.rem(slab, 2) == meta[4])
    def _():
        lap_ref[0, p, slab // 2, tile, :] += strength

    moved = cour_ref[z, tile, :] * strength
    field[then, z + 2, tile, :] += moved
    inject_ref[0, z, tile, :] -= count[0, z, tile, :] * moved


def adjoint_kernel(meta, own, mate, over, far, cour, lap_ref, inject, grad_ref, field, total):
    step = pl.program_id(0)
    planes, rows, lanes = own.shape[1:]
    groups = rows // 8

    @pl.when(step == 0)
    def _():
        load_blocks(meta, (own, mate, over, far), field, planes, rows)

        @pl.loop(0, 4 * planes)
        def _(z):
            field[0, z + 2] = field[0, z + 2] * cour[z]
            field[1, z + 2] = field[1, z + 2] * cour[z]

        @pl.loop(0, 2 * planes)
        def _(index):
            total[index] = jnp.zeros((rows, lanes), jnp.float32)

    now = lax.rem(step, 2)
    then = 1 - now

    def body(z, chip, p):
        center, lap = lap12(field, now, z)
        newer = 2.0 * center - field[then, z + 2] + cour[z] * (lap - inject[0, z])
        field[then, z + 2] = newer
        if chip is not None:
            at = chip * planes + p
            total[at] = total[at] + newer * lap_ref[0, p, chip]

    for_owned(meta, planes, body)

    @pl.when(step == pl.num_programs(0) - 1)
    def _():
        @pl.loop(0, 2 * planes)
        def _(index):
            chip, p = index // planes, index % planes
            z = (2 * chip + meta[4]) * planes + p
            value = total[index] / (12.0 * cour[z])
            for i in range(groups):
                grad_ref[p, chip, pl.ds(i, 8, stride=groups), :] = value[i * 8 : (i + 1) * 8]


def whole_shards(
    courant_sq, momentum, fwd_prev, fwd_cur, adj_next, adj_cur, observed, src_cells, rec_cells, ckpt_step
):
    _, planes, rows_x, rows_y = fwd_cur.shape
    steps = observed.shape[1]
    chip, core = lax.axis_index("chip"), lax.axis_index("core")
    groups = rows_x // 8
    planes_all = 4 * planes
    cells_all = planes_all * rows_x * rows_y
    swap = [(0, 1), (1, 0)]

    def pick(pair, shot):
        return jnp.stack([lax.dynamic_index_in_dim(f, shot, 0, keepdims=False) for f in pair])

    forward = (fwd_prev, fwd_cur)
    adjoint = (adj_next, adj_cur)
    c2 = lax.ppermute(courant_sq, "chip", swap)
    over = lax.ppermute(pick(forward, 1 - chip), "chip", swap)
    own = pick(forward, chip)
    mate = lax.ppermute(own, "core", swap)
    c1 = lax.ppermute(courant_sq, "core", swap)

    cells = lax.dynamic_index_in_dim(rec_cells, chip, 0, keepdims=False)
    traces = lax.dynamic_index_in_dim(observed, chip, 0, keepdims=False)
    placed = scatter(cells, traces, planes_all, rows_x, rows_y)
    placed = placed.reshape(steps + 1, planes_all, rows_x, rows_y)

    over, to_send = lax.optimization_barrier((over, pick(adjoint, 1 - chip)))
    far = lax.ppermute(over, "core", swap)
    c3 = lax.ppermute(c2, "core", swap)
    adj_over = lax.ppermute(to_send, "chip", swap)
    adj_own = pick(adjoint, chip)
    adj_mate = lax.ppermute(adj_own, "core", swap)

    source = lax.dynamic_index_in_dim(src_cells, chip, 0, keepdims=False)
    x = (source // rows_y) % rows_x
    slabs = [2 * chip + core, 2 * chip + 1 - core, 2 * (1 - chip) + core, 2 * (1 - chip) + 1 - core]
    meta = jnp.stack(
        [slab * planes for slab in slabs]
        + [core, source // (rows_x * rows_y), (x % groups) * 8, x // groups, source % rows_y]
    ).astype(jnp.int32)
    wave = jnp.stack([wave_value(ckpt_step, k) for k in range(steps)])

    field_block = pl.BlockSpec((2, planes, rows_x, rows_y), lambda k: (0, 0, 0, 0))
    slab_block = pl.BlockSpec((planes, rows_x, rows_y), lambda k: (0, 0, 0))
    whole_block = pl.BlockSpec((planes_all, rows_x, rows_y), lambda k: (0, 0, 0))
    step_block = pl.BlockSpec((1, planes_all, rows_x, rows_y), lambda k: (k, 0, 0, 0))
    count_block = pl.BlockSpec((1, planes_all, rows_x, rows_y), lambda k: (steps, 0, 0, 0))
    lap_shape = (planes, 2, rows_x, rows_y)
    smem = pl.BlockSpec(memory_space=pltpu.SMEM)
    scratch = pltpu.VMEM((2, planes_all + 4, rows_x, rows_y), jnp.float32)
    params = pltpu.CompilerParams(vmem_limit_bytes=48 * 2**20)
    cost = pl.CostEstimate(flops=30 * steps * cells_all, bytes_accessed=16 * steps * cells_all, transcendentals=0)
    laps, inject, cour = pl.pallas_call(
        forward_kernel,
        grid=(steps,),
        in_specs=[smem, smem] + [field_block] * 4 + [slab_block] * 4 + [step_block, count_block],
        out_specs=[pl.BlockSpec((1, *lap_shape), lambda k: (k, 0, 0, 0, 0)), step_block, whole_block],
        out_shape=[
            jax.ShapeDtypeStruct((steps, *lap_shape), jnp.float32),
            jax.ShapeDtypeStruct((steps, planes_all, rows_x, rows_y), jnp.float32),
            jax.ShapeDtypeStruct((planes_all, rows_x, rows_y), jnp.float32),
        ],
        scratch_shapes=[scratch],
        compiler_params=params,
        cost_estimate=cost,
        name="forward_steps",
    )(meta, wave, own, mate, over, far, courant_sq, c1, c2, c3, placed, placed)

    adj_far = lax.ppermute(adj_over, "core", swap)
    back_block = pl.BlockSpec((1, planes_all, rows_x, rows_y), lambda k: (steps - 1 - k, 0, 0, 0))
    gradient = pl.pallas_call(
        adjoint_kernel,
        grid=(steps,),
        in_specs=[smem]
        + [field_block] * 4
        + [whole_block, pl.BlockSpec((1, *lap_shape), lambda k: (steps - 1 - k, 0, 0, 0, 0)), back_block],
        out_specs=pl.BlockSpec(lap_shape, lambda k: (0, 0, 0, 0)),
        out_shape=jax.ShapeDtypeStruct(lap_shape, jnp.float32),
        scratch_shapes=[scratch, pltpu.VMEM((2 * planes, rows_x, rows_y), jnp.float32)],
        compiler_params=params,
        cost_estimate=cost,
        name="adjoint_steps",
    )(meta, adj_own, adj_mate, adj_over, adj_far, cour, laps, inject)

    shot = lax.axis_index("shot")
    first = (2 * chip + core) * planes
    depths = (first + jnp.arange(planes)).astype(jnp.float32)
    weights = 1.0 + 2.0 * depths / (planes_all - 1)
    parts = gradient.reshape(2 * planes, rows_x, rows_y)
    parts = lax.all_to_all(parts, ("shot", "chip"), 0, 0, tiled=True)
    weight = lax.dynamic_index_in_dim(weights, shot, 0)
    scaled = weight * jnp.sum(parts, axis=0)
    moment = lax.dynamic_index_in_dim(momentum, shot, 0, keepdims=False)
    sums = jnp.stack(
        [
            jnp.sum(scaled * scaled),
            jnp.sum(weight * moment * moment),
            jnp.sum(weight * moment * scaled),
            jnp.sum(weight * scaled * scaled),
        ]
    )
    carried = jnp.concatenate([scaled, jnp.broadcast_to(jnp.pad(sums, (0, 4))[:, None], (8, rows_y))], 0)
    spread = jnp.broadcast_to(carried[None], (planes, rows_x + 8, rows_y))
    spread = lax.all_to_all(spread, "shot", 0, 0, tiled=True)
    scaled = spread[:, :rows_x]
    sums = jnp.sum(spread[:, rows_x:], axis=0)
    sums = lax.all_to_all(jnp.broadcast_to(sums[None], (4, 8, rows_y)), ("chip", "core"), 0, 0, tiled=True)
    sums = jnp.sum(sums, axis=0)[:, 0]
    factor = lax.rsqrt(sums[0] / cells_all + EPSILON)
    kinetic = 0.5 * (sums[1] - factor * sums[2] + 0.25 * factor * factor * sums[3]) / cells_all
    return momentum - 0.5 * factor * scaled, kinetic


def solution(mesh):
    shots, slabs = mesh.shape["shot"], mesh.shape["depth"]

    def placed(depth):
        field = P("shot", depth, None, None)
        slab = P(depth, None, None)
        inputs = (slab, slab, field, field, field, field, P("shot", None, None), P("shot"), P("shot", None), P())
        return dict(in_specs=inputs, out_specs=(slab, P()), check_vma=False)

    slab_plan = jax.shard_map(slab_shards, mesh=mesh, **placed("depth"))
    if slabs != 4:
        return slab_plan
    chips = Mesh(mesh.devices.reshape(shots, 2, 2), ("shot", "chip", "core"))
    whole_plan = jax.shard_map(whole_shards, mesh=chips, **placed(("chip", "core")))

    def run(courant_sq, momentum, fwd_prev, *rest):
        total, planes, rows_x, rows_y = fwd_prev.shape
        fits = total == 2 * shots and planes == 4 * shots and rows_y == 128 and rows_x % 16 == 0
        plan = whole_plan if fits else slab_plan
        return plan(courant_sq, momentum, fwd_prev, *rest)

    return run
```

```python
import functools

import jax
import jax.numpy as jnp
from jax import lax
from jax.experimental import pallas as pl
from jax.experimental.pallas import tpu as pltpu
from jax.sharding import Mesh
from jax.sharding import PartitionSpec as P

CENTER = -2.5
NEAR = 4.0 / 3.0
FAR = -1.0 / 12.0
AMPLITUDE = 100.0
EPSILON = 1e-06


def with_halo(value, sides, width):
    for axis, dim in sides:
        size, length = (lax.axis_size(axis), value.shape[dim])
        up = [(i, (i + 1) % size) for i in range(size - 1)]
        down = [(j, i) for i, j in up]
        last = lax.slice_in_dim(value, length - width, length, axis=dim)
        leading = lax.slice_in_dim(value, 0, width, axis=dim)
        before = lax.ppermute(last, axis, up)
        after = lax.ppermute(leading, axis, down)
        value = jnp.concatenate([before, value, after], axis=dim)
    return value


def laplace(padded):
    lateral = jnp.pad(padded[:, 2:-2], ((0, 0), (0, 0), (2, 2), (2, 2)))
    center = padded[:, 2:-2]
    along_z = NEAR * (padded[:, 1:-3] + padded[:, 3:-1]) + FAR * (padded[:, :-4] + padded[:, 4:])
    along_x = NEAR * (lateral[:, :, 1:-3, 2:-2] + lateral[:, :, 3:-1, 2:-2]) + FAR * (
        lateral[:, :, :-4, 2:-2] + lateral[:, :, 4:, 2:-2]
    )
    along_y = NEAR * (lateral[:, :, 2:-2, 1:-3] + lateral[:, :, 2:-2, 3:-1]) + FAR * (
        lateral[:, :, 2:-2, :-4] + lateral[:, :, 2:-2, 4:]
    )
    return 3.0 * CENTER * center + along_z + along_x + along_y


def locate(field, cell_ids, first_plane):
    shot_count, planes, rows_x, rows_y = field.shape
    plane_cells = rows_x * rows_y
    local_index = cell_ids - first_plane * plane_cells
    inside = (local_index >= 0) & (local_index < planes * plane_cells)
    target = jnp.where(inside, local_index, 0)
    return (inside, target)


def inject(field, cell_ids, values, first_plane):
    shot_count = field.shape[0]
    inside, target = locate(field, cell_ids, first_plane)
    amount = jnp.where(inside, values, jnp.zeros_like(values))
    flattened = field.reshape(shot_count, -1)
    lanes = jnp.arange(shot_count)[:, None]
    flattened = flattened.at[lanes, target].add(amount)
    return flattened.reshape(field.shape)


def sample(field, cell_ids, first_plane):
    shot_count = field.shape[0]
    inside, target = locate(field, cell_ids, first_plane)
    values = jnp.take_along_axis(field.reshape(shot_count, -1), target, axis=1)
    return jnp.where(inside, values, jnp.zeros_like(values))


def wave_value(start, step):
    cycle = jnp.mod(start + jnp.int32(step), jnp.int32(48))
    phase = (cycle.astype(jnp.float32) - 24.0) / 12.0
    return AMPLITUDE * (1.0 - 2.0 * phase * phase) * jnp.exp(-phase * phase)


def statistics(scaled, moment, weight, cells_all):
    grand_total = lax.psum(jnp.sum(scaled * scaled), ("shot", "depth"))
    factor = lax.rsqrt(grand_total / cells_all + EPSILON)
    halfway = moment - 0.5 * factor * scaled
    energy = lax.psum(jnp.sum(weight * halfway * halfway), ("shot", "depth"))
    return (factor, 0.5 * energy / cells_all)


def slab_shards(
    courant_sq,
    momentum,
    fwd_prev,
    fwd_cur,
    adj_next,
    adj_cur,
    observed,
    src_cells,
    rec_cells,
    ckpt_step,
):
    shot_count, planes, rows_x, rows_y = fwd_cur.shape
    steps_all = observed.shape[1]
    first_plane = lax.axis_index("depth") * planes
    total_planes = planes * lax.axis_size("depth")
    cells_all = total_planes * rows_x * rows_y
    sources = src_cells[:, None]
    older, current = (fwd_prev, fwd_cur)
    laplacians = []
    misfits = []
    for step in range(steps_all):
        padded = with_halo(current, (("depth", 1),), 2)
        strength = jnp.full(sources.shape, wave_value(ckpt_step, step), jnp.float32)
        laplacian = inject(laplace(padded), sources, strength, first_plane)
        newer = 2.0 * current - older + courant_sq * laplacian
        misfits.append(sample(newer, rec_cells, first_plane) - observed[:, step, :])
        laplacians.append(laplacian)
        older, current = (current, newer)
    adj_later, adj_now = (adj_next, adj_cur)
    gradient = jnp.zeros((planes, rows_x, rows_y), jnp.float32)
    for step in reversed(range(steps_all)):
        padded = with_halo(courant_sq * adj_now, (("depth", 1),), 2)
        adj_new = 2.0 * adj_now - adj_later + laplace(padded)
        adj_new = inject(adj_new, rec_cells, misfits[step], first_plane)
        gradient = gradient + jnp.sum(adj_new * laplacians[step], axis=0)
        adj_later, adj_now = (adj_now, adj_new)
    depths = (first_plane + jnp.arange(planes)).astype(jnp.float32)
    weight = (1.0 + 2.0 * depths / (total_planes - 1))[:, None, None]
    share_rows = rows_x // lax.axis_size("shot")
    offset = lax.axis_index("shot") * share_rows
    moment_share = lax.dynamic_slice_in_dim(momentum, offset, share_rows, 1)
    gradient = lax.psum(gradient, "shot")
    scaled = weight * gradient
    scaled_share = lax.dynamic_slice_in_dim(scaled, offset, share_rows, 1)
    factor, kinetic = statistics(scaled_share, moment_share, weight, cells_all)
    momentum_half = momentum - 0.5 * factor * scaled
    return (momentum_half, kinetic)


def interleave(dst, dst_at, src, src_at, rows, factor=None):
    groups = rows // 8
    for i in range(groups):
        value = src[(*src_at, pl.ds(i, 8, stride=groups), slice(None))]
        if factor is not None:
            value = value * factor
        dst[(*dst_at, pl.ds(i * 8, 8), slice(None))] = value


def lap12(field, z):
    center = field[z + 2]
    rows, lanes = center.shape
    sub = lax.broadcasted_iota(jnp.int32, (8, lanes), 0)
    lane = lax.broadcasted_iota(jnp.int32, (rows, lanes), 1)

    def later(block):
        return jnp.where(sub < 7, pltpu.roll(block, 7, 0), 0.0)

    def earlier(block):
        return jnp.where(sub > 0, pltpu.roll(block, 1, 0), 0.0)

    first, second = center[0:8], center[8:16]
    last, before = center[rows - 8 :], center[rows - 16 : rows - 8]
    late = later(first)
    early = earlier(last)
    near = jnp.concatenate([center[8:], late], 0) + jnp.concatenate([early, center[:-8]], 0)
    far = jnp.concatenate([center[16:], late, later(second)], 0) + jnp.concatenate(
        [earlier(before), early, center[:-16]], 0
    )
    near = near + (field[z + 1] + field[z + 3])
    far = far + (field[z] + field[z + 4])
    near = near + jnp.where(lane >= 1, pltpu.roll(center, 1, 1), 0.0)
    near = near + jnp.where(lane < lanes - 1, pltpu.roll(center, lanes - 1, 1), 0.0)
    far = far + jnp.where(lane >= 2, pltpu.roll(center, 2, 1), 0.0)
    far = far + jnp.where(lane < lanes - 2, pltpu.roll(center, lanes - 2, 1), 0.0)
    return center, 16.0 * near - far - 90.0 * center


def scatter_kernel(row_ref, y_ref, obs_ref, out_ref, spread):
    receivers, steps = obs_ref.shape
    lanes = out_ref.shape[2]
    tile = out_ref.shape[1]

    @pl.when(pl.program_id(0) == 0)
    def _():
        lane = lax.broadcasted_iota(jnp.int32, (receivers, lanes), 1)
        at = lane == y_ref[...]
        for k in range(steps):
            column = obs_ref[:, k : k + 1]
            high = column.astype(jnp.bfloat16).astype(jnp.float32)
            low = column - high
            cols = pl.ds(k * lanes, lanes)
            spread[0, :, cols] = jnp.where(at, high, 0.0).astype(jnp.bfloat16)
            spread[1, :, cols] = jnp.where(at, low, 0.0).astype(jnp.bfloat16)
        cols = pl.ds(steps * lanes, lanes)
        spread[0, :, cols] = jnp.where(at, 1.0, 0.0).astype(jnp.bfloat16)
        spread[1, :, cols] = jnp.zeros((receivers, lanes), jnp.bfloat16)

    ids = lax.broadcasted_iota(jnp.int32, (tile, receivers), 0) + pl.program_id(0) * tile
    chosen = jnp.where(ids == row_ref[...], 1.0, 0.0).astype(jnp.bfloat16)
    total = jnp.dot(chosen, spread[0], preferred_element_type=jnp.float32)
    total = total + jnp.dot(chosen, spread[1], preferred_element_type=jnp.float32)
    for k in range(steps + 1):
        out_ref[k] = total[:, k * lanes : (k + 1) * lanes]


def scatter(cells, observed, planes_all, rows_x, rows_y):
    steps, receivers = observed.shape
    groups = rows_x // 8
    x = (cells // rows_y) % rows_x
    row = (cells // (rows_x * rows_y)) * rows_x + (x % groups) * 8 + x // groups
    lanes = cells % rows_y
    rows_all = planes_all * rows_x
    tile = 256
    return pl.pallas_call(
        scatter_kernel,
        grid=(rows_all // tile,),
        in_specs=[
            pl.BlockSpec((1, receivers), lambda t: (0, 0)),
            pl.BlockSpec((receivers, 1), lambda t: (0, 0)),
            pl.BlockSpec((receivers, steps), lambda t: (0, 0)),
        ],
        out_specs=pl.BlockSpec((steps + 1, tile, rows_y), lambda t: (0, t, 0)),
        out_shape=jax.ShapeDtypeStruct((steps + 1, rows_all, rows_y), jnp.float32),
        scratch_shapes=[pltpu.VMEM((2, receivers, (steps + 1) * rows_y), jnp.bfloat16)],
        compiler_params=pltpu.CompilerParams(vmem_limit_bytes=32 * 2**20),
        cost_estimate=pl.CostEstimate(
            flops=4 * rows_all * receivers * (steps + 1) * rows_y,
            bytes_accessed=4 * (steps + 1) * rows_all * rows_y,
            transcendentals=0,
        ),
        name="receiver_scatter",
    )(row[None, :], lanes[:, None], observed.T)


def load_blocks(meta, blocks, first, second, planes, rows):
    ends = first.shape[0]
    for field in (first, second):
        for z in (0, 1, ends - 2, ends - 1):
            field[z] = jnp.zeros(field.shape[1:], jnp.float32)
    for b, block in enumerate(blocks):

        @pl.loop(0, planes)
        def _(p):
            z = meta[b] + p + 2
            interleave(first, (z,), block, (0, p), rows)
            interleave(second, (z,), block, (1, p), rows)


BATCH = 4


def for_owned(meta, planes, body):
    for owned in (True, False):
        core = meta[4] if owned else 1 - meta[4]

        @pl.loop(0, 2 * planes // BATCH)
        def _(index):
            chip, p = index // (planes // BATCH), (index % (planes // BATCH)) * BATCH
            z = (2 * chip + core) * planes + p
            body(z, chip if owned else None, p)


def forward_kernel(
    meta, wave, own, mate, over, far, c0, c1, c2, c3, obs, count, lap_ref, inject_ref, cour_ref, even, odd
):
    pair = pl.program_id(0)
    planes, rows, lanes = c0.shape

    @pl.when(pair == 0)
    def _():
        load_blocks(meta, (own, mate, over, far), odd, even, planes, rows)
        for b, block in enumerate((c0, c1, c2, c3)):

            @pl.loop(0, planes)
            def _(p):
                interleave(cour_ref, (meta[b] + p,), block, (p,), rows, 1.0 / 12.0)

    for half, now, then in ((0, even, odd), (1, odd, even)):

        def body(z, chip, p):
            olds = [then[z + j + 2] for j in range(BATCH)]
            for j, old in enumerate(olds):
                center, lap = lap12(now, z + j)
                if chip is not None:
                    lap_ref[half, p + j, chip] = lap
                newer = 2.0 * center - old + cour_ref[z + j] * lap
                then[z + j + 2] = newer
                inject_ref[half, z + j] = obs[half, z + j] - count[0, z + j] * newer

        for_owned(meta, planes, body)

        z, row, lane = meta[5], pl.multiple_of(meta[6], 8), meta[8]
        here = (lax.broadcasted_iota(jnp.int32, (8, lanes), 0) == meta[7]) & (
            lax.broadcasted_iota(jnp.int32, (8, lanes), 1) == lane
        )
        strength = jnp.where(here, 12.0 * wave[2 * pair + half], 0.0)
        tile = pl.ds(row, 8)
        slab, p = z // planes, lax.rem(z, planes)

        @pl.when(lax.rem(slab, 2) == meta[4])
        def _():
            lap_ref[half, p, slab // 2, tile, :] += strength

        moved = cour_ref[z, tile, :] * strength
        then[z + 2, tile, :] += moved
        inject_ref[half, z, tile, :] -= count[0, z, tile, :] * moved


def adjoint_kernel(meta, own, mate, over, far, cour, lap_ref, inject, grad_ref, even, odd, total):
    pair = pl.program_id(0)
    planes, rows, lanes = own.shape[1:]
    groups = rows // 8

    @pl.when(pair == 0)
    def _():
        load_blocks(meta, (own, mate, over, far), odd, even, planes, rows)

        @pl.loop(0, 4 * planes)
        def _(z):
            even[z + 2] = even[z + 2] * cour[z]
            odd[z + 2] = odd[z + 2] * cour[z]

        @pl.loop(0, 2 * planes)
        def _(index):
            total[index] = jnp.zeros((rows, lanes), jnp.float32)

    for half, now, then in ((1, even, odd), (0, odd, even)):

        def body(z, chip, p):
            olds = [then[z + j + 2] for j in range(BATCH)]
            if chip is not None:
                sums = [total[chip * planes + p + j] for j in range(BATCH)]
            for j, old in enumerate(olds):
                center, lap = lap12(now, z + j)
                newer = 2.0 * center - old + cour[z + j] * (lap - inject[half, z + j])
                then[z + j + 2] = newer
                if chip is not None:
                    total[chip * planes + p + j] = sums[j] + newer * lap_ref[half, p + j, chip]

        for_owned(meta, planes, body)

    @pl.when(pair == pl.num_programs(0) - 1)
    def _():
        @pl.loop(0, 2 * planes)
        def _(index):
            chip, p = index // planes, index % planes
            z = (2 * chip + meta[4]) * planes + p
            value = total[index] / (12.0 * cour[z])
            for i in range(groups):
                grad_ref[p, chip, pl.ds(i, 8, stride=groups), :] = value[i * 8 : (i + 1) * 8]


def whole_shards(
    courant_sq, momentum, fwd_prev, fwd_cur, adj_next, adj_cur, observed, src_cells, rec_cells, ckpt_step
):
    _, planes, rows_x, rows_y = fwd_cur.shape
    steps = observed.shape[1]
    chip, core = lax.axis_index("chip"), lax.axis_index("core")
    groups = rows_x // 8
    planes_all = 4 * planes
    cells_all = planes_all * rows_x * rows_y
    swap = [(0, 1), (1, 0)]

    def pick(pair, shot):
        return jnp.stack([lax.dynamic_index_in_dim(f, shot, 0, keepdims=False) for f in pair])

    forward = (fwd_prev, fwd_cur)
    adjoint = (adj_next, adj_cur)
    c2 = lax.ppermute(courant_sq, "chip", swap)
    over = lax.ppermute(pick(forward, 1 - chip), "chip", swap)
    own = pick(forward, chip)
    mate = lax.ppermute(own, "core", swap)
    c1 = lax.ppermute(courant_sq, "core", swap)

    cells = lax.dynamic_index_in_dim(rec_cells, chip, 0, keepdims=False)
    traces = lax.dynamic_index_in_dim(observed, chip, 0, keepdims=False)
    placed = scatter(cells, traces, planes_all, rows_x, rows_y)
    placed = placed.reshape(steps + 1, planes_all, rows_x, rows_y)

    over, c2, placed, to_send = lax.optimization_barrier((over, c2, placed, pick(adjoint, 1 - chip)))
    far = lax.ppermute(over, "core", swap)
    c3 = lax.ppermute(c2, "core", swap)
    adj_over = lax.ppermute(to_send, "chip", swap)
    adj_own = pick(adjoint, chip)
    adj_mate = lax.ppermute(adj_own, "core", swap)

    source = lax.dynamic_index_in_dim(src_cells, chip, 0, keepdims=False)
    x = (source // rows_y) % rows_x
    slabs = [2 * chip + core, 2 * chip + 1 - core, 2 * (1 - chip) + core, 2 * (1 - chip) + 1 - core]
    meta = jnp.stack(
        [slab * planes for slab in slabs]
        + [core, source // (rows_x * rows_y), (x % groups) * 8, x // groups, source % rows_y]
    ).astype(jnp.int32)
    wave = jnp.stack([wave_value(ckpt_step, k) for k in range(steps)])

    field_block = pl.BlockSpec((2, planes, rows_x, rows_y), lambda k: (0, 0, 0, 0))
    slab_block = pl.BlockSpec((planes, rows_x, rows_y), lambda k: (0, 0, 0))
    whole_block = pl.BlockSpec((planes_all, rows_x, rows_y), lambda k: (0, 0, 0))
    step_block = pl.BlockSpec((2, planes_all, rows_x, rows_y), lambda k: (k, 0, 0, 0))
    count_block = pl.BlockSpec((1, planes_all, rows_x, rows_y), lambda k: (steps, 0, 0, 0))
    lap_shape = (planes, 2, rows_x, rows_y)
    smem = pl.BlockSpec(memory_space=pltpu.SMEM)
    scratch = pltpu.VMEM((planes_all + 4, rows_x, rows_y), jnp.float32)
    params = pltpu.CompilerParams(vmem_limit_bytes=48 * 2**20)
    cost = pl.CostEstimate(flops=30 * steps * cells_all, bytes_accessed=16 * steps * cells_all, transcendentals=0)
    laps, inject, cour = pl.pallas_call(
        forward_kernel,
        grid=(steps // 2,),
        in_specs=[smem, smem] + [field_block] * 4 + [slab_block] * 4 + [step_block, count_block],
        out_specs=[pl.BlockSpec((2, *lap_shape), lambda k: (k, 0, 0, 0, 0)), step_block, whole_block],
        out_shape=[
            jax.ShapeDtypeStruct((steps, *lap_shape), jnp.float32),
            jax.ShapeDtypeStruct((steps, planes_all, rows_x, rows_y), jnp.float32),
            jax.ShapeDtypeStruct((planes_all, rows_x, rows_y), jnp.float32),
        ],
        scratch_shapes=[scratch, scratch],
        compiler_params=params,
        cost_estimate=cost,
        name="forward_steps",
    )(meta, wave, own, mate, over, far, courant_sq, c1, c2, c3, placed, placed)

    adj_over, laps = lax.optimization_barrier((adj_over, laps))
    adj_far = lax.ppermute(adj_over, "core", swap)
    back_block = pl.BlockSpec((2, planes_all, rows_x, rows_y), lambda k: (steps // 2 - 1 - k, 0, 0, 0))
    gradient = pl.pallas_call(
        adjoint_kernel,
        grid=(steps // 2,),
        in_specs=[smem]
        + [field_block] * 4
        + [whole_block, pl.BlockSpec((2, *lap_shape), lambda k: (steps // 2 - 1 - k, 0, 0, 0, 0)), back_block],
        out_specs=pl.BlockSpec(lap_shape, lambda k: (0, 0, 0, 0)),
        out_shape=jax.ShapeDtypeStruct(lap_shape, jnp.float32),
        scratch_shapes=[scratch, scratch, pltpu.VMEM((2 * planes, rows_x, rows_y), jnp.float32)],
        compiler_params=params,
        cost_estimate=cost,
        name="adjoint_steps",
    )(meta, adj_own, adj_mate, adj_over, adj_far, cour, laps, inject)

    shot = lax.axis_index("shot")
    first = (2 * chip + core) * planes
    depths = (first + jnp.arange(planes)).astype(jnp.float32)
    weights = 1.0 + 2.0 * depths / (planes_all - 1)
    parts = gradient.reshape(2 * planes, rows_x, rows_y)
    parts = lax.all_to_all(parts, ("shot", "chip"), 0, 0, tiled=True)
    weight = lax.dynamic_index_in_dim(weights, shot, 0)
    scaled = weight * jnp.sum(parts, axis=0)
    moment = lax.dynamic_index_in_dim(momentum, shot, 0, keepdims=False)
    sums = jnp.stack(
        [
            jnp.sum(scaled * scaled),
            jnp.sum(weight * moment * moment),
            jnp.sum(weight * moment * scaled),
            jnp.sum(weight * scaled * scaled),
        ]
    )
    carried = jnp.concatenate([scaled, jnp.broadcast_to(jnp.pad(sums, (0, 4))[:, None], (8, rows_y))], 0)
    spread = jnp.broadcast_to(carried[None], (planes, rows_x + 8, rows_y))
    spread = lax.all_to_all(spread, "shot", 0, 0, tiled=True)
    scaled = spread[:, :rows_x]
    sums = jnp.sum(spread[:, rows_x:], axis=0)
    sums = lax.all_to_all(jnp.broadcast_to(sums[None], (4, 8, rows_y)), ("chip", "core"), 0, 0, tiled=True)
    sums = jnp.sum(sums, axis=0)[:, 0]
    factor = lax.rsqrt(sums[0] / cells_all + EPSILON)
    kinetic = 0.5 * (sums[1] - factor * sums[2] + 0.25 * factor * factor * sums[3]) / cells_all
    return momentum - 0.5 * factor * scaled, kinetic


def solution(mesh):
    shots, slabs = mesh.shape["shot"], mesh.shape["depth"]

    def placed(depth):
        field = P("shot", depth, None, None)
        slab = P(depth, None, None)
        inputs = (slab, slab, field, field, field, field, P("shot", None, None), P("shot"), P("shot", None), P())
        return dict(in_specs=inputs, out_specs=(slab, P()), check_vma=False)

    slab_plan = jax.shard_map(slab_shards, mesh=mesh, **placed("depth"))
    if slabs != 4:
        return slab_plan
    chips = Mesh(mesh.devices.reshape(shots, 2, 2), ("shot", "chip", "core"))
    whole_plan = jax.shard_map(whole_shards, mesh=chips, **placed(("chip", "core")))

    def run(courant_sq, momentum, fwd_prev, *rest):
        total, planes, rows_x, rows_y = fwd_prev.shape
        fits = total == 2 * shots and planes == 4 * shots and rows_y == 128 and rows_x % 16 == 0 and planes % 8 == 0
        plan = whole_plan if fits else slab_plan
        return plan(courant_sq, momentum, fwd_prev, *rest)

    return run
```

```python
import functools

import jax
import jax.numpy as jnp
from jax import lax
from jax.experimental import pallas as pl
from jax.experimental.pallas import tpu as pltpu
from jax.sharding import Mesh
from jax.sharding import PartitionSpec as P

CENTER = -2.5
NEAR = 4.0 / 3.0
FAR = -1.0 / 12.0
AMPLITUDE = 100.0
EPSILON = 1e-06


def with_halo(value, sides, width):
    for axis, dim in sides:
        size, length = (lax.axis_size(axis), value.shape[dim])
        up = [(i, (i + 1) % size) for i in range(size - 1)]
        down = [(j, i) for i, j in up]
        last = lax.slice_in_dim(value, length - width, length, axis=dim)
        leading = lax.slice_in_dim(value, 0, width, axis=dim)
        before = lax.ppermute(last, axis, up)
        after = lax.ppermute(leading, axis, down)
        value = jnp.concatenate([before, value, after], axis=dim)
    return value


def laplace(padded):
    lateral = jnp.pad(padded[:, 2:-2], ((0, 0), (0, 0), (2, 2), (2, 2)))
    center = padded[:, 2:-2]
    along_z = NEAR * (padded[:, 1:-3] + padded[:, 3:-1]) + FAR * (padded[:, :-4] + padded[:, 4:])
    along_x = NEAR * (lateral[:, :, 1:-3, 2:-2] + lateral[:, :, 3:-1, 2:-2]) + FAR * (
        lateral[:, :, :-4, 2:-2] + lateral[:, :, 4:, 2:-2]
    )
    along_y = NEAR * (lateral[:, :, 2:-2, 1:-3] + lateral[:, :, 2:-2, 3:-1]) + FAR * (
        lateral[:, :, 2:-2, :-4] + lateral[:, :, 2:-2, 4:]
    )
    return 3.0 * CENTER * center + along_z + along_x + along_y


def locate(field, cell_ids, first_plane):
    shot_count, planes, rows_x, rows_y = field.shape
    plane_cells = rows_x * rows_y
    local_index = cell_ids - first_plane * plane_cells
    inside = (local_index >= 0) & (local_index < planes * plane_cells)
    target = jnp.where(inside, local_index, 0)
    return (inside, target)


def inject(field, cell_ids, values, first_plane):
    shot_count = field.shape[0]
    inside, target = locate(field, cell_ids, first_plane)
    amount = jnp.where(inside, values, jnp.zeros_like(values))
    flattened = field.reshape(shot_count, -1)
    lanes = jnp.arange(shot_count)[:, None]
    flattened = flattened.at[lanes, target].add(amount)
    return flattened.reshape(field.shape)


def sample(field, cell_ids, first_plane):
    shot_count = field.shape[0]
    inside, target = locate(field, cell_ids, first_plane)
    values = jnp.take_along_axis(field.reshape(shot_count, -1), target, axis=1)
    return jnp.where(inside, values, jnp.zeros_like(values))


def wave_value(start, step):
    cycle = jnp.mod(start + jnp.int32(step), jnp.int32(48))
    phase = (cycle.astype(jnp.float32) - 24.0) / 12.0
    return AMPLITUDE * (1.0 - 2.0 * phase * phase) * jnp.exp(-phase * phase)


def statistics(scaled, moment, weight, cells_all):
    grand_total = lax.psum(jnp.sum(scaled * scaled), ("shot", "depth"))
    factor = lax.rsqrt(grand_total / cells_all + EPSILON)
    halfway = moment - 0.5 * factor * scaled
    energy = lax.psum(jnp.sum(weight * halfway * halfway), ("shot", "depth"))
    return (factor, 0.5 * energy / cells_all)


def slab_shards(
    courant_sq,
    momentum,
    fwd_prev,
    fwd_cur,
    adj_next,
    adj_cur,
    observed,
    src_cells,
    rec_cells,
    ckpt_step,
):
    shot_count, planes, rows_x, rows_y = fwd_cur.shape
    steps_all = observed.shape[1]
    first_plane = lax.axis_index("depth") * planes
    total_planes = planes * lax.axis_size("depth")
    cells_all = total_planes * rows_x * rows_y
    sources = src_cells[:, None]
    older, current = (fwd_prev, fwd_cur)
    laplacians = []
    misfits = []
    for step in range(steps_all):
        padded = with_halo(current, (("depth", 1),), 2)
        strength = jnp.full(sources.shape, wave_value(ckpt_step, step), jnp.float32)
        laplacian = inject(laplace(padded), sources, strength, first_plane)
        newer = 2.0 * current - older + courant_sq * laplacian
        misfits.append(sample(newer, rec_cells, first_plane) - observed[:, step, :])
        laplacians.append(laplacian)
        older, current = (current, newer)
    adj_later, adj_now = (adj_next, adj_cur)
    gradient = jnp.zeros((planes, rows_x, rows_y), jnp.float32)
    for step in reversed(range(steps_all)):
        padded = with_halo(courant_sq * adj_now, (("depth", 1),), 2)
        adj_new = 2.0 * adj_now - adj_later + laplace(padded)
        adj_new = inject(adj_new, rec_cells, misfits[step], first_plane)
        gradient = gradient + jnp.sum(adj_new * laplacians[step], axis=0)
        adj_later, adj_now = (adj_now, adj_new)
    depths = (first_plane + jnp.arange(planes)).astype(jnp.float32)
    weight = (1.0 + 2.0 * depths / (total_planes - 1))[:, None, None]
    share_rows = rows_x // lax.axis_size("shot")
    offset = lax.axis_index("shot") * share_rows
    moment_share = lax.dynamic_slice_in_dim(momentum, offset, share_rows, 1)
    gradient = lax.psum(gradient, "shot")
    scaled = weight * gradient
    scaled_share = lax.dynamic_slice_in_dim(scaled, offset, share_rows, 1)
    factor, kinetic = statistics(scaled_share, moment_share, weight, cells_all)
    momentum_half = momentum - 0.5 * factor * scaled
    return (momentum_half, kinetic)


def interleave(dst, dst_at, src, src_at, rows, factor=None):
    groups = rows // 8
    for i in range(groups):
        value = src[(*src_at, pl.ds(i, 8, stride=groups), slice(None))]
        if factor is not None:
            value = value * factor
        dst[(*dst_at, pl.ds(i * 8, 8), slice(None))] = value


def band(lanes):
    near = jnp.abs(lax.broadcasted_iota(jnp.int32, (2 * lanes, lanes), 0) % lanes - lax.broadcasted_iota(jnp.int32, (2 * lanes, lanes), 1))
    return jnp.where(near == 0, -90.0, jnp.where(near == 1, 16.0, jnp.where(near == 2, -1.0, 0.0))).astype(jnp.bfloat16)


def laps12(field, z, banded):
    rows, lanes = field.shape[1:]
    sub = lax.broadcasted_iota(jnp.int32, (8, lanes), 0)

    def later(block):
        return jnp.where(sub < 7, pltpu.roll(block, 7, 0), 0.0)

    def earlier(block):
        return jnp.where(sub > 0, pltpu.roll(block, 1, 0), 0.0)

    whole = field[pl.ds(z + 2, BATCH)].reshape(BATCH * rows, lanes)
    high = whole.astype(jnp.bfloat16)
    low = (whole - high.astype(jnp.float32)).astype(jnp.bfloat16)
    along_y = jnp.dot(jnp.concatenate([high, low], 1), banded, preferred_element_type=jnp.float32)
    results = []
    for j in range(BATCH):
        center = field[z + j + 2]
        first, second = center[0:8], center[8:16]
        last, before = center[rows - 8 :], center[rows - 16 : rows - 8]
        late, early = later(first), earlier(last)
        near = jnp.concatenate([center[8:], late], 0) + jnp.concatenate([early, center[:-8]], 0)
        far = jnp.concatenate([center[16:], late, later(second)], 0) + jnp.concatenate(
            [earlier(before), early, center[:-16]], 0
        )
        near = near + (field[z + j + 1] + field[z + j + 3])
        far = far + (field[z + j] + field[z + j + 4])
        results.append((center, 16.0 * near - far + along_y[j * rows : (j + 1) * rows]))
    return results


def scatter_kernel(row_ref, y_ref, obs_ref, out_ref, spread):
    receivers, steps = obs_ref.shape
    lanes = out_ref.shape[2]
    tile = out_ref.shape[1]

    @pl.when(pl.program_id(0) == 0)
    def _():
        lane = lax.broadcasted_iota(jnp.int32, (receivers, lanes), 1)
        at = lane == y_ref[...]
        for k in range(steps):
            column = obs_ref[:, k : k + 1]
            high = column.astype(jnp.bfloat16).astype(jnp.float32)
            low = column - high
            cols = pl.ds(k * lanes, lanes)
            spread[0, :, cols] = jnp.where(at, high, 0.0).astype(jnp.bfloat16)
            spread[1, :, cols] = jnp.where(at, low, 0.0).astype(jnp.bfloat16)
        cols = pl.ds(steps * lanes, lanes)
        spread[0, :, cols] = jnp.where(at, 1.0, 0.0).astype(jnp.bfloat16)
        spread[1, :, cols] = jnp.zeros((receivers, lanes), jnp.bfloat16)

    ids = lax.broadcasted_iota(jnp.int32, (tile, receivers), 0) + pl.program_id(0) * tile
    chosen = jnp.where(ids == row_ref[...], 1.0, 0.0).astype(jnp.bfloat16)
    total = jnp.dot(chosen, spread[0], preferred_element_type=jnp.float32)
    total = total + jnp.dot(chosen, spread[1], preferred_element_type=jnp.float32)
    for k in range(steps + 1):
        out_ref[k] = total[:, k * lanes : (k + 1) * lanes]


def scatter(cells, observed, planes_all, rows_x, rows_y):
    steps, receivers = observed.shape
    groups = rows_x // 8
    x = (cells // rows_y) % rows_x
    row = (cells // (rows_x * rows_y)) * rows_x + (x % groups) * 8 + x // groups
    lanes = cells % rows_y
    rows_all = planes_all * rows_x
    tile = 256
    return pl.pallas_call(
        scatter_kernel,
        grid=(rows_all // tile,),
        in_specs=[
            pl.BlockSpec((1, receivers), lambda t: (0, 0)),
            pl.BlockSpec((receivers, 1), lambda t: (0, 0)),
            pl.BlockSpec((receivers, steps), lambda t: (0, 0)),
        ],
        out_specs=pl.BlockSpec((steps + 1, tile, rows_y), lambda t: (0, t, 0)),
        out_shape=jax.ShapeDtypeStruct((steps + 1, rows_all, rows_y), jnp.float32),
        scratch_shapes=[pltpu.VMEM((2, receivers, (steps + 1) * rows_y), jnp.bfloat16)],
        compiler_params=pltpu.CompilerParams(vmem_limit_bytes=32 * 2**20),
        cost_estimate=pl.CostEstimate(
            flops=4 * rows_all * receivers * (steps + 1) * rows_y,
            bytes_accessed=4 * (steps + 1) * rows_all * rows_y,
            transcendentals=0,
        ),
        name="receiver_scatter",
    )(row[None, :], lanes[:, None], observed.T)


def place(planes):
    chip, core = lax.axis_index("chip"), lax.axis_index("core")
    slabs = (2 * chip + core, 2 * chip + 1 - core, 2 * (1 - chip) + core, 2 * (1 - chip) + 1 - core)
    return chip, core, [slab * planes for slab in slabs]


def load_blocks(slabs, blocks, first, second, planes, rows):
    ends = first.shape[0]
    for field in (first, second):
        for z in (0, 1, ends - 2, ends - 1):
            field[z] = jnp.zeros(field.shape[1:], jnp.float32)
    for slab, block in zip(slabs, blocks):

        @pl.loop(0, planes)
        def _(p):
            z = slab + p + 2
            interleave(first, (z,), block, (0, p), rows)
            interleave(second, (z,), block, (1, p), rows)


BATCH = 4


def for_owned(mine, planes, body):
    for owned in (True, False):
        core = mine if owned else 1 - mine

        @pl.loop(0, 2 * planes // BATCH)
        def _(index):
            chip, p = index // (planes // BATCH), (index % (planes // BATCH)) * BATCH
            z = (2 * chip + core) * planes + p
            body(z, chip if owned else None, p)


def forward_kernel(
    start, sources, own, mate, over, far, c0, c1, c2, c3, obs, count, lap_ref, inject_ref, cour_ref, even, odd, banded
):
    pair = pl.program_id(0)
    planes, rows, lanes = c0.shape
    groups = rows // 8
    chip, core, slabs = place(planes)

    @pl.when(pair == 0)
    def _():
        banded[...] = band(lanes)
        load_blocks(slabs, (own, mate, over, far), odd, even, planes, rows)
        for slab, block in zip(slabs, (c0, c1, c2, c3)):

            @pl.loop(0, planes)
            def _(p):
                interleave(cour_ref, (slab + p,), block, (p,), rows, 1.0 / 12.0)

    for half, now, then in ((0, even, odd), (1, odd, even)):

        def body(z, chip, p):
            olds = [then[z + j + 2] for j in range(BATCH)]
            for j, (center, lap) in enumerate(laps12(now, z, banded[...])):
                old = olds[j]
                if chip is not None:
                    lap_ref[half, p + j, chip] = lap
                newer = 2.0 * center - old + cour_ref[z + j] * lap
                then[z + j + 2] = newer
                inject_ref[half, z + j] = obs[half, z + j] - count[0, z + j] * newer

        for_owned(core, planes, body)

        cell = sources[chip]
        z, x, lane = cell // (rows * lanes), cell // lanes % rows, cell % lanes
        row = pl.multiple_of(x % groups * 8, 8)
        here = (lax.broadcasted_iota(jnp.int32, (8, lanes), 0) == x // groups) & (
            lax.broadcasted_iota(jnp.int32, (8, lanes), 1) == lane
        )
        cycle = (start[0] + 2 * pair + half) % 48
        phase = (jnp.full((8, lanes), cycle, jnp.int32).astype(jnp.float32) - 24.0) / 12.0
        wave = AMPLITUDE * (1.0 - 2.0 * phase * phase) * jnp.exp(-phase * phase)
        strength = jnp.where(here, 12.0 * wave, 0.0)
        tile = pl.ds(row, 8)
        slab, p = z // planes, lax.rem(z, planes)

        @pl.when(lax.rem(slab, 2) == core)
        def _():
            lap_ref[half, p, slab // 2, tile, :] += strength

        moved = cour_ref[z, tile, :] * strength
        then[z + 2, tile, :] += moved
        inject_ref[half, z, tile, :] -= count[0, z, tile, :] * moved


def adjoint_kernel(own, mate, over, far, cour, lap_ref, inject, keep_ref, send_ref, even, odd, total, banded):
    pair = pl.program_id(0)
    planes, rows, lanes = own.shape[1:]
    groups = rows // 8
    chip_here, core, slabs = place(planes)

    @pl.when(pair == 0)
    def _():
        banded[...] = band(lanes)
        load_blocks(slabs, (own, mate, over, far), odd, even, planes, rows)

        @pl.loop(0, 4 * planes)
        def _(z):
            even[z + 2] = even[z + 2] * cour[z]
            odd[z + 2] = odd[z + 2] * cour[z]

        @pl.loop(0, 2 * planes)
        def _(index):
            total[index] = jnp.zeros((rows, lanes), jnp.float32)

    for half, now, then in ((1, even, odd), (0, odd, even)):

        def body(z, chip, p):
            olds = [then[z + j + 2] for j in range(BATCH)]
            if chip is not None:
                sums = [total[chip * planes + p + j] for j in range(BATCH)]
            for j, (center, lap) in enumerate(laps12(now, z, banded[...])):
                old = olds[j]
                newer = 2.0 * center - old + cour[z + j] * (lap - inject[half, z + j])
                then[z + j + 2] = newer
                if chip is not None:
                    total[chip * planes + p + j] = sums[j] + newer * lap_ref[half, p + j, chip]

        for_owned(core, planes, body)

    @pl.when(pair == pl.num_programs(0) - 1)
    def _():
        for ref, chip in ((keep_ref, chip_here), (send_ref, 1 - chip_here)):

            @pl.loop(0, planes)
            def _(p):
                z = (2 * chip + core) * planes + p
                weight = 1.0 + 2.0 * jnp.full((rows, lanes), z, jnp.int32).astype(jnp.float32) / (4 * planes - 1)
                value = weight * total[chip * planes + p] / (12.0 * cour[z])
                for i in range(groups):
                    ref[p, pl.ds(i, 8, stride=groups), :] = value[i * 8 : (i + 1) * 8]


def halve_kernel(mine, other, keep, send):
    y = lax.axis_index("shot") % 2
    count = keep.shape[0]
    for ref, half in ((keep, y), (send, 1 - y)):
        for p in range(count):
            ref[p] = mine[half * count + p] + other[half * count + p]


def quarter_kernel(mine, other, *parts):
    z = lax.axis_index("shot") // 2
    for j, ref in enumerate(parts):
        at = flip(z, j)
        ref[...] = mine[at] + other[at]


def flip(index, bits):
    result = index
    for bit in (1, 2):
        if bits & bit:
            result = jnp.where(index // bit % 2 == 1, result - bit, result + bit)
    return result


def arrange_kernel(mine, other, out):
    shot = lax.axis_index("shot")
    z, y = shot // 2, shot % 2
    quarter = mine.shape[0]
    for part, half in ((mine, y), (other, 1 - y)):
        for j in range(quarter):
            out[half * quarter + flip(z, j)] = part[j]


def sums_kernel(p0, p1, p2, p3, momentum, out):
    rows, lanes = p0.shape
    shot = lax.axis_index("shot")
    chip, core = lax.axis_index("chip"), lax.axis_index("core")
    planes = momentum.shape[0]
    at = (shot % 2) * (planes // 2) + shot // 2
    z = (2 * chip + core) * planes + at
    scaled = (p0[...] + p1[...]) + (p2[...] + p3[...])
    weight = 1.0 + 2.0 * jnp.full((1, lanes), z, jnp.int32).astype(jnp.float32) / (4 * planes - 1)
    moment = momentum[at]

    def total(value):
        by_lane = jnp.sum(value, axis=0, keepdims=True)
        return jnp.broadcast_to(jnp.sum(by_lane, axis=1, keepdims=True), (1, lanes))

    square = total(scaled * scaled)
    out[0:rows] = scaled
    out[rows : rows + 8] = jnp.concatenate(
        [
            square,
            weight * total(moment * moment),
            weight * total(moment * scaled),
            weight * square,
            jnp.zeros((4, lanes), jnp.float32),
        ],
        0,
    )


def add_sums_kernel(mine, other, out):
    rows = mine.shape[1] - 8
    total = jnp.zeros(out.shape, jnp.float32)
    for j in range(mine.shape[0]):
        total = total + (mine[j, rows:] + other[j, rows:])
    out[...] = total


def finish_kernel(mine, other, momentum, s0, s1, s2, s3, out, kinetic):
    quarter, rows, lanes = mine.shape
    rows = rows - 8
    cells = 4.0 * momentum.shape[0] * rows * lanes
    shot = lax.axis_index("shot")
    z, y = shot // 2, shot % 2
    sums = (s0[...] + s1[...]) + (s2[...] + s3[...])
    factor = lax.rsqrt(sums[0:1] / cells + EPSILON)
    energy = 0.5 * (sums[1:2] - factor * sums[2:3] + 0.25 * factor * factor * sums[3:4]) / cells
    kinetic[0] = energy[0, 0]
    step = 0.5 * factor
    for part, half in ((mine, y), (other, 1 - y)):
        for j in range(quarter):
            at = half * quarter + flip(z, j)
            out[at] = momentum[at] - step * part[j, 0:rows]


def local(kernel, outs, *arrays):
    vmem = pl.BlockSpec(memory_space=pltpu.VMEM)
    shapes = [jax.ShapeDtypeStruct(shape, jnp.float32) for shape in outs]
    single = len(outs) == 1
    return pl.pallas_call(
        kernel,
        in_specs=[vmem] * len(arrays),
        out_specs=vmem if single else [vmem] * len(outs),
        out_shape=shapes[0] if single else shapes,
        compiler_params=pltpu.CompilerParams(vmem_limit_bytes=8 * 2**20),
        name=kernel.__name__,
    )(*arrays)


def exchange(value, axes, sizes, bits):
    return lax.ppermute(value, axes, [(i, i ^ bits) for i in range(sizes)])


def whole_shards(
    courant_sq, momentum, fwd_prev, fwd_cur, adj_next, adj_cur, observed, src_cells, rec_cells, ckpt_step
):
    _, planes, rows_x, rows_y = fwd_cur.shape
    steps = observed.shape[1]
    chip, core = lax.axis_index("chip"), lax.axis_index("core")
    groups = rows_x // 8
    planes_all = 4 * planes
    cells_all = planes_all * rows_x * rows_y
    swap = [(0, 1), (1, 0)]

    def pick(pair, shot):
        return jnp.stack([lax.dynamic_index_in_dim(f, shot, 0, keepdims=False) for f in pair])

    forward = (fwd_prev, fwd_cur)
    adjoint = (adj_next, adj_cur)
    shots = planes

    shot = lax.axis_index("shot")
    at = (shot % 2) * (planes // 2) + shot // 2
    piece = lax.ppermute(lax.dynamic_index_in_dim(courant_sq, at, 0), "chip", swap)
    outgoing = pick(forward, 1 - chip)
    over = lax.ppermute(outgoing, "chip", swap)
    outgoing, fwd_prev, fwd_cur = lax.optimization_barrier((outgoing, fwd_prev, fwd_cur))
    own = pick((fwd_prev, fwd_cur), chip)
    mate = lax.ppermute(own, "core", swap)
    c1 = lax.ppermute(courant_sq, "core", swap)
    pieces = [piece] + [exchange(piece, "shot", shots, 2 * j) for j in (1, 2, 3)]
    quarter = jnp.concatenate(pieces, 0)
    other = exchange(quarter, "shot", shots, 1)
    c2 = local(arrange_kernel, [courant_sq.shape], quarter, other)

    cells = lax.dynamic_index_in_dim(rec_cells, chip, 0, keepdims=False)
    traces = lax.dynamic_index_in_dim(observed, chip, 0, keepdims=False)
    placed = scatter(cells, traces, planes_all, rows_x, rows_y)
    placed = placed.reshape(steps + 1, planes_all, rows_x, rows_y)

    c3 = lax.ppermute(c2, "core", swap)
    over, c3, placed, to_send = lax.optimization_barrier((over, c3, placed, pick(adjoint, 1 - chip)))
    far = lax.ppermute(over, "core", swap)
    adj_over = lax.ppermute(to_send, "chip", swap)
    adj_own = pick(adjoint, chip)
    adj_mate = lax.ppermute(adj_own, "core", swap)

    field_block = pl.BlockSpec((2, planes, rows_x, rows_y), lambda k: (0, 0, 0, 0))
    slab_block = pl.BlockSpec((planes, rows_x, rows_y), lambda k: (0, 0, 0))
    whole_block = pl.BlockSpec((planes_all, rows_x, rows_y), lambda k: (0, 0, 0))
    step_block = pl.BlockSpec((2, planes_all, rows_x, rows_y), lambda k: (k, 0, 0, 0))
    count_block = pl.BlockSpec((1, planes_all, rows_x, rows_y), lambda k: (steps, 0, 0, 0))
    lap_shape = (planes, 2, rows_x, rows_y)
    smem = pl.BlockSpec(memory_space=pltpu.SMEM)
    scratch = pltpu.VMEM((planes_all + 4, rows_x, rows_y), jnp.float32)
    band_scratch = pltpu.VMEM((2 * rows_y, rows_y), jnp.bfloat16)
    params = pltpu.CompilerParams(vmem_limit_bytes=28 * 2**20)
    cost = pl.CostEstimate(flops=30 * steps * cells_all, bytes_accessed=16 * steps * cells_all, transcendentals=0)
    laps, inject, cour = pl.pallas_call(
        forward_kernel,
        grid=(steps // 2,),
        in_specs=[smem, smem] + [field_block] * 4 + [slab_block] * 4 + [step_block, count_block],
        out_specs=[pl.BlockSpec((2, *lap_shape), lambda k: (k, 0, 0, 0, 0)), step_block, whole_block],
        out_shape=[
            jax.ShapeDtypeStruct((steps, *lap_shape), jnp.float32),
            jax.ShapeDtypeStruct((steps, planes_all, rows_x, rows_y), jnp.float32),
            jax.ShapeDtypeStruct((planes_all, rows_x, rows_y), jnp.float32),
        ],
        scratch_shapes=[scratch, scratch, band_scratch],
        compiler_params=params,
        cost_estimate=cost,
        name="forward_steps",
    )(ckpt_step[None], src_cells, own, mate, over, far, courant_sq, c1, c2, c3, placed, placed)

    adj_over, laps = lax.optimization_barrier((adj_over, laps))
    adj_far = lax.ppermute(adj_over, "core", swap)
    back_block = pl.BlockSpec((2, planes_all, rows_x, rows_y), lambda k: (steps // 2 - 1 - k, 0, 0, 0))
    keep, send = pl.pallas_call(
        adjoint_kernel,
        grid=(steps // 2,),
        in_specs=[field_block] * 4
        + [whole_block, pl.BlockSpec((2, *lap_shape), lambda k: (steps // 2 - 1 - k, 0, 0, 0, 0)), back_block],
        out_specs=[slab_block, slab_block],
        out_shape=[jax.ShapeDtypeStruct((planes, rows_x, rows_y), jnp.float32)] * 2,
        scratch_shapes=[scratch, scratch, pltpu.VMEM((2 * planes, rows_x, rows_y), jnp.float32), band_scratch],
        compiler_params=params,
        cost_estimate=cost,
        name="adjoint_steps",
    )(adj_own, adj_mate, adj_over, adj_far, cour, laps, inject)

    plane = (rows_x, rows_y)
    received = lax.ppermute(send, "chip", swap)
    keep, send = local(halve_kernel, [(planes // 2, *plane)] * 2, keep, received)
    received = exchange(send, "shot", shots, 1)
    parts = local(quarter_kernel, [plane] * 4, keep, received)
    parts = [parts[0]] + [exchange(parts[j], "shot", shots, 2 * j) for j in (1, 2, 3)]
    summed = local(sums_kernel, [(rows_x + 8, rows_y)], *parts, momentum)
    quarter = jnp.stack([summed] + [exchange(summed, "shot", shots, 2 * j) for j in (1, 2, 3)])
    other = exchange(quarter, "shot", shots, 1)
    sums = local(add_sums_kernel, [(8, rows_y)], quarter, other)
    depth = ("chip", "core")
    all_sums = [sums] + [exchange(sums, depth, 4, bits) for bits in (1, 2, 3)]
    vmem = pl.BlockSpec(memory_space=pltpu.VMEM)
    momentum_half, kinetic = pl.pallas_call(
        finish_kernel,
        in_specs=[vmem] * 7,
        out_specs=[vmem, smem],
        out_shape=[jax.ShapeDtypeStruct(momentum.shape, jnp.float32), jax.ShapeDtypeStruct((1,), jnp.float32)],
        compiler_params=pltpu.CompilerParams(vmem_limit_bytes=8 * 2**20),
        name="finish",
    )(quarter, other, momentum, *all_sums)
    return momentum_half, kinetic[0]


def solution(mesh):
    shots, slabs = mesh.shape["shot"], mesh.shape["depth"]

    def placed(depth):
        field = P("shot", depth, None, None)
        slab = P(depth, None, None)
        inputs = (slab, slab, field, field, field, field, P("shot", None, None), P("shot"), P("shot", None), P())
        return dict(in_specs=inputs, out_specs=(slab, P()), check_vma=False)

    slab_plan = jax.shard_map(slab_shards, mesh=mesh, **placed("depth"))
    if slabs != 4 or shots != 8:
        return slab_plan
    chips = Mesh(mesh.devices.reshape(shots, 2, 2), ("shot", "chip", "core"))
    whole_plan = jax.shard_map(whole_shards, mesh=chips, **placed(("chip", "core")))

    def run(courant_sq, momentum, fwd_prev, *rest):
        total, planes, rows_x, rows_y = fwd_prev.shape
        steps = rest[3].shape[1]
        fits = total == 2 * shots and planes == 4 * shots and rows_y == 128 and rows_x % 16 == 0 and steps % 2 == 0
        plan = whole_plan if fits else slab_plan
        return plan(courant_sq, momentum, fwd_prev, *rest)

    return run
```

```python
import functools

import jax
import jax.numpy as jnp
from jax import lax
from jax.experimental import pallas as pl
from jax.experimental.pallas import tpu as pltpu
from jax.sharding import Mesh
from jax.sharding import PartitionSpec as P

CENTER = -2.5
NEAR = 4.0 / 3.0
FAR = -1.0 / 12.0
AMPLITUDE = 100.0
EPSILON = 1e-06


def with_halo(value, sides, width):
    for axis, dim in sides:
        size, length = (lax.axis_size(axis), value.shape[dim])
        up = [(i, (i + 1) % size) for i in range(size - 1)]
        down = [(j, i) for i, j in up]
        last = lax.slice_in_dim(value, length - width, length, axis=dim)
        leading = lax.slice_in_dim(value, 0, width, axis=dim)
        before = lax.ppermute(last, axis, up)
        after = lax.ppermute(leading, axis, down)
        value = jnp.concatenate([before, value, after], axis=dim)
    return value


def laplace(padded):
    lateral = jnp.pad(padded[:, 2:-2], ((0, 0), (0, 0), (2, 2), (2, 2)))
    center = padded[:, 2:-2]
    along_z = NEAR * (padded[:, 1:-3] + padded[:, 3:-1]) + FAR * (padded[:, :-4] + padded[:, 4:])
    along_x = NEAR * (lateral[:, :, 1:-3, 2:-2] + lateral[:, :, 3:-1, 2:-2]) + FAR * (
        lateral[:, :, :-4, 2:-2] + lateral[:, :, 4:, 2:-2]
    )
    along_y = NEAR * (lateral[:, :, 2:-2, 1:-3] + lateral[:, :, 2:-2, 3:-1]) + FAR * (
        lateral[:, :, 2:-2, :-4] + lateral[:, :, 2:-2, 4:]
    )
    return 3.0 * CENTER * center + along_z + along_x + along_y


def locate(field, cell_ids, first_plane):
    shot_count, planes, rows_x, rows_y = field.shape
    plane_cells = rows_x * rows_y
    local_index = cell_ids - first_plane * plane_cells
    inside = (local_index >= 0) & (local_index < planes * plane_cells)
    target = jnp.where(inside, local_index, 0)
    return (inside, target)


def inject(field, cell_ids, values, first_plane):
    shot_count = field.shape[0]
    inside, target = locate(field, cell_ids, first_plane)
    amount = jnp.where(inside, values, jnp.zeros_like(values))
    flattened = field.reshape(shot_count, -1)
    lanes = jnp.arange(shot_count)[:, None]
    flattened = flattened.at[lanes, target].add(amount)
    return flattened.reshape(field.shape)


def sample(field, cell_ids, first_plane):
    shot_count = field.shape[0]
    inside, target = locate(field, cell_ids, first_plane)
    values = jnp.take_along_axis(field.reshape(shot_count, -1), target, axis=1)
    return jnp.where(inside, values, jnp.zeros_like(values))


def wave_value(start, step):
    cycle = jnp.mod(start + jnp.int32(step), jnp.int32(48))
    phase = (cycle.astype(jnp.float32) - 24.0) / 12.0
    return AMPLITUDE * (1.0 - 2.0 * phase * phase) * jnp.exp(-phase * phase)


def statistics(scaled, moment, weight, cells_all):
    grand_total = lax.psum(jnp.sum(scaled * scaled), ("shot", "depth"))
    factor = lax.rsqrt(grand_total / cells_all + EPSILON)
    halfway = moment - 0.5 * factor * scaled
    energy = lax.psum(jnp.sum(weight * halfway * halfway), ("shot", "depth"))
    return (factor, 0.5 * energy / cells_all)


def slab_shards(
    courant_sq,
    momentum,
    fwd_prev,
    fwd_cur,
    adj_next,
    adj_cur,
    observed,
    src_cells,
    rec_cells,
    ckpt_step,
):
    shot_count, planes, rows_x, rows_y = fwd_cur.shape
    steps_all = observed.shape[1]
    first_plane = lax.axis_index("depth") * planes
    total_planes = planes * lax.axis_size("depth")
    cells_all = total_planes * rows_x * rows_y
    sources = src_cells[:, None]
    older, current = (fwd_prev, fwd_cur)
    laplacians = []
    misfits = []
    for step in range(steps_all):
        padded = with_halo(current, (("depth", 1),), 2)
        strength = jnp.full(sources.shape, wave_value(ckpt_step, step), jnp.float32)
        laplacian = inject(laplace(padded), sources, strength, first_plane)
        newer = 2.0 * current - older + courant_sq * laplacian
        misfits.append(sample(newer, rec_cells, first_plane) - observed[:, step, :])
        laplacians.append(laplacian)
        older, current = (current, newer)
    adj_later, adj_now = (adj_next, adj_cur)
    gradient = jnp.zeros((planes, rows_x, rows_y), jnp.float32)
    for step in reversed(range(steps_all)):
        padded = with_halo(courant_sq * adj_now, (("depth", 1),), 2)
        adj_new = 2.0 * adj_now - adj_later + laplace(padded)
        adj_new = inject(adj_new, rec_cells, misfits[step], first_plane)
        gradient = gradient + jnp.sum(adj_new * laplacians[step], axis=0)
        adj_later, adj_now = (adj_now, adj_new)
    depths = (first_plane + jnp.arange(planes)).astype(jnp.float32)
    weight = (1.0 + 2.0 * depths / (total_planes - 1))[:, None, None]
    share_rows = rows_x // lax.axis_size("shot")
    offset = lax.axis_index("shot") * share_rows
    moment_share = lax.dynamic_slice_in_dim(momentum, offset, share_rows, 1)
    gradient = lax.psum(gradient, "shot")
    scaled = weight * gradient
    scaled_share = lax.dynamic_slice_in_dim(scaled, offset, share_rows, 1)
    factor, kinetic = statistics(scaled_share, moment_share, weight, cells_all)
    momentum_half = momentum - 0.5 * factor * scaled
    return (momentum_half, kinetic)


def interleave(dst, slab, src, factor=None):
    planes, rows = src.shape[0], src.shape[1]
    groups = rows // 8

    @pl.loop(0, planes)
    def _(p):
        for i in range(groups):
            value = src[p, pl.ds(i, 8, stride=groups), :]
            if factor is not None:
                value = value * factor
            dst[(*slab, p, pl.ds(i * 8, 8), slice(None))] = value


def pick_kernel(across, *refs):
    count = len(across)
    fields, outs, (held, sems) = refs[: 2 * count], refs[2 * count : 3 * count], refs[3 * count :]
    chip = lax.axis_index("chip")
    copies = []
    for n in range(2 * count):
        shot = 1 - chip if across[n // 2] else chip
        copies.append(pltpu.make_async_copy(fields[n].at[shot], held.at[n], sems.at[n]))
        copies[-1].start()
    for n in range(2 * count):
        copies[n].wait()
        interleave(outs[n // 2], (n % 2,), held.at[n])


def pick(*pairs, after=None):
    kernel = functools.partial(pick_kernel, tuple(pair[2] for pair in pairs))
    fields = [field for pair in pairs for field in pair[:2]]
    if after is not None:
        kernel, plain = (lambda mark, *refs: plain(*refs)), kernel
        fields = [after] + fields
    shape = pairs[0][0].shape[1:]
    vmem = pl.BlockSpec(memory_space=pltpu.VMEM)
    return pl.pallas_call(
        kernel,
        in_specs=[pl.BlockSpec(memory_space=pl.ANY)] * len(fields),
        out_specs=[vmem] * len(pairs),
        out_shape=[jax.ShapeDtypeStruct((2, *shape), jnp.float32)] * len(pairs),
        scratch_shapes=[pltpu.VMEM((2 * len(pairs), *shape), jnp.float32), pltpu.SemaphoreType.DMA((2 * len(pairs),))],
        compiler_params=pltpu.CompilerParams(vmem_limit_bytes=8 * 2**20),
        name="pick",
    )(*fields)


def courant_kernel(courant, whole, piece):
    shot = lax.axis_index("shot")
    interleave(whole, (), courant, 1.0 / 12.0)
    piece[0] = whole[(shot % 2) * (courant.shape[0] // 2) + shot // 2]


def band(lanes):
    near = jnp.abs(lax.broadcasted_iota(jnp.int32, (2 * lanes, lanes), 0) % lanes - lax.broadcasted_iota(jnp.int32, (2 * lanes, lanes), 1))
    return jnp.where(near == 0, -90.0, jnp.where(near == 1, 16.0, jnp.where(near == 2, -1.0, 0.0))).astype(jnp.bfloat16)


def laps12(field, z, banded):
    rows, lanes = field.shape[1:]
    sub = lax.broadcasted_iota(jnp.int32, (8, lanes), 0)

    def later(block):
        return jnp.where(sub < 7, pltpu.roll(block, 7, 0), 0.0)

    def earlier(block):
        return jnp.where(sub > 0, pltpu.roll(block, 1, 0), 0.0)

    whole = field[pl.ds(z + 2, BATCH)].reshape(BATCH * rows, lanes)
    high = whole.astype(jnp.bfloat16)
    low = (whole - high.astype(jnp.float32)).astype(jnp.bfloat16)
    along_y = jnp.dot(jnp.concatenate([high, low], 1), banded, preferred_element_type=jnp.float32)
    results = []
    for j in range(BATCH):
        center = field[z + j + 2]
        first, second = center[0:8], center[8:16]
        last, before = center[rows - 8 :], center[rows - 16 : rows - 8]
        late, early = later(first), earlier(last)
        near = jnp.concatenate([center[8:], late], 0) + jnp.concatenate([early, center[:-8]], 0)
        far = jnp.concatenate([center[16:], late, later(second)], 0) + jnp.concatenate(
            [earlier(before), early, center[:-16]], 0
        )
        near = near + (field[z + j + 1] + field[z + j + 3])
        far = far + (field[z + j] + field[z + j + 4])
        results.append((center, 16.0 * near - far + along_y[j * rows : (j + 1) * rows]))
    return results


def scatter_kernel(row_ref, y_ref, obs_ref, out_ref, mark, spread):
    receivers, steps = obs_ref.shape
    lanes = out_ref.shape[2]
    tile = out_ref.shape[1]

    @pl.when(pl.program_id(0) == 0)
    def _():
        lane = lax.broadcasted_iota(jnp.int32, (receivers, lanes), 1)
        at = lane == y_ref[...]
        for k in range(steps):
            column = obs_ref[:, k : k + 1]
            high = column.astype(jnp.bfloat16).astype(jnp.float32)
            low = column - high
            cols = pl.ds(k * lanes, lanes)
            spread[0:receivers, cols] = jnp.where(at, high, 0.0).astype(jnp.bfloat16)
            spread[receivers:, cols] = jnp.where(at, low, 0.0).astype(jnp.bfloat16)
        cols = pl.ds(steps * lanes, lanes)
        spread[0:receivers, cols] = jnp.where(at, 1.0, 0.0).astype(jnp.bfloat16)
        spread[receivers:, cols] = jnp.zeros((receivers, lanes), jnp.bfloat16)
        mark[...] = jnp.zeros(mark.shape, jnp.float32)

    ids = lax.broadcasted_iota(jnp.int32, (tile, receivers), 0) + pl.program_id(0) * tile
    chosen = jnp.where(ids == row_ref[...], 1.0, 0.0).astype(jnp.bfloat16)
    total = jnp.dot(jnp.concatenate([chosen, chosen], 1), spread[...], preferred_element_type=jnp.float32)
    for k in range(steps + 1):
        out_ref[k] = total[:, k * lanes : (k + 1) * lanes]


def scatter(cells, observed, planes_all, rows_x, rows_y):
    steps, receivers = observed.shape
    groups = rows_x // 8
    x = (cells // rows_y) % rows_x
    row = (cells // (rows_x * rows_y)) * rows_x + (x % groups) * 8 + x // groups
    lanes = cells % rows_y
    rows_all = planes_all * rows_x
    tile = 256
    return pl.pallas_call(
        scatter_kernel,
        grid=(rows_all // tile,),
        in_specs=[
            pl.BlockSpec((1, receivers), lambda t: (0, 0)),
            pl.BlockSpec((receivers, 1), lambda t: (0, 0)),
            pl.BlockSpec((receivers, steps), lambda t: (0, 0)),
        ],
        out_specs=[
            pl.BlockSpec((steps + 1, tile, rows_y), lambda t: (0, t, 0)),
            pl.BlockSpec((8, rows_y), lambda t: (0, 0)),
        ],
        out_shape=[
            jax.ShapeDtypeStruct((steps + 1, rows_all, rows_y), jnp.float32),
            jax.ShapeDtypeStruct((8, rows_y), jnp.float32),
        ],
        scratch_shapes=[pltpu.VMEM((2 * receivers, (steps + 1) * rows_y), jnp.bfloat16)],
        compiler_params=pltpu.CompilerParams(vmem_limit_bytes=20 * 2**20),
        cost_estimate=pl.CostEstimate(
            flops=4 * rows_all * receivers * (steps + 1) * rows_y,
            bytes_accessed=4 * (steps + 1) * rows_all * rows_y,
            transcendentals=0,
        ),
        name="receiver_scatter",
    )(row[None, :], lanes[:, None], observed.T)


def place(planes):
    chip, core = lax.axis_index("chip"), lax.axis_index("core")
    slabs = (2 * chip + core, 2 * chip + 1 - core, 2 * (1 - chip) + core, 2 * (1 - chip) + 1 - core)
    return chip, core, [slab * planes for slab in slabs]


def load_blocks(slabs, blocks, first, second):
    ends = first.shape[0]
    planes = blocks[0].shape[1]
    for field in (first, second):
        for z in (0, 1, ends - 2, ends - 1):
            field[z] = jnp.zeros(field.shape[1:], jnp.float32)
    for slab, block in zip(slabs, blocks):

        @pl.loop(0, planes)
        def _(p):
            first[slab + p + 2] = block[0, p]
            second[slab + p + 2] = block[1, p]


BATCH = 4


def for_owned(mine, planes, body):
    for owned in (True, False):
        core = mine if owned else 1 - mine

        @pl.loop(0, 2 * planes // BATCH)
        def _(index):
            chip, p = index // (planes // BATCH), (index % (planes // BATCH)) * BATCH
            z = (2 * chip + core) * planes + p
            body(z, chip if owned else None, p)


def forward_kernel(
    start, sources, own, mate, over, far, c0, c1, c2, c3, placed, laps, inject, cour, mark, even, odd, banded
):
    planes, rows, lanes = c0.shape
    steps = laps.shape[0]
    groups = rows // 8
    chip_here, core, slabs = place(planes)
    mark[...] = jnp.zeros(mark.shape, jnp.float32)
    banded[...] = band(lanes)
    load_blocks(slabs, (own, mate, over, far), odd, even)
    for slab, block in zip(slabs, (c0, c1, c2, c3)):

        @pl.loop(0, planes)
        def _(p):
            cour[slab + p] = block[p]

    cell = sources[chip_here]
    source_z, x, lane = cell // (rows * lanes), cell // lanes % rows, cell % lanes
    tile = pl.ds(pl.multiple_of(x % groups * 8, 8), 8)
    here = (lax.broadcasted_iota(jnp.int32, (8, lanes), 0) == x // groups) & (
        lax.broadcasted_iota(jnp.int32, (8, lanes), 1) == lane
    )
    source_slab, source_p = source_z // planes, lax.rem(source_z, planes)

    def advance(k, now, then):
        def body(z, chip, p):
            olds = [then[z + j + 2] for j in range(BATCH)]
            for j, (center, lap) in enumerate(laps12(now, z, banded[...])):
                if chip is not None:
                    laps[k, p + j, chip] = lap
                newer = 2.0 * center - olds[j] + cour[z + j] * lap
                then[z + j + 2] = newer
                inject[k, z + j] = placed[k, z + j] - placed[steps, z + j] * newer

        for_owned(core, planes, body)

        cycle = (start[0] + k) % 48
        phase = (jnp.full((8, lanes), cycle, jnp.int32).astype(jnp.float32) - 24.0) / 12.0
        wave = AMPLITUDE * (1.0 - 2.0 * phase * phase) * jnp.exp(-phase * phase)
        strength = jnp.where(here, 12.0 * wave, 0.0)

        @pl.when(lax.rem(source_slab, 2) == core)
        def _():
            laps[k, source_p, source_slab // 2, tile, :] += strength

        moved = cour[source_z, tile, :] * strength
        then[source_z + 2, tile, :] += moved
        inject[k, source_z, tile, :] -= placed[steps, source_z, tile, :] * moved

    @pl.loop(0, steps // 2)
    def _(pair):
        advance(2 * pair, even, odd)
        advance(2 * pair + 1, odd, even)


def adjoint_kernel(mark, own, mate, over, far, cour, laps, inject, keep_ref, send_ref, even, odd, total, banded):
    planes, rows, lanes = own.shape[1:]
    steps = laps.shape[0]
    groups = rows // 8
    chip_here, core, slabs = place(planes)
    banded[...] = band(lanes)
    load_blocks(slabs, (own, mate, over, far), odd, even)

    @pl.loop(0, 4 * planes)
    def _(z):
        even[z + 2] = even[z + 2] * cour[z]
        odd[z + 2] = odd[z + 2] * cour[z]

    @pl.loop(0, 2 * planes)
    def _(index):
        total[index] = jnp.zeros((rows, lanes), jnp.float32)

    def advance(k, now, then):
        def body(z, chip, p):
            olds = [then[z + j + 2] for j in range(BATCH)]
            if chip is not None:
                sums = [total[chip * planes + p + j] for j in range(BATCH)]
            for j, (center, lap) in enumerate(laps12(now, z, banded[...])):
                newer = 2.0 * center - olds[j] + cour[z + j] * (lap - inject[k, z + j])
                then[z + j + 2] = newer
                if chip is not None:
                    total[chip * planes + p + j] = sums[j] + newer * laps[k, p + j, chip]

        for_owned(core, planes, body)

    @pl.loop(0, steps // 2)
    def _(pair):
        advance(steps - 1 - 2 * pair, even, odd)
        advance(steps - 2 - 2 * pair, odd, even)

    for ref, chip in ((keep_ref, chip_here), (send_ref, 1 - chip_here)):

        @pl.loop(0, planes)
        def _(p):
            z = (2 * chip + core) * planes + p
            weight = 1.0 + 2.0 * jnp.full((rows, lanes), z, jnp.int32).astype(jnp.float32) / (4 * planes - 1)
            value = weight * total[chip * planes + p] / (12.0 * cour[z])
            for i in range(groups):
                ref[p, pl.ds(i, 8, stride=groups), :] = value[i * 8 : (i + 1) * 8]


def halve_kernel(bit, mine, other, keep, send):
    half = lax.axis_index("shot") // bit % 2
    count = keep.shape[0]
    for ref, part in ((keep, half), (send, 1 - half)):
        for p in range(count):
            ref[p] = mine[part * count + p] + other[part * count + p]


def add_kernel(mine, other, out):
    out[...] = mine[...] + other[...]


def flip(index, bits):
    result = index
    for bit in (1, 2):
        if bits & bit:
            result = jnp.where(index // bit % 2 == 1, result - bit, result + bit)
    return result


def arrange_kernel(mine, other, out):
    shot = lax.axis_index("shot")
    z, y = shot // 2, shot % 2
    quarter = mine.shape[0]
    for part, half in ((mine, y), (other, 1 - y)):
        for j in range(quarter):
            out[half * quarter + flip(z, j)] = part[j]


def first_plane(shot, planes):
    return (shot % 2) * (planes // 2) + (shot // 2 % 2) * (planes // 4)


def sums_kernel(mine, other, momentum, data, sums):
    count, rows, lanes = mine.shape
    planes = momentum.shape[0]
    chip, core = lax.axis_index("chip"), lax.axis_index("core")
    first = first_plane(lax.axis_index("shot"), planes)
    parts = [jnp.zeros((rows, lanes), jnp.float32)] * 4
    for j in range(count):
        scaled = mine[j] + other[j]
        data[j * rows : (j + 1) * rows] = scaled
        z = (2 * chip + core) * planes + first + j
        weight = 1.0 + 2.0 * jnp.full((1, lanes), z, jnp.int32).astype(jnp.float32) / (4 * planes - 1)
        moment = momentum[first + j]
        square = scaled * scaled
        terms = (square, weight * moment * moment, weight * moment * scaled, weight * square)
        parts = [part + term for part, term in zip(parts, terms)]

    def total(value):
        by_lane = jnp.sum(value, axis=0, keepdims=True)
        return jnp.broadcast_to(jnp.sum(by_lane, axis=1, keepdims=True), (1, lanes))

    value = jnp.concatenate([total(part) for part in parts] + [jnp.zeros((4, lanes), jnp.float32)], 0)
    data[count * rows :] = value
    sums[...] = value


def join_kernel(mine, other, s0, s1, s2, data, sums):
    rows = mine.shape[0] - 8
    data[0:rows] = mine[0:rows]
    data[rows : 2 * rows] = other[0:rows]
    value = (s0[...] + s1[...]) + (other[rows:] + s2[...])
    data[2 * rows :] = value
    sums[...] = value


def finish_kernel(mine, other, momentum, s0, s1, s2, out, kinetic):
    planes, rows, lanes = momentum.shape
    cells = 4.0 * planes * rows * lanes
    shot = lax.axis_index("shot")
    sums = (s0[...] + s1[...]) + (other[planes // 2 * rows :] + s2[...])
    factor = lax.rsqrt(sums[0:1] / cells + EPSILON)
    energy = 0.5 * (sums[1:2] - factor * sums[2:3] + 0.25 * factor * factor * sums[3:4]) / cells
    kinetic[0] = energy[0, 0]
    step = 0.5 * factor
    quarter = planes // 4
    for part, group in ((mine, shot), (other, flip(shot, 1))):
        for number, first in enumerate((first_plane(group, planes), first_plane(flip(group, 2), planes))):
            for j in range(quarter):
                at = (number * quarter + j) * rows
                out[first + j] = momentum[first + j] - step * part[at : at + rows]


def local(kernel, outs, *arrays, name=None, limit=8):
    vmem = pl.BlockSpec(memory_space=pltpu.VMEM)
    shapes = [jax.ShapeDtypeStruct(shape, jnp.float32) for shape in outs]
    single = len(outs) == 1
    return pl.pallas_call(
        kernel,
        in_specs=[vmem] * len(arrays),
        out_specs=vmem if single else [vmem] * len(outs),
        out_shape=shapes[0] if single else shapes,
        compiler_params=pltpu.CompilerParams(vmem_limit_bytes=limit * 2**20),
        name=name or kernel.__name__,
    )(*arrays)


def exchange(value, bits):
    axes = ("shot", "chip", "core")
    return lax.ppermute(value, axes, [(i, i ^ bits) for i in range(lax.axis_size(axes))])


CORE, CHIP, Y, NEAR_Z, FAR_Z = 1, 2, 4, 8, 16


def whole_shards(
    courant_sq, momentum, fwd_prev, fwd_cur, adj_next, adj_cur, observed, src_cells, rec_cells, ckpt_step
):
    _, planes, rows_x, rows_y = fwd_cur.shape
    steps = observed.shape[1]
    chip = lax.axis_index("chip")
    planes_all = 4 * planes
    cells_all = planes_all * rows_x * rows_y
    vmem, smem = pl.BlockSpec(memory_space=pltpu.VMEM), pl.BlockSpec(memory_space=pltpu.SMEM)

    (outgoing,) = pick((fwd_prev, fwd_cur, True))
    over = exchange(outgoing, CHIP)

    c0, piece = local(courant_kernel, [courant_sq.shape, (1, rows_x, rows_y)], courant_sq)
    piece = exchange(piece, CHIP)
    (own,) = pick((fwd_prev, fwd_cur, False))
    mate = exchange(own, CORE)
    c1 = exchange(c0, CORE)
    quarter = jnp.concatenate([piece] + [exchange(piece, j * NEAR_Z) for j in (1, 2, 3)], 0)
    other = exchange(quarter, Y)
    c2 = local(arrange_kernel, [courant_sq.shape], quarter, other)
    c3 = exchange(c2, CORE)

    cells = lax.dynamic_index_in_dim(rec_cells, chip, 0, keepdims=False)
    traces = lax.dynamic_index_in_dim(observed, chip, 0, keepdims=False)
    placed, mark = scatter(cells, traces, planes_all, rows_x, rows_y)
    placed = placed.reshape(steps + 1, planes_all, rows_x, rows_y)

    adj_outgoing, adj_own = pick((adj_next, adj_cur, True), (adj_next, adj_cur, False), after=mark)
    far = exchange(over, CORE)
    adj_over = exchange(adj_outgoing, CHIP)
    adj_mate = exchange(adj_own, CORE)

    scratch = pltpu.VMEM((planes_all + 4, rows_x, rows_y), jnp.float32)
    band_scratch = pltpu.VMEM((2 * rows_y, rows_y), jnp.bfloat16)
    params = pltpu.CompilerParams(vmem_limit_bytes=20 * 2**20)
    cost = pl.CostEstimate(flops=30 * steps * cells_all, bytes_accessed=16 * steps * cells_all, transcendentals=0)
    laps, inject, cour, mark = pl.pallas_call(
        forward_kernel,
        in_specs=[smem, smem] + [vmem] * 9,
        out_specs=[vmem] * 4,
        out_shape=[
            jax.ShapeDtypeStruct((steps, planes, 2, rows_x, rows_y), jnp.float32),
            jax.ShapeDtypeStruct((steps, planes_all, rows_x, rows_y), jnp.float32),
            jax.ShapeDtypeStruct((planes_all, rows_x, rows_y), jnp.float32),
            jax.ShapeDtypeStruct((8, rows_y), jnp.float32),
        ],
        scratch_shapes=[scratch, scratch, band_scratch],
        compiler_params=params,
        cost_estimate=cost,
        name="forward_steps",
    )(ckpt_step[None], src_cells, own, mate, over, far, c0, c1, c2, c3, placed)

    adj_over, mark = lax.optimization_barrier((adj_over, mark))
    adj_far = exchange(adj_over, CORE)
    slab = jax.ShapeDtypeStruct(courant_sq.shape, jnp.float32)
    keep, send = pl.pallas_call(
        adjoint_kernel,
        in_specs=[pl.BlockSpec(memory_space=pl.ANY)] + [vmem] * 7,
        out_specs=[vmem, vmem],
        out_shape=[slab, slab],
        scratch_shapes=[scratch, scratch, pltpu.VMEM((2 * planes, rows_x, rows_y), jnp.float32), band_scratch],
        compiler_params=params,
        cost_estimate=cost,
        name="adjoint_steps",
    )(mark, adj_own, adj_mate, adj_over, adj_far, cour, laps, inject)

    half, quarter = (planes // 2, rows_x, rows_y), (planes // 4, rows_x, rows_y)
    keep, send = local(functools.partial(halve_kernel, 1), [half] * 2, keep, exchange(send, CHIP), name="halve_y")
    keep, send = local(functools.partial(halve_kernel, 2), [quarter] * 2, keep, exchange(send, Y), name="halve_z")
    part = local(add_kernel, [quarter], keep, exchange(send, NEAR_Z))
    rows, sums_shape = planes // 4 * rows_x, (8, rows_y)
    data, sums = local(sums_kernel, [(rows + 8, rows_y), sums_shape], part, exchange(part, FAR_Z), momentum)
    received = exchange(data, NEAR_Z)
    others = [exchange(sums, CORE), exchange(sums, NEAR_Z + CORE)]
    data, sums = local(join_kernel, [(2 * rows + 8, rows_y), sums_shape], data, received, sums, *others)
    received = exchange(data, Y)
    others = [exchange(sums, CHIP), exchange(sums, Y + CHIP)]
    momentum_half, kinetic = pl.pallas_call(
        finish_kernel,
        in_specs=[vmem] * 6,
        out_specs=[vmem, smem],
        out_shape=[slab, jax.ShapeDtypeStruct((1,), jnp.float32)],
        compiler_params=pltpu.CompilerParams(vmem_limit_bytes=8 * 2**20),
        name="finish",
    )(data, received, momentum, sums, *others)
    return momentum_half, kinetic[0]


def solution(mesh):
    shots, slabs = mesh.shape["shot"], mesh.shape["depth"]

    def placed(depth):
        field = P("shot", depth, None, None)
        slab = P(depth, None, None)
        inputs = (slab, slab, field, field, field, field, P("shot", None, None), P("shot"), P("shot", None), P())
        return dict(in_specs=inputs, out_specs=(slab, P()), check_vma=False)

    slab_plan = jax.shard_map(slab_shards, mesh=mesh, **placed("depth"))
    if slabs != 4 or shots != 8:
        return slab_plan
    chips = Mesh(mesh.devices.reshape(shots, 2, 2), ("shot", "chip", "core"))
    whole_plan = jax.shard_map(whole_shards, mesh=chips, **placed(("chip", "core")))

    def run(courant_sq, momentum, fwd_prev, *rest):
        total, planes, rows_x, rows_y = fwd_prev.shape
        steps = rest[3].shape[1]
        fits = total == 2 * shots and planes == 4 * shots and rows_y == 128 and rows_x % 16 == 0 and steps % 2 == 0
        plan = whole_plan if fits else slab_plan
        return plan(courant_sq, momentum, fwd_prev, *rest)

    return run
```

```python
import functools

import jax
import jax.numpy as jnp
from jax import lax
from jax.experimental import pallas as pl
from jax.experimental.pallas import tpu as pltpu
from jax.sharding import Mesh
from jax.sharding import PartitionSpec as P

CENTER = -2.5
NEAR = 4.0 / 3.0
FAR = -1.0 / 12.0
AMPLITUDE = 100.0
EPSILON = 1e-06


def with_halo(value, sides, width):
    for axis, dim in sides:
        size, length = (lax.axis_size(axis), value.shape[dim])
        up = [(i, (i + 1) % size) for i in range(size - 1)]
        down = [(j, i) for i, j in up]
        last = lax.slice_in_dim(value, length - width, length, axis=dim)
        leading = lax.slice_in_dim(value, 0, width, axis=dim)
        before = lax.ppermute(last, axis, up)
        after = lax.ppermute(leading, axis, down)
        value = jnp.concatenate([before, value, after], axis=dim)
    return value


def laplace(padded):
    lateral = jnp.pad(padded[:, 2:-2], ((0, 0), (0, 0), (2, 2), (2, 2)))
    center = padded[:, 2:-2]
    along_z = NEAR * (padded[:, 1:-3] + padded[:, 3:-1]) + FAR * (padded[:, :-4] + padded[:, 4:])
    along_x = NEAR * (lateral[:, :, 1:-3, 2:-2] + lateral[:, :, 3:-1, 2:-2]) + FAR * (
        lateral[:, :, :-4, 2:-2] + lateral[:, :, 4:, 2:-2]
    )
    along_y = NEAR * (lateral[:, :, 2:-2, 1:-3] + lateral[:, :, 2:-2, 3:-1]) + FAR * (
        lateral[:, :, 2:-2, :-4] + lateral[:, :, 2:-2, 4:]
    )
    return 3.0 * CENTER * center + along_z + along_x + along_y


def locate(field, cell_ids, first_plane):
    shot_count, planes, rows_x, rows_y = field.shape
    plane_cells = rows_x * rows_y
    local_index = cell_ids - first_plane * plane_cells
    inside = (local_index >= 0) & (local_index < planes * plane_cells)
    target = jnp.where(inside, local_index, 0)
    return (inside, target)


def inject(field, cell_ids, values, first_plane):
    shot_count = field.shape[0]
    inside, target = locate(field, cell_ids, first_plane)
    amount = jnp.where(inside, values, jnp.zeros_like(values))
    flattened = field.reshape(shot_count, -1)
    lanes = jnp.arange(shot_count)[:, None]
    flattened = flattened.at[lanes, target].add(amount)
    return flattened.reshape(field.shape)


def sample(field, cell_ids, first_plane):
    shot_count = field.shape[0]
    inside, target = locate(field, cell_ids, first_plane)
    values = jnp.take_along_axis(field.reshape(shot_count, -1), target, axis=1)
    return jnp.where(inside, values, jnp.zeros_like(values))


def wave_value(start, step):
    cycle = jnp.mod(start + jnp.int32(step), jnp.int32(48))
    phase = (cycle.astype(jnp.float32) - 24.0) / 12.0
    return AMPLITUDE * (1.0 - 2.0 * phase * phase) * jnp.exp(-phase * phase)


def statistics(scaled, moment, weight, cells_all):
    grand_total = lax.psum(jnp.sum(scaled * scaled), ("shot", "depth"))
    factor = lax.rsqrt(grand_total / cells_all + EPSILON)
    halfway = moment - 0.5 * factor * scaled
    energy = lax.psum(jnp.sum(weight * halfway * halfway), ("shot", "depth"))
    return (factor, 0.5 * energy / cells_all)


def slab_shards(
    courant_sq,
    momentum,
    fwd_prev,
    fwd_cur,
    adj_next,
    adj_cur,
    observed,
    src_cells,
    rec_cells,
    ckpt_step,
):
    shot_count, planes, rows_x, rows_y = fwd_cur.shape
    steps_all = observed.shape[1]
    first_plane = lax.axis_index("depth") * planes
    total_planes = planes * lax.axis_size("depth")
    cells_all = total_planes * rows_x * rows_y
    sources = src_cells[:, None]
    older, current = (fwd_prev, fwd_cur)
    laplacians = []
    misfits = []
    for step in range(steps_all):
        padded = with_halo(current, (("depth", 1),), 2)
        strength = jnp.full(sources.shape, wave_value(ckpt_step, step), jnp.float32)
        laplacian = inject(laplace(padded), sources, strength, first_plane)
        newer = 2.0 * current - older + courant_sq * laplacian
        misfits.append(sample(newer, rec_cells, first_plane) - observed[:, step, :])
        laplacians.append(laplacian)
        older, current = (current, newer)
    adj_later, adj_now = (adj_next, adj_cur)
    gradient = jnp.zeros((planes, rows_x, rows_y), jnp.float32)
    for step in reversed(range(steps_all)):
        padded = with_halo(courant_sq * adj_now, (("depth", 1),), 2)
        adj_new = 2.0 * adj_now - adj_later + laplace(padded)
        adj_new = inject(adj_new, rec_cells, misfits[step], first_plane)
        gradient = gradient + jnp.sum(adj_new * laplacians[step], axis=0)
        adj_later, adj_now = (adj_now, adj_new)
    depths = (first_plane + jnp.arange(planes)).astype(jnp.float32)
    weight = (1.0 + 2.0 * depths / (total_planes - 1))[:, None, None]
    share_rows = rows_x // lax.axis_size("shot")
    offset = lax.axis_index("shot") * share_rows
    moment_share = lax.dynamic_slice_in_dim(momentum, offset, share_rows, 1)
    gradient = lax.psum(gradient, "shot")
    scaled = weight * gradient
    scaled_share = lax.dynamic_slice_in_dim(scaled, offset, share_rows, 1)
    factor, kinetic = statistics(scaled_share, moment_share, weight, cells_all)
    momentum_half = momentum - 0.5 * factor * scaled
    return (momentum_half, kinetic)


def interleave(dst, slab, src, factor=None):
    planes, rows = src.shape[0], src.shape[1]
    groups = rows // 8

    @pl.loop(0, planes)
    def _(p):
        for i in range(groups):
            value = src[p, pl.ds(i, 8, stride=groups), :]
            if factor is not None:
                value = value * factor
            dst[(*slab, p, pl.ds(i * 8, 8), slice(None))] = value


def pick_kernel(across, *refs):
    count = len(across)
    fields, outs, (held, sems) = refs[: 2 * count], refs[2 * count : 3 * count], refs[3 * count :]
    chip = lax.axis_index("chip")
    copies = []
    for n in range(2 * count):
        shot = 1 - chip if across[n // 2] else chip
        copies.append(pltpu.make_async_copy(fields[n].at[shot], held.at[n], sems.at[n]))
        copies[-1].start()
    for n in range(2 * count):
        copies[n].wait()
        interleave(outs[n // 2], (n % 2,), held.at[n])


def pick(*pairs, after=None, grant=4):
    plain = functools.partial(pick_kernel, tuple(pair[2] for pair in pairs))
    fields = [field for pair in pairs for field in pair[:2]]
    shape = fields[0].shape[1:]
    vmem, hbm = pl.BlockSpec(memory_space=pltpu.VMEM), pl.BlockSpec(memory_space=pltpu.HBM)
    marks = [] if after is None else [after]
    return pl.pallas_call(
        lambda *refs: plain(*refs[len(marks) :]),
        in_specs=[vmem] * len(marks) + [hbm] * len(fields),
        out_specs=[vmem] * len(pairs),
        out_shape=[jax.ShapeDtypeStruct((2, *shape), jnp.float32)] * len(pairs),
        scratch_shapes=[pltpu.VMEM((len(fields), *shape), jnp.float32), pltpu.SemaphoreType.DMA((len(fields),))],
        compiler_params=pltpu.CompilerParams(vmem_limit_bytes=grant * 2**20),
        name="pick",
    )(*marks, *fields)


def courant_kernel(courant, whole, piece):
    interleave(whole, (), courant, 1.0 / 12.0)
    count = piece.shape[0]
    piece[...] = whole[pl.ds(lax.axis_index("shot") % 2 * count, count)]


def band(lanes):
    near = jnp.abs(lax.broadcasted_iota(jnp.int32, (2 * lanes, lanes), 0) % lanes - lax.broadcasted_iota(jnp.int32, (2 * lanes, lanes), 1))
    return jnp.where(near == 0, -90.0, jnp.where(near == 1, 16.0, jnp.where(near == 2, -1.0, 0.0))).astype(jnp.bfloat16)


def along_y(field, z, banded, out):
    rows, lanes = field.shape[1:]
    whole = field[pl.ds(z + 2, BATCH)].reshape(BATCH * rows, lanes)
    high = whole.astype(jnp.bfloat16)
    low = (whole - high.astype(jnp.float32)).astype(jnp.bfloat16)
    out[...] = jnp.dot(jnp.concatenate([high, low], 1), banded[...], preferred_element_type=jnp.float32)


def laps12(field, z, y_part, fetch, finish):
    rows, lanes = field.shape[1:]
    groups = rows // 8
    sub = lax.broadcasted_iota(jnp.int32, (8, lanes), 0)

    def later(block):
        return jnp.where(sub < 7, pltpu.roll(block, 7, 0), 0.0)

    def earlier(block):
        return jnp.where(sub > 0, pltpu.roll(block, 1, 0), 0.0)

    for base in range(0, BATCH, PLANES):
        held = {}

        def tile(j, i):
            if (j, i) not in held:
                if i < 0:
                    held[j, i] = earlier(tile(j, i + groups))
                elif i >= groups:
                    held[j, i] = later(tile(j, i - groups))
                else:
                    held[j, i] = field[z + j + 2, i * 8 : (i + 1) * 8]
            return held[j, i]

        def load(i):
            found = []
            for j in range(base, base + PLANES):
                center = tile(j, i)
                near = (tile(j, i - 1), tile(j, i + 1), tile(j - 1, i), tile(j + 1, i))
                far = (tile(j, i - 2), tile(j, i + 2), tile(j - 2, i), tile(j + 2, i))
                at = (j * groups + i) * 8
                found.append((center, near, far, y_part[at : at + 8], fetch(j, slice(i * 8, i * 8 + 8))))
            return found

        ready = load(0)
        for i in range(groups):
            upcoming = load(i + 1) if i + 1 < groups else None
            for j, (center, near, far, part, extra) in enumerate(ready):
                near = (near[0] + near[1]) + (near[2] + near[3])
                far = (far[0] + far[1]) + (far[2] + far[3])
                finish(base + j, slice(i * 8, i * 8 + 8), center, 16.0 * near + (part - far), extra)
            ready = upcoming


def scatter_kernel(row_ref, y_ref, obs_ref, out_ref, mark, second, spread):
    receivers, steps = obs_ref.shape
    lanes = out_ref.shape[2]
    tile = out_ref.shape[1]

    @pl.when(pl.program_id(0) == 0)
    def _():
        lane = lax.broadcasted_iota(jnp.int32, (receivers, lanes), 1)
        at = lane == y_ref[...]
        for k in range(steps):
            column = obs_ref[:, k : k + 1]
            high = column.astype(jnp.bfloat16).astype(jnp.float32)
            low = column - high
            cols = pl.ds(k * lanes, lanes)
            spread[0:receivers, cols] = jnp.where(at, high, 0.0).astype(jnp.bfloat16)
            spread[receivers:, cols] = jnp.where(at, low, 0.0).astype(jnp.bfloat16)
        cols = pl.ds(steps * lanes, lanes)
        spread[0:receivers, cols] = jnp.where(at, 1.0, 0.0).astype(jnp.bfloat16)
        spread[receivers:, cols] = jnp.zeros((receivers, lanes), jnp.bfloat16)
        mark[...] = jnp.zeros(mark.shape, jnp.float32)
        second[...] = jnp.zeros(mark.shape, jnp.float32)

    ids = lax.broadcasted_iota(jnp.int32, (tile, receivers), 0) + pl.program_id(0) * tile
    chosen = jnp.where(ids == row_ref[...], 1.0, 0.0).astype(jnp.bfloat16)
    total = jnp.dot(jnp.concatenate([chosen, chosen], 1), spread[...], preferred_element_type=jnp.float32)
    for k in range(steps + 1):
        out_ref[k] = total[:, k * lanes : (k + 1) * lanes]


def scatter(cells, observed, planes_all, rows_x, rows_y):
    steps, receivers = observed.shape
    groups = rows_x // 8
    x = (cells // rows_y) % rows_x
    row = (cells // (rows_x * rows_y)) * rows_x + (x % groups) * 8 + x // groups
    lanes = cells % rows_y
    rows_all = planes_all * rows_x
    tile = 256
    return pl.pallas_call(
        scatter_kernel,
        grid=(rows_all // tile,),
        in_specs=[
            pl.BlockSpec((1, receivers), lambda t: (0, 0)),
            pl.BlockSpec((receivers, 1), lambda t: (0, 0)),
            pl.BlockSpec((receivers, steps), lambda t: (0, 0)),
        ],
        out_specs=[
            pl.BlockSpec((steps + 1, tile, rows_y), lambda t: (0, t, 0)),
            pl.BlockSpec((8, rows_y), lambda t: (0, 0)),
            pl.BlockSpec((8, rows_y), lambda t: (0, 0)),
        ],
        out_shape=[
            jax.ShapeDtypeStruct((steps + 1, rows_all, rows_y), jnp.float32),
            jax.ShapeDtypeStruct((8, rows_y), jnp.float32),
            jax.ShapeDtypeStruct((8, rows_y), jnp.float32),
        ],
        scratch_shapes=[pltpu.VMEM((2 * receivers, (steps + 1) * rows_y), jnp.bfloat16)],
        compiler_params=pltpu.CompilerParams(vmem_limit_bytes=8 * 2**20),
        cost_estimate=pl.CostEstimate(
            flops=4 * rows_all * receivers * (steps + 1) * rows_y,
            bytes_accessed=4 * (steps + 1) * rows_all * rows_y,
            transcendentals=0,
        ),
        name="receiver_scatter",
    )(row[None, :], lanes[:, None], observed.T)


def place(planes):
    chip, core = lax.axis_index("chip"), lax.axis_index("core")
    slabs = (2 * chip + core, 2 * chip + 1 - core, 2 * (1 - chip) + core, 2 * (1 - chip) + 1 - core)
    return chip, core, [slab * planes for slab in slabs]


def load_blocks(slabs, blocks, first, second):
    ends = first.shape[0]
    planes = blocks[0].shape[1]
    for field in (first, second):
        for z in (0, 1, ends - 2, ends - 1):
            field[z] = jnp.zeros(field.shape[1:], jnp.float32)
    for slab, block in zip(slabs, blocks):

        @pl.loop(0, planes)
        def _(p):
            first[slab + p + 2] = block[0, p]
            second[slab + p + 2] = block[1, p]


BATCH = 4
PLANES = 2


def sweep(core, planes, field, banded, y_first, y_second, work):
    order = [(chip, owned) for owned in (True, False) for chip in (0, 1)]
    parts = (y_first, y_second)

    def first(chip, owned):
        return (2 * chip + (core if owned else 1 - core)) * planes

    along_y(field, first(*order[0]), banded, y_first)
    for owned in (True, False):

        @pl.loop(0, 2)
        def _(chip):
            z = first(chip, owned)
            onward = jnp.where(chip == 0, first(1, owned), first(0, False))
            for n in range(planes // BATCH):
                last = n == planes // BATCH - 1
                along_y(field, onward if last else z + (n + 1) * BATCH, banded, parts[(n + 1) % 2])
                work(z + n * BATCH, parts[n % 2], chip if owned else None, n * BATCH)


def forward_kernel(
    start, sources, scattered, own, mate, over, far, c0, c1, c2, c3, placed, laps, inject, cour, mark, even, odd, banded, y0, y1
):
    planes, rows, lanes = c0.shape
    steps = laps.shape[0]
    groups = rows // 8
    chip_here, core, slabs = place(planes)
    mark[...] = jnp.zeros(mark.shape, jnp.float32)
    banded[...] = band(lanes)
    load_blocks(slabs, (own, mate, over, far), odd, even)
    for slab, block in zip(slabs, (c0, c1, c2, c3)):

        @pl.loop(0, planes)
        def _(p):
            cour[slab + p] = block[p]

    cell = sources[chip_here]
    source_z, x, lane = cell // (rows * lanes), cell // lanes % rows, cell % lanes
    tile = pl.ds(pl.multiple_of(x % groups * 8, 8), 8)
    here = (lax.broadcasted_iota(jnp.int32, (8, lanes), 0) == x // groups) & (
        lax.broadcasted_iota(jnp.int32, (8, lanes), 1) == lane
    )
    source_slab, source_p = source_z // planes, lax.rem(source_z, planes)

    def advance(k, now, then):
        def work(z, y_part, chip, p):
            def fetch(j, rows):
                return then[z + j + 2, rows], cour[z + j, rows], placed[k, z + j, rows], placed[steps, z + j, rows]

            def finish(j, rows, center, lap, extra):
                old, speed, traces, count = extra
                if chip is not None:
                    laps[k, p + j, chip, rows] = lap
                newer = 2.0 * center - old + speed * lap
                then[z + j + 2, rows] = newer
                inject[k, z + j, rows] = traces - count * newer

            laps12(now, z, y_part, fetch, finish)

        sweep(core, planes, now, banded, y0, y1, work)

        cycle = (start[0] + k) % 48
        phase = (jnp.full((8, lanes), cycle, jnp.int32).astype(jnp.float32) - 24.0) / 12.0
        wave = AMPLITUDE * (1.0 - 2.0 * phase * phase) * jnp.exp(-phase * phase)
        strength = jnp.where(here, 12.0 * wave, 0.0)

        @pl.when(lax.rem(source_slab, 2) == core)
        def _():
            laps[k, source_p, source_slab // 2, tile, :] += strength

        moved = cour[source_z, tile, :] * strength
        then[source_z + 2, tile, :] += moved
        inject[k, source_z, tile, :] -= placed[steps, source_z, tile, :] * moved

    @pl.loop(0, steps // 2)
    def _(pair):
        advance(2 * pair, even, odd)
        advance(2 * pair + 1, odd, even)


def adjoint_kernel(mark, own, mate, over, far, cour, laps, inject, keep_a, send_a, keep_b, send_b, even, odd, total, banded, y0, y1):
    planes, rows, lanes = own.shape[1:]
    steps = laps.shape[0]
    groups = rows // 8
    chip_here, core, slabs = place(planes)
    banded[...] = band(lanes)
    load_blocks(slabs, (own, mate, over, far), odd, even)

    @pl.loop(0, 4 * planes)
    def _(z):
        even[z + 2] = even[z + 2] * cour[z]
        odd[z + 2] = odd[z + 2] * cour[z]

    @pl.loop(0, 2 * planes)
    def _(index):
        total[index] = jnp.zeros((rows, lanes), jnp.float32)

    def advance(k, now, then):
        def work(z, y_part, chip, p):
            def fetch(j, rows):
                extra = (then[z + j + 2, rows], cour[z + j, rows], inject[k, z + j, rows])
                if chip is not None:
                    extra += (total[chip * planes + p + j, rows], laps[k, p + j, chip, rows])
                return extra

            def finish(j, rows, center, lap, extra):
                newer = 2.0 * center - extra[0] + extra[1] * (lap - extra[2])
                then[z + j + 2, rows] = newer
                if chip is not None:
                    total[chip * planes + p + j, rows] = extra[3] + newer * extra[4]

            laps12(now, z, y_part, fetch, finish)

        sweep(core, planes, now, banded, y0, y1, work)

    @pl.loop(0, steps // 2)
    def _(pair):
        advance(steps - 1 - 2 * pair, even, odd)
        advance(steps - 2 - 2 * pair, odd, even)

    half, quarter = planes // 2, planes // 4
    y = lax.axis_index("shot") % 2
    here, there = chip_here, 1 - chip_here
    runs = [(keep_a, 0, half, here, 0), (send_a, 0, half, there, 0)]
    for ref, side in ((keep_b, y), (send_b, 1 - y)):
        runs += [(ref, 0, quarter, here, half + side * quarter), (ref, quarter, quarter, there, half + side * quarter)]
    for ref, at, count, chip, start in runs:

        @pl.loop(0, count)
        def _(n):
            p = start + n
            z = (2 * chip + core) * planes + p
            weight = 1.0 + 2.0 * jnp.full((rows, lanes), z, jnp.int32).astype(jnp.float32) / (4 * planes - 1)
            value = weight * total[chip * planes + p] / (12.0 * cour[z])
            for i in range(groups):
                ref[at + n, pl.ds(i, 8, stride=groups), :] = value[i * 8 : (i + 1) * 8]


def cross_kernel(keep_a, other_a, keep_b, other_b, next_a, send_a, next_b, send_b):
    y = lax.axis_index("shot") % 2
    count = next_a.shape[0]
    for ref, part in ((next_a, y), (send_a, 1 - y)):
        for p in range(count):
            ref[p] = keep_a[part * count + p] + other_a[part * count + p]
    for ref, part in ((next_b, 0), (send_b, 1)):
        for p in range(count):
            ref[p] = keep_b[part * count + p] + other_b[part * count + p]


def choose_kernel(keep_a, other_a, keep_b, other_b, keep, send):
    second = lax.axis_index("shot") // 2 % 2 == 1
    first_half = keep_a[...] + other_a[...]
    second_half = keep_b[...] + other_b[...]
    keep[...] = jnp.where(second, second_half, first_half)
    send[...] = jnp.where(second, first_half, second_half)


def add_kernel(mine, other, out):
    out[...] = mine[...] + other[...]


def add_sums_kernel(s0, s1, s2, s3, out):
    out[...] = (s0[...] + s1[...]) + (s2[...] + s3[...])


def flip(index, bits):
    result = index
    for bit in (1, 2):
        if bits & bit:
            result = jnp.where(index // bit % 2 == 1, result - bit, result + bit)
    return result


def arrange_kernel(mine, other, out):
    y = lax.axis_index("shot") % 2
    count = mine.shape[0]
    out[pl.ds(y * count, count)] = mine[...]
    out[pl.ds((1 - y) * count, count)] = other[...]


def first_plane(shot, planes):
    return (shot // 2 % 2) * (planes // 2) + (shot % 2) * (planes // 4)


def sums_kernel(mine, other, momentum, data, sums):
    count, rows, lanes = mine.shape
    planes = momentum.shape[0]
    chip, core = lax.axis_index("chip"), lax.axis_index("core")
    first = first_plane(lax.axis_index("shot"), planes)
    parts = [jnp.zeros((rows, lanes), jnp.float32)] * 4
    for j in range(count):
        scaled = mine[j] + other[j]
        data[j] = scaled
        z = (2 * chip + core) * planes + first + j
        weight = 1.0 + 2.0 * jnp.full((1, lanes), z, jnp.int32).astype(jnp.float32) / (4 * planes - 1)
        moment = momentum[first + j]
        square = scaled * scaled
        terms = (square, weight * moment * moment, weight * moment * scaled, weight * square)
        parts = [part + term for part, term in zip(parts, terms)]

    def total(value):
        by_lane = jnp.sum(value, axis=0, keepdims=True)
        return jnp.broadcast_to(jnp.sum(by_lane, axis=1, keepdims=True), (1, lanes))

    sums[...] = jnp.concatenate([total(part) for part in parts] + [jnp.zeros((4, lanes), jnp.float32)], 0)


def finish_kernel(d0, d1, d2, d3, momentum, s0, s1, s2, s3, out, kinetic):
    planes, rows, lanes = momentum.shape
    cells = 4.0 * planes * rows * lanes
    shot = lax.axis_index("shot")
    sums = (s0[...] + s1[...]) + (s2[...] + s3[...])
    factor = lax.rsqrt(sums[0:1] / cells + EPSILON)
    energy = 0.5 * (sums[1:2] - factor * sums[2:3] + 0.25 * factor * factor * sums[3:4]) / cells
    kinetic[0] = energy[0, 0]
    step = 0.5 * factor
    for bits, data in enumerate((d0, d1, d2, d3)):
        first = first_plane(flip(shot, bits), planes)
        for j in range(planes // 4):
            out[first + j] = momentum[first + j] - step * data[j]


def local(kernel, outs, *arrays):
    vmem = pl.BlockSpec(memory_space=pltpu.VMEM)
    shapes = [jax.ShapeDtypeStruct(shape, jnp.float32) for shape in outs]
    single = len(outs) == 1
    return pl.pallas_call(
        kernel,
        in_specs=[vmem] * len(arrays),
        out_specs=vmem if single else [vmem] * len(outs),
        out_shape=shapes[0] if single else shapes,
        compiler_params=pltpu.CompilerParams(vmem_limit_bytes=4 * 2**20),
        name=kernel.__name__,
    )(*arrays)


def exchange(value, bits):
    axes = ("shot", "chip", "core")
    return lax.ppermute(value, axes, [(i, i ^ bits) for i in range(lax.axis_size(axes))])


CORE, CHIP, Y, NEAR_Z, FAR_Z = 1, 2, 4, 8, 16


def whole_shards(
    courant_sq, momentum, fwd_prev, fwd_cur, adj_next, adj_cur, observed, src_cells, rec_cells, ckpt_step
):
    _, planes, rows_x, rows_y = fwd_cur.shape
    steps = observed.shape[1]
    chip = lax.axis_index("chip")
    planes_all = 4 * planes
    cells_all = planes_all * rows_x * rows_y
    vmem, smem = pl.BlockSpec(memory_space=pltpu.VMEM), pl.BlockSpec(memory_space=pltpu.SMEM)

    (outgoing,) = pick((fwd_prev, fwd_cur, True), grant=62)
    over = exchange(outgoing, CHIP)

    c0, piece = local(courant_kernel, [courant_sq.shape, (planes // 2, rows_x, rows_y)], courant_sq)
    piece = exchange(piece, CHIP)
    (own,) = pick((fwd_prev, fwd_cur, False))
    mate = exchange(own, CORE)
    c1 = exchange(c0, CORE)
    c2 = local(arrange_kernel, [courant_sq.shape], piece, exchange(piece, Y))
    c3 = exchange(c2, CORE)

    cells = lax.dynamic_index_in_dim(rec_cells, chip, 0, keepdims=False)
    traces = lax.dynamic_index_in_dim(observed, chip, 0, keepdims=False)
    placed, mark, second = scatter(cells, traces, planes_all, rows_x, rows_y)
    placed = placed.reshape(steps + 1, planes_all, rows_x, rows_y)

    adj_outgoing, adj_own = pick((adj_next, adj_cur, True), (adj_next, adj_cur, False), after=mark)
    over, second = lax.optimization_barrier((over, second))
    far = exchange(over, CORE)
    adj_over = exchange(adj_outgoing, CHIP)
    adj_mate = exchange(adj_own, CORE)

    scratch = pltpu.VMEM((planes_all + 4, rows_x, rows_y), jnp.float32)
    y_scratch = pltpu.VMEM((BATCH * rows_x, rows_y), jnp.float32)
    step_scratch = [scratch, scratch, pltpu.VMEM((2 * rows_y, rows_y), jnp.bfloat16), y_scratch, y_scratch]
    params = pltpu.CompilerParams(vmem_limit_bytes=6 * 2**20)
    cost = pl.CostEstimate(flops=30 * steps * cells_all, bytes_accessed=16 * steps * cells_all, transcendentals=0)
    laps, inject, cour, mark = pl.pallas_call(
        forward_kernel,
        in_specs=[smem, smem, pl.BlockSpec(memory_space=pl.ANY)] + [vmem] * 9,
        out_specs=[vmem] * 4,
        out_shape=[
            jax.ShapeDtypeStruct((steps, planes, 2, rows_x, rows_y), jnp.float32),
            jax.ShapeDtypeStruct((steps, planes_all, rows_x, rows_y), jnp.float32),
            jax.ShapeDtypeStruct((planes_all, rows_x, rows_y), jnp.float32),
            jax.ShapeDtypeStruct((8, rows_y), jnp.float32),
        ],
        scratch_shapes=step_scratch,
        compiler_params=params,
        cost_estimate=cost,
        name="forward_steps",
    )(ckpt_step[None], src_cells, second, own, mate, over, far, c0, c1, c2, c3, placed)

    adj_over, mark = lax.optimization_barrier((adj_over, mark))
    adj_far = exchange(adj_over, CORE)
    slab = jax.ShapeDtypeStruct(courant_sq.shape, jnp.float32)
    half, quarter = (planes // 2, rows_x, rows_y), (planes // 4, rows_x, rows_y)
    keep_a, send_a, keep_b, send_b = pl.pallas_call(
        adjoint_kernel,
        in_specs=[pl.BlockSpec(memory_space=pl.ANY)] + [vmem] * 7,
        out_specs=[vmem] * 4,
        out_shape=[jax.ShapeDtypeStruct(half, jnp.float32)] * 4,
        scratch_shapes=step_scratch[:2] + [pltpu.VMEM((2 * planes, rows_x, rows_y), jnp.float32)] + step_scratch[2:],
        compiler_params=params,
        cost_estimate=cost,
        name="adjoint_steps",
    )(mark, adj_own, adj_mate, adj_over, adj_far, cour, laps, inject)

    other_a, other_b = exchange(send_a, CHIP), exchange(send_b, Y)
    keep_a, send_a, keep_b, send_b = local(cross_kernel, [quarter] * 4, keep_a, other_a, keep_b, other_b)
    other_a, other_b = exchange(send_a, Y), exchange(send_b, CHIP)
    keep, send = local(choose_kernel, [quarter] * 2, keep_a, other_a, keep_b, other_b)
    part = local(add_kernel, [quarter], keep, exchange(send, NEAR_Z))
    data, sums = local(sums_kernel, [quarter, (8, rows_y)], part, exchange(part, FAR_Z), momentum)

    planes_back = [data] + [exchange(data, bits) for bits in (NEAR_Z, Y, NEAR_Z + Y)]
    sums = [sums] + [exchange(sums, bits) for bits in (CORE, CHIP, CORE + CHIP)]
    sums = local(add_sums_kernel, [(8, rows_y)], *sums)
    sums = [sums] + [exchange(sums, bits) for bits in (NEAR_Z, Y, NEAR_Z + Y)]
    back = (0, 2, 1, 3)
    momentum_half, kinetic = pl.pallas_call(
        finish_kernel,
        in_specs=[vmem] * 9,
        out_specs=[vmem, smem],
        out_shape=[jax.ShapeDtypeStruct(momentum.shape, jnp.float32), jax.ShapeDtypeStruct((1,), jnp.float32)],
        compiler_params=pltpu.CompilerParams(vmem_limit_bytes=4 * 2**20),
        name="finish",
    )(*[planes_back[n] for n in back], momentum, *[sums[n] for n in back])
    return momentum_half, kinetic[0]


def solution(mesh):
    shots, slabs = mesh.shape["shot"], mesh.shape["depth"]

    def placed(depth):
        field = P("shot", depth, None, None)
        slab = P(depth, None, None)
        inputs = (slab, slab, field, field, field, field, P("shot", None, None), P("shot"), P("shot", None), P())
        return dict(in_specs=inputs, out_specs=(slab, P()), check_vma=False)

    slab_plan = jax.shard_map(slab_shards, mesh=mesh, **placed("depth"))
    if slabs != 4 or shots != 8:
        return slab_plan
    chips = Mesh(mesh.devices.reshape(shots, 2, 2), ("shot", "chip", "core"))
    whole_plan = jax.shard_map(whole_shards, mesh=chips, **placed(("chip", "core")))

    def run(courant_sq, momentum, fwd_prev, *rest):
        total, planes, rows_x, rows_y = fwd_prev.shape
        steps = rest[3].shape[1]
        fits = total == 2 * shots and planes == 4 * shots and rows_y == 128 and rows_x % 16 == 0 and steps % 2 == 0
        plan = whole_plan if fits else slab_plan
        return plan(courant_sq, momentum, fwd_prev, *rest)

    return run
```

```python
import functools

import jax
import jax.numpy as jnp
from jax import lax
from jax.experimental import pallas as pl
from jax.experimental.pallas import tpu as pltpu
from jax.sharding import Mesh
from jax.sharding import PartitionSpec as P

CENTER = -2.5
NEAR = 4.0 / 3.0
FAR = -1.0 / 12.0
AMPLITUDE = 100.0
EPSILON = 1e-06


def with_halo(value, sides, width):
    for axis, dim in sides:
        size, length = (lax.axis_size(axis), value.shape[dim])
        up = [(i, (i + 1) % size) for i in range(size - 1)]
        down = [(j, i) for i, j in up]
        last = lax.slice_in_dim(value, length - width, length, axis=dim)
        leading = lax.slice_in_dim(value, 0, width, axis=dim)
        before = lax.ppermute(last, axis, up)
        after = lax.ppermute(leading, axis, down)
        value = jnp.concatenate([before, value, after], axis=dim)
    return value


def laplace(padded):
    lateral = jnp.pad(padded[:, 2:-2], ((0, 0), (0, 0), (2, 2), (2, 2)))
    center = padded[:, 2:-2]
    along_z = NEAR * (padded[:, 1:-3] + padded[:, 3:-1]) + FAR * (padded[:, :-4] + padded[:, 4:])
    along_x = NEAR * (lateral[:, :, 1:-3, 2:-2] + lateral[:, :, 3:-1, 2:-2]) + FAR * (
        lateral[:, :, :-4, 2:-2] + lateral[:, :, 4:, 2:-2]
    )
    along_y = NEAR * (lateral[:, :, 2:-2, 1:-3] + lateral[:, :, 2:-2, 3:-1]) + FAR * (
        lateral[:, :, 2:-2, :-4] + lateral[:, :, 2:-2, 4:]
    )
    return 3.0 * CENTER * center + along_z + along_x + along_y


def locate(field, cell_ids, first_plane):
    shot_count, planes, rows_x, rows_y = field.shape
    plane_cells = rows_x * rows_y
    local_index = cell_ids - first_plane * plane_cells
    inside = (local_index >= 0) & (local_index < planes * plane_cells)
    target = jnp.where(inside, local_index, 0)
    return (inside, target)


def inject(field, cell_ids, values, first_plane):
    shot_count = field.shape[0]
    inside, target = locate(field, cell_ids, first_plane)
    amount = jnp.where(inside, values, jnp.zeros_like(values))
    flattened = field.reshape(shot_count, -1)
    lanes = jnp.arange(shot_count)[:, None]
    flattened = flattened.at[lanes, target].add(amount)
    return flattened.reshape(field.shape)


def sample(field, cell_ids, first_plane):
    shot_count = field.shape[0]
    inside, target = locate(field, cell_ids, first_plane)
    values = jnp.take_along_axis(field.reshape(shot_count, -1), target, axis=1)
    return jnp.where(inside, values, jnp.zeros_like(values))


def wave_value(start, step):
    cycle = jnp.mod(start + jnp.int32(step), jnp.int32(48))
    phase = (cycle.astype(jnp.float32) - 24.0) / 12.0
    return AMPLITUDE * (1.0 - 2.0 * phase * phase) * jnp.exp(-phase * phase)


def statistics(scaled, moment, weight, cells_all):
    grand_total = lax.psum(jnp.sum(scaled * scaled), ("shot", "depth"))
    factor = lax.rsqrt(grand_total / cells_all + EPSILON)
    halfway = moment - 0.5 * factor * scaled
    energy = lax.psum(jnp.sum(weight * halfway * halfway), ("shot", "depth"))
    return (factor, 0.5 * energy / cells_all)


def slab_shards(
    courant_sq,
    momentum,
    fwd_prev,
    fwd_cur,
    adj_next,
    adj_cur,
    observed,
    src_cells,
    rec_cells,
    ckpt_step,
):
    shot_count, planes, rows_x, rows_y = fwd_cur.shape
    steps_all = observed.shape[1]
    first_plane = lax.axis_index("depth") * planes
    total_planes = planes * lax.axis_size("depth")
    cells_all = total_planes * rows_x * rows_y
    sources = src_cells[:, None]
    older, current = (fwd_prev, fwd_cur)
    laplacians = []
    misfits = []
    for step in range(steps_all):
        padded = with_halo(current, (("depth", 1),), 2)
        strength = jnp.full(sources.shape, wave_value(ckpt_step, step), jnp.float32)
        laplacian = inject(laplace(padded), sources, strength, first_plane)
        newer = 2.0 * current - older + courant_sq * laplacian
        misfits.append(sample(newer, rec_cells, first_plane) - observed[:, step, :])
        laplacians.append(laplacian)
        older, current = (current, newer)
    adj_later, adj_now = (adj_next, adj_cur)
    gradient = jnp.zeros((planes, rows_x, rows_y), jnp.float32)
    for step in reversed(range(steps_all)):
        padded = with_halo(courant_sq * adj_now, (("depth", 1),), 2)
        adj_new = 2.0 * adj_now - adj_later + laplace(padded)
        adj_new = inject(adj_new, rec_cells, misfits[step], first_plane)
        gradient = gradient + jnp.sum(adj_new * laplacians[step], axis=0)
        adj_later, adj_now = (adj_now, adj_new)
    depths = (first_plane + jnp.arange(planes)).astype(jnp.float32)
    weight = (1.0 + 2.0 * depths / (total_planes - 1))[:, None, None]
    share_rows = rows_x // lax.axis_size("shot")
    offset = lax.axis_index("shot") * share_rows
    moment_share = lax.dynamic_slice_in_dim(momentum, offset, share_rows, 1)
    gradient = lax.psum(gradient, "shot")
    scaled = weight * gradient
    scaled_share = lax.dynamic_slice_in_dim(scaled, offset, share_rows, 1)
    factor, kinetic = statistics(scaled_share, moment_share, weight, cells_all)
    momentum_half = momentum - 0.5 * factor * scaled
    return (momentum_half, kinetic)


def interleave(dst, slab, src, factor=None):
    planes, rows = src.shape[0], src.shape[1]
    groups = rows // 8

    @pl.loop(0, planes)
    def _(p):
        for i in range(groups):
            value = src[p, pl.ds(i, 8, stride=groups), :]
            if factor is not None:
                value = value * factor
            dst[(*slab, p, pl.ds(i * 8, 8), slice(None))] = value


def pick_kernel(across, *refs):
    count = len(across)
    fields, outs, (held, sems) = refs[: 2 * count], refs[2 * count : 3 * count], refs[3 * count :]
    chip = lax.axis_index("chip")
    copies = []
    for n in range(2 * count):
        shot = 1 - chip if across[n // 2] else chip
        copies.append(pltpu.make_async_copy(fields[n].at[shot], held.at[n], sems.at[n]))
        copies[-1].start()
    for n in range(2 * count):
        copies[n].wait()
        interleave(outs[n // 2], (n % 2,), held.at[n])


def pick(*pairs, after=None, grant=16):
    plain = functools.partial(pick_kernel, tuple(pair[2] for pair in pairs))
    fields = [field for pair in pairs for field in pair[:2]]
    shape = fields[0].shape[1:]
    vmem, hbm = pl.BlockSpec(memory_space=pltpu.VMEM), pl.BlockSpec(memory_space=pltpu.HBM)
    marks = [] if after is None else [after]
    return pl.pallas_call(
        lambda *refs: plain(*refs[len(marks) :]),
        in_specs=[vmem] * len(marks) + [hbm] * len(fields),
        out_specs=[vmem] * len(pairs),
        out_shape=[jax.ShapeDtypeStruct((2, *shape), jnp.float32)] * len(pairs),
        scratch_shapes=[pltpu.VMEM((len(fields), *shape), jnp.float32), pltpu.SemaphoreType.DMA((len(fields),))],
        compiler_params=pltpu.CompilerParams(vmem_limit_bytes=grant * 2**18),
        name="pick",
    )(*marks, *fields)


def courant_kernel(courant, whole, piece):
    interleave(whole, (), courant, 1.0 / 12.0)
    count = piece.shape[0]
    piece[...] = whole[pl.ds(lax.axis_index("shot") % 2 * count, count)]


def band(lanes):
    near = jnp.abs(lax.broadcasted_iota(jnp.int32, (2 * lanes, lanes), 0) % lanes - lax.broadcasted_iota(jnp.int32, (2 * lanes, lanes), 1))
    return jnp.where(near == 0, -90.0, jnp.where(near == 1, 16.0, jnp.where(near == 2, -1.0, 0.0))).astype(jnp.bfloat16)


def along_y(field, z, banded, out):
    rows, lanes = field.shape[1:]
    whole = field[pl.ds(z + 2, BATCH)].reshape(BATCH * rows, lanes)
    high = whole.astype(jnp.bfloat16)
    low = (whole - high.astype(jnp.float32)).astype(jnp.bfloat16)
    out[...] = jnp.dot(jnp.concatenate([high, low], 1), banded[...], preferred_element_type=jnp.float32)


def y_shifts(center):
    lanes = center.shape[1]
    lane = lax.broadcasted_iota(jnp.int32, center.shape, 1)

    def shift(by):
        inside = lane >= by if by > 0 else lane < lanes + by
        return jnp.where(inside, pltpu.roll(center, by % lanes, 1), 0.0)

    return shift(1) + shift(-1), shift(2) + shift(-2)


def laps12(field, z, y_part, fetch, finish):
    rows, lanes = field.shape[1:]
    groups = rows // 8
    sub = lax.broadcasted_iota(jnp.int32, (8, lanes), 0)

    def later(block):
        return jnp.where(sub < 7, pltpu.roll(block, 7, 0), 0.0)

    def earlier(block):
        return jnp.where(sub > 0, pltpu.roll(block, 1, 0), 0.0)

    for base in range(0, BATCH, PLANES):
        held = {}

        def tile(j, i):
            if (j, i) not in held:
                if i < 0:
                    held[j, i] = earlier(tile(j, i + groups))
                elif i >= groups:
                    held[j, i] = later(tile(j, i - groups))
                else:
                    held[j, i] = field[z + j + 2, i * 8 : (i + 1) * 8]
            return held[j, i]

        def load(i):
            found = []
            for j in range(base, base + PLANES):
                center = tile(j, i)
                near = (tile(j, i - 1), tile(j, i + 1), tile(j - 1, i), tile(j + 1, i))
                far = (tile(j, i - 2), tile(j, i + 2), tile(j - 2, i), tile(j + 2, i))
                at = (j * groups + i) * 8
                part = y_shifts(center) if y_part is None else y_part[at : at + 8]
                found.append((center, near, far, part, fetch(j, slice(i * 8, i * 8 + 8))))
            return found

        ready = load(0)
        for i in range(groups):
            upcoming = load(i + 1) if i + 1 < groups else None
            for j, (center, near, far, part, extra) in enumerate(ready):
                near = (near[0] + near[1]) + (near[2] + near[3])
                far = (far[0] + far[1]) + (far[2] + far[3])
                if y_part is None:
                    lap = 16.0 * (near + part[0]) - (far + part[1]) - 90.0 * center
                else:
                    lap = 16.0 * near + (part - far)
                finish(base + j, slice(i * 8, i * 8 + 8), center, lap, extra)
            ready = upcoming


def scatter_kernel(rows_x, cells_ref, observed_ref, out_ref, mark, second, row_ref, spread):
    _, steps, receivers = observed_ref.shape
    lanes = out_ref.shape[2]
    tile = out_ref.shape[1]
    groups = rows_x // 8

    @pl.when(pl.program_id(0) == 0)
    def _():
        chip = lax.axis_index("chip")
        cells = cells_ref[pl.ds(chip, 1)]
        x = cells // lanes % rows_x
        row_ref[...] = cells // (rows_x * lanes) * rows_x + x % groups * 8 + x // groups
        on_lanes = jnp.concatenate(
            [
                observed_ref[chip],
                jnp.broadcast_to((cells % lanes).astype(jnp.float32), (8, receivers)),
                jnp.zeros((lanes - steps - 8, receivers), jnp.float32),
            ],
            0,
        )
        columns = on_lanes.T
        lane = lax.broadcasted_iota(jnp.int32, (receivers, lanes), 1).astype(jnp.float32)
        at = lane == columns[:, steps : steps + 1]
        for k in range(steps):
            column = columns[:, k : k + 1]
            high = column.astype(jnp.bfloat16).astype(jnp.float32)
            low = column - high
            cols = pl.ds(k * lanes, lanes)
            spread[0:receivers, cols] = jnp.where(at, high, 0.0).astype(jnp.bfloat16)
            spread[receivers:, cols] = jnp.where(at, low, 0.0).astype(jnp.bfloat16)
        cols = pl.ds(steps * lanes, lanes)
        spread[0:receivers, cols] = jnp.where(at, 1.0, 0.0).astype(jnp.bfloat16)
        spread[receivers:, cols] = jnp.zeros((receivers, lanes), jnp.bfloat16)
        mark[...] = jnp.zeros(mark.shape, jnp.float32)
        second[...] = jnp.zeros(mark.shape, jnp.float32)

    ids = lax.broadcasted_iota(jnp.int32, (tile, receivers), 0) + pl.program_id(0) * tile
    chosen = jnp.where(ids == row_ref[...], 1.0, 0.0).astype(jnp.bfloat16)
    total = jnp.dot(jnp.concatenate([chosen, chosen], 1), spread[...], preferred_element_type=jnp.float32)
    for k in range(steps + 1):
        out_ref[k] = total[:, k * lanes : (k + 1) * lanes]


def scatter(rec_cells, observed, planes_all, rows_x, rows_y):
    _, steps, receivers = observed.shape
    rows_all = planes_all * rows_x
    tile = 256
    mark = jax.ShapeDtypeStruct((8, rows_y), jnp.float32)
    mark_block = pl.BlockSpec((8, rows_y), lambda t: (0, 0))
    return pl.pallas_call(
        functools.partial(scatter_kernel, rows_x),
        grid=(rows_all // tile,),
        in_specs=[
            pl.BlockSpec((2, receivers), lambda t: (0, 0)),
            pl.BlockSpec((2, steps, receivers), lambda t: (0, 0, 0)),
        ],
        out_specs=[pl.BlockSpec((steps + 1, tile, rows_y), lambda t: (0, t, 0)), mark_block, mark_block],
        out_shape=[jax.ShapeDtypeStruct((steps + 1, rows_all, rows_y), jnp.float32), mark, mark],
        scratch_shapes=[
            pltpu.VMEM((1, receivers), jnp.int32),
            pltpu.VMEM((2 * receivers, (steps + 1) * rows_y), jnp.bfloat16),
        ],
        compiler_params=pltpu.CompilerParams(vmem_limit_bytes=56 * 2**20),
        cost_estimate=pl.CostEstimate(
            flops=4 * rows_all * receivers * (steps + 1) * rows_y,
            bytes_accessed=4 * (steps + 1) * rows_all * rows_y,
            transcendentals=0,
        ),
        name="receiver_scatter",
    )(rec_cells, observed)


def place(planes):
    chip, core = lax.axis_index("chip"), lax.axis_index("core")
    slabs = (2 * chip + core, 2 * chip + 1 - core, 2 * (1 - chip) + core, 2 * (1 - chip) + 1 - core)
    return chip, core, [slab * planes for slab in slabs]


def load_blocks(slabs, blocks, first, second):
    ends = first.shape[0]
    planes = blocks[0].shape[1]
    for field in (first, second):
        for z in (0, 1, ends - 2, ends - 1):
            field[z] = jnp.zeros(field.shape[1:], jnp.float32)
    for slab, block in zip(slabs, blocks):

        @pl.loop(0, planes)
        def _(p):
            first[slab + p + 2] = block[0, p]
            second[slab + p + 2] = block[1, p]


BATCH = 4
PLANES = 2


def sweep(core, planes, field, banded, y_first, y_second, work):
    order = [(chip, owned) for owned in (True, False) for chip in (0, 1)]
    parts = (y_first, y_second)

    def first(chip, owned):
        return (2 * chip + (core if owned else 1 - core)) * planes

    along_y(field, first(*order[0]), banded, y_first)
    for owned in (True, False):
        for chip in (0, 1):
            z = first(chip, owned)
            onward = first(1, owned) if chip == 0 else first(0, False)
            for n in range(planes // BATCH):
                last = n == planes // BATCH - 1
                if not last or chip == 0 or owned:
                    along_y(field, onward if last else z + (n + 1) * BATCH, banded, parts[(n + 1) % 2])
                work(z + n * BATCH, parts[n % 2], chip if owned else None, n * BATCH)


def sweep_shifts(core, planes, work):
    for owned in (True, False):

        @pl.loop(0, 2)
        def _(chip):
            z = (2 * chip + (core if owned else 1 - core)) * planes
            for p in range(0, planes, BATCH):
                work(z + p, None, chip if owned else None, p)


def forward_kernel(
    start, sources, scattered, own, mate, over, far, c0, c1, c2, c3, placed, laps, inject, cour, mark, even, odd, traces_even, traces_odd, counts, sems
):
    planes, rows, lanes = c0.shape
    steps = laps.shape[0]
    groups = rows // 8
    chip_here, core, slabs = place(planes)
    mark[...] = jnp.zeros(mark.shape, jnp.float32)

    def copy(k, slot):
        return pltpu.make_async_copy(placed.at[k], (traces_even, traces_odd)[slot], sems.at[slot])

    copy(0, 0).start()
    count_copy = pltpu.make_async_copy(placed.at[steps], counts, sems.at[2])
    count_copy.start()
    copy(1, 1).start()
    load_blocks(slabs, (own, mate, over, far), odd, even)
    for slab, block in zip(slabs, (c0, c1, c2, c3)):

        @pl.loop(0, planes)
        def _(p):
            cour[slab + p] = block[p]

    cell = sources[chip_here]
    source_z, x, lane = cell // (rows * lanes), cell // lanes % rows, cell % lanes
    tile = pl.ds(pl.multiple_of(x % groups * 8, 8), 8)
    here = (lax.broadcasted_iota(jnp.int32, (8, lanes), 0) == x // groups) & (
        lax.broadcasted_iota(jnp.int32, (8, lanes), 1) == lane
    )
    source_slab, source_p = source_z // planes, lax.rem(source_z, planes)

    def advance(k, now, then, observed, slot):
        copy(k, slot).wait()

        def work(z, y_part, chip, p):
            def fetch(j, rows):
                return then[z + j + 2, rows], cour[z + j, rows], observed[z + j, rows], counts[z + j, rows]

            def finish(j, rows, center, lap, extra):
                old, speed, traces, count = extra
                if chip is not None:
                    laps[k, p + j, chip, rows] = lap
                newer = 2.0 * center - old + speed * lap
                then[z + j + 2, rows] = newer
                inject[k, z + j, rows] = traces - count * newer

            laps12(now, z, y_part, fetch, finish)

        sweep_shifts(core, planes, work)

        @pl.when(k + 2 < steps)
        def _():
            copy(k + 2, slot).start()

        cycle = (start[0] + k) % 48
        phase = (jnp.full((8, lanes), cycle, jnp.int32).astype(jnp.float32) - 24.0) / 12.0
        wave = AMPLITUDE * (1.0 - 2.0 * phase * phase) * jnp.exp(-phase * phase)
        strength = jnp.where(here, 12.0 * wave, 0.0)

        @pl.when(lax.rem(source_slab, 2) == core)
        def _():
            laps[k, source_p, source_slab // 2, tile, :] += strength

        moved = cour[source_z, tile, :] * strength
        then[source_z + 2, tile, :] += moved
        inject[k, source_z, tile, :] -= counts[source_z, tile, :] * moved

    count_copy.wait()

    @pl.loop(0, steps // 2)
    def _(pair):
        advance(2 * pair, even, odd, traces_even, 0)
        advance(2 * pair + 1, odd, even, traces_odd, 1)


def adjoint_kernel(mark, own, mate, over, far, cour, laps, inject, keep_a, send_a, keep_b, send_b, even, odd, total, banded, y0, y1):
    planes, rows, lanes = own.shape[1:]
    steps = laps.shape[0]
    groups = rows // 8
    chip_here, core, slabs = place(planes)
    banded[...] = band(lanes)
    load_blocks(slabs, (own, mate, over, far), odd, even)

    @pl.loop(0, 4 * planes)
    def _(z):
        even[z + 2] = even[z + 2] * cour[z]
        odd[z + 2] = odd[z + 2] * cour[z]

    @pl.loop(0, 2 * planes)
    def _(index):
        total[index] = jnp.zeros((rows, lanes), jnp.float32)

    def advance(k, now, then):
        def work(z, y_part, chip, p):
            def fetch(j, rows):
                extra = (then[z + j + 2, rows], cour[z + j, rows], inject[k, z + j, rows])
                if chip is not None:
                    extra += (total[chip * planes + p + j, rows], laps[k, p + j, chip, rows])
                return extra

            def finish(j, rows, center, lap, extra):
                newer = 2.0 * center - extra[0] + extra[1] * (lap - extra[2])
                then[z + j + 2, rows] = newer
                if chip is not None:
                    total[chip * planes + p + j, rows] = extra[3] + newer * extra[4]

            laps12(now, z, y_part, fetch, finish)

        sweep(core, planes, now, banded, y0, y1, work)

    @pl.loop(0, steps // 2)
    def _(pair):
        advance(steps - 1 - 2 * pair, even, odd)
        advance(steps - 2 - 2 * pair, odd, even)

    half, quarter = planes // 2, planes // 4
    y = lax.axis_index("shot") % 2
    here, there = chip_here, 1 - chip_here
    runs = [(keep_a, 0, half, here, 0), (send_a, 0, half, there, 0)]
    for ref, side in ((keep_b, y), (send_b, 1 - y)):
        runs += [(ref, 0, quarter, here, half + side * quarter), (ref, quarter, quarter, there, half + side * quarter)]
    for ref, at, count, chip, start in runs:

        @pl.loop(0, count)
        def _(n):
            p = start + n
            z = (2 * chip + core) * planes + p
            weight = 1.0 + 2.0 * jnp.full((rows, lanes), z, jnp.int32).astype(jnp.float32) / (4 * planes - 1)
            value = weight * total[chip * planes + p] / (12.0 * cour[z])
            for i in range(groups):
                ref[at + n, pl.ds(i, 8, stride=groups), :] = value[i * 8 : (i + 1) * 8]


def cross_kernel(keep_a, other_a, keep_b, other_b, next_a, send_a, next_b, send_b):
    y = lax.axis_index("shot") % 2
    count = next_a.shape[0]
    for ref, part in ((next_a, y), (send_a, 1 - y)):
        for p in range(count):
            ref[p] = keep_a[part * count + p] + other_a[part * count + p]
    for ref, part in ((next_b, 0), (send_b, 1)):
        for p in range(count):
            ref[p] = keep_b[part * count + p] + other_b[part * count + p]


def choose_kernel(keep_a, other_a, keep_b, other_b, keep, send):
    second = lax.axis_index("shot") // 2 % 2 == 1
    first_half = keep_a[...] + other_a[...]
    second_half = keep_b[...] + other_b[...]
    keep[...] = jnp.where(second, second_half, first_half)
    send[...] = jnp.where(second, first_half, second_half)


def add_kernel(mine, other, out):
    out[...] = mine[...] + other[...]


def flip(index, bits):
    result = index
    for bit in (1, 2):
        if bits & bit:
            result = jnp.where(index // bit % 2 == 1, result - bit, result + bit)
    return result


def arrange_kernel(mine, other, out):
    y = lax.axis_index("shot") % 2
    count = mine.shape[0]
    out[pl.ds(y * count, count)] = mine[...]
    out[pl.ds((1 - y) * count, count)] = other[...]


def first_plane(shot, planes):
    return (shot // 2 % 2) * (planes // 2) + (shot % 2) * (planes // 4)


def sums_kernel(mine, other, momentum, data, sums):
    count, rows, lanes = mine.shape
    planes = momentum.shape[0]
    chip, core = lax.axis_index("chip"), lax.axis_index("core")
    first = first_plane(lax.axis_index("shot"), planes)
    parts = [jnp.zeros((rows, lanes), jnp.float32)] * 4
    for j in range(count):
        scaled = mine[j] + other[j]
        data[j * rows : (j + 1) * rows] = scaled
        z = (2 * chip + core) * planes + first + j
        weight = 1.0 + 2.0 * jnp.full((1, lanes), z, jnp.int32).astype(jnp.float32) / (4 * planes - 1)
        moment = momentum[first + j]
        square = scaled * scaled
        terms = (square, weight * moment * moment, weight * moment * scaled, weight * square)
        parts = [part + term for part, term in zip(parts, terms)]

    def total(value):
        by_lane = jnp.sum(value, axis=0, keepdims=True)
        return jnp.broadcast_to(jnp.sum(by_lane, axis=1, keepdims=True), (1, lanes))

    value = jnp.concatenate([total(part) for part in parts] + [jnp.zeros((4, lanes), jnp.float32)], 0)
    data[count * rows :] = value
    sums[...] = value


def join_kernel(mine, other, s0, s1, s2, data, sums):
    rows = mine.shape[0] - 8
    data[0:rows] = mine[0:rows]
    data[rows : 2 * rows] = other[0:rows]
    value = (s0[...] + s1[...]) + (other[rows:] + s2[...])
    data[2 * rows :] = value
    sums[...] = value


def finish_kernel(mine, other, momentum, s0, s1, s2, out, kinetic):
    planes, rows, lanes = momentum.shape
    cells = 4.0 * planes * rows * lanes
    shot = lax.axis_index("shot")
    sums = (s0[...] + s1[...]) + (other[planes // 2 * rows :] + s2[...])
    factor = lax.rsqrt(sums[0:1] / cells + EPSILON)
    energy = 0.5 * (sums[1:2] - factor * sums[2:3] + 0.25 * factor * factor * sums[3:4]) / cells
    kinetic[0] = energy[0, 0]
    step = 0.5 * factor
    quarter = planes // 4
    for part, group in ((mine, shot), (other, flip(shot, 1))):
        for number, first in enumerate((first_plane(group, planes), first_plane(flip(group, 2), planes))):
            for j in range(quarter):
                at = (number * quarter + j) * rows
                out[first + j] = momentum[first + j] - step * part[at : at + rows]


def local(kernel, outs, *arrays):
    vmem = pl.BlockSpec(memory_space=pltpu.VMEM)
    shapes = [jax.ShapeDtypeStruct(shape, jnp.float32) for shape in outs]
    single = len(outs) == 1
    return pl.pallas_call(
        kernel,
        in_specs=[vmem] * len(arrays),
        out_specs=vmem if single else [vmem] * len(outs),
        out_shape=shapes[0] if single else shapes,
        compiler_params=pltpu.CompilerParams(vmem_limit_bytes=4 * 2**20),
        name=kernel.__name__,
    )(*arrays)


def exchange(value, bits):
    axes = ("shot", "chip", "core")
    return lax.ppermute(value, axes, [(i, i ^ bits) for i in range(lax.axis_size(axes))])


CORE, CHIP, Y, NEAR_Z, FAR_Z = 1, 2, 4, 8, 16


def whole_shards(
    courant_sq, momentum, fwd_prev, fwd_cur, adj_next, adj_cur, observed, src_cells, rec_cells, ckpt_step
):
    _, planes, rows_x, rows_y = fwd_cur.shape
    steps = observed.shape[1]
    planes_all = 4 * planes
    cells_all = planes_all * rows_x * rows_y
    vmem, smem = pl.BlockSpec(memory_space=pltpu.VMEM), pl.BlockSpec(memory_space=pltpu.SMEM)

    (outgoing,) = pick((fwd_prev, fwd_cur, True), grant=253)
    over = exchange(outgoing, CHIP)

    c0, piece = local(courant_kernel, [courant_sq.shape, (planes // 2, rows_x, rows_y)], courant_sq)
    piece = exchange(piece, CHIP)
    (own,) = pick((fwd_prev, fwd_cur, False))
    mate = exchange(own, CORE)
    c1 = exchange(c0, CORE)
    c2 = local(arrange_kernel, [courant_sq.shape], piece, exchange(piece, Y))
    c3 = exchange(c2, CORE)

    placed, mark, second = scatter(rec_cells, observed, planes_all, rows_x, rows_y)
    placed = placed.reshape(steps + 1, planes_all, rows_x, rows_y)

    adj_outgoing, adj_own = pick((adj_next, adj_cur, True), (adj_next, adj_cur, False), after=mark)
    over, second = lax.optimization_barrier((over, second))
    far = exchange(over, CORE)
    adj_over = exchange(adj_outgoing, CHIP)
    adj_mate = exchange(adj_own, CORE)

    scratch = pltpu.VMEM((planes_all + 4, rows_x, rows_y), jnp.float32)
    whole = pltpu.VMEM((planes_all, rows_x, rows_y), jnp.float32)
    y_scratch = pltpu.VMEM((BATCH * rows_x, rows_y), jnp.float32)
    step_scratch = [scratch, scratch, pltpu.VMEM((2 * rows_y, rows_y), jnp.bfloat16), y_scratch, y_scratch]
    params = pltpu.CompilerParams(vmem_limit_bytes=6 * 2**20)
    cost = pl.CostEstimate(flops=30 * steps * cells_all, bytes_accessed=16 * steps * cells_all, transcendentals=0)
    laps, inject, cour, mark = pl.pallas_call(
        forward_kernel,
        in_specs=[smem, smem, pl.BlockSpec(memory_space=pl.ANY)] + [vmem] * 8 + [pl.BlockSpec(memory_space=pltpu.HBM)],
        out_specs=[vmem] * 4,
        out_shape=[
            jax.ShapeDtypeStruct((steps, planes, 2, rows_x, rows_y), jnp.float32),
            jax.ShapeDtypeStruct((steps, planes_all, rows_x, rows_y), jnp.float32),
            jax.ShapeDtypeStruct((planes_all, rows_x, rows_y), jnp.float32),
            jax.ShapeDtypeStruct((8, rows_y), jnp.float32),
        ],
        scratch_shapes=[scratch, scratch, whole, whole, whole, pltpu.SemaphoreType.DMA((3,))],
        compiler_params=pltpu.CompilerParams(vmem_limit_bytes=33 * 2**20),
        cost_estimate=cost,
        name="forward_steps",
    )(ckpt_step[None], src_cells, second, own, mate, over, far, c0, c1, c2, c3, placed)

    adj_over, mark = lax.optimization_barrier((adj_over, mark))
    adj_far = exchange(adj_over, CORE)
    slab = jax.ShapeDtypeStruct(courant_sq.shape, jnp.float32)
    half, quarter = (planes // 2, rows_x, rows_y), (planes // 4, rows_x, rows_y)
    keep_a, send_a, keep_b, send_b = pl.pallas_call(
        adjoint_kernel,
        in_specs=[pl.BlockSpec(memory_space=pl.ANY)] + [vmem] * 7,
        out_specs=[vmem] * 4,
        out_shape=[jax.ShapeDtypeStruct(half, jnp.float32)] * 4,
        scratch_shapes=step_scratch[:2] + [pltpu.VMEM((2 * planes, rows_x, rows_y), jnp.float32)] + step_scratch[2:],
        compiler_params=params,
        cost_estimate=cost,
        name="adjoint_steps",
    )(mark, adj_own, adj_mate, adj_over, adj_far, cour, laps, inject)

    other_a, other_b = exchange(send_a, CHIP), exchange(send_b, Y)
    keep_a, send_a, keep_b, send_b = local(cross_kernel, [quarter] * 4, keep_a, other_a, keep_b, other_b)
    other_a, other_b = exchange(send_a, Y), exchange(send_b, CHIP)
    keep, send = local(choose_kernel, [quarter] * 2, keep_a, other_a, keep_b, other_b)
    part = local(add_kernel, [quarter], keep, exchange(send, NEAR_Z))
    rows, sums_shape = planes // 4 * rows_x, (8, rows_y)
    data, sums = local(sums_kernel, [(rows + 8, rows_y), sums_shape], part, exchange(part, FAR_Z), momentum)

    received = exchange(data, NEAR_Z)
    others = [exchange(sums, CORE), exchange(sums, NEAR_Z + CORE)]
    data, sums = local(join_kernel, [(2 * rows + 8, rows_y), sums_shape], data, received, sums, *others)
    received = exchange(data, Y)
    others = [exchange(sums, CHIP), exchange(sums, Y + CHIP)]
    momentum_half, kinetic = pl.pallas_call(
        finish_kernel,
        in_specs=[vmem] * 6,
        out_specs=[vmem, smem],
        out_shape=[jax.ShapeDtypeStruct(momentum.shape, jnp.float32), jax.ShapeDtypeStruct((1,), jnp.float32)],
        compiler_params=pltpu.CompilerParams(vmem_limit_bytes=4 * 2**20),
        name="finish",
    )(data, received, momentum, sums, *others)
    return momentum_half, kinetic[0]


def solution(mesh):
    shots, slabs = mesh.shape["shot"], mesh.shape["depth"]

    def placed(depth):
        field = P("shot", depth, None, None)
        slab = P(depth, None, None)
        inputs = (slab, slab, field, field, field, field, P("shot", None, None), P("shot"), P("shot", None), P())
        return dict(in_specs=inputs, out_specs=(slab, P()), check_vma=False)

    slab_plan = jax.shard_map(slab_shards, mesh=mesh, **placed("depth"))
    if slabs != 4 or shots != 8:
        return slab_plan
    chips = Mesh(mesh.devices.reshape(shots, 2, 2), ("shot", "chip", "core"))
    whole_plan = jax.shard_map(whole_shards, mesh=chips, **placed(("chip", "core")))

    def run(courant_sq, momentum, fwd_prev, *rest):
        total, planes, rows_x, rows_y = fwd_prev.shape
        steps = rest[3].shape[1]
        fits = total == 2 * shots and planes == 4 * shots and rows_y == 128 and rows_x % 16 == 0 and steps % 2 == 0
        plan = whole_plan if fits else slab_plan
        return plan(courant_sq, momentum, fwd_prev, *rest)

    return run
```

```python
import functools

import jax
import jax.numpy as jnp
from jax import lax
from jax.experimental import pallas as pl
from jax.experimental.pallas import tpu as pltpu
from jax.sharding import Mesh
from jax.sharding import PartitionSpec as P

CENTER = -2.5
NEAR = 4.0 / 3.0
FAR = -1.0 / 12.0
AMPLITUDE = 100.0
EPSILON = 1e-06


def with_halo(value, sides, width):
    for axis, dim in sides:
        size, length = (lax.axis_size(axis), value.shape[dim])
        up = [(i, (i + 1) % size) for i in range(size - 1)]
        down = [(j, i) for i, j in up]
        last = lax.slice_in_dim(value, length - width, length, axis=dim)
        leading = lax.slice_in_dim(value, 0, width, axis=dim)
        before = lax.ppermute(last, axis, up)
        after = lax.ppermute(leading, axis, down)
        value = jnp.concatenate([before, value, after], axis=dim)
    return value


def laplace(padded):
    lateral = jnp.pad(padded[:, 2:-2], ((0, 0), (0, 0), (2, 2), (2, 2)))
    center = padded[:, 2:-2]
    along_z = NEAR * (padded[:, 1:-3] + padded[:, 3:-1]) + FAR * (padded[:, :-4] + padded[:, 4:])
    along_x = NEAR * (lateral[:, :, 1:-3, 2:-2] + lateral[:, :, 3:-1, 2:-2]) + FAR * (
        lateral[:, :, :-4, 2:-2] + lateral[:, :, 4:, 2:-2]
    )
    along_y = NEAR * (lateral[:, :, 2:-2, 1:-3] + lateral[:, :, 2:-2, 3:-1]) + FAR * (
        lateral[:, :, 2:-2, :-4] + lateral[:, :, 2:-2, 4:]
    )
    return 3.0 * CENTER * center + along_z + along_x + along_y


def locate(field, cell_ids, first_plane):
    shot_count, planes, rows_x, rows_y = field.shape
    plane_cells = rows_x * rows_y
    local_index = cell_ids - first_plane * plane_cells
    inside = (local_index >= 0) & (local_index < planes * plane_cells)
    target = jnp.where(inside, local_index, 0)
    return (inside, target)


def inject(field, cell_ids, values, first_plane):
    shot_count = field.shape[0]
    inside, target = locate(field, cell_ids, first_plane)
    amount = jnp.where(inside, values, jnp.zeros_like(values))
    flattened = field.reshape(shot_count, -1)
    lanes = jnp.arange(shot_count)[:, None]
    flattened = flattened.at[lanes, target].add(amount)
    return flattened.reshape(field.shape)


def sample(field, cell_ids, first_plane):
    shot_count = field.shape[0]
    inside, target = locate(field, cell_ids, first_plane)
    values = jnp.take_along_axis(field.reshape(shot_count, -1), target, axis=1)
    return jnp.where(inside, values, jnp.zeros_like(values))


def wave_value(start, step):
    cycle = jnp.mod(start + jnp.int32(step), jnp.int32(48))
    phase = (cycle.astype(jnp.float32) - 24.0) / 12.0
    return AMPLITUDE * (1.0 - 2.0 * phase * phase) * jnp.exp(-phase * phase)


def statistics(scaled, moment, weight, cells_all):
    grand_total = lax.psum(jnp.sum(scaled * scaled), ("shot", "depth"))
    factor = lax.rsqrt(grand_total / cells_all + EPSILON)
    halfway = moment - 0.5 * factor * scaled
    energy = lax.psum(jnp.sum(weight * halfway * halfway), ("shot", "depth"))
    return (factor, 0.5 * energy / cells_all)


def slab_shards(
    courant_sq,
    momentum,
    fwd_prev,
    fwd_cur,
    adj_next,
    adj_cur,
    observed,
    src_cells,
    rec_cells,
    ckpt_step,
):
    shot_count, planes, rows_x, rows_y = fwd_cur.shape
    steps_all = observed.shape[1]
    first_plane = lax.axis_index("depth") * planes
    total_planes = planes * lax.axis_size("depth")
    cells_all = total_planes * rows_x * rows_y
    sources = src_cells[:, None]
    older, current = (fwd_prev, fwd_cur)
    laplacians = []
    misfits = []
    for step in range(steps_all):
        padded = with_halo(current, (("depth", 1),), 2)
        strength = jnp.full(sources.shape, wave_value(ckpt_step, step), jnp.float32)
        laplacian = inject(laplace(padded), sources, strength, first_plane)
        newer = 2.0 * current - older + courant_sq * laplacian
        misfits.append(sample(newer, rec_cells, first_plane) - observed[:, step, :])
        laplacians.append(laplacian)
        older, current = (current, newer)
    adj_later, adj_now = (adj_next, adj_cur)
    gradient = jnp.zeros((planes, rows_x, rows_y), jnp.float32)
    for step in reversed(range(steps_all)):
        padded = with_halo(courant_sq * adj_now, (("depth", 1),), 2)
        adj_new = 2.0 * adj_now - adj_later + laplace(padded)
        adj_new = inject(adj_new, rec_cells, misfits[step], first_plane)
        gradient = gradient + jnp.sum(adj_new * laplacians[step], axis=0)
        adj_later, adj_now = (adj_now, adj_new)
    depths = (first_plane + jnp.arange(planes)).astype(jnp.float32)
    weight = (1.0 + 2.0 * depths / (total_planes - 1))[:, None, None]
    share_rows = rows_x // lax.axis_size("shot")
    offset = lax.axis_index("shot") * share_rows
    moment_share = lax.dynamic_slice_in_dim(momentum, offset, share_rows, 1)
    gradient = lax.psum(gradient, "shot")
    scaled = weight * gradient
    scaled_share = lax.dynamic_slice_in_dim(scaled, offset, share_rows, 1)
    factor, kinetic = statistics(scaled_share, moment_share, weight, cells_all)
    momentum_half = momentum - 0.5 * factor * scaled
    return (momentum_half, kinetic)


def interleave(dst, slab, src, factor=None):
    planes, rows = src.shape[0], src.shape[1]
    groups = rows // 8

    @pl.loop(0, planes)
    def _(p):
        for i in range(groups):
            value = src[p, pl.ds(i, 8, stride=groups), :]
            if factor is not None:
                value = value * factor
            dst[(*slab, p, pl.ds(i * 8, 8), slice(None))] = value


def pick_kernel(across, *refs):
    count = len(across)
    fields, outs, (held, sems) = refs[: 2 * count], refs[2 * count : 3 * count], refs[3 * count :]
    chip = lax.axis_index("chip")
    copies = []
    for n in range(2 * count):
        shot = 1 - chip if across[n // 2] else chip
        copies.append(pltpu.make_async_copy(fields[n].at[shot], held.at[n], sems.at[n]))
        copies[-1].start()
    for n in range(2 * count):
        copies[n].wait()
        interleave(outs[n // 2], (n % 2,), held.at[n])


def pick(*pairs, after):
    plain = functools.partial(pick_kernel, tuple(pair[2] for pair in pairs))
    fields = [field for pair in pairs for field in pair[:2]]
    shape = fields[0].shape[1:]
    vmem, hbm = pl.BlockSpec(memory_space=pltpu.VMEM), pl.BlockSpec(memory_space=pltpu.HBM)
    return pl.pallas_call(
        lambda mark, *refs: plain(*refs),
        in_specs=[vmem] + [hbm] * len(fields),
        out_specs=[vmem] * len(pairs),
        out_shape=[jax.ShapeDtypeStruct((2, *shape), jnp.float32)] * len(pairs),
        scratch_shapes=[pltpu.VMEM((len(fields), *shape), jnp.float32), pltpu.SemaphoreType.DMA((len(fields),))],
        compiler_params=pltpu.CompilerParams(vmem_limit_bytes=4 * 2**20),
        name="pick",
    )(after, *fields)


def first_kernel(first, second, courant, outgoing, whole, piece, held, held_courant, sems):
    shot = 1 - lax.axis_index("chip")
    copies = [
        pltpu.make_async_copy(first.at[shot], held.at[0], sems.at[0]),
        pltpu.make_async_copy(second.at[shot], held.at[1], sems.at[1]),
        pltpu.make_async_copy(courant, held_courant, sems.at[2]),
    ]
    for copy in copies:
        copy.start()
    for n in range(2):
        copies[n].wait()
        interleave(outgoing, (n,), held.at[n])
    copies[2].wait()
    interleave(whole, (), held_courant, 1.0 / 12.0)
    count = piece.shape[0]
    piece[...] = whole[pl.ds(lax.axis_index("shot") % 2 * count, count)]


def band(lanes):
    near = jnp.abs(lax.broadcasted_iota(jnp.int32, (2 * lanes, lanes), 0) % lanes - lax.broadcasted_iota(jnp.int32, (2 * lanes, lanes), 1))
    return jnp.where(near == 0, -90.0, jnp.where(near == 1, 16.0, jnp.where(near == 2, -1.0, 0.0))).astype(jnp.bfloat16)


def along_y(field, z, banded, out):
    rows, lanes = field.shape[1:]
    whole = field[pl.ds(z + 2, BATCH)].reshape(BATCH * rows, lanes)
    high = whole.astype(jnp.bfloat16)
    low = (whole - high.astype(jnp.float32)).astype(jnp.bfloat16)
    out[...] = jnp.dot(jnp.concatenate([high, low], 1), banded[...], preferred_element_type=jnp.float32)


def laps12(field, z, y_part, fetch, finish):
    rows, lanes = field.shape[1:]
    groups = rows // 8
    sub = lax.broadcasted_iota(jnp.int32, (8, lanes), 0)

    def later(block):
        return jnp.where(sub < 7, pltpu.roll(block, 7, 0), 0.0)

    def earlier(block):
        return jnp.where(sub > 0, pltpu.roll(block, 1, 0), 0.0)

    for base in range(0, BATCH, PLANES):
        held = {}

        def tile(j, i):
            if (j, i) not in held:
                if i < 0:
                    held[j, i] = earlier(tile(j, i + groups))
                elif i >= groups:
                    held[j, i] = later(tile(j, i - groups))
                else:
                    held[j, i] = field[z + j + 2, i * 8 : (i + 1) * 8]
            return held[j, i]

        def load(i):
            found = []
            for j in range(base, base + PLANES):
                center = tile(j, i)
                near = (tile(j, i - 1), tile(j, i + 1), tile(j - 1, i), tile(j + 1, i))
                far = (tile(j, i - 2), tile(j, i + 2), tile(j - 2, i), tile(j + 2, i))
                at = (j * groups + i) * 8
                found.append((center, near, far, y_part[at : at + 8], fetch(j, slice(i * 8, i * 8 + 8))))
            return found

        ready = load(0)
        for i in range(groups):
            upcoming = load(i + 1) if i + 1 < groups else None
            for j, (center, near, far, part, extra) in enumerate(ready):
                near = (near[0] + near[1]) + (near[2] + near[3])
                far = (far[0] + far[1]) + (far[2] + far[3])
                finish(base + j, slice(i * 8, i * 8 + 8), center, 16.0 * near + (part - far), extra)
            ready = upcoming


def scatter_kernel(rows_x, cells_ref, observed_ref, out_ref, mark, row_ref, spread):
    _, steps, receivers = observed_ref.shape
    lanes = out_ref.shape[2]
    tile = out_ref.shape[1]
    groups = rows_x // 8

    @pl.when(pl.program_id(0) == 0)
    def _():
        chip = lax.axis_index("chip")
        cells = cells_ref[pl.ds(chip, 1)]
        x = cells // lanes % rows_x
        row_ref[...] = cells // (rows_x * lanes) * rows_x + x % groups * 8 + x // groups
        on_lanes = jnp.concatenate(
            [
                observed_ref[chip],
                jnp.broadcast_to((cells % lanes).astype(jnp.float32), (8, receivers)),
                jnp.zeros((lanes - steps - 8, receivers), jnp.float32),
            ],
            0,
        )
        columns = on_lanes.T
        lane = lax.broadcasted_iota(jnp.int32, (receivers, lanes), 1).astype(jnp.float32)
        at = lane == columns[:, steps : steps + 1]
        for k in range(steps):
            column = columns[:, k : k + 1]
            high = column.astype(jnp.bfloat16).astype(jnp.float32)
            low = column - high
            cols = pl.ds(k * lanes, lanes)
            spread[0:receivers, cols] = jnp.where(at, high, 0.0).astype(jnp.bfloat16)
            spread[receivers:, cols] = jnp.where(at, low, 0.0).astype(jnp.bfloat16)
        cols = pl.ds(steps * lanes, lanes)
        spread[0:receivers, cols] = jnp.where(at, 1.0, 0.0).astype(jnp.bfloat16)
        spread[receivers:, cols] = jnp.zeros((receivers, lanes), jnp.bfloat16)
        mark[...] = jnp.zeros(mark.shape, jnp.float32)

    ids = lax.broadcasted_iota(jnp.int32, (tile, receivers), 0) + pl.program_id(0) * tile
    chosen = jnp.where(ids == row_ref[...], 1.0, 0.0).astype(jnp.bfloat16)
    total = jnp.dot(jnp.concatenate([chosen, chosen], 1), spread[...], preferred_element_type=jnp.float32)
    for k in range(steps + 1):
        out_ref[k] = total[:, k * lanes : (k + 1) * lanes]


def scatter(rec_cells, observed, planes_all, rows_x, rows_y):
    _, steps, receivers = observed.shape
    rows_all = planes_all * rows_x
    tile = 512
    mark = jax.ShapeDtypeStruct((8, rows_y), jnp.float32)
    mark_block = pl.BlockSpec((8, rows_y), lambda t: (0, 0))
    return pl.pallas_call(
        functools.partial(scatter_kernel, rows_x),
        grid=(rows_all // tile,),
        in_specs=[
            pl.BlockSpec((2, receivers), lambda t: (0, 0)),
            pl.BlockSpec((2, steps, receivers), lambda t: (0, 0, 0)),
        ],
        out_specs=[pl.BlockSpec((steps + 1, tile, rows_y), lambda t: (0, t, 0)), mark_block],
        out_shape=[jax.ShapeDtypeStruct((steps + 1, rows_all, rows_y), jnp.float32), mark],
        scratch_shapes=[
            pltpu.VMEM((1, receivers), jnp.int32),
            pltpu.VMEM((2 * receivers, (steps + 1) * rows_y), jnp.bfloat16),
        ],
        compiler_params=pltpu.CompilerParams(vmem_limit_bytes=56 * 2**20),
        cost_estimate=pl.CostEstimate(
            flops=4 * rows_all * receivers * (steps + 1) * rows_y,
            bytes_accessed=4 * (steps + 1) * rows_all * rows_y,
            transcendentals=0,
        ),
        name="receiver_scatter",
    )(rec_cells, observed)


def place(planes):
    chip, core = lax.axis_index("chip"), lax.axis_index("core")
    slabs = (2 * chip + core, 2 * chip + 1 - core, 2 * (1 - chip) + core, 2 * (1 - chip) + 1 - core)
    return chip, core, [slab * planes for slab in slabs]


def load_blocks(slabs, blocks, first, second):
    ends = first.shape[0]
    planes = blocks[0].shape[1]
    for field in (first, second):
        for z in (0, 1, ends - 2, ends - 1):
            field[z] = jnp.zeros(field.shape[1:], jnp.float32)
    for slab, block in zip(slabs, blocks):

        @pl.loop(0, planes)
        def _(p):
            first[slab + p + 2] = block[0, p]
            second[slab + p + 2] = block[1, p]


BATCH = 4
PLANES = 2


def sweep(core, planes, field, banded, y_first, y_second, work):
    order = [(chip, owned) for owned in (True, False) for chip in (0, 1)]
    parts = (y_first, y_second)

    def first(chip, owned):
        return (2 * chip + (core if owned else 1 - core)) * planes

    along_y(field, first(*order[0]), banded, y_first)
    for owned in (True, False):
        for chip in (0, 1):
            z = first(chip, owned)
            onward = first(1, owned) if chip == 0 else first(0, False)
            for n in range(planes // BATCH):
                last = n == planes // BATCH - 1
                if not last or chip == 0 or owned:
                    along_y(field, onward if last else z + (n + 1) * BATCH, banded, parts[(n + 1) % 2])
                work(z + n * BATCH, parts[n % 2], chip if owned else None, n * BATCH)


def forward_kernel(
    start, sources, arranged, own, mate, over, far, c0, c1, c2, c3, placed, laps, inject, cour, mark, even, odd, banded, y0, y1,
    traces_even, traces_odd, counts, sems
):
    planes, rows, lanes = c0.shape
    steps = laps.shape[0]
    groups = rows // 8
    chip_here, core, slabs = place(planes)
    mark[...] = jnp.zeros(mark.shape, jnp.float32)

    def copy(k, slot):
        return pltpu.make_async_copy(placed.at[k], (traces_even, traces_odd)[slot], sems.at[slot])

    copy(0, 0).start()
    count_copy = pltpu.make_async_copy(placed.at[steps], counts, sems.at[2])
    count_copy.start()
    copy(1, 1).start()
    banded[...] = band(lanes)
    load_blocks(slabs, (own, mate, over, far), odd, even)
    for slab, block in zip(slabs, (c0, c1, c2, c3)):

        @pl.loop(0, planes)
        def _(p):
            cour[slab + p] = block[p]

    cell = sources[chip_here]
    source_z, x, lane = cell // (rows * lanes), cell // lanes % rows, cell % lanes
    tile = pl.ds(pl.multiple_of(x % groups * 8, 8), 8)
    here = (lax.broadcasted_iota(jnp.int32, (8, lanes), 0) == x // groups) & (
        lax.broadcasted_iota(jnp.int32, (8, lanes), 1) == lane
    )
    source_slab, source_p = source_z // planes, lax.rem(source_z, planes)

    def advance(k, now, then, observed, slot):
        copy(k, slot).wait()

        def work(z, y_part, chip, p):
            def fetch(j, rows):
                return then[z + j + 2, rows], cour[z + j, rows], observed[z + j, rows], counts[z + j, rows]

            def finish(j, rows, center, lap, extra):
                old, speed, traces, count = extra
                if chip is not None:
                    laps[k, p + j, chip, rows] = lap
                newer = 2.0 * center - old + speed * lap
                then[z + j + 2, rows] = newer
                inject[k, z + j, rows] = traces - count * newer

            laps12(now, z, y_part, fetch, finish)

        sweep(core, planes, now, banded, y0, y1, work)

        @pl.when(k + 2 < steps)
        def _():
            copy(k + 2, slot).start()

        cycle = (start[0] + k) % 48
        phase = (jnp.full((8, lanes), cycle, jnp.int32).astype(jnp.float32) - 24.0) / 12.0
        wave = AMPLITUDE * (1.0 - 2.0 * phase * phase) * jnp.exp(-phase * phase)
        strength = jnp.where(here, 12.0 * wave, 0.0)

        @pl.when(lax.rem(source_slab, 2) == core)
        def _():
            laps[k, source_p, source_slab // 2, tile, :] += strength

        moved = cour[source_z, tile, :] * strength
        then[source_z + 2, tile, :] += moved
        inject[k, source_z, tile, :] -= counts[source_z, tile, :] * moved

    count_copy.wait()

    @pl.loop(0, steps // 2)
    def _(pair):
        advance(2 * pair, even, odd, traces_even, 0)
        advance(2 * pair + 1, odd, even, traces_odd, 1)


def adjoint_kernel(mark, own, mate, over, far, cour, laps, inject, keep, send_x, send_y, send_xy, even, odd, total, banded, y0, y1):
    planes, rows, lanes = own.shape[1:]
    steps = laps.shape[0]
    groups = rows // 8
    chip_here, core, slabs = place(planes)
    banded[...] = band(lanes)
    load_blocks(slabs, (own, mate, over, far), odd, even)

    @pl.loop(0, 4 * planes)
    def _(z):
        even[z + 2] = even[z + 2] * cour[z]
        odd[z + 2] = odd[z + 2] * cour[z]

    @pl.loop(0, 2 * planes)
    def _(index):
        total[index] = jnp.zeros((rows, lanes), jnp.float32)

    def advance(k, now, then):
        def work(z, y_part, chip, p):
            def fetch(j, rows):
                extra = (then[z + j + 2, rows], cour[z + j, rows], inject[k, z + j, rows])
                if chip is not None:
                    extra += (total[chip * planes + p + j, rows], laps[k, p + j, chip, rows])
                return extra

            def finish(j, rows, center, lap, extra):
                newer = 2.0 * center - extra[0] + extra[1] * (lap - extra[2])
                then[z + j + 2, rows] = newer
                if chip is not None:
                    total[chip * planes + p + j, rows] = extra[3] + newer * extra[4]

            laps12(now, z, y_part, fetch, finish)

        sweep(core, planes, now, banded, y0, y1, work)

    @pl.loop(0, steps // 2)
    def _(pair):
        advance(steps - 1 - 2 * pair, even, odd)
        advance(steps - 2 - 2 * pair, odd, even)

    count = keep.shape[0]
    mine, others = lax.axis_index("shot") % 2 * count, (1 - lax.axis_index("shot") % 2) * count
    here, there = chip_here, 1 - chip_here
    for ref, chip, start in ((keep, here, mine), (send_x, there, mine), (send_y, here, others), (send_xy, there, others)):

        @pl.loop(0, count)
        def _(n):
            p = start + n
            z = (2 * chip + core) * planes + p
            weight = 1.0 + 2.0 * jnp.full((rows, lanes), z, jnp.int32).astype(jnp.float32) / (4 * planes - 1)
            value = weight * total[chip * planes + p] / (12.0 * cour[z])
            for i in range(groups):
                ref[n, pl.ds(i, 8, stride=groups), :] = value[i * 8 : (i + 1) * 8]


def square_kernel(mine, by_x, by_y, by_xy, keep, send):
    half = lax.axis_index("shot") // 2 % 2
    count = keep.shape[0]
    for ref, part in ((keep, half), (send, 1 - half)):
        for p in range(count):
            at = part * count + p
            ref[p] = (mine[at] + by_x[at]) + (by_y[at] + by_xy[at])


def add_kernel(mine, other, out):
    out[...] = mine[...] + other[...]


def flip(index, bits):
    result = index
    for bit in (1, 2):
        if bits & bit:
            result = jnp.where(index // bit % 2 == 1, result - bit, result + bit)
    return result


def after_kernel(mark, value, out):
    out[...] = value[...]


def arrange_kernel(mine, other, out, mark):
    mark[...] = jnp.zeros(mark.shape, jnp.float32)
    y = lax.axis_index("shot") % 2
    count = mine.shape[0]
    out[pl.ds(y * count, count)] = mine[...]
    out[pl.ds((1 - y) * count, count)] = other[...]


def first_plane(shot, planes):
    return (shot % 2) * (planes // 2) + (shot // 2 % 2) * (planes // 4)


def sums_kernel(mine, other, momentum, data, sums):
    count, rows, lanes = mine.shape
    planes = momentum.shape[0]
    chip, core = lax.axis_index("chip"), lax.axis_index("core")
    first = first_plane(lax.axis_index("shot"), planes)
    parts = [jnp.zeros((rows, lanes), jnp.float32)] * 4
    for j in range(count):
        scaled = mine[j] + other[j]
        data[j * rows : (j + 1) * rows] = scaled
        z = (2 * chip + core) * planes + first + j
        weight = 1.0 + 2.0 * jnp.full((1, lanes), z, jnp.int32).astype(jnp.float32) / (4 * planes - 1)
        moment = momentum[first + j]
        square = scaled * scaled
        terms = (square, weight * moment * moment, weight * moment * scaled, weight * square)
        parts = [part + term for part, term in zip(parts, terms)]

    def total(value):
        by_lane = jnp.sum(value, axis=0, keepdims=True)
        return jnp.broadcast_to(jnp.sum(by_lane, axis=1, keepdims=True), (1, lanes))

    value = jnp.concatenate([total(part) for part in parts] + [jnp.zeros((4, lanes), jnp.float32)], 0)
    data[count * rows :] = value
    sums[...] = value


def join_kernel(mine, other, s0, s1, s2, data, sums):
    rows = mine.shape[0] - 8
    data[0:rows] = mine[0:rows]
    data[rows : 2 * rows] = other[0:rows]
    value = (s0[...] + s1[...]) + (other[rows:] + s2[...])
    data[2 * rows :] = value
    sums[...] = value


def finish_kernel(mine, other, momentum, s0, s1, s2, out, kinetic):
    planes, rows, lanes = momentum.shape
    cells = 4.0 * planes * rows * lanes
    shot = lax.axis_index("shot")
    sums = (s0[...] + s1[...]) + (other[planes // 2 * rows :] + s2[...])
    factor = lax.rsqrt(sums[0:1] / cells + EPSILON)
    energy = 0.5 * (sums[1:2] - factor * sums[2:3] + 0.25 * factor * factor * sums[3:4]) / cells
    kinetic[0] = energy[0, 0]
    step = 0.5 * factor
    quarter = planes // 4
    for part, group in ((mine, shot), (other, flip(shot, 1))):
        for number, first in enumerate((first_plane(group, planes), first_plane(flip(group, 2), planes))):
            for j in range(quarter):
                at = (number * quarter + j) * rows
                out[first + j] = momentum[first + j] - step * part[at : at + rows]


def local(kernel, outs, *arrays):
    vmem = pl.BlockSpec(memory_space=pltpu.VMEM)
    shapes = [jax.ShapeDtypeStruct(shape, jnp.float32) for shape in outs]
    single = len(outs) == 1
    return pl.pallas_call(
        kernel,
        in_specs=[vmem] * len(arrays),
        out_specs=vmem if single else [vmem] * len(outs),
        out_shape=shapes[0] if single else shapes,
        compiler_params=pltpu.CompilerParams(vmem_limit_bytes=4 * 2**20),
        name=kernel.__name__,
    )(*arrays)


def exchange(value, bits):
    axes = ("shot", "chip", "core")
    return lax.ppermute(value, axes, [(i, i ^ bits) for i in range(lax.axis_size(axes))])


CORE, CHIP, Y, NEAR_Z, FAR_Z = 1, 2, 4, 8, 16


def whole_shards(
    courant_sq, momentum, fwd_prev, fwd_cur, adj_next, adj_cur, observed, src_cells, rec_cells, ckpt_step
):
    _, planes, rows_x, rows_y = fwd_cur.shape
    steps = observed.shape[1]
    planes_all = 4 * planes
    cells_all = planes_all * rows_x * rows_y
    vmem, smem = pl.BlockSpec(memory_space=pltpu.VMEM), pl.BlockSpec(memory_space=pltpu.SMEM)

    hbm = pl.BlockSpec(memory_space=pltpu.HBM)
    outgoing, c0, piece = pl.pallas_call(
        first_kernel,
        in_specs=[hbm] * 3,
        out_specs=[vmem] * 3,
        out_shape=[
            jax.ShapeDtypeStruct((2, planes, rows_x, rows_y), jnp.float32),
            jax.ShapeDtypeStruct(courant_sq.shape, jnp.float32),
            jax.ShapeDtypeStruct((planes // 2, rows_x, rows_y), jnp.float32),
        ],
        scratch_shapes=[
            pltpu.VMEM((2, planes, rows_x, rows_y), jnp.float32),
            pltpu.VMEM(courant_sq.shape, jnp.float32),
            pltpu.SemaphoreType.DMA((3,)),
        ],
        compiler_params=pltpu.CompilerParams(vmem_limit_bytes=63 * 2**20),
        name="first_to_cross",
    )(fwd_prev, fwd_cur, courant_sq)

    over = exchange(outgoing, CHIP)
    piece = exchange(piece, CHIP)

    placed, mark = scatter(rec_cells, observed, planes_all, rows_x, rows_y)
    placed = placed.reshape(steps + 1, planes_all, rows_x, rows_y)

    adj_outgoing, adj_own, own = pick(
        (adj_next, adj_cur, True), (adj_next, adj_cur, False), (fwd_prev, fwd_cur, False), after=mark
    )
    mate = exchange(own, CORE)
    piece = local(after_kernel, [piece.shape], mark, piece)
    c2, arranged = local(arrange_kernel, [courant_sq.shape, (8, rows_y)], piece, exchange(piece, Y))
    c1, c3 = exchange(c0, CORE), exchange(c2, CORE)
    over, arranged = lax.optimization_barrier((over, arranged))
    far = exchange(over, CORE)
    adj_over = exchange(adj_outgoing, CHIP)
    adj_mate = exchange(adj_own, CORE)

    scratch = pltpu.VMEM((planes_all + 4, rows_x, rows_y), jnp.float32)
    whole = pltpu.VMEM((planes_all, rows_x, rows_y), jnp.float32)
    y_scratch = pltpu.VMEM((BATCH * rows_x, rows_y), jnp.float32)
    step_scratch = [scratch, scratch, pltpu.VMEM((2 * rows_y, rows_y), jnp.bfloat16), y_scratch, y_scratch]
    params = pltpu.CompilerParams(vmem_limit_bytes=6 * 2**20)
    cost = pl.CostEstimate(flops=30 * steps * cells_all, bytes_accessed=16 * steps * cells_all, transcendentals=0)
    laps, inject, cour, mark = pl.pallas_call(
        forward_kernel,
        in_specs=[smem, smem, pl.BlockSpec(memory_space=pl.ANY)] + [vmem] * 8 + [pl.BlockSpec(memory_space=pltpu.HBM)],
        out_specs=[vmem] * 4,
        out_shape=[
            jax.ShapeDtypeStruct((steps, planes, 2, rows_x, rows_y), jnp.float32),
            jax.ShapeDtypeStruct((steps, planes_all, rows_x, rows_y), jnp.float32),
            jax.ShapeDtypeStruct((planes_all, rows_x, rows_y), jnp.float32),
            jax.ShapeDtypeStruct((8, rows_y), jnp.float32),
        ],
        scratch_shapes=step_scratch + [whole, whole, whole, pltpu.SemaphoreType.DMA((3,))],
        compiler_params=pltpu.CompilerParams(vmem_limit_bytes=33 * 2**20),
        cost_estimate=cost,
        name="forward_steps",
    )(ckpt_step[None], src_cells, arranged, own, mate, over, far, c0, c1, c2, c3, placed)

    adj_over, mark = lax.optimization_barrier((adj_over, mark))
    adj_far = exchange(adj_over, CORE)
    slab = jax.ShapeDtypeStruct(courant_sq.shape, jnp.float32)
    half, quarter = (planes // 2, rows_x, rows_y), (planes // 4, rows_x, rows_y)
    keep, send_x, send_y, send_xy = pl.pallas_call(
        adjoint_kernel,
        in_specs=[pl.BlockSpec(memory_space=pl.ANY)] + [vmem] * 7,
        out_specs=[vmem] * 4,
        out_shape=[jax.ShapeDtypeStruct(half, jnp.float32)] * 4,
        scratch_shapes=step_scratch[:2] + [pltpu.VMEM((2 * planes, rows_x, rows_y), jnp.float32)] + step_scratch[2:],
        compiler_params=params,
        cost_estimate=cost,
        name="adjoint_steps",
    )(mark, adj_own, adj_mate, adj_over, adj_far, cour, laps, inject)

    by_xy, by_x, by_y = exchange(send_xy, CHIP + Y), exchange(send_x, CHIP), exchange(send_y, Y)
    keep, send = local(square_kernel, [quarter] * 2, keep, by_x, by_y, by_xy)
    part = local(add_kernel, [quarter], keep, exchange(send, NEAR_Z))
    rows, sums_shape = planes // 4 * rows_x, (8, rows_y)
    data, sums = local(sums_kernel, [(rows + 8, rows_y), sums_shape], part, exchange(part, FAR_Z), momentum)

    received = exchange(data, NEAR_Z)
    others = [exchange(sums, CORE), exchange(sums, NEAR_Z + CORE)]
    data, sums = local(join_kernel, [(2 * rows + 8, rows_y), sums_shape], data, received, sums, *others)
    received = exchange(data, Y)
    others = [exchange(sums, CHIP), exchange(sums, Y + CHIP)]
    momentum_half, kinetic = pl.pallas_call(
        finish_kernel,
        in_specs=[vmem] * 6,
        out_specs=[vmem, smem],
        out_shape=[jax.ShapeDtypeStruct(momentum.shape, jnp.float32), jax.ShapeDtypeStruct((1,), jnp.float32)],
        compiler_params=pltpu.CompilerParams(vmem_limit_bytes=4 * 2**20),
        name="finish",
    )(data, received, momentum, sums, *others)
    return momentum_half, kinetic[0]


def solution(mesh):
    shots, slabs = mesh.shape["shot"], mesh.shape["depth"]

    def placed(depth):
        field = P("shot", depth, None, None)
        slab = P(depth, None, None)
        inputs = (slab, slab, field, field, field, field, P("shot", None, None), P("shot"), P("shot", None), P())
        return dict(in_specs=inputs, out_specs=(slab, P()), check_vma=False)

    slab_plan = jax.shard_map(slab_shards, mesh=mesh, **placed("depth"))
    if slabs != 4 or shots != 8:
        return slab_plan
    chips = Mesh(mesh.devices.reshape(shots, 2, 2), ("shot", "chip", "core"))
    whole_plan = jax.shard_map(whole_shards, mesh=chips, **placed(("chip", "core")))

    def run(courant_sq, momentum, fwd_prev, *rest):
        total, planes, rows_x, rows_y = fwd_prev.shape
        steps = rest[3].shape[1]
        fits = total == 2 * shots and planes == 4 * shots and rows_y == 128 and rows_x % 16 == 0 and steps % 2 == 0
        plan = whole_plan if fits else slab_plan
        return plan(courant_sq, momentum, fwd_prev, *rest)

    return run
```

```python
import functools

import jax
import jax.numpy as jnp
from jax import lax
from jax.experimental import pallas as pl
from jax.experimental.pallas import tpu as pltpu
from jax.sharding import Mesh
from jax.sharding import PartitionSpec as P

CENTER = -2.5
NEAR = 4.0 / 3.0
FAR = -1.0 / 12.0
AMPLITUDE = 100.0
EPSILON = 1e-06


def with_halo(value, sides, width):
    for axis, dim in sides:
        size, length = (lax.axis_size(axis), value.shape[dim])
        up = [(i, (i + 1) % size) for i in range(size - 1)]
        down = [(j, i) for i, j in up]
        last = lax.slice_in_dim(value, length - width, length, axis=dim)
        leading = lax.slice_in_dim(value, 0, width, axis=dim)
        before = lax.ppermute(last, axis, up)
        after = lax.ppermute(leading, axis, down)
        value = jnp.concatenate([before, value, after], axis=dim)
    return value


def laplace(padded):
    lateral = jnp.pad(padded[:, 2:-2], ((0, 0), (0, 0), (2, 2), (2, 2)))
    center = padded[:, 2:-2]
    along_z = NEAR * (padded[:, 1:-3] + padded[:, 3:-1]) + FAR * (padded[:, :-4] + padded[:, 4:])
    along_x = NEAR * (lateral[:, :, 1:-3, 2:-2] + lateral[:, :, 3:-1, 2:-2]) + FAR * (
        lateral[:, :, :-4, 2:-2] + lateral[:, :, 4:, 2:-2]
    )
    along_y = NEAR * (lateral[:, :, 2:-2, 1:-3] + lateral[:, :, 2:-2, 3:-1]) + FAR * (
        lateral[:, :, 2:-2, :-4] + lateral[:, :, 2:-2, 4:]
    )
    return 3.0 * CENTER * center + along_z + along_x + along_y


def locate(field, cell_ids, first_plane):
    shot_count, planes, rows_x, rows_y = field.shape
    plane_cells = rows_x * rows_y
    local_index = cell_ids - first_plane * plane_cells
    inside = (local_index >= 0) & (local_index < planes * plane_cells)
    target = jnp.where(inside, local_index, 0)
    return (inside, target)


def inject(field, cell_ids, values, first_plane):
    shot_count = field.shape[0]
    inside, target = locate(field, cell_ids, first_plane)
    amount = jnp.where(inside, values, jnp.zeros_like(values))
    flattened = field.reshape(shot_count, -1)
    lanes = jnp.arange(shot_count)[:, None]
    flattened = flattened.at[lanes, target].add(amount)
    return flattened.reshape(field.shape)


def sample(field, cell_ids, first_plane):
    shot_count = field.shape[0]
    inside, target = locate(field, cell_ids, first_plane)
    values = jnp.take_along_axis(field.reshape(shot_count, -1), target, axis=1)
    return jnp.where(inside, values, jnp.zeros_like(values))


def wave_value(start, step):
    cycle = jnp.mod(start + jnp.int32(step), jnp.int32(48))
    phase = (cycle.astype(jnp.float32) - 24.0) / 12.0
    return AMPLITUDE * (1.0 - 2.0 * phase * phase) * jnp.exp(-phase * phase)


def statistics(scaled, moment, weight, cells_all):
    grand_total = lax.psum(jnp.sum(scaled * scaled), ("shot", "depth"))
    factor = lax.rsqrt(grand_total / cells_all + EPSILON)
    halfway = moment - 0.5 * factor * scaled
    energy = lax.psum(jnp.sum(weight * halfway * halfway), ("shot", "depth"))
    return (factor, 0.5 * energy / cells_all)


def slab_shards(
    courant_sq,
    momentum,
    fwd_prev,
    fwd_cur,
    adj_next,
    adj_cur,
    observed,
    src_cells,
    rec_cells,
    ckpt_step,
):
    shot_count, planes, rows_x, rows_y = fwd_cur.shape
    steps_all = observed.shape[1]
    first_plane = lax.axis_index("depth") * planes
    total_planes = planes * lax.axis_size("depth")
    cells_all = total_planes * rows_x * rows_y
    sources = src_cells[:, None]
    older, current = (fwd_prev, fwd_cur)
    laplacians = []
    misfits = []
    for step in range(steps_all):
        padded = with_halo(current, (("depth", 1),), 2)
        strength = jnp.full(sources.shape, wave_value(ckpt_step, step), jnp.float32)
        laplacian = inject(laplace(padded), sources, strength, first_plane)
        newer = 2.0 * current - older + courant_sq * laplacian
        misfits.append(sample(newer, rec_cells, first_plane) - observed[:, step, :])
        laplacians.append(laplacian)
        older, current = (current, newer)
    adj_later, adj_now = (adj_next, adj_cur)
    gradient = jnp.zeros((planes, rows_x, rows_y), jnp.float32)
    for step in reversed(range(steps_all)):
        padded = with_halo(courant_sq * adj_now, (("depth", 1),), 2)
        adj_new = 2.0 * adj_now - adj_later + laplace(padded)
        adj_new = inject(adj_new, rec_cells, misfits[step], first_plane)
        gradient = gradient + jnp.sum(adj_new * laplacians[step], axis=0)
        adj_later, adj_now = (adj_now, adj_new)
    depths = (first_plane + jnp.arange(planes)).astype(jnp.float32)
    weight = (1.0 + 2.0 * depths / (total_planes - 1))[:, None, None]
    share_rows = rows_x // lax.axis_size("shot")
    offset = lax.axis_index("shot") * share_rows
    moment_share = lax.dynamic_slice_in_dim(momentum, offset, share_rows, 1)
    gradient = lax.psum(gradient, "shot")
    scaled = weight * gradient
    scaled_share = lax.dynamic_slice_in_dim(scaled, offset, share_rows, 1)
    factor, kinetic = statistics(scaled_share, moment_share, weight, cells_all)
    momentum_half = momentum - 0.5 * factor * scaled
    return (momentum_half, kinetic)


def interleave(dst, slab, src, factor=None):
    planes, rows = src.shape[0], src.shape[1]
    groups = rows // 8

    @pl.loop(0, planes)
    def _(p):
        for i in range(groups):
            value = src[p, pl.ds(i, 8, stride=groups), :]
            if factor is not None:
                value = value * factor
            dst[(*slab, p, pl.ds(i * 8, 8), slice(None))] = value


def pick_kernel(across, *refs):
    count = len(across)
    fields, outs, (held, sems) = refs[: 2 * count], refs[2 * count : 3 * count], refs[3 * count :]
    chip = lax.axis_index("chip")
    copies = []
    for n in range(2 * count):
        shot = 1 - chip if across[n // 2] else chip
        copies.append(pltpu.make_async_copy(fields[n].at[shot], held.at[n], sems.at[n]))
        copies[-1].start()
    for n in range(2 * count):
        copies[n].wait()
        interleave(outs[n // 2], (n % 2,), held.at[n])


def pick(*pairs, earlier):
    plain = functools.partial(pick_kernel, tuple(pair[2] for pair in pairs))
    fields = [field for pair in pairs for field in pair[:2]]
    shape = fields[0].shape[1:]
    vmem, hbm = pl.BlockSpec(memory_space=pltpu.VMEM), pl.BlockSpec(memory_space=pltpu.HBM)
    return pl.pallas_call(
        lambda earlier, *refs: plain(*refs),
        in_specs=[pl.BlockSpec(memory_space=pl.ANY)] + [hbm] * len(fields),
        out_specs=[vmem] * len(pairs),
        out_shape=[jax.ShapeDtypeStruct((2, *shape), jnp.float32)] * len(pairs),
        scratch_shapes=[pltpu.VMEM((len(fields), *shape), jnp.float32), pltpu.SemaphoreType.DMA((len(fields),))],
        compiler_params=pltpu.CompilerParams(vmem_limit_bytes=4 * 2**20),
        name="pick",
    )(earlier, *fields)


def first_kernel(first, second, courant, outgoing, whole, piece, held_courant, sems):
    shot = 1 - lax.axis_index("chip")
    copies = [
        pltpu.make_async_copy(courant, held_courant, sems.at[0]),
        pltpu.make_async_copy(first.at[shot], outgoing.at[0], sems.at[1]),
        pltpu.make_async_copy(second.at[shot], outgoing.at[1], sems.at[2]),
    ]
    for copy in copies:
        copy.start()
    copies[0].wait()
    interleave(whole, (), held_courant, 1.0 / 12.0)
    count = piece.shape[0]
    piece[...] = whole[pl.ds(lax.axis_index("shot") % 2 * count, count)]
    copies[1].wait()
    copies[2].wait()


def band(lanes):
    near = jnp.abs(lax.broadcasted_iota(jnp.int32, (2 * lanes, lanes), 0) % lanes - lax.broadcasted_iota(jnp.int32, (2 * lanes, lanes), 1))
    return jnp.where(near == 0, -90.0, jnp.where(near == 1, 16.0, jnp.where(near == 2, -1.0, 0.0))).astype(jnp.bfloat16)


def along_y(field, z, banded, out):
    rows, lanes = field.shape[1:]
    whole = field[pl.ds(z + 2, BATCH)].reshape(BATCH * rows, lanes)
    high = whole.astype(jnp.bfloat16)
    low = (whole - high.astype(jnp.float32)).astype(jnp.bfloat16)
    out[...] = jnp.dot(jnp.concatenate([high, low], 1), banded[...], preferred_element_type=jnp.float32)


def laps12(field, z, y_part, fetch, finish):
    rows, lanes = field.shape[1:]
    groups = rows // 8
    sub = lax.broadcasted_iota(jnp.int32, (8, lanes), 0)

    def later(block):
        return jnp.where(sub < 7, pltpu.roll(block, 7, 0), 0.0)

    def earlier(block):
        return jnp.where(sub > 0, pltpu.roll(block, 1, 0), 0.0)

    for base in range(0, BATCH, PLANES):
        held = {}

        def tile(j, i):
            if (j, i) not in held:
                if i < 0:
                    held[j, i] = earlier(tile(j, i + groups))
                elif i >= groups:
                    held[j, i] = later(tile(j, i - groups))
                else:
                    held[j, i] = field[z + j + 2, i * 8 : (i + 1) * 8]
            return held[j, i]

        def load(i):
            found = []
            for j in range(base, base + PLANES):
                center = tile(j, i)
                near = (tile(j, i - 1), tile(j, i + 1), tile(j - 1, i), tile(j + 1, i))
                far = (tile(j, i - 2), tile(j, i + 2), tile(j - 2, i), tile(j + 2, i))
                at = (j * groups + i) * 8
                found.append((center, near, far, y_part[at : at + 8], fetch(j, slice(i * 8, i * 8 + 8))))
            return found

        ready = load(0)
        for i in range(groups):
            upcoming = load(i + 1) if i + 1 < groups else None
            for j, (center, near, far, part, extra) in enumerate(ready):
                near = (near[0] + near[1]) + (near[2] + near[3])
                far = (far[0] + far[1]) + (far[2] + far[3])
                finish(base + j, slice(i * 8, i * 8 + 8), center, 16.0 * near + (part - far), extra)
            ready = upcoming


def scatter_kernel(rows_x, cells_ref, observed_ref, out_ref, mark, row_ref, spread):
    _, steps, receivers = observed_ref.shape
    lanes = out_ref.shape[2]
    tile = out_ref.shape[1]
    groups = rows_x // 8

    @pl.when(pl.program_id(0) == 0)
    def _():
        chip = lax.axis_index("chip")
        cells = cells_ref[pl.ds(chip, 1)]
        x = cells // lanes % rows_x
        row_ref[...] = cells // (rows_x * lanes) * rows_x + x % groups * 8 + x // groups
        on_lanes = jnp.concatenate(
            [
                observed_ref[chip],
                jnp.broadcast_to((cells % lanes).astype(jnp.float32), (8, receivers)),
                jnp.zeros((lanes - steps - 8, receivers), jnp.float32),
            ],
            0,
        )
        columns = on_lanes.T
        lane = lax.broadcasted_iota(jnp.int32, (receivers, lanes), 1).astype(jnp.float32)
        at = lane == columns[:, steps : steps + 1]
        for k in range(steps):
            column = columns[:, k : k + 1]
            high = column.astype(jnp.bfloat16).astype(jnp.float32)
            low = column - high
            cols = pl.ds(k * lanes, lanes)
            spread[0:receivers, cols] = jnp.where(at, high, 0.0).astype(jnp.bfloat16)
            spread[receivers:, cols] = jnp.where(at, low, 0.0).astype(jnp.bfloat16)
        cols = pl.ds(steps * lanes, lanes)
        spread[0:receivers, cols] = jnp.where(at, 1.0, 0.0).astype(jnp.bfloat16)
        spread[receivers:, cols] = jnp.zeros((receivers, lanes), jnp.bfloat16)
        mark[...] = jnp.zeros(mark.shape, jnp.float32)

    ids = lax.broadcasted_iota(jnp.int32, (tile, receivers), 0) + pl.program_id(0) * tile
    chosen = jnp.where(ids == row_ref[...], 1.0, 0.0).astype(jnp.bfloat16)
    total = jnp.dot(jnp.concatenate([chosen, chosen], 1), spread[...], preferred_element_type=jnp.float32)
    for k in range(steps + 1):
        out_ref[k] = total[:, k * lanes : (k + 1) * lanes]


def scatter(rec_cells, observed, planes_all, rows_x, rows_y):
    _, steps, receivers = observed.shape
    rows_all = planes_all * rows_x
    tile = 512
    return pl.pallas_call(
        functools.partial(scatter_kernel, rows_x),
        grid=(rows_all // tile,),
        in_specs=[
            pl.BlockSpec((2, receivers), lambda t: (0, 0)),
            pl.BlockSpec((2, steps, receivers), lambda t: (0, 0, 0)),
        ],
        out_specs=[
            pl.BlockSpec((steps + 1, tile, rows_y), lambda t: (0, t, 0)),
            pl.BlockSpec((8, rows_y), lambda t: (0, 0)),
        ],
        out_shape=[
            jax.ShapeDtypeStruct((steps + 1, rows_all, rows_y), jnp.float32),
            jax.ShapeDtypeStruct((8, rows_y), jnp.float32),
        ],
        scratch_shapes=[
            pltpu.VMEM((1, receivers), jnp.int32),
            pltpu.VMEM((2 * receivers, (steps + 1) * rows_y), jnp.bfloat16),
        ],
        compiler_params=pltpu.CompilerParams(vmem_limit_bytes=56 * 2**20),
        cost_estimate=pl.CostEstimate(
            flops=4 * rows_all * receivers * (steps + 1) * rows_y,
            bytes_accessed=4 * (steps + 1) * rows_all * rows_y,
            transcendentals=0,
        ),
        name="receiver_scatter",
    )(rec_cells, observed)


def place(planes):
    chip, core = lax.axis_index("chip"), lax.axis_index("core")
    slabs = (2 * chip + core, 2 * chip + 1 - core, 2 * (1 - chip) + core, 2 * (1 - chip) + 1 - core)
    return chip, core, [slab * planes for slab in slabs]


def load_blocks(slabs, blocks, first, second, raw=False, factor=None):
    ends, rows, lanes = first.shape
    planes, groups = blocks[0].shape[1], rows // 8
    for field in (first, second):
        for z in (0, 1, ends - 2, ends - 1):
            field[z] = jnp.zeros((rows, lanes), jnp.float32)
    for b, (slab, block) in enumerate(zip(slabs, blocks)):

        @pl.loop(0, planes)
        def _(p):
            for n, field in enumerate((first, second)):
                if raw and b >= 2:
                    tiles = [block[n, p, pl.ds(i, 8, stride=groups), :] for i in range(groups)]
                    value = jnp.concatenate(tiles, 0)
                else:
                    value = block[n, p]
                if factor is not None:
                    value = value * factor[slab + p]
                field[slab + p + 2] = value


BATCH = 4
PLANES = 2


def sweep(core, planes, field, banded, y_first, y_second, work):
    order = [(chip, owned) for owned in (True, False) for chip in (0, 1)]
    parts = (y_first, y_second)

    def first(chip, owned):
        return (2 * chip + (core if owned else 1 - core)) * planes

    along_y(field, first(*order[0]), banded, y_first)
    for owned in (True, False):
        for chip in (0, 1):
            z = first(chip, owned)
            onward = first(1, owned) if chip == 0 else first(0, False)
            for n in range(planes // BATCH):
                last = n == planes // BATCH - 1
                if not last or chip == 0 or owned:
                    along_y(field, onward if last else z + (n + 1) * BATCH, banded, parts[(n + 1) % 2])
                work(z + n * BATCH, parts[n % 2], chip if owned else None, n * BATCH)


def forward_kernel(
    start, sources, own, mate, over, far, c0, c1, p0, p1, p2, p3, placed, laps, inject, cour, last, even, odd, banded, y0, y1,
    traces_even, traces_odd, counts, sems
):
    planes, rows, lanes = c0.shape
    steps = laps.shape[0]
    groups = rows // 8
    chip_here, core, slabs = place(planes)

    def copy(k, slot):
        return pltpu.make_async_copy(placed.at[k], (traces_even, traces_odd)[slot], sems.at[slot])

    copy(0, 0).start()
    count_copy = pltpu.make_async_copy(placed.at[steps], counts, sems.at[2])
    count_copy.start()
    copy(1, 1).start()
    banded[...] = band(lanes)
    load_blocks(slabs, (own, mate, over, far), odd, even, raw=True)
    mine = lax.axis_index("shot") % 2 * (planes // 2)
    other = planes // 2 - mine
    courant_at = (slabs[0], slabs[1], slabs[2] + mine, slabs[2] + other, slabs[3] + mine, slabs[3] + other)
    for z, block in zip(courant_at, (c0, c1, p0, p1, p2, p3)):

        @pl.loop(0, block.shape[0])
        def _(p):
            cour[z + p] = block[p]

    @pl.loop(0, 2 * planes)
    def _(index):
        z = (2 * (index // planes) + core) * planes + index % planes
        weight = 1.0 + 2.0 * jnp.full((rows, lanes), z, jnp.int32).astype(jnp.float32) / (4 * planes - 1)
        last[index] = weight / (12.0 * cour[z])

    cell = sources[chip_here]
    source_z, x, lane = cell // (rows * lanes), cell // lanes % rows, cell % lanes
    tile = pl.ds(pl.multiple_of(x % groups * 8, 8), 8)
    here = (lax.broadcasted_iota(jnp.int32, (8, lanes), 0) == x // groups) & (
        lax.broadcasted_iota(jnp.int32, (8, lanes), 1) == lane
    )
    source_slab, source_p = source_z // planes, lax.rem(source_z, planes)

    def advance(k, now, then, observed, slot):
        copy(k, slot).wait()

        def work(z, y_part, chip, p):
            def fetch(j, rows):
                return then[z + j + 2, rows], cour[z + j, rows], observed[z + j, rows], counts[z + j, rows]

            def finish(j, rows, center, lap, extra):
                old, speed, traces, count = extra
                if chip is not None:
                    laps[k, p + j, chip, rows] = lap
                newer = 2.0 * center - old + speed * lap
                then[z + j + 2, rows] = newer
                inject[k, z + j, rows] = traces - count * newer

            laps12(now, z, y_part, fetch, finish)

        cycle = (start[0] + k) % 48
        phase = (jnp.full((8, lanes), cycle, jnp.int32).astype(jnp.float32) - 24.0) / 12.0
        wave = AMPLITUDE * (1.0 - 2.0 * phase * phase) * jnp.exp(-phase * phase)
        strength = jnp.where(here, 12.0 * wave, 0.0)
        moved = cour[source_z, tile, :] * strength

        sweep(core, planes, now, banded, y0, y1, work)

        owned = jnp.where(lax.rem(source_slab, 2) == core, strength, 0.0)
        laps[k, source_p, source_slab // 2, tile, :] += owned
        then[source_z + 2, tile, :] += moved
        inject[k, source_z, tile, :] -= counts[source_z, tile, :] * moved

        @pl.when(k + 2 < steps)
        def _():
            copy(k + 2, slot).start()

    count_copy.wait()

    @pl.loop(0, steps // 2)
    def _(pair):
        advance(2 * pair, even, odd, traces_even, 0)
        advance(2 * pair + 1, odd, even, traces_odd, 1)


def adjoint_kernel(own, mate, over, far, cour, laps, inject, last, keep, send_x, send_y, send_xy, even, odd, total, banded, y0, y1):
    planes, rows, lanes = own.shape[1:]
    steps = laps.shape[0]
    groups = rows // 8
    chip_here, core, slabs = place(planes)
    banded[...] = band(lanes)
    load_blocks(slabs, (own, mate, over, far), odd, even, factor=cour)

    @pl.loop(0, 2 * planes)
    def _(index):
        total[index] = jnp.zeros((rows, lanes), jnp.float32)

    def advance(k, now, then):
        def work(z, y_part, chip, p):
            def fetch(j, rows):
                extra = (then[z + j + 2, rows], cour[z + j, rows], inject[k, z + j, rows])
                if chip is not None:
                    extra += (total[chip * planes + p + j, rows], laps[k, p + j, chip, rows])
                return extra

            def finish(j, rows, center, lap, extra):
                newer = 2.0 * center - extra[0] + extra[1] * (lap - extra[2])
                then[z + j + 2, rows] = newer
                if chip is not None:
                    total[chip * planes + p + j, rows] = extra[3] + newer * extra[4]

            laps12(now, z, y_part, fetch, finish)

        sweep(core, planes, now, banded, y0, y1, work)

    @pl.loop(0, steps // 2)
    def _(pair):
        advance(steps - 1 - 2 * pair, even, odd)
        advance(steps - 2 - 2 * pair, odd, even)

    count = keep.shape[0]
    mine, others = lax.axis_index("shot") % 2 * count, (1 - lax.axis_index("shot") % 2) * count
    here, there = chip_here, 1 - chip_here
    for ref, chip, start in ((keep, here, mine), (send_x, there, mine), (send_y, here, others), (send_xy, there, others)):

        @pl.loop(0, count)
        def _(n):
            p = start + n
            value = total[chip * planes + p] * last[chip * planes + p]
            for i in range(groups):
                ref[n, pl.ds(i, 8, stride=groups), :] = value[i * 8 : (i + 1) * 8]


def square_kernel(mine, by_x, by_y, by_xy, keep, send):
    half = lax.axis_index("shot") // 2 % 2
    count = keep.shape[0]
    for ref, part in ((keep, half), (send, 1 - half)):
        for p in range(count):
            at = part * count + p
            ref[p] = (mine[at] + by_x[at]) + (by_y[at] + by_xy[at])


def add_kernel(mine, other, out):
    out[...] = mine[...] + other[...]


def flip(index, bits):
    result = index
    for bit in (1, 2):
        if bits & bit:
            result = jnp.where(index // bit % 2 == 1, result - bit, result + bit)
    return result


def after_kernel(earlier, value, out):
    out[...] = value[...]


def after(earlier, value):
    vmem, anywhere = pl.BlockSpec(memory_space=pltpu.VMEM), pl.BlockSpec(memory_space=pl.ANY)
    return pl.pallas_call(
        after_kernel,
        in_specs=[anywhere, vmem],
        out_specs=vmem,
        out_shape=jax.ShapeDtypeStruct(value.shape, jnp.float32),
        compiler_params=pltpu.CompilerParams(vmem_limit_bytes=4 * 2**20),
        name="after",
    )(earlier, value)


def first_plane(shot, planes):
    return (shot % 2) * (planes // 2) + (shot // 2 % 2) * (planes // 4)


def sums_kernel(mine, other, momentum, data, sums):
    count, rows, lanes = mine.shape
    planes = momentum.shape[0]
    chip, core = lax.axis_index("chip"), lax.axis_index("core")
    first = first_plane(lax.axis_index("shot"), planes)
    parts = [jnp.zeros((rows, lanes), jnp.float32)] * 4
    for j in range(count):
        scaled = mine[j] + other[j]
        data[j * rows : (j + 1) * rows] = scaled
        z = (2 * chip + core) * planes + first + j
        weight = 1.0 + 2.0 * jnp.full((1, lanes), z, jnp.int32).astype(jnp.float32) / (4 * planes - 1)
        moment = momentum[first + j]
        square = scaled * scaled
        terms = (square, weight * moment * moment, weight * moment * scaled, weight * square)
        parts = [part + term for part, term in zip(parts, terms)]

    def total(value):
        by_lane = jnp.sum(value, axis=0, keepdims=True)
        return jnp.broadcast_to(jnp.sum(by_lane, axis=1, keepdims=True), (1, lanes))

    value = jnp.concatenate([total(part) for part in parts] + [jnp.zeros((4, lanes), jnp.float32)], 0)
    data[count * rows :] = value
    sums[...] = value


def join_kernel(mine, other, s0, s1, s2, data, sums):
    rows = mine.shape[0] - 8
    data[0:rows] = mine[0:rows]
    data[rows : 2 * rows] = other[0:rows]
    value = (s0[...] + s1[...]) + (other[rows:] + s2[...])
    data[2 * rows :] = value
    sums[...] = value


def finish_kernel(mine, other, momentum, s0, s1, s2, out, kinetic):
    planes, rows, lanes = momentum.shape
    cells = 4.0 * planes * rows * lanes
    shot = lax.axis_index("shot")
    sums = (s0[...] + s1[...]) + (other[planes // 2 * rows :] + s2[...])
    factor = lax.rsqrt(sums[0:1] / cells + EPSILON)
    energy = 0.5 * (sums[1:2] - factor * sums[2:3] + 0.25 * factor * factor * sums[3:4]) / cells
    kinetic[0] = energy[0, 0]
    step = 0.5 * factor
    quarter = planes // 4
    for part, group in ((mine, shot), (other, flip(shot, 1))):
        for number, first in enumerate((first_plane(group, planes), first_plane(flip(group, 2), planes))):
            for j in range(quarter):
                at = (number * quarter + j) * rows
                out[first + j] = momentum[first + j] - step * part[at : at + rows]


def local(kernel, outs, *arrays):
    vmem = pl.BlockSpec(memory_space=pltpu.VMEM)
    shapes = [jax.ShapeDtypeStruct(shape, jnp.float32) for shape in outs]
    single = len(outs) == 1
    return pl.pallas_call(
        kernel,
        in_specs=[vmem] * len(arrays),
        out_specs=vmem if single else [vmem] * len(outs),
        out_shape=shapes[0] if single else shapes,
        compiler_params=pltpu.CompilerParams(vmem_limit_bytes=4 * 2**20),
        name=kernel.__name__,
    )(*arrays)


def exchange(value, bits):
    axes = ("shot", "chip", "core")
    return lax.ppermute(value, axes, [(i, i ^ bits) for i in range(lax.axis_size(axes))])


CORE, CHIP, Y, NEAR_Z, FAR_Z = 1, 2, 4, 8, 16


def whole_shards(
    courant_sq, momentum, fwd_prev, fwd_cur, adj_next, adj_cur, observed, src_cells, rec_cells, ckpt_step
):
    _, planes, rows_x, rows_y = fwd_cur.shape
    steps = observed.shape[1]
    planes_all = 4 * planes
    cells_all = planes_all * rows_x * rows_y
    vmem, smem = pl.BlockSpec(memory_space=pltpu.VMEM), pl.BlockSpec(memory_space=pltpu.SMEM)

    hbm = pl.BlockSpec(memory_space=pltpu.HBM)
    outgoing, c0, piece = pl.pallas_call(
        first_kernel,
        in_specs=[hbm] * 3,
        out_specs=[hbm, vmem, vmem],
        out_shape=[
            jax.ShapeDtypeStruct((2, planes, rows_x, rows_y), jnp.float32),
            jax.ShapeDtypeStruct(courant_sq.shape, jnp.float32),
            jax.ShapeDtypeStruct((planes // 2, rows_x, rows_y), jnp.float32),
        ],
        scratch_shapes=[
            pltpu.VMEM(courant_sq.shape, jnp.float32),
            pltpu.SemaphoreType.DMA((3,)),
        ],
        compiler_params=pltpu.CompilerParams(vmem_limit_bytes=63 * 2**20),
        name="first_to_cross",
    )(fwd_prev, fwd_cur, courant_sq)

    over = exchange(outgoing, CHIP)
    piece = exchange(piece, CHIP)

    placed, mark = scatter(rec_cells, observed, planes_all, rows_x, rows_y)
    placed = placed.reshape(steps + 1, planes_all, rows_x, rows_y)

    adj_outgoing, adj_own, own = pick(
        (adj_next, adj_cur, True), (adj_next, adj_cur, False), (fwd_prev, fwd_cur, False), earlier=mark
    )
    mate = exchange(own, CORE)
    piece = after(adj_own, piece)
    pieces = [piece, exchange(piece, Y), exchange(piece, CORE), exchange(piece, Y + CORE)]
    c1 = exchange(c0, CORE)
    over = after(pieces[3], over)
    far = exchange(over, CORE)
    adj_over = exchange(adj_outgoing, CHIP)
    adj_mate = exchange(adj_own, CORE)

    scratch = pltpu.VMEM((planes_all + 4, rows_x, rows_y), jnp.float32)
    whole = pltpu.VMEM((planes_all, rows_x, rows_y), jnp.float32)
    y_scratch = pltpu.VMEM((BATCH * rows_x, rows_y), jnp.float32)
    step_scratch = [scratch, scratch, pltpu.VMEM((2 * rows_y, rows_y), jnp.bfloat16), y_scratch, y_scratch]
    params = pltpu.CompilerParams(vmem_limit_bytes=6 * 2**20)
    cost = pl.CostEstimate(flops=30 * steps * cells_all, bytes_accessed=16 * steps * cells_all, transcendentals=0)
    laps, inject, cour, last = pl.pallas_call(
        forward_kernel,
        in_specs=[smem, smem] + [vmem] * 10 + [pl.BlockSpec(memory_space=pltpu.HBM)],
        out_specs=[vmem] * 4,
        out_shape=[
            jax.ShapeDtypeStruct((steps, planes, 2, rows_x, rows_y), jnp.float32),
            jax.ShapeDtypeStruct((steps, planes_all, rows_x, rows_y), jnp.float32),
            jax.ShapeDtypeStruct((planes_all, rows_x, rows_y), jnp.float32),
            jax.ShapeDtypeStruct((2 * planes, rows_x, rows_y), jnp.float32),
        ],
        scratch_shapes=step_scratch + [whole, whole, whole, pltpu.SemaphoreType.DMA((3,))],
        compiler_params=pltpu.CompilerParams(vmem_limit_bytes=33 * 2**20),
        cost_estimate=pl.CostEstimate(flops=1000, bytes_accessed=1000, transcendentals=0),
        name="forward_steps",
    )(ckpt_step[None], src_cells, own, mate, over, far, c0, c1, *pieces, placed)

    adj_over = after(laps, adj_over)
    adj_far = exchange(adj_over, CORE)
    slab = jax.ShapeDtypeStruct(courant_sq.shape, jnp.float32)
    half, quarter = (planes // 2, rows_x, rows_y), (planes // 4, rows_x, rows_y)
    keep, send_x, send_y, send_xy = pl.pallas_call(
        adjoint_kernel,
        in_specs=[vmem] * 8,
        out_specs=[vmem] * 4,
        out_shape=[jax.ShapeDtypeStruct(half, jnp.float32)] * 4,
        scratch_shapes=step_scratch[:2] + [pltpu.VMEM((2 * planes, rows_x, rows_y), jnp.float32)] + step_scratch[2:],
        compiler_params=params,
        cost_estimate=cost,
        name="adjoint_steps",
    )(adj_own, adj_mate, adj_over, adj_far, cour, laps, inject, last)

    by_xy, by_x, by_y = exchange(send_xy, CHIP + Y), exchange(send_x, CHIP), exchange(send_y, Y)
    keep, send = local(square_kernel, [quarter] * 2, keep, by_x, by_y, by_xy)
    part = local(add_kernel, [quarter], keep, exchange(send, NEAR_Z))
    rows, sums_shape = planes // 4 * rows_x, (8, rows_y)
    data, sums = local(sums_kernel, [(rows + 8, rows_y), sums_shape], part, exchange(part, FAR_Z), momentum)

    received = exchange(data, NEAR_Z)
    others = [exchange(sums, CORE), exchange(sums, NEAR_Z + CORE)]
    data, sums = local(join_kernel, [(2 * rows + 8, rows_y), sums_shape], data, received, sums, *others)
    received = exchange(data, Y)
    others = [exchange(sums, CHIP), exchange(sums, Y + CHIP)]
    momentum_half, kinetic = pl.pallas_call(
        finish_kernel,
        in_specs=[vmem] * 6,
        out_specs=[vmem, smem],
        out_shape=[jax.ShapeDtypeStruct(momentum.shape, jnp.float32), jax.ShapeDtypeStruct((1,), jnp.float32)],
        compiler_params=pltpu.CompilerParams(vmem_limit_bytes=4 * 2**20),
        name="finish",
    )(data, received, momentum, sums, *others)
    return momentum_half, kinetic[0]


def solution(mesh):
    shots, slabs = mesh.shape["shot"], mesh.shape["depth"]

    def placed(depth):
        field = P("shot", depth, None, None)
        slab = P(depth, None, None)
        inputs = (slab, slab, field, field, field, field, P("shot", None, None), P("shot"), P("shot", None), P())
        return dict(in_specs=inputs, out_specs=(slab, P()), check_vma=False)

    slab_plan = jax.shard_map(slab_shards, mesh=mesh, **placed("depth"))
    if slabs != 4 or shots != 8:
        return slab_plan
    chips = Mesh(mesh.devices.reshape(shots, 2, 2), ("shot", "chip", "core"))
    whole_plan = jax.shard_map(whole_shards, mesh=chips, **placed(("chip", "core")))

    def run(courant_sq, momentum, fwd_prev, *rest):
        total, planes, rows_x, rows_y = fwd_prev.shape
        steps = rest[3].shape[1]
        fits = total == 2 * shots and planes == 4 * shots and rows_y == 128 and rows_x % 16 == 0 and steps % 2 == 0
        plan = whole_plan if fits else slab_plan
        return plan(courant_sq, momentum, fwd_prev, *rest)

    return run
```

```python
import functools

import jax
import jax.numpy as jnp
from jax import lax
from jax.experimental import pallas as pl
from jax.experimental.pallas import tpu as pltpu
from jax.sharding import Mesh
from jax.sharding import PartitionSpec as P

CENTER = -2.5
NEAR = 4.0 / 3.0
FAR = -1.0 / 12.0
AMPLITUDE = 100.0
EPSILON = 1e-06


def with_halo(value, sides, width):
    for axis, dim in sides:
        size, length = (lax.axis_size(axis), value.shape[dim])
        up = [(i, (i + 1) % size) for i in range(size - 1)]
        down = [(j, i) for i, j in up]
        last = lax.slice_in_dim(value, length - width, length, axis=dim)
        leading = lax.slice_in_dim(value, 0, width, axis=dim)
        before = lax.ppermute(last, axis, up)
        after = lax.ppermute(leading, axis, down)
        value = jnp.concatenate([before, value, after], axis=dim)
    return value


def laplace(padded):
    lateral = jnp.pad(padded[:, 2:-2], ((0, 0), (0, 0), (2, 2), (2, 2)))
    center = padded[:, 2:-2]
    along_z = NEAR * (padded[:, 1:-3] + padded[:, 3:-1]) + FAR * (padded[:, :-4] + padded[:, 4:])
    along_x = NEAR * (lateral[:, :, 1:-3, 2:-2] + lateral[:, :, 3:-1, 2:-2]) + FAR * (
        lateral[:, :, :-4, 2:-2] + lateral[:, :, 4:, 2:-2]
    )
    along_y = NEAR * (lateral[:, :, 2:-2, 1:-3] + lateral[:, :, 2:-2, 3:-1]) + FAR * (
        lateral[:, :, 2:-2, :-4] + lateral[:, :, 2:-2, 4:]
    )
    return 3.0 * CENTER * center + along_z + along_x + along_y


def locate(field, cell_ids, first_plane):
    shot_count, planes, rows_x, rows_y = field.shape
    plane_cells = rows_x * rows_y
    local_index = cell_ids - first_plane * plane_cells
    inside = (local_index >= 0) & (local_index < planes * plane_cells)
    target = jnp.where(inside, local_index, 0)
    return (inside, target)


def inject(field, cell_ids, values, first_plane):
    shot_count = field.shape[0]
    inside, target = locate(field, cell_ids, first_plane)
    amount = jnp.where(inside, values, jnp.zeros_like(values))
    flattened = field.reshape(shot_count, -1)
    lanes = jnp.arange(shot_count)[:, None]
    flattened = flattened.at[lanes, target].add(amount)
    return flattened.reshape(field.shape)


def sample(field, cell_ids, first_plane):
    shot_count = field.shape[0]
    inside, target = locate(field, cell_ids, first_plane)
    values = jnp.take_along_axis(field.reshape(shot_count, -1), target, axis=1)
    return jnp.where(inside, values, jnp.zeros_like(values))


def wave_value(start, step):
    cycle = jnp.mod(start + jnp.int32(step), jnp.int32(48))
    phase = (cycle.astype(jnp.float32) - 24.0) / 12.0
    return AMPLITUDE * (1.0 - 2.0 * phase * phase) * jnp.exp(-phase * phase)


def statistics(scaled, moment, weight, cells_all):
    grand_total = lax.psum(jnp.sum(scaled * scaled), ("shot", "depth"))
    factor = lax.rsqrt(grand_total / cells_all + EPSILON)
    halfway = moment - 0.5 * factor * scaled
    energy = lax.psum(jnp.sum(weight * halfway * halfway), ("shot", "depth"))
    return (factor, 0.5 * energy / cells_all)


def slab_shards(
    courant_sq,
    momentum,
    fwd_prev,
    fwd_cur,
    adj_next,
    adj_cur,
    observed,
    src_cells,
    rec_cells,
    ckpt_step,
):
    shot_count, planes, rows_x, rows_y = fwd_cur.shape
    steps_all = observed.shape[1]
    first_plane = lax.axis_index("depth") * planes
    total_planes = planes * lax.axis_size("depth")
    cells_all = total_planes * rows_x * rows_y
    sources = src_cells[:, None]
    older, current = (fwd_prev, fwd_cur)
    laplacians = []
    misfits = []
    for step in range(steps_all):
        padded = with_halo(current, (("depth", 1),), 2)
        strength = jnp.full(sources.shape, wave_value(ckpt_step, step), jnp.float32)
        laplacian = inject(laplace(padded), sources, strength, first_plane)
        newer = 2.0 * current - older + courant_sq * laplacian
        misfits.append(sample(newer, rec_cells, first_plane) - observed[:, step, :])
        laplacians.append(laplacian)
        older, current = (current, newer)
    adj_later, adj_now = (adj_next, adj_cur)
    gradient = jnp.zeros((planes, rows_x, rows_y), jnp.float32)
    for step in reversed(range(steps_all)):
        padded = with_halo(courant_sq * adj_now, (("depth", 1),), 2)
        adj_new = 2.0 * adj_now - adj_later + laplace(padded)
        adj_new = inject(adj_new, rec_cells, misfits[step], first_plane)
        gradient = gradient + jnp.sum(adj_new * laplacians[step], axis=0)
        adj_later, adj_now = (adj_now, adj_new)
    depths = (first_plane + jnp.arange(planes)).astype(jnp.float32)
    weight = (1.0 + 2.0 * depths / (total_planes - 1))[:, None, None]
    share_rows = rows_x // lax.axis_size("shot")
    offset = lax.axis_index("shot") * share_rows
    moment_share = lax.dynamic_slice_in_dim(momentum, offset, share_rows, 1)
    gradient = lax.psum(gradient, "shot")
    scaled = weight * gradient
    scaled_share = lax.dynamic_slice_in_dim(scaled, offset, share_rows, 1)
    factor, kinetic = statistics(scaled_share, moment_share, weight, cells_all)
    momentum_half = momentum - 0.5 * factor * scaled
    return (momentum_half, kinetic)


def interleave(dst, slab, src, factor=None):
    planes, rows = src.shape[0], src.shape[1]
    groups = rows // 8

    @pl.loop(0, planes)
    def _(p):
        for i in range(groups):
            value = src[p, pl.ds(i, 8, stride=groups), :]
            if factor is not None:
                value = value * factor
            dst[(*slab, p, pl.ds(i * 8, 8), slice(None))] = value


def pick_kernel(across, *refs):
    count = len(across)
    fields, outs, (held, sems) = refs[: 2 * count], refs[2 * count : 3 * count], refs[3 * count :]
    chip = lax.axis_index("chip")
    copies = []
    for n in range(2 * count):
        shot = 1 - chip if across[n // 2] else chip
        copies.append(pltpu.make_async_copy(fields[n].at[shot], held.at[n], sems.at[n]))
        copies[-1].start()
    for n in range(2 * count):
        copies[n].wait()
        interleave(outs[n // 2], (n % 2,), held.at[n])


def pick(*pairs, earlier):
    plain = functools.partial(pick_kernel, tuple(pair[2] for pair in pairs))
    fields = [field for pair in pairs for field in pair[:2]]
    shape = fields[0].shape[1:]
    vmem, hbm = pl.BlockSpec(memory_space=pltpu.VMEM), pl.BlockSpec(memory_space=pltpu.HBM)
    return pl.pallas_call(
        lambda earlier, *refs: plain(*refs),
        in_specs=[pl.BlockSpec(memory_space=pl.ANY)] + [hbm] * len(fields),
        out_specs=[vmem] * len(pairs),
        out_shape=[jax.ShapeDtypeStruct((2, *shape), jnp.float32)] * len(pairs),
        scratch_shapes=[pltpu.VMEM((len(fields), *shape), jnp.float32), pltpu.SemaphoreType.DMA((len(fields),))],
        compiler_params=pltpu.CompilerParams(vmem_limit_bytes=4 * 2**20),
        name="pick",
    )(earlier, *fields)


def first_kernel(first, second, courant, outgoing, whole, piece, held, held_courant, sems):
    shot = 1 - lax.axis_index("chip")
    copies = [
        pltpu.make_async_copy(first.at[shot], held.at[0], sems.at[0]),
        pltpu.make_async_copy(second.at[shot], held.at[1], sems.at[1]),
        pltpu.make_async_copy(courant, held_courant, sems.at[2]),
    ]
    for copy in copies:
        copy.start()
    for n in range(2):
        copies[n].wait()
        interleave(outgoing, (n,), held.at[n])
    copies[2].wait()
    interleave(whole, (), held_courant, 1.0 / 12.0)
    count = piece.shape[0]
    piece[...] = whole[pl.ds(lax.axis_index("shot") % 2 * count, count)]


def band(lanes):
    near = jnp.abs(lax.broadcasted_iota(jnp.int32, (2 * lanes, lanes), 0) % lanes - lax.broadcasted_iota(jnp.int32, (2 * lanes, lanes), 1))
    return jnp.where(near == 0, -90.0, jnp.where(near == 1, 16.0, jnp.where(near == 2, -1.0, 0.0))).astype(jnp.bfloat16)


def along_y(field, z, banded, out):
    rows, lanes = field.shape[1:]
    whole = field[pl.ds(z + 2, BATCH)].reshape(BATCH * rows, lanes)
    high = whole.astype(jnp.bfloat16)
    low = (whole - high.astype(jnp.float32)).astype(jnp.bfloat16)
    out[...] = jnp.dot(jnp.concatenate([high, low], 1), banded[...], preferred_element_type=jnp.float32)


def laps12(field, z, y_part, fetch, finish):
    rows, lanes = field.shape[1:]
    groups = rows // 8
    sub = lax.broadcasted_iota(jnp.int32, (8, lanes), 0)

    def later(block):
        return jnp.where(sub < 7, pltpu.roll(block, 7, 0), 0.0)

    def earlier(block):
        return jnp.where(sub > 0, pltpu.roll(block, 1, 0), 0.0)

    for base in range(0, BATCH, PLANES):
        held = {}

        def tile(j, i):
            if (j, i) not in held:
                if i < 0:
                    held[j, i] = earlier(tile(j, i + groups))
                elif i >= groups:
                    held[j, i] = later(tile(j, i - groups))
                else:
                    held[j, i] = field[z + j + 2, i * 8 : (i + 1) * 8]
            return held[j, i]

        def load(i):
            found = []
            for j in range(base, base + PLANES):
                center = tile(j, i)
                near = (tile(j, i - 1), tile(j, i + 1), tile(j - 1, i), tile(j + 1, i))
                far = (tile(j, i - 2), tile(j, i + 2), tile(j - 2, i), tile(j + 2, i))
                at = (j * groups + i) * 8
                found.append((center, near, far, y_part[at : at + 8], fetch(j, slice(i * 8, i * 8 + 8))))
            return found

        ready = load(0)
        for i in range(groups):
            upcoming = load(i + 1) if i + 1 < groups else None
            for j, (center, near, far, part, extra) in enumerate(ready):
                near = (near[0] + near[1]) + (near[2] + near[3])
                far = (far[0] + far[1]) + (far[2] + far[3])
                finish(base + j, slice(i * 8, i * 8 + 8), center, 16.0 * near + (part - far), extra)
            ready = upcoming


def scatter_kernel(rows_x, cells_ref, observed_ref, out_ref, mark, row_ref, spread):
    _, steps, receivers = observed_ref.shape
    lanes = out_ref.shape[2]
    tile = out_ref.shape[1]
    groups = rows_x // 8

    @pl.when(pl.program_id(0) == 0)
    def _():
        chip = lax.axis_index("chip")
        cells = cells_ref[pl.ds(chip, 1)]
        x = cells // lanes % rows_x
        row_ref[...] = cells // (rows_x * lanes) * rows_x + x % groups * 8 + x // groups
        on_lanes = jnp.concatenate(
            [
                observed_ref[chip],
                jnp.broadcast_to((cells % lanes).astype(jnp.float32), (8, receivers)),
                jnp.zeros((lanes - steps - 8, receivers), jnp.float32),
            ],
            0,
        )
        columns = on_lanes.T
        lane = lax.broadcasted_iota(jnp.int32, (receivers, lanes), 1).astype(jnp.float32)
        at = lane == columns[:, steps : steps + 1]
        for k in range(steps):
            column = columns[:, k : k + 1]
            high = column.astype(jnp.bfloat16).astype(jnp.float32)
            low = column - high
            cols = pl.ds(k * lanes, lanes)
            spread[0:receivers, cols] = jnp.where(at, high, 0.0).astype(jnp.bfloat16)
            spread[receivers:, cols] = jnp.where(at, low, 0.0).astype(jnp.bfloat16)
        cols = pl.ds(steps * lanes, lanes)
        spread[0:receivers, cols] = jnp.where(at, 1.0, 0.0).astype(jnp.bfloat16)
        spread[receivers:, cols] = jnp.zeros((receivers, lanes), jnp.bfloat16)
        mark[...] = jnp.zeros(mark.shape, jnp.float32)

    ids = lax.broadcasted_iota(jnp.int32, (tile, receivers), 0) + pl.program_id(0) * tile
    chosen = jnp.where(ids == row_ref[...], 1.0, 0.0).astype(jnp.bfloat16)
    total = jnp.dot(jnp.concatenate([chosen, chosen], 1), spread[...], preferred_element_type=jnp.float32)
    for k in range(steps + 1):
        out_ref[k] = total[:, k * lanes : (k + 1) * lanes]


def scatter(rec_cells, observed, planes_all, rows_x, rows_y):
    _, steps, receivers = observed.shape
    rows_all = planes_all * rows_x
    tile = 512
    return pl.pallas_call(
        functools.partial(scatter_kernel, rows_x),
        grid=(rows_all // tile,),
        in_specs=[
            pl.BlockSpec((2, receivers), lambda t: (0, 0)),
            pl.BlockSpec((2, steps, receivers), lambda t: (0, 0, 0)),
        ],
        out_specs=[
            pl.BlockSpec((steps + 1, tile, rows_y), lambda t: (0, t, 0)),
            pl.BlockSpec((8, rows_y), lambda t: (0, 0)),
        ],
        out_shape=[
            jax.ShapeDtypeStruct((steps + 1, rows_all, rows_y), jnp.float32),
            jax.ShapeDtypeStruct((8, rows_y), jnp.float32),
        ],
        scratch_shapes=[
            pltpu.VMEM((1, receivers), jnp.int32),
            pltpu.VMEM((2 * receivers, (steps + 1) * rows_y), jnp.bfloat16),
        ],
        compiler_params=pltpu.CompilerParams(vmem_limit_bytes=56 * 2**20),
        cost_estimate=pl.CostEstimate(
            flops=4 * rows_all * receivers * (steps + 1) * rows_y,
            bytes_accessed=4 * (steps + 1) * rows_all * rows_y,
            transcendentals=0,
        ),
        name="receiver_scatter",
    )(rec_cells, observed)


def place(planes):
    chip, core = lax.axis_index("chip"), lax.axis_index("core")
    slabs = (2 * chip + core, 2 * chip + 1 - core, 2 * (1 - chip) + core, 2 * (1 - chip) + 1 - core)
    return chip, core, [slab * planes for slab in slabs]


def load_blocks(slabs, blocks, first, second, factor=None):
    ends, rows, lanes = first.shape
    planes = blocks[0].shape[1]
    for field in (first, second):
        for z in (0, 1, ends - 2, ends - 1):
            field[z] = jnp.zeros((rows, lanes), jnp.float32)
    for slab, block in zip(slabs, blocks):
        for p in range(planes):
            values = block[0, p], block[1, p]
            if factor is not None:
                speed = factor[slab + p]
                values = values[0] * speed, values[1] * speed
            first[slab + p + 2], second[slab + p + 2] = values


BATCH = 4
PLANES = 2


def sweep(core, planes, field, banded, y_first, y_second, work):
    order = [(chip, owned) for owned in (True, False) for chip in (0, 1)]
    parts = (y_first, y_second)

    def first(chip, owned):
        return (2 * chip + (core if owned else 1 - core)) * planes

    along_y(field, first(*order[0]), banded, y_first)
    for owned in (True, False):
        for chip in (0, 1):
            z = first(chip, owned)
            onward = first(1, owned) if chip == 0 else first(0, False)
            for n in range(planes // BATCH):
                last = n == planes // BATCH - 1
                if not last or chip == 0 or owned:
                    along_y(field, onward if last else z + (n + 1) * BATCH, banded, parts[(n + 1) % 2])
                work(z + n * BATCH, parts[n % 2], chip if owned else None, n * BATCH)


def forward_kernel(
    start, sources, own, mate, over, far, c0, c1, c2, c3, placed, laps, inject, cour, last, even, odd, banded, y0, y1,
    held, sems
):
    planes, rows, lanes = c0.shape
    steps = laps.shape[0]
    groups = rows // 8
    chip_here, core, slabs = place(planes)

    def parts(k):
        for n in range(4):
            at = pl.ds(n * planes, planes)
            yield pltpu.make_async_copy(placed.at[k, at], held.at[k, at], sems.at[k, n])

    for k in (steps, 0, 1, 2):
        for part in parts(k):
            part.start()
    banded[...] = band(lanes)
    load_blocks(slabs, (own, mate, over, far), odd, even)
    for slab, block in zip(slabs, (c0, c1, c2, c3)):
        for p in range(planes):
            cour[slab + p] = block[p]

    for index in range(2 * planes):
        z = (2 * (index // planes) + core) * planes + index % planes
        weight = 1.0 + 2.0 * jnp.full((rows, lanes), z, jnp.int32).astype(jnp.float32) / (4 * planes - 1)
        last[index] = weight / (12.0 * cour[z])

    cell = sources[chip_here]
    source_z, x, lane = cell // (rows * lanes), cell // lanes % rows, cell % lanes
    tile = pl.ds(pl.multiple_of(x % groups * 8, 8), 8)
    here = (lax.broadcasted_iota(jnp.int32, (8, lanes), 0) == x // groups) & (
        lax.broadcasted_iota(jnp.int32, (8, lanes), 1) == lane
    )
    source_slab, source_p = source_z // planes, lax.rem(source_z, planes)

    def advance(k, now, then):
        @pl.when(k + 3 < steps)
        def _():
            for part in parts(k + 3):
                part.start()

        for part in parts(k):
            part.wait()

        def work(z, y_part, chip, p):
            def fetch(j, rows):
                return then[z + j + 2, rows], cour[z + j, rows], held[k, z + j, rows], held[steps, z + j, rows]

            def finish(j, rows, center, lap, extra):
                old, speed, traces, count = extra
                if chip is not None:
                    laps[k, p + j, chip, rows] = lap
                newer = 2.0 * center - old + speed * lap
                then[z + j + 2, rows] = newer
                inject[k, z + j, rows] = traces - count * newer

            laps12(now, z, y_part, fetch, finish)

        cycle = (start[0] + k) % 48
        phase = (jnp.full((8, lanes), cycle, jnp.int32).astype(jnp.float32) - 24.0) / 12.0
        wave = AMPLITUDE * (1.0 - 2.0 * phase * phase) * jnp.exp(-phase * phase)
        strength = jnp.where(here, 12.0 * wave, 0.0)
        moved = cour[source_z, tile, :] * strength

        sweep(core, planes, now, banded, y0, y1, work)

        owned = jnp.where(lax.rem(source_slab, 2) == core, strength, 0.0)
        laps[k, source_p, source_slab // 2, tile, :] += owned
        then[source_z + 2, tile, :] += moved
        inject[k, source_z, tile, :] -= held[steps, source_z, tile, :] * moved

    for part in parts(steps):
        part.wait()

    @pl.loop(0, steps // 2)
    def _(pair):
        advance(2 * pair, even, odd)
        advance(2 * pair + 1, odd, even)


def adjoint_kernel(own, mate, over, far, cour, laps, inject, last, keep, send_x, send_y, send_xy, even, odd, total, banded, y0, y1):
    planes, rows, lanes = own.shape[1:]
    steps = laps.shape[0]
    groups = rows // 8
    chip_here, core, slabs = place(planes)
    banded[...] = band(lanes)
    load_blocks(slabs, (own, mate, over, far), odd, even, factor=cour)

    total[...] = jnp.zeros(total.shape, jnp.float32)

    def advance(k, now, then):
        def work(z, y_part, chip, p):
            def fetch(j, rows):
                extra = (then[z + j + 2, rows], cour[z + j, rows], inject[k, z + j, rows])
                if chip is not None:
                    extra += (total[chip * planes + p + j, rows], laps[k, p + j, chip, rows])
                return extra

            def finish(j, rows, center, lap, extra):
                newer = 2.0 * center - extra[0] + extra[1] * (lap - extra[2])
                then[z + j + 2, rows] = newer
                if chip is not None:
                    total[chip * planes + p + j, rows] = extra[3] + newer * extra[4]

            laps12(now, z, y_part, fetch, finish)

        sweep(core, planes, now, banded, y0, y1, work)

    @pl.loop(0, steps // 2)
    def _(pair):
        advance(steps - 1 - 2 * pair, even, odd)
        advance(steps - 2 - 2 * pair, odd, even)

    count = keep.shape[0]
    mine, others = lax.axis_index("shot") % 2 * count, (1 - lax.axis_index("shot") % 2) * count
    here, there = chip_here, 1 - chip_here
    for ref, chip, start in ((keep, here, mine), (send_x, there, mine), (send_y, here, others), (send_xy, there, others)):

        @pl.loop(0, count)
        def _(n):
            p = start + n
            value = total[chip * planes + p] * last[chip * planes + p]
            for i in range(groups):
                ref[n, pl.ds(i, 8, stride=groups), :] = value[i * 8 : (i + 1) * 8]


def square_kernel(mine, by_x, by_y, by_xy, keep, send):
    half = lax.axis_index("shot") // 2 % 2
    count = keep.shape[0]
    for ref, part in ((keep, half), (send, 1 - half)):
        for p in range(count):
            at = part * count + p
            ref[p] = (mine[at] + by_x[at]) + (by_y[at] + by_xy[at])


def add_kernel(mine, other, out):
    out[...] = mine[...] + other[...]


def flip(index, bits):
    result = index
    for bit in (1, 2):
        if bits & bit:
            result = jnp.where(index // bit % 2 == 1, result - bit, result + bit)
    return result


def after_kernel(earlier, value, out):
    out[...] = value[...]


def after(earlier, value):
    vmem, anywhere = pl.BlockSpec(memory_space=pltpu.VMEM), pl.BlockSpec(memory_space=pl.ANY)
    return pl.pallas_call(
        after_kernel,
        in_specs=[anywhere, vmem],
        out_specs=vmem,
        out_shape=jax.ShapeDtypeStruct(value.shape, jnp.float32),
        compiler_params=pltpu.CompilerParams(vmem_limit_bytes=4 * 2**20),
        name="after",
    )(earlier, value)


def arrange_kernel(mine, other, out):
    y = lax.axis_index("shot") % 2
    count = mine.shape[0]
    out[pl.ds(y * count, count)] = mine[...]
    out[pl.ds((1 - y) * count, count)] = other[...]


def first_plane(shot, planes):
    return (shot % 2) * (planes // 2) + (shot // 2 % 2) * (planes // 4)


def sums_kernel(mine, other, momentum, data, sums):
    count, rows, lanes = mine.shape
    planes = momentum.shape[0]
    chip, core = lax.axis_index("chip"), lax.axis_index("core")
    first = first_plane(lax.axis_index("shot"), planes)
    parts = [jnp.zeros((rows, lanes), jnp.float32)] * 4
    for j in range(count):
        scaled = mine[j] + other[j]
        data[j * rows : (j + 1) * rows] = scaled
        z = (2 * chip + core) * planes + first + j
        weight = 1.0 + 2.0 * jnp.full((1, lanes), z, jnp.int32).astype(jnp.float32) / (4 * planes - 1)
        moment = momentum[first + j]
        square = scaled * scaled
        terms = (square, weight * moment * moment, weight * moment * scaled, weight * square)
        parts = [part + term for part, term in zip(parts, terms)]

    def total(value):
        by_lane = jnp.sum(value, axis=0, keepdims=True)
        return jnp.broadcast_to(jnp.sum(by_lane, axis=1, keepdims=True), (1, lanes))

    value = jnp.concatenate([total(part) for part in parts] + [jnp.zeros((4, lanes), jnp.float32)], 0)
    data[count * rows :] = value
    sums[...] = value


def join_kernel(mine, other, s0, s1, s2, data, sums):
    rows = mine.shape[0] - 8
    data[0:rows] = mine[0:rows]
    data[rows : 2 * rows] = other[0:rows]
    value = (s0[...] + s1[...]) + (other[rows:] + s2[...])
    data[2 * rows :] = value
    sums[...] = value


def finish_kernel(mine, other, momentum, s0, s1, s2, out, kinetic):
    planes, rows, lanes = momentum.shape
    cells = 4.0 * planes * rows * lanes
    shot = lax.axis_index("shot")
    sums = (s0[...] + s1[...]) + (other[planes // 2 * rows :] + s2[...])
    factor = lax.rsqrt(sums[0:1] / cells + EPSILON)
    energy = 0.5 * (sums[1:2] - factor * sums[2:3] + 0.25 * factor * factor * sums[3:4]) / cells
    kinetic[0] = energy[0, 0]
    step = 0.5 * factor
    quarter = planes // 4
    for part, group in ((mine, shot), (other, flip(shot, 1))):
        for number, first in enumerate((first_plane(group, planes), first_plane(flip(group, 2), planes))):
            for j in range(quarter):
                at = (number * quarter + j) * rows
                out[first + j] = momentum[first + j] - step * part[at : at + rows]


def local(kernel, outs, *arrays):
    vmem = pl.BlockSpec(memory_space=pltpu.VMEM)
    shapes = [jax.ShapeDtypeStruct(shape, jnp.float32) for shape in outs]
    single = len(outs) == 1
    return pl.pallas_call(
        kernel,
        in_specs=[vmem] * len(arrays),
        out_specs=vmem if single else [vmem] * len(outs),
        out_shape=shapes[0] if single else shapes,
        compiler_params=pltpu.CompilerParams(vmem_limit_bytes=4 * 2**20),
        name=kernel.__name__,
    )(*arrays)


def exchange(value, bits):
    axes = ("shot", "chip", "core")
    return lax.ppermute(value, axes, [(i, i ^ bits) for i in range(lax.axis_size(axes))])


CORE, CHIP, Y, NEAR_Z, FAR_Z = 1, 2, 4, 8, 16


def whole_shards(
    courant_sq, momentum, fwd_prev, fwd_cur, adj_next, adj_cur, observed, src_cells, rec_cells, ckpt_step
):
    _, planes, rows_x, rows_y = fwd_cur.shape
    steps = observed.shape[1]
    planes_all = 4 * planes
    cells_all = planes_all * rows_x * rows_y
    vmem, smem = pl.BlockSpec(memory_space=pltpu.VMEM), pl.BlockSpec(memory_space=pltpu.SMEM)

    hbm = pl.BlockSpec(memory_space=pltpu.HBM)
    outgoing, c0, piece = pl.pallas_call(
        first_kernel,
        in_specs=[hbm] * 3,
        out_specs=[vmem] * 3,
        out_shape=[
            jax.ShapeDtypeStruct((2, planes, rows_x, rows_y), jnp.float32),
            jax.ShapeDtypeStruct(courant_sq.shape, jnp.float32),
            jax.ShapeDtypeStruct((planes // 2, rows_x, rows_y), jnp.float32),
        ],
        scratch_shapes=[
            pltpu.VMEM((2, planes, rows_x, rows_y), jnp.float32),
            pltpu.VMEM(courant_sq.shape, jnp.float32),
            pltpu.SemaphoreType.DMA((3,)),
        ],
        compiler_params=pltpu.CompilerParams(vmem_limit_bytes=63 * 2**20),
        name="first_to_cross",
    )(fwd_prev, fwd_cur, courant_sq)

    over = exchange(outgoing, CHIP)
    piece = exchange(piece, CHIP)

    placed, mark = scatter(rec_cells, observed, planes_all, rows_x, rows_y)
    placed = placed.reshape(steps + 1, planes_all, rows_x, rows_y)

    piece = after(mark, piece)
    adj_outgoing, adj_own, own = pick(
        (adj_next, adj_cur, True), (adj_next, adj_cur, False), (fwd_prev, fwd_cur, False), earlier=piece
    )
    mate = exchange(own, CORE)
    c2 = local(arrange_kernel, [courant_sq.shape], piece, exchange(piece, Y))
    c1, c3 = exchange(c0, CORE), exchange(c2, CORE)
    over = after(c2, over)
    far = exchange(over, CORE)
    adj_over = exchange(adj_outgoing, CHIP)
    adj_mate = exchange(adj_own, CORE)

    scratch = pltpu.VMEM((planes_all + 4, rows_x, rows_y), jnp.float32)
    y_scratch = pltpu.VMEM((BATCH * rows_x, rows_y), jnp.float32)
    step_scratch = [scratch, scratch, pltpu.VMEM((2 * rows_y, rows_y), jnp.bfloat16), y_scratch, y_scratch]
    params = pltpu.CompilerParams(vmem_limit_bytes=6 * 2**20)
    cost = pl.CostEstimate(flops=30 * steps * cells_all, bytes_accessed=16 * steps * cells_all, transcendentals=0)
    laps, inject, cour, last = pl.pallas_call(
        forward_kernel,
        in_specs=[smem, smem] + [vmem] * 8 + [pl.BlockSpec(memory_space=pltpu.HBM)],
        out_specs=[vmem] * 4,
        out_shape=[
            jax.ShapeDtypeStruct((steps, planes, 2, rows_x, rows_y), jnp.float32),
            jax.ShapeDtypeStruct((steps, planes_all, rows_x, rows_y), jnp.float32),
            jax.ShapeDtypeStruct((planes_all, rows_x, rows_y), jnp.float32),
            jax.ShapeDtypeStruct((2 * planes, rows_x, rows_y), jnp.float32),
        ],
        scratch_shapes=step_scratch
        + [pltpu.VMEM((steps + 1, planes_all, rows_x, rows_y), jnp.float32), pltpu.SemaphoreType.DMA((steps + 1, 4))],
        compiler_params=pltpu.CompilerParams(vmem_limit_bytes=33 * 2**20),
        cost_estimate=pl.CostEstimate(flops=1000, bytes_accessed=1000, transcendentals=0),
        name="forward_steps",
    )(ckpt_step[None], src_cells, own, mate, over, far, c0, c1, c2, c3, placed)

    adj_over = after(laps, adj_over)
    adj_far = exchange(adj_over, CORE)
    slab = jax.ShapeDtypeStruct(courant_sq.shape, jnp.float32)
    half, quarter = (planes // 2, rows_x, rows_y), (planes // 4, rows_x, rows_y)
    keep, send_x, send_y, send_xy = pl.pallas_call(
        adjoint_kernel,
        in_specs=[vmem] * 8,
        out_specs=[vmem] * 4,
        out_shape=[jax.ShapeDtypeStruct(half, jnp.float32)] * 4,
        scratch_shapes=step_scratch[:2] + [pltpu.VMEM((2 * planes, rows_x, rows_y), jnp.float32)] + step_scratch[2:],
        compiler_params=params,
        cost_estimate=cost,
        name="adjoint_steps",
    )(adj_own, adj_mate, adj_over, adj_far, cour, laps, inject, last)

    by_xy, by_x, by_y = exchange(send_xy, CHIP + Y), exchange(send_x, CHIP), exchange(send_y, Y)
    keep, send = local(square_kernel, [quarter] * 2, keep, by_x, by_y, by_xy)
    part = local(add_kernel, [quarter], keep, exchange(send, NEAR_Z))
    rows, sums_shape = planes // 4 * rows_x, (8, rows_y)
    data, sums = local(sums_kernel, [(rows + 8, rows_y), sums_shape], part, exchange(part, FAR_Z), momentum)

    received = exchange(data, NEAR_Z)
    others = [exchange(sums, CORE), exchange(sums, NEAR_Z + CORE)]
    data, sums = local(join_kernel, [(2 * rows + 8, rows_y), sums_shape], data, received, sums, *others)
    received = exchange(data, Y)
    others = [exchange(sums, CHIP), exchange(sums, Y + CHIP)]
    momentum_half, kinetic = pl.pallas_call(
        finish_kernel,
        in_specs=[vmem] * 6,
        out_specs=[vmem, smem],
        out_shape=[jax.ShapeDtypeStruct(momentum.shape, jnp.float32), jax.ShapeDtypeStruct((1,), jnp.float32)],
        compiler_params=pltpu.CompilerParams(vmem_limit_bytes=4 * 2**20),
        name="finish",
    )(data, received, momentum, sums, *others)
    return momentum_half, kinetic[0]


def solution(mesh):
    shots, slabs = mesh.shape["shot"], mesh.shape["depth"]

    def placed(depth):
        field = P("shot", depth, None, None)
        slab = P(depth, None, None)
        inputs = (slab, slab, field, field, field, field, P("shot", None, None), P("shot"), P("shot", None), P())
        return dict(in_specs=inputs, out_specs=(slab, P()), check_vma=False)

    slab_plan = jax.shard_map(slab_shards, mesh=mesh, **placed("depth"))
    if slabs != 4 or shots != 8:
        return slab_plan
    chips = Mesh(mesh.devices.reshape(shots, 2, 2), ("shot", "chip", "core"))
    whole_plan = jax.shard_map(whole_shards, mesh=chips, **placed(("chip", "core")))

    def run(courant_sq, momentum, fwd_prev, *rest):
        total, planes, rows_x, rows_y = fwd_prev.shape
        steps = rest[3].shape[1]
        fits = total == 2 * shots and planes == 4 * shots and rows_y == 128 and rows_x % 16 == 0 and steps % 2 == 0
        plan = whole_plan if fits else slab_plan
        return plan(courant_sq, momentum, fwd_prev, *rest)

    return run
```

```python
import functools

import jax
import jax.numpy as jnp
from jax import lax
from jax.experimental import pallas as pl
from jax.experimental.pallas import tpu as pltpu
from jax.sharding import Mesh
from jax.sharding import PartitionSpec as P

CENTER = -2.5
NEAR = 4.0 / 3.0
FAR = -1.0 / 12.0
AMPLITUDE = 100.0
EPSILON = 1e-06


def with_halo(value, sides, width):
    for axis, dim in sides:
        size, length = (lax.axis_size(axis), value.shape[dim])
        up = [(i, (i + 1) % size) for i in range(size - 1)]
        down = [(j, i) for i, j in up]
        last = lax.slice_in_dim(value, length - width, length, axis=dim)
        leading = lax.slice_in_dim(value, 0, width, axis=dim)
        before = lax.ppermute(last, axis, up)
        after = lax.ppermute(leading, axis, down)
        value = jnp.concatenate([before, value, after], axis=dim)
    return value


def laplace(padded):
    lateral = jnp.pad(padded[:, 2:-2], ((0, 0), (0, 0), (2, 2), (2, 2)))
    center = padded[:, 2:-2]
    along_z = NEAR * (padded[:, 1:-3] + padded[:, 3:-1]) + FAR * (padded[:, :-4] + padded[:, 4:])
    along_x = NEAR * (lateral[:, :, 1:-3, 2:-2] + lateral[:, :, 3:-1, 2:-2]) + FAR * (
        lateral[:, :, :-4, 2:-2] + lateral[:, :, 4:, 2:-2]
    )
    along_y = NEAR * (lateral[:, :, 2:-2, 1:-3] + lateral[:, :, 2:-2, 3:-1]) + FAR * (
        lateral[:, :, 2:-2, :-4] + lateral[:, :, 2:-2, 4:]
    )
    return 3.0 * CENTER * center + along_z + along_x + along_y


def locate(field, cell_ids, first_plane):
    shot_count, planes, rows_x, rows_y = field.shape
    plane_cells = rows_x * rows_y
    local_index = cell_ids - first_plane * plane_cells
    inside = (local_index >= 0) & (local_index < planes * plane_cells)
    target = jnp.where(inside, local_index, 0)
    return (inside, target)


def inject(field, cell_ids, values, first_plane):
    shot_count = field.shape[0]
    inside, target = locate(field, cell_ids, first_plane)
    amount = jnp.where(inside, values, jnp.zeros_like(values))
    flattened = field.reshape(shot_count, -1)
    lanes = jnp.arange(shot_count)[:, None]
    flattened = flattened.at[lanes, target].add(amount)
    return flattened.reshape(field.shape)


def sample(field, cell_ids, first_plane):
    shot_count = field.shape[0]
    inside, target = locate(field, cell_ids, first_plane)
    values = jnp.take_along_axis(field.reshape(shot_count, -1), target, axis=1)
    return jnp.where(inside, values, jnp.zeros_like(values))


def wave_value(start, step):
    cycle = jnp.mod(start + jnp.int32(step), jnp.int32(48))
    phase = (cycle.astype(jnp.float32) - 24.0) / 12.0
    return AMPLITUDE * (1.0 - 2.0 * phase * phase) * jnp.exp(-phase * phase)


def statistics(scaled, moment, weight, cells_all):
    grand_total = lax.psum(jnp.sum(scaled * scaled), ("shot", "depth"))
    factor = lax.rsqrt(grand_total / cells_all + EPSILON)
    halfway = moment - 0.5 * factor * scaled
    energy = lax.psum(jnp.sum(weight * halfway * halfway), ("shot", "depth"))
    return (factor, 0.5 * energy / cells_all)


def slab_shards(
    courant_sq,
    momentum,
    fwd_prev,
    fwd_cur,
    adj_next,
    adj_cur,
    observed,
    src_cells,
    rec_cells,
    ckpt_step,
):
    shot_count, planes, rows_x, rows_y = fwd_cur.shape
    steps_all = observed.shape[1]
    first_plane = lax.axis_index("depth") * planes
    total_planes = planes * lax.axis_size("depth")
    cells_all = total_planes * rows_x * rows_y
    sources = src_cells[:, None]
    older, current = (fwd_prev, fwd_cur)
    laplacians = []
    misfits = []
    for step in range(steps_all):
        padded = with_halo(current, (("depth", 1),), 2)
        strength = jnp.full(sources.shape, wave_value(ckpt_step, step), jnp.float32)
        laplacian = inject(laplace(padded), sources, strength, first_plane)
        newer = 2.0 * current - older + courant_sq * laplacian
        misfits.append(sample(newer, rec_cells, first_plane) - observed[:, step, :])
        laplacians.append(laplacian)
        older, current = (current, newer)
    adj_later, adj_now = (adj_next, adj_cur)
    gradient = jnp.zeros((planes, rows_x, rows_y), jnp.float32)
    for step in reversed(range(steps_all)):
        padded = with_halo(courant_sq * adj_now, (("depth", 1),), 2)
        adj_new = 2.0 * adj_now - adj_later + laplace(padded)
        adj_new = inject(adj_new, rec_cells, misfits[step], first_plane)
        gradient = gradient + jnp.sum(adj_new * laplacians[step], axis=0)
        adj_later, adj_now = (adj_now, adj_new)
    depths = (first_plane + jnp.arange(planes)).astype(jnp.float32)
    weight = (1.0 + 2.0 * depths / (total_planes - 1))[:, None, None]
    share_rows = rows_x // lax.axis_size("shot")
    offset = lax.axis_index("shot") * share_rows
    moment_share = lax.dynamic_slice_in_dim(momentum, offset, share_rows, 1)
    gradient = lax.psum(gradient, "shot")
    scaled = weight * gradient
    scaled_share = lax.dynamic_slice_in_dim(scaled, offset, share_rows, 1)
    factor, kinetic = statistics(scaled_share, moment_share, weight, cells_all)
    momentum_half = momentum - 0.5 * factor * scaled
    return (momentum_half, kinetic)


def interleave(dst, slab, src, factor=None):
    planes, rows = src.shape[0], src.shape[1]
    groups = rows // 8

    @pl.loop(0, planes)
    def _(p):
        for i in range(groups):
            value = src[p, pl.ds(i, 8, stride=groups), :]
            if factor is not None:
                value = value * factor
            dst[(*slab, p, pl.ds(i * 8, 8), slice(None))] = value


def pick_kernel(across, *refs):
    count = len(across)
    fields, outs, (held, sems) = refs[: 2 * count], refs[2 * count : 3 * count], refs[3 * count :]
    chip = lax.axis_index("chip")
    copies = []
    for n in range(2 * count):
        shot = 1 - chip if across[n // 2] else chip
        copies.append(pltpu.make_async_copy(fields[n].at[shot], held.at[n], sems.at[n]))
        copies[-1].start()
    for n in range(2 * count):
        copies[n].wait()
        interleave(outs[n // 2], (n % 2,), held.at[n])


def pick(*pairs, earlier):
    plain = functools.partial(pick_kernel, tuple(pair[2] for pair in pairs))
    fields = [field for pair in pairs for field in pair[:2]]
    shape = fields[0].shape[1:]
    vmem, hbm = pl.BlockSpec(memory_space=pltpu.VMEM), pl.BlockSpec(memory_space=pltpu.HBM)
    return pl.pallas_call(
        lambda earlier, *refs: plain(*refs),
        in_specs=[pl.BlockSpec(memory_space=pl.ANY)] + [hbm] * len(fields),
        out_specs=[vmem] * len(pairs),
        out_shape=[jax.ShapeDtypeStruct((2, *shape), jnp.float32)] * len(pairs),
        scratch_shapes=[pltpu.VMEM((len(fields), *shape), jnp.float32), pltpu.SemaphoreType.DMA((len(fields),))],
        compiler_params=pltpu.CompilerParams(vmem_limit_bytes=4 * 2**20),
        name="pick",
    )(earlier, *fields)


def first_kernel(first, second, courant, outgoing, whole, piece, held, held_courant, sems):
    shot = 1 - lax.axis_index("chip")
    copies = [
        pltpu.make_async_copy(first.at[shot], held.at[0], sems.at[0]),
        pltpu.make_async_copy(second.at[shot], held.at[1], sems.at[1]),
        pltpu.make_async_copy(courant, held_courant, sems.at[2]),
    ]
    for copy in copies:
        copy.start()
    for n in range(2):
        copies[n].wait()
        interleave(outgoing, (n,), held.at[n])
    copies[2].wait()
    interleave(whole, (), held_courant, 1.0 / 12.0)
    count = piece.shape[0]
    piece[...] = whole[pl.ds(lax.axis_index("shot") % 2 * count, count)]


def band(lanes):
    near = jnp.abs(lax.broadcasted_iota(jnp.int32, (2 * lanes, lanes), 0) % lanes - lax.broadcasted_iota(jnp.int32, (2 * lanes, lanes), 1))
    return jnp.where(near == 0, -90.0, jnp.where(near == 1, 16.0, jnp.where(near == 2, -1.0, 0.0))).astype(jnp.bfloat16)


def along_y(field, z, banded, out):
    rows, lanes = field.shape[1:]
    whole = field[pl.ds(z + 2, BATCH)].reshape(BATCH * rows, lanes)
    high = whole.astype(jnp.bfloat16)
    low = (whole - high.astype(jnp.float32)).astype(jnp.bfloat16)
    out[...] = jnp.dot(jnp.concatenate([high, low], 1), banded[...], preferred_element_type=jnp.float32)


def laps12(field, z, y_part, fetch, finish):
    rows, lanes = field.shape[1:]
    groups = rows // 8
    sub = lax.broadcasted_iota(jnp.int32, (8, lanes), 0)

    def later(block):
        return jnp.where(sub < 7, pltpu.roll(block, 7, 0), 0.0)

    def earlier(block):
        return jnp.where(sub > 0, pltpu.roll(block, 1, 0), 0.0)

    for base in range(0, BATCH, PLANES):
        held = {}

        def tile(j, i):
            if (j, i) not in held:
                if i < 0:
                    held[j, i] = earlier(tile(j, i + groups))
                elif i >= groups:
                    held[j, i] = later(tile(j, i - groups))
                else:
                    held[j, i] = field[z + j + 2, i * 8 : (i + 1) * 8]
            return held[j, i]

        def load(i):
            found = []
            for j in range(base, base + PLANES):
                center = tile(j, i)
                near = (tile(j, i - 1), tile(j, i + 1), tile(j - 1, i), tile(j + 1, i))
                far = (tile(j, i - 2), tile(j, i + 2), tile(j - 2, i), tile(j + 2, i))
                at = (j * groups + i) * 8
                found.append((center, near, far, y_part[at : at + 8], fetch(j, slice(i * 8, i * 8 + 8))))
            return found

        ready = load(0)
        for i in range(groups):
            upcoming = load(i + 1) if i + 1 < groups else None
            for j, (center, near, far, part, extra) in enumerate(ready):
                near = (near[0] + near[1]) + (near[2] + near[3])
                far = (far[0] + far[1]) + (far[2] + far[3])
                finish(base + j, slice(i * 8, i * 8 + 8), center, 16.0 * near + (part - far), extra)
            ready = upcoming


def scatter_kernel(rows_x, cells_ref, observed_ref, out_ref, mark, row_ref, spread):
    _, steps, receivers = observed_ref.shape
    lanes = out_ref.shape[2]
    tile = out_ref.shape[1]
    groups = rows_x // 8

    @pl.when(pl.program_id(0) == 0)
    def _():
        chip = lax.axis_index("chip")
        cells = cells_ref[pl.ds(chip, 1)]
        x = cells // lanes % rows_x
        row_ref[...] = cells // (rows_x * lanes) * rows_x + x % groups * 8 + x // groups
        on_lanes = jnp.concatenate(
            [
                observed_ref[chip],
                jnp.broadcast_to((cells % lanes).astype(jnp.float32), (8, receivers)),
                jnp.zeros((lanes - steps - 8, receivers), jnp.float32),
            ],
            0,
        )
        columns = on_lanes.T
        lane = lax.broadcasted_iota(jnp.int32, (receivers, lanes), 1).astype(jnp.float32)
        at = lane == columns[:, steps : steps + 1]
        for k in range(steps):
            column = columns[:, k : k + 1]
            high = column.astype(jnp.bfloat16).astype(jnp.float32)
            low = column - high
            cols = pl.ds(k * lanes, lanes)
            spread[0:receivers, cols] = jnp.where(at, high, 0.0).astype(jnp.bfloat16)
            spread[receivers:, cols] = jnp.where(at, low, 0.0).astype(jnp.bfloat16)
        cols = pl.ds(steps * lanes, lanes)
        spread[0:receivers, cols] = jnp.where(at, 1.0, 0.0).astype(jnp.bfloat16)
        spread[receivers:, cols] = jnp.zeros((receivers, lanes), jnp.bfloat16)
        mark[...] = jnp.zeros(mark.shape, jnp.float32)

    ids = lax.broadcasted_iota(jnp.int32, (tile, receivers), 0) + pl.program_id(0) * tile
    chosen = jnp.where(ids == row_ref[...], 1.0, 0.0).astype(jnp.bfloat16)
    total = jnp.dot(jnp.concatenate([chosen, chosen], 1), spread[...], preferred_element_type=jnp.float32)
    for k in range(steps + 1):
        out_ref[k] = total[:, k * lanes : (k + 1) * lanes]


def scatter(rec_cells, observed, planes_all, rows_x, rows_y):
    _, steps, receivers = observed.shape
    rows_all = planes_all * rows_x
    tile = 512
    return pl.pallas_call(
        functools.partial(scatter_kernel, rows_x),
        grid=(rows_all // tile,),
        in_specs=[
            pl.BlockSpec((2, receivers), lambda t: (0, 0)),
            pl.BlockSpec((2, steps, receivers), lambda t: (0, 0, 0)),
        ],
        out_specs=[
            pl.BlockSpec((steps + 1, tile, rows_y), lambda t: (0, t, 0)),
            pl.BlockSpec((8, rows_y), lambda t: (0, 0)),
        ],
        out_shape=[
            jax.ShapeDtypeStruct((steps + 1, rows_all, rows_y), jnp.float32),
            jax.ShapeDtypeStruct((8, rows_y), jnp.float32),
        ],
        scratch_shapes=[
            pltpu.VMEM((1, receivers), jnp.int32),
            pltpu.VMEM((2 * receivers, (steps + 1) * rows_y), jnp.bfloat16),
        ],
        compiler_params=pltpu.CompilerParams(vmem_limit_bytes=56 * 2**20),
        cost_estimate=pl.CostEstimate(
            flops=4 * rows_all * receivers * (steps + 1) * rows_y,
            bytes_accessed=4 * (steps + 1) * rows_all * rows_y,
            transcendentals=0,
        ),
        name="receiver_scatter",
    )(rec_cells, observed)


def place(planes):
    chip, core = lax.axis_index("chip"), lax.axis_index("core")
    slabs = (2 * chip + core, 2 * chip + 1 - core, 2 * (1 - chip) + core, 2 * (1 - chip) + 1 - core)
    return chip, core, [slab * planes for slab in slabs]


def load_blocks(slabs, blocks, first, second, factor=None):
    ends, rows, lanes = first.shape
    planes = blocks[0].shape[1]
    for field in (first, second):
        for z in (0, 1, ends - 2, ends - 1):
            field[z] = jnp.zeros((rows, lanes), jnp.float32)
    for slab, block in zip(slabs, blocks):
        for p in range(planes):
            values = block[0, p], block[1, p]
            if factor is not None:
                speed = factor[slab + p]
                values = values[0] * speed, values[1] * speed
            first[slab + p + 2], second[slab + p + 2] = values


BATCH = 4
PLANES = 2


def sweep(core, planes, field, banded, y_first, y_second, work):
    order = [(chip, owned) for owned in (True, False) for chip in (0, 1)]
    parts = (y_first, y_second)

    def first(chip, owned):
        return (2 * chip + (core if owned else 1 - core)) * planes

    along_y(field, first(*order[0]), banded, y_first)
    for owned in (True, False):
        for chip in (0, 1):
            z = first(chip, owned)
            onward = first(1, owned) if chip == 0 else first(0, False)
            for n in range(planes // BATCH):
                last = n == planes // BATCH - 1
                if not last or chip == 0 or owned:
                    along_y(field, onward if last else z + (n + 1) * BATCH, banded, parts[(n + 1) % 2])
                work(z + n * BATCH, parts[n % 2], chip if owned else None, n * BATCH)


def forward_kernel(
    start, sources, own, mate, over, far, c0, c1, c2, c3, placed, laps, history, held, cour, last,
    even, odd, banded, y0, y1, sems, sems_even, sems_odd
):
    planes, rows, lanes = c0.shape
    steps = laps.shape[0]
    groups = rows // 8
    chip_here, core, slabs = place(planes)

    fetches = []
    for k in range(steps + 1):
        for n in range(4):
            at = pl.ds(n * planes, planes)
            fetches.append(pltpu.make_async_copy(placed.at[k, at], held.at[k, at], sems.at[k, n]))
            fetches[-1].start()

    def keep(k, field, done):
        for n in range(4):
            source = field.at[pl.ds(n * planes + 2, planes)]
            yield pltpu.make_async_copy(source, history.at[k, pl.ds(n * planes, planes)], done.at[n])

    banded[...] = band(lanes)
    load_blocks(slabs, (own, mate, over, far), odd, even)
    for slab, block in zip(slabs, (c0, c1, c2, c3)):
        for p in range(planes):
            cour[slab + p] = block[p]

    for index in range(2 * planes):
        z = (2 * (index // planes) + core) * planes + index % planes
        weight = 1.0 + 2.0 * jnp.full((rows, lanes), z, jnp.int32).astype(jnp.float32) / (4 * planes - 1)
        last[index] = weight / (12.0 * cour[z])

    cell = sources[chip_here]
    source_z, x, lane = cell // (rows * lanes), cell // lanes % rows, cell % lanes
    tile = pl.ds(pl.multiple_of(x % groups * 8, 8), 8)
    here = (lax.broadcasted_iota(jnp.int32, (8, lanes), 0) == x // groups) & (
        lax.broadcasted_iota(jnp.int32, (8, lanes), 1) == lane
    )
    source_slab, source_p = source_z // planes, lax.rem(source_z, planes)

    def advance(k, now, then, done):
        @pl.when(k >= 2)
        def _():
            for copy in keep(k - 2, then, done):
                copy.wait()

        def work(z, y_part, chip, p):
            def fetch(j, rows):
                return then[z + j + 2, rows], cour[z + j, rows]

            def finish(j, rows, center, lap, extra):
                old, speed = extra
                if chip is not None:
                    laps[k, p + j, chip, rows] = lap
                then[z + j + 2, rows] = 2.0 * center - old + speed * lap

            laps12(now, z, y_part, fetch, finish)

        cycle = (start[0] + k) % 48
        phase = (jnp.full((8, lanes), cycle, jnp.int32).astype(jnp.float32) - 24.0) / 12.0
        wave = AMPLITUDE * (1.0 - 2.0 * phase * phase) * jnp.exp(-phase * phase)
        strength = jnp.where(here, 12.0 * wave, 0.0)
        moved = cour[source_z, tile, :] * strength

        sweep(core, planes, now, banded, y0, y1, work)

        owned = jnp.where(lax.rem(source_slab, 2) == core, strength, 0.0)
        laps[k, source_p, source_slab // 2, tile, :] += owned
        then[source_z + 2, tile, :] += moved
        for copy in keep(k, then, done):
            copy.start()

    @pl.loop(0, steps // 2)
    def _(pair):
        advance(2 * pair, even, odd, sems_odd)
        advance(2 * pair + 1, odd, even, sems_even)

    for k, field, done in ((steps - 2, odd, sems_odd), (steps - 1, even, sems_even)):
        for copy in keep(k, field, done):
            copy.wait()
    for fetch in fetches:
        fetch.wait()


def inject_kernel(held, history, inject):
    steps, planes_all = history.shape[:2]

    @pl.loop(0, planes_all)
    def _(z):
        count = held[steps, z]
        for k in range(steps):
            inject[k, z] = held[k, z] - count * history[k, z]


def adjoint_kernel(own, mate, over, far, cour, laps, inject, last, keep, send_x, send_y, send_xy, even, odd, total, banded, y0, y1):
    planes, rows, lanes = own.shape[1:]
    steps = laps.shape[0]
    groups = rows // 8
    chip_here, core, slabs = place(planes)
    banded[...] = band(lanes)
    load_blocks(slabs, (own, mate, over, far), odd, even, factor=cour)

    total[...] = jnp.zeros(total.shape, jnp.float32)

    def advance(k, now, then):
        def work(z, y_part, chip, p):
            def fetch(j, rows):
                extra = (then[z + j + 2, rows], cour[z + j, rows], inject[k, z + j, rows])
                if chip is not None:
                    extra += (total[chip * planes + p + j, rows], laps[k, p + j, chip, rows])
                return extra

            def finish(j, rows, center, lap, extra):
                newer = 2.0 * center - extra[0] + extra[1] * (lap - extra[2])
                then[z + j + 2, rows] = newer
                if chip is not None:
                    total[chip * planes + p + j, rows] = extra[3] + newer * extra[4]

            laps12(now, z, y_part, fetch, finish)

        sweep(core, planes, now, banded, y0, y1, work)

    @pl.loop(0, steps // 2)
    def _(pair):
        advance(steps - 1 - 2 * pair, even, odd)
        advance(steps - 2 - 2 * pair, odd, even)

    count = keep.shape[0]
    mine, others = lax.axis_index("shot") % 2 * count, (1 - lax.axis_index("shot") % 2) * count
    here, there = chip_here, 1 - chip_here
    for ref, chip, start in ((keep, here, mine), (send_x, there, mine), (send_y, here, others), (send_xy, there, others)):

        @pl.loop(0, count)
        def _(n):
            p = start + n
            value = total[chip * planes + p] * last[chip * planes + p]
            for i in range(groups):
                ref[n, pl.ds(i, 8, stride=groups), :] = value[i * 8 : (i + 1) * 8]


def square_kernel(mine, by_x, by_y, by_xy, keep, send):
    half = lax.axis_index("shot") // 2 % 2
    count = keep.shape[0]
    for ref, part in ((keep, half), (send, 1 - half)):
        for p in range(count):
            at = part * count + p
            ref[p] = (mine[at] + by_x[at]) + (by_y[at] + by_xy[at])


def add_kernel(mine, other, out):
    out[...] = mine[...] + other[...]


def flip(index, bits):
    result = index
    for bit in (1, 2):
        if bits & bit:
            result = jnp.where(index // bit % 2 == 1, result - bit, result + bit)
    return result


def after_kernel(earlier, value, out):
    out[...] = value[...]


def after(earlier, value):
    vmem, anywhere = pl.BlockSpec(memory_space=pltpu.VMEM), pl.BlockSpec(memory_space=pl.ANY)
    return pl.pallas_call(
        after_kernel,
        in_specs=[anywhere, vmem],
        out_specs=vmem,
        out_shape=jax.ShapeDtypeStruct(value.shape, jnp.float32),
        compiler_params=pltpu.CompilerParams(vmem_limit_bytes=4 * 2**20),
        name="after",
    )(earlier, value)


def arrange_kernel(mine, other, out):
    y = lax.axis_index("shot") % 2
    count = mine.shape[0]
    out[pl.ds(y * count, count)] = mine[...]
    out[pl.ds((1 - y) * count, count)] = other[...]


def first_plane(shot, planes):
    return (shot % 2) * (planes // 2) + (shot // 2 % 2) * (planes // 4)


def sums_kernel(mine, other, momentum, data, sums):
    count, rows, lanes = mine.shape
    planes = momentum.shape[0]
    chip, core = lax.axis_index("chip"), lax.axis_index("core")
    first = first_plane(lax.axis_index("shot"), planes)
    parts = [jnp.zeros((rows, lanes), jnp.float32)] * 4
    for j in range(count):
        scaled = mine[j] + other[j]
        data[j * rows : (j + 1) * rows] = scaled
        z = (2 * chip + core) * planes + first + j
        weight = 1.0 + 2.0 * jnp.full((1, lanes), z, jnp.int32).astype(jnp.float32) / (4 * planes - 1)
        moment = momentum[first + j]
        square = scaled * scaled
        terms = (square, weight * moment * moment, weight * moment * scaled, weight * square)
        parts = [part + term for part, term in zip(parts, terms)]

    def total(value):
        by_lane = jnp.sum(value, axis=0, keepdims=True)
        return jnp.broadcast_to(jnp.sum(by_lane, axis=1, keepdims=True), (1, lanes))

    value = jnp.concatenate([total(part) for part in parts] + [jnp.zeros((4, lanes), jnp.float32)], 0)
    data[count * rows :] = value
    sums[...] = value


def join_kernel(mine, other, s0, s1, s2, data, sums):
    rows = mine.shape[0] - 8
    data[0:rows] = mine[0:rows]
    data[rows : 2 * rows] = other[0:rows]
    value = (s0[...] + s1[...]) + (other[rows:] + s2[...])
    data[2 * rows :] = value
    sums[...] = value


def finish_kernel(mine, other, momentum, s0, s1, s2, out, kinetic):
    planes, rows, lanes = momentum.shape
    cells = 4.0 * planes * rows * lanes
    shot = lax.axis_index("shot")
    sums = (s0[...] + s1[...]) + (other[planes // 2 * rows :] + s2[...])
    factor = lax.rsqrt(sums[0:1] / cells + EPSILON)
    energy = 0.5 * (sums[1:2] - factor * sums[2:3] + 0.25 * factor * factor * sums[3:4]) / cells
    kinetic[0] = energy[0, 0]
    step = 0.5 * factor
    quarter = planes // 4
    for part, group in ((mine, shot), (other, flip(shot, 1))):
        for number, first in enumerate((first_plane(group, planes), first_plane(flip(group, 2), planes))):
            for j in range(quarter):
                at = (number * quarter + j) * rows
                out[first + j] = momentum[first + j] - step * part[at : at + rows]


def local(kernel, outs, *arrays):
    vmem = pl.BlockSpec(memory_space=pltpu.VMEM)
    shapes = [jax.ShapeDtypeStruct(shape, jnp.float32) for shape in outs]
    single = len(outs) == 1
    return pl.pallas_call(
        kernel,
        in_specs=[vmem] * len(arrays),
        out_specs=vmem if single else [vmem] * len(outs),
        out_shape=shapes[0] if single else shapes,
        compiler_params=pltpu.CompilerParams(vmem_limit_bytes=4 * 2**20),
        name=kernel.__name__,
    )(*arrays)


def exchange(value, bits):
    axes = ("shot", "chip", "core")
    return lax.ppermute(value, axes, [(i, i ^ bits) for i in range(lax.axis_size(axes))])


CORE, CHIP, Y, NEAR_Z, FAR_Z = 1, 2, 4, 8, 16


def whole_shards(
    courant_sq, momentum, fwd_prev, fwd_cur, adj_next, adj_cur, observed, src_cells, rec_cells, ckpt_step
):
    _, planes, rows_x, rows_y = fwd_cur.shape
    steps = observed.shape[1]
    planes_all = 4 * planes
    cells_all = planes_all * rows_x * rows_y
    vmem, smem = pl.BlockSpec(memory_space=pltpu.VMEM), pl.BlockSpec(memory_space=pltpu.SMEM)

    hbm = pl.BlockSpec(memory_space=pltpu.HBM)
    outgoing, c0, piece = pl.pallas_call(
        first_kernel,
        in_specs=[hbm] * 3,
        out_specs=[vmem] * 3,
        out_shape=[
            jax.ShapeDtypeStruct((2, planes, rows_x, rows_y), jnp.float32),
            jax.ShapeDtypeStruct(courant_sq.shape, jnp.float32),
            jax.ShapeDtypeStruct((planes // 2, rows_x, rows_y), jnp.float32),
        ],
        scratch_shapes=[
            pltpu.VMEM((2, planes, rows_x, rows_y), jnp.float32),
            pltpu.VMEM(courant_sq.shape, jnp.float32),
            pltpu.SemaphoreType.DMA((3,)),
        ],
        compiler_params=pltpu.CompilerParams(vmem_limit_bytes=63 * 2**20),
        name="first_to_cross",
    )(fwd_prev, fwd_cur, courant_sq)

    over = exchange(outgoing, CHIP)
    piece = exchange(piece, CHIP)

    placed, mark = scatter(rec_cells, observed, planes_all, rows_x, rows_y)
    placed = placed.reshape(steps + 1, planes_all, rows_x, rows_y)

    piece = after(mark, piece)
    adj_outgoing, adj_own, own = pick(
        (adj_next, adj_cur, True), (adj_next, adj_cur, False), (fwd_prev, fwd_cur, False), earlier=piece
    )
    mate = exchange(own, CORE)
    c2 = local(arrange_kernel, [courant_sq.shape], piece, exchange(piece, Y))
    c1, c3 = exchange(c0, CORE), exchange(c2, CORE)
    over = after(c2, over)
    far = exchange(over, CORE)
    adj_over = exchange(adj_outgoing, CHIP)
    adj_mate = exchange(adj_own, CORE)

    scratch = pltpu.VMEM((planes_all + 4, rows_x, rows_y), jnp.float32)
    y_scratch = pltpu.VMEM((BATCH * rows_x, rows_y), jnp.float32)
    step_scratch = [scratch, scratch, pltpu.VMEM((2 * rows_y, rows_y), jnp.bfloat16), y_scratch, y_scratch]
    params = pltpu.CompilerParams(vmem_limit_bytes=6 * 2**20)
    cost = pl.CostEstimate(flops=30 * steps * cells_all, bytes_accessed=16 * steps * cells_all, transcendentals=0)
    laps, history, held, cour, last = pl.pallas_call(
        forward_kernel,
        in_specs=[smem, smem] + [vmem] * 8 + [pl.BlockSpec(memory_space=pltpu.HBM)],
        out_specs=[vmem] * 5,
        out_shape=[
            jax.ShapeDtypeStruct((steps, planes, 2, rows_x, rows_y), jnp.float32),
            jax.ShapeDtypeStruct((steps, planes_all, rows_x, rows_y), jnp.float32),
            jax.ShapeDtypeStruct((steps + 1, planes_all, rows_x, rows_y), jnp.float32),
            jax.ShapeDtypeStruct((planes_all, rows_x, rows_y), jnp.float32),
            jax.ShapeDtypeStruct((2 * planes, rows_x, rows_y), jnp.float32),
        ],
        scratch_shapes=step_scratch
        + [
            pltpu.SemaphoreType.DMA((steps + 1, 4)),
            pltpu.SemaphoreType.DMA((4,)),
            pltpu.SemaphoreType.DMA((4,)),
        ],
        compiler_params=pltpu.CompilerParams(vmem_limit_bytes=30 * 2**20),
        cost_estimate=pl.CostEstimate(flops=1000, bytes_accessed=1000, transcendentals=0),
        name="forward_steps",
    )(ckpt_step[None], src_cells, own, mate, over, far, c0, c1, c2, c3, placed)

    adj_over = after(laps, adj_over)
    adj_far = exchange(adj_over, CORE)
    inject = pl.pallas_call(
        inject_kernel,
        in_specs=[vmem] * 2,
        out_specs=vmem,
        out_shape=jax.ShapeDtypeStruct(history.shape, jnp.float32),
        compiler_params=pltpu.CompilerParams(vmem_limit_bytes=4 * 2**20),
        name="inject",
    )(held, history)
    slab = jax.ShapeDtypeStruct(courant_sq.shape, jnp.float32)
    half, quarter = (planes // 2, rows_x, rows_y), (planes // 4, rows_x, rows_y)
    keep, send_x, send_y, send_xy = pl.pallas_call(
        adjoint_kernel,
        in_specs=[vmem] * 8,
        out_specs=[vmem] * 4,
        out_shape=[jax.ShapeDtypeStruct(half, jnp.float32)] * 4,
        scratch_shapes=step_scratch[:2] + [pltpu.VMEM((2 * planes, rows_x, rows_y), jnp.float32)] + step_scratch[2:],
        compiler_params=params,
        cost_estimate=cost,
        name="adjoint_steps",
    )(adj_own, adj_mate, adj_over, adj_far, cour, laps, inject, last)

    by_xy, by_x, by_y = exchange(send_xy, CHIP + Y), exchange(send_x, CHIP), exchange(send_y, Y)
    keep, send = local(square_kernel, [quarter] * 2, keep, by_x, by_y, by_xy)
    part = local(add_kernel, [quarter], keep, exchange(send, NEAR_Z))
    rows, sums_shape = planes // 4 * rows_x, (8, rows_y)
    data, sums = local(sums_kernel, [(rows + 8, rows_y), sums_shape], part, exchange(part, FAR_Z), momentum)

    received = exchange(data, NEAR_Z)
    others = [exchange(sums, CORE), exchange(sums, NEAR_Z + CORE)]
    data, sums = local(join_kernel, [(2 * rows + 8, rows_y), sums_shape], data, received, sums, *others)
    received = exchange(data, Y)
    others = [exchange(sums, CHIP), exchange(sums, Y + CHIP)]
    momentum_half, kinetic = pl.pallas_call(
        finish_kernel,
        in_specs=[vmem] * 6,
        out_specs=[vmem, smem],
        out_shape=[jax.ShapeDtypeStruct(momentum.shape, jnp.float32), jax.ShapeDtypeStruct((1,), jnp.float32)],
        compiler_params=pltpu.CompilerParams(vmem_limit_bytes=4 * 2**20),
        name="finish",
    )(data, received, momentum, sums, *others)
    return momentum_half, kinetic[0]


def solution(mesh):
    shots, slabs = mesh.shape["shot"], mesh.shape["depth"]

    def placed(depth):
        field = P("shot", depth, None, None)
        slab = P(depth, None, None)
        inputs = (slab, slab, field, field, field, field, P("shot", None, None), P("shot"), P("shot", None), P())
        return dict(in_specs=inputs, out_specs=(slab, P()), check_vma=False)

    slab_plan = jax.shard_map(slab_shards, mesh=mesh, **placed("depth"))
    if slabs != 4 or shots != 8:
        return slab_plan
    chips = Mesh(mesh.devices.reshape(shots, 2, 2), ("shot", "chip", "core"))
    whole_plan = jax.shard_map(whole_shards, mesh=chips, **placed(("chip", "core")))

    def run(courant_sq, momentum, fwd_prev, *rest):
        total, planes, rows_x, rows_y = fwd_prev.shape
        steps = rest[3].shape[1]
        fits = total == 2 * shots and planes == 4 * shots and rows_y == 128 and rows_x % 16 == 0 and steps % 2 == 0
        plan = whole_plan if fits else slab_plan
        return plan(courant_sq, momentum, fwd_prev, *rest)

    return run
```

```python
import functools

import jax
import jax.numpy as jnp
from jax import lax
from jax.experimental import pallas as pl
from jax.experimental.pallas import tpu as pltpu
from jax.sharding import Mesh
from jax.sharding import PartitionSpec as P

CENTER = -2.5
NEAR = 4.0 / 3.0
FAR = -1.0 / 12.0
AMPLITUDE = 100.0
EPSILON = 1e-06


def with_halo(value, sides, width):
    for axis, dim in sides:
        size, length = (lax.axis_size(axis), value.shape[dim])
        up = [(i, (i + 1) % size) for i in range(size - 1)]
        down = [(j, i) for i, j in up]
        last = lax.slice_in_dim(value, length - width, length, axis=dim)
        leading = lax.slice_in_dim(value, 0, width, axis=dim)
        before = lax.ppermute(last, axis, up)
        after = lax.ppermute(leading, axis, down)
        value = jnp.concatenate([before, value, after], axis=dim)
    return value


def laplace(padded):
    lateral = jnp.pad(padded[:, 2:-2], ((0, 0), (0, 0), (2, 2), (2, 2)))
    center = padded[:, 2:-2]
    along_z = NEAR * (padded[:, 1:-3] + padded[:, 3:-1]) + FAR * (padded[:, :-4] + padded[:, 4:])
    along_x = NEAR * (lateral[:, :, 1:-3, 2:-2] + lateral[:, :, 3:-1, 2:-2]) + FAR * (
        lateral[:, :, :-4, 2:-2] + lateral[:, :, 4:, 2:-2]
    )
    along_y = NEAR * (lateral[:, :, 2:-2, 1:-3] + lateral[:, :, 2:-2, 3:-1]) + FAR * (
        lateral[:, :, 2:-2, :-4] + lateral[:, :, 2:-2, 4:]
    )
    return 3.0 * CENTER * center + along_z + along_x + along_y


def locate(field, cell_ids, first_plane):
    shot_count, planes, rows_x, rows_y = field.shape
    plane_cells = rows_x * rows_y
    local_index = cell_ids - first_plane * plane_cells
    inside = (local_index >= 0) & (local_index < planes * plane_cells)
    target = jnp.where(inside, local_index, 0)
    return (inside, target)


def inject(field, cell_ids, values, first_plane):
    shot_count = field.shape[0]
    inside, target = locate(field, cell_ids, first_plane)
    amount = jnp.where(inside, values, jnp.zeros_like(values))
    flattened = field.reshape(shot_count, -1)
    lanes = jnp.arange(shot_count)[:, None]
    flattened = flattened.at[lanes, target].add(amount)
    return flattened.reshape(field.shape)


def sample(field, cell_ids, first_plane):
    shot_count = field.shape[0]
    inside, target = locate(field, cell_ids, first_plane)
    values = jnp.take_along_axis(field.reshape(shot_count, -1), target, axis=1)
    return jnp.where(inside, values, jnp.zeros_like(values))


def wave_value(start, step):
    cycle = jnp.mod(start + jnp.int32(step), jnp.int32(48))
    phase = (cycle.astype(jnp.float32) - 24.0) / 12.0
    return AMPLITUDE * (1.0 - 2.0 * phase * phase) * jnp.exp(-phase * phase)


def statistics(scaled, moment, weight, cells_all):
    grand_total = lax.psum(jnp.sum(scaled * scaled), ("shot", "depth"))
    factor = lax.rsqrt(grand_total / cells_all + EPSILON)
    halfway = moment - 0.5 * factor * scaled
    energy = lax.psum(jnp.sum(weight * halfway * halfway), ("shot", "depth"))
    return (factor, 0.5 * energy / cells_all)


def slab_shards(
    courant_sq,
    momentum,
    fwd_prev,
    fwd_cur,
    adj_next,
    adj_cur,
    observed,
    src_cells,
    rec_cells,
    ckpt_step,
):
    shot_count, planes, rows_x, rows_y = fwd_cur.shape
    steps_all = observed.shape[1]
    first_plane = lax.axis_index("depth") * planes
    total_planes = planes * lax.axis_size("depth")
    cells_all = total_planes * rows_x * rows_y
    sources = src_cells[:, None]
    older, current = (fwd_prev, fwd_cur)
    laplacians = []
    misfits = []
    for step in range(steps_all):
        padded = with_halo(current, (("depth", 1),), 2)
        strength = jnp.full(sources.shape, wave_value(ckpt_step, step), jnp.float32)
        laplacian = inject(laplace(padded), sources, strength, first_plane)
        newer = 2.0 * current - older + courant_sq * laplacian
        misfits.append(sample(newer, rec_cells, first_plane) - observed[:, step, :])
        laplacians.append(laplacian)
        older, current = (current, newer)
    adj_later, adj_now = (adj_next, adj_cur)
    gradient = jnp.zeros((planes, rows_x, rows_y), jnp.float32)
    for step in reversed(range(steps_all)):
        padded = with_halo(courant_sq * adj_now, (("depth", 1),), 2)
        adj_new = 2.0 * adj_now - adj_later + laplace(padded)
        adj_new = inject(adj_new, rec_cells, misfits[step], first_plane)
        gradient = gradient + jnp.sum(adj_new * laplacians[step], axis=0)
        adj_later, adj_now = (adj_now, adj_new)
    depths = (first_plane + jnp.arange(planes)).astype(jnp.float32)
    weight = (1.0 + 2.0 * depths / (total_planes - 1))[:, None, None]
    share_rows = rows_x // lax.axis_size("shot")
    offset = lax.axis_index("shot") * share_rows
    moment_share = lax.dynamic_slice_in_dim(momentum, offset, share_rows, 1)
    gradient = lax.psum(gradient, "shot")
    scaled = weight * gradient
    scaled_share = lax.dynamic_slice_in_dim(scaled, offset, share_rows, 1)
    factor, kinetic = statistics(scaled_share, moment_share, weight, cells_all)
    momentum_half = momentum - 0.5 * factor * scaled
    return (momentum_half, kinetic)


def interleave(dst, slab, src, factor=None):
    planes, rows = src.shape[0], src.shape[1]
    groups = rows // 8

    @pl.loop(0, planes)
    def _(p):
        for i in range(groups):
            value = src[p, pl.ds(i, 8, stride=groups), :]
            if factor is not None:
                value = value * factor
            dst[(*slab, p, pl.ds(i * 8, 8), slice(None))] = value


def pick_kernel(across, *refs):
    count = len(across)
    fields, outs, (held, sems) = refs[: 2 * count], refs[2 * count : 3 * count], refs[3 * count :]
    chip = lax.axis_index("chip")
    copies = []
    for n in range(2 * count):
        shot = 1 - chip if across[n // 2] else chip
        copies.append(pltpu.make_async_copy(fields[n].at[shot], held.at[n], sems.at[n]))
        copies[-1].start()
    for n in range(2 * count):
        copies[n].wait()
        interleave(outs[n // 2], (n % 2,), held.at[n])


def pick(*pairs, earlier):
    plain = functools.partial(pick_kernel, tuple(pair[2] for pair in pairs))
    fields = [field for pair in pairs for field in pair[:2]]
    shape = fields[0].shape[1:]
    vmem, hbm = pl.BlockSpec(memory_space=pltpu.VMEM), pl.BlockSpec(memory_space=pltpu.HBM)
    return pl.pallas_call(
        lambda earlier, *refs: plain(*refs),
        in_specs=[pl.BlockSpec(memory_space=pl.ANY)] + [hbm] * len(fields),
        out_specs=[vmem] * len(pairs),
        out_shape=[jax.ShapeDtypeStruct((2, *shape), jnp.float32)] * len(pairs),
        scratch_shapes=[pltpu.VMEM((len(fields), *shape), jnp.float32), pltpu.SemaphoreType.DMA((len(fields),))],
        compiler_params=pltpu.CompilerParams(vmem_limit_bytes=4 * 2**20),
        name="pick",
    )(earlier, *fields)


def first_kernel(first, second, courant, outgoing, whole, piece, held, held_courant, sems):
    shot = 1 - lax.axis_index("chip")
    copies = [
        pltpu.make_async_copy(first.at[shot], held.at[0], sems.at[0]),
        pltpu.make_async_copy(second.at[shot], held.at[1], sems.at[1]),
        pltpu.make_async_copy(courant, held_courant, sems.at[2]),
    ]
    for copy in copies:
        copy.start()
    for n in range(2):
        copies[n].wait()
        interleave(outgoing, (n,), held.at[n])
    copies[2].wait()
    interleave(whole, (), held_courant, 1.0 / 12.0)
    count = piece.shape[0]
    piece[...] = whole[pl.ds(lax.axis_index("shot") % 2 * count, count)]


def band(lanes):
    near = jnp.abs(lax.broadcasted_iota(jnp.int32, (2 * lanes, lanes), 0) % lanes - lax.broadcasted_iota(jnp.int32, (2 * lanes, lanes), 1))
    return jnp.where(near == 0, -90.0, jnp.where(near == 1, 16.0, jnp.where(near == 2, -1.0, 0.0))).astype(jnp.bfloat16)


def along_y(field, z, banded, out):
    rows, lanes = field.shape[1:]
    whole = field[pl.ds(z + 2, BATCH)].reshape(BATCH * rows, lanes)
    high = whole.astype(jnp.bfloat16)
    low = (whole - high.astype(jnp.float32)).astype(jnp.bfloat16)
    out[...] = jnp.dot(jnp.concatenate([high, low], 1), banded[...], preferred_element_type=jnp.float32)


def laps12(field, z, y_part, fetch, finish):
    rows, lanes = field.shape[1:]
    groups = rows // 8
    sub = lax.broadcasted_iota(jnp.int32, (8, lanes), 0)

    def later(block):
        return jnp.where(sub < 7, pltpu.roll(block, 7, 0), 0.0)

    def earlier(block):
        return jnp.where(sub > 0, pltpu.roll(block, 1, 0), 0.0)

    for base in range(0, BATCH, PLANES):
        held = {}

        def tile(j, i):
            if (j, i) not in held:
                if i < 0:
                    held[j, i] = earlier(tile(j, i + groups))
                elif i >= groups:
                    held[j, i] = later(tile(j, i - groups))
                else:
                    held[j, i] = field[z + j + 2, i * 8 : (i + 1) * 8]
            return held[j, i]

        def load(i):
            found = []
            for j in range(base, base + PLANES):
                center = tile(j, i)
                near = (tile(j, i - 1), tile(j, i + 1), tile(j - 1, i), tile(j + 1, i))
                far = (tile(j, i - 2), tile(j, i + 2), tile(j - 2, i), tile(j + 2, i))
                at = (j * groups + i) * 8
                found.append((center, near, far, y_part[at : at + 8], fetch(j, slice(i * 8, i * 8 + 8))))
            return found

        ready = load(0)
        for i in range(groups):
            upcoming = load(i + 1) if i + 1 < groups else None
            for j, (center, near, far, part, extra) in enumerate(ready):
                near = (near[0] + near[1]) + (near[2] + near[3])
                far = (far[0] + far[1]) + (far[2] + far[3])
                finish(base + j, slice(i * 8, i * 8 + 8), center, 16.0 * near + (part - far), extra)
            ready = upcoming


def scatter_kernel(rows_x, cells_ref, observed_ref, out_ref, mark, row_ref, spread):
    _, steps, receivers = observed_ref.shape
    lanes = out_ref.shape[2]
    tile = out_ref.shape[1]
    groups = rows_x // 8

    @pl.when(pl.program_id(0) == 0)
    def _():
        chip = lax.axis_index("chip")
        cells = cells_ref[pl.ds(chip, 1)]
        x = cells // lanes % rows_x
        row_ref[...] = cells // (rows_x * lanes) * rows_x + x % groups * 8 + x // groups
        on_lanes = jnp.concatenate(
            [
                observed_ref[chip],
                jnp.broadcast_to((cells % lanes).astype(jnp.float32), (8, receivers)),
                jnp.zeros((lanes - steps - 8, receivers), jnp.float32),
            ],
            0,
        )
        columns = on_lanes.T
        lane = lax.broadcasted_iota(jnp.int32, (receivers, lanes), 1).astype(jnp.float32)
        at = lane == columns[:, steps : steps + 1]
        for k in range(steps):
            column = columns[:, k : k + 1]
            high = column.astype(jnp.bfloat16).astype(jnp.float32)
            low = column - high
            cols = pl.ds(k * lanes, lanes)
            spread[0:receivers, cols] = jnp.where(at, high, 0.0).astype(jnp.bfloat16)
            spread[receivers:, cols] = jnp.where(at, low, 0.0).astype(jnp.bfloat16)
        cols = pl.ds(steps * lanes, lanes)
        spread[0:receivers, cols] = jnp.where(at, 1.0, 0.0).astype(jnp.bfloat16)
        spread[receivers:, cols] = jnp.zeros((receivers, lanes), jnp.bfloat16)
        mark[...] = jnp.zeros(mark.shape, jnp.float32)

    ids = lax.broadcasted_iota(jnp.int32, (tile, receivers), 0) + pl.program_id(0) * tile
    chosen = jnp.where(ids == row_ref[...], 1.0, 0.0).astype(jnp.bfloat16)
    total = jnp.dot(jnp.concatenate([chosen, chosen], 1), spread[...], preferred_element_type=jnp.float32)
    for k in range(steps + 1):
        out_ref[k] = total[:, k * lanes : (k + 1) * lanes]


def scatter(rec_cells, observed, planes_all, rows_x, rows_y):
    _, steps, receivers = observed.shape
    rows_all = planes_all * rows_x
    tile = 512
    return pl.pallas_call(
        functools.partial(scatter_kernel, rows_x),
        grid=(rows_all // tile,),
        in_specs=[
            pl.BlockSpec((2, receivers), lambda t: (0, 0)),
            pl.BlockSpec((2, steps, receivers), lambda t: (0, 0, 0)),
        ],
        out_specs=[
            pl.BlockSpec((steps + 1, tile, rows_y), lambda t: (0, t, 0)),
            pl.BlockSpec((8, rows_y), lambda t: (0, 0)),
        ],
        out_shape=[
            jax.ShapeDtypeStruct((steps + 1, rows_all, rows_y), jnp.float32),
            jax.ShapeDtypeStruct((8, rows_y), jnp.float32),
        ],
        scratch_shapes=[
            pltpu.VMEM((1, receivers), jnp.int32),
            pltpu.VMEM((2 * receivers, (steps + 1) * rows_y), jnp.bfloat16),
        ],
        compiler_params=pltpu.CompilerParams(vmem_limit_bytes=56 * 2**20),
        cost_estimate=pl.CostEstimate(
            flops=4 * rows_all * receivers * (steps + 1) * rows_y,
            bytes_accessed=4 * (steps + 1) * rows_all * rows_y,
            transcendentals=0,
        ),
        name="receiver_scatter",
    )(rec_cells, observed)


def place(planes):
    chip, core = lax.axis_index("chip"), lax.axis_index("core")
    slabs = (2 * chip + core, 2 * chip + 1 - core, 2 * (1 - chip) + core, 2 * (1 - chip) + 1 - core)
    return chip, core, [slab * planes for slab in slabs]


def load_blocks(slabs, blocks, first, second, factor=None):
    ends, rows, lanes = first.shape
    planes = blocks[0].shape[1]
    for field in (first, second):
        for z in (0, 1, ends - 2, ends - 1):
            field[z] = jnp.zeros((rows, lanes), jnp.float32)
    for slab, block in zip(slabs, blocks):
        for p in range(planes):
            values = block[0, p], block[1, p]
            if factor is not None:
                speed = factor[slab + p]
                values = values[0] * speed, values[1] * speed
            first[slab + p + 2], second[slab + p + 2] = values


BATCH = 4
PLANES = 2


def sweep(core, planes, field, banded, y_first, y_second, work):
    order = [(chip, owned) for owned in (True, False) for chip in (0, 1)]
    parts = (y_first, y_second)

    def first(chip, owned):
        return (2 * chip + (core if owned else 1 - core)) * planes

    along_y(field, first(*order[0]), banded, y_first)
    for owned in (True, False):
        for chip in (0, 1):
            z = first(chip, owned)
            onward = first(1, owned) if chip == 0 else first(0, False)
            for n in range(planes // BATCH):
                last = n == planes // BATCH - 1
                if not last or chip == 0 or owned:
                    along_y(field, onward if last else z + (n + 1) * BATCH, banded, parts[(n + 1) % 2])
                work(z + n * BATCH, parts[n % 2], chip if owned else None, n * BATCH)


def forward_kernel(
    start, sources, own, mate, over, far, c0, c1, c2, c3, laps, history, cour, last,
    even, odd, banded, y0, y1, sems_even, sems_odd
):
    planes, rows, lanes = c0.shape
    steps = laps.shape[0]
    groups = rows // 8
    chip_here, core, slabs = place(planes)

    def keep(k, field, done):
        for n in range(4):
            source = field.at[pl.ds(n * planes + 2, planes)]
            yield pltpu.make_async_copy(source, history.at[k, pl.ds(n * planes, planes)], done.at[n])

    banded[...] = band(lanes)
    load_blocks(slabs, (own, mate, over, far), odd, even)
    for slab, block in zip(slabs, (c0, c1, c2, c3)):
        for p in range(planes):
            cour[slab + p] = block[p]

    for index in range(2 * planes):
        z = (2 * (index // planes) + core) * planes + index % planes
        weight = 1.0 + 2.0 * jnp.full((rows, lanes), z, jnp.int32).astype(jnp.float32) / (4 * planes - 1)
        last[index] = weight / (12.0 * cour[z])

    cell = sources[chip_here]
    source_z, x, lane = cell // (rows * lanes), cell // lanes % rows, cell % lanes
    tile = pl.ds(pl.multiple_of(x % groups * 8, 8), 8)
    here = (lax.broadcasted_iota(jnp.int32, (8, lanes), 0) == x // groups) & (
        lax.broadcasted_iota(jnp.int32, (8, lanes), 1) == lane
    )
    source_slab, source_p = source_z // planes, lax.rem(source_z, planes)

    def advance(k, now, then, done):
        @pl.when(k >= 2)
        def _():
            for copy in keep(k - 2, then, done):
                copy.wait()

        def work(z, y_part, chip, p):
            def fetch(j, rows):
                return then[z + j + 2, rows], cour[z + j, rows]

            def finish(j, rows, center, lap, extra):
                old, speed = extra
                if chip is not None:
                    laps[k, p + j, chip, rows] = lap
                then[z + j + 2, rows] = 2.0 * center - old + speed * lap

            laps12(now, z, y_part, fetch, finish)

        cycle = (start[0] + k) % 48
        phase = (jnp.full((8, lanes), cycle, jnp.int32).astype(jnp.float32) - 24.0) / 12.0
        wave = AMPLITUDE * (1.0 - 2.0 * phase * phase) * jnp.exp(-phase * phase)
        strength = jnp.where(here, 12.0 * wave, 0.0)
        moved = cour[source_z, tile, :] * strength

        sweep(core, planes, now, banded, y0, y1, work)

        owned = jnp.where(lax.rem(source_slab, 2) == core, strength, 0.0)
        laps[k, source_p, source_slab // 2, tile, :] += owned
        then[source_z + 2, tile, :] += moved
        for copy in keep(k, then, done):
            copy.start()

    @pl.loop(0, steps // 2)
    def _(pair):
        advance(2 * pair, even, odd, sems_odd)
        advance(2 * pair + 1, odd, even, sems_even)

    for k, field, done in ((steps - 2, odd, sems_odd), (steps - 1, even, sems_even)):
        for copy in keep(k, field, done):
            copy.wait()


def inject_kernel(placed, history, inject):
    steps, planes_all = history.shape[:2]

    @pl.loop(0, planes_all)
    def _(z):
        count = placed[steps, z]
        for k in range(steps):
            inject[k, z] = placed[k, z] - count * history[k, z]


def adjoint_kernel(own, mate, over, far, cour, laps, inject, last, keep, send_x, send_y, send_xy, even, odd, total, banded, y0, y1):
    planes, rows, lanes = own.shape[1:]
    steps = laps.shape[0]
    groups = rows // 8
    chip_here, core, slabs = place(planes)
    banded[...] = band(lanes)
    load_blocks(slabs, (own, mate, over, far), odd, even, factor=cour)

    total[...] = jnp.zeros(total.shape, jnp.float32)

    def advance(k, now, then):
        def work(z, y_part, chip, p):
            def fetch(j, rows):
                extra = (then[z + j + 2, rows], cour[z + j, rows], inject[k, z + j, rows])
                if chip is not None:
                    extra += (total[chip * planes + p + j, rows], laps[k, p + j, chip, rows])
                return extra

            def finish(j, rows, center, lap, extra):
                newer = 2.0 * center - extra[0] + extra[1] * (lap - extra[2])
                then[z + j + 2, rows] = newer
                if chip is not None:
                    total[chip * planes + p + j, rows] = extra[3] + newer * extra[4]

            laps12(now, z, y_part, fetch, finish)

        sweep(core, planes, now, banded, y0, y1, work)

    @pl.loop(0, steps // 2)
    def _(pair):
        advance(steps - 1 - 2 * pair, even, odd)
        advance(steps - 2 - 2 * pair, odd, even)

    count = keep.shape[0]
    mine, others = lax.axis_index("shot") % 2 * count, (1 - lax.axis_index("shot") % 2) * count
    here, there = chip_here, 1 - chip_here
    for ref, chip, start in ((keep, here, mine), (send_x, there, mine), (send_y, here, others), (send_xy, there, others)):

        @pl.loop(0, count)
        def _(n):
            p = start + n
            value = total[chip * planes + p] * last[chip * planes + p]
            for i in range(groups):
                ref[n, pl.ds(i, 8, stride=groups), :] = value[i * 8 : (i + 1) * 8]


def square_kernel(mine, by_x, by_y, by_xy, keep, send):
    half = lax.axis_index("shot") // 2 % 2
    count = keep.shape[0]
    for ref, part in ((keep, half), (send, 1 - half)):
        for p in range(count):
            at = part * count + p
            ref[p] = (mine[at] + by_x[at]) + (by_y[at] + by_xy[at])


def add_kernel(mine, other, out):
    out[...] = mine[...] + other[...]


def flip(index, bits):
    result = index
    for bit in (1, 2):
        if bits & bit:
            result = jnp.where(index // bit % 2 == 1, result - bit, result + bit)
    return result


def after_kernel(earlier, value, out):
    out[...] = value[...]


def after(earlier, value):
    vmem, anywhere = pl.BlockSpec(memory_space=pltpu.VMEM), pl.BlockSpec(memory_space=pl.ANY)
    return pl.pallas_call(
        after_kernel,
        in_specs=[anywhere, vmem],
        out_specs=vmem,
        out_shape=jax.ShapeDtypeStruct(value.shape, jnp.float32),
        compiler_params=pltpu.CompilerParams(vmem_limit_bytes=4 * 2**20),
        name="after",
    )(earlier, value)


def arrange_kernel(mine, other, out):
    y = lax.axis_index("shot") % 2
    count = mine.shape[0]
    out[pl.ds(y * count, count)] = mine[...]
    out[pl.ds((1 - y) * count, count)] = other[...]


def first_plane(shot, planes):
    return (shot % 2) * (planes // 2) + (shot // 2 % 2) * (planes // 4)


def sums_kernel(mine, other, momentum, data, sums):
    count, rows, lanes = mine.shape
    planes = momentum.shape[0]
    chip, core = lax.axis_index("chip"), lax.axis_index("core")
    first = first_plane(lax.axis_index("shot"), planes)
    parts = [jnp.zeros((rows, lanes), jnp.float32)] * 4
    for j in range(count):
        scaled = mine[j] + other[j]
        data[j * rows : (j + 1) * rows] = scaled
        z = (2 * chip + core) * planes + first + j
        weight = 1.0 + 2.0 * jnp.full((1, lanes), z, jnp.int32).astype(jnp.float32) / (4 * planes - 1)
        moment = momentum[first + j]
        square = scaled * scaled
        terms = (square, weight * moment * moment, weight * moment * scaled, weight * square)
        parts = [part + term for part, term in zip(parts, terms)]

    def total(value):
        by_lane = jnp.sum(value, axis=0, keepdims=True)
        return jnp.broadcast_to(jnp.sum(by_lane, axis=1, keepdims=True), (1, lanes))

    value = jnp.concatenate([total(part) for part in parts] + [jnp.zeros((4, lanes), jnp.float32)], 0)
    data[count * rows :] = value
    sums[...] = value


def join_kernel(mine, other, s0, s1, s2, data, sums):
    rows = mine.shape[0] - 8
    data[0:rows] = mine[0:rows]
    data[rows : 2 * rows] = other[0:rows]
    value = (s0[...] + s1[...]) + (other[rows:] + s2[...])
    data[2 * rows :] = value
    sums[...] = value


def finish_kernel(mine, other, momentum, s0, s1, s2, out, kinetic):
    planes, rows, lanes = momentum.shape
    cells = 4.0 * planes * rows * lanes
    shot = lax.axis_index("shot")
    sums = (s0[...] + s1[...]) + (other[planes // 2 * rows :] + s2[...])
    factor = lax.rsqrt(sums[0:1] / cells + EPSILON)
    energy = 0.5 * (sums[1:2] - factor * sums[2:3] + 0.25 * factor * factor * sums[3:4]) / cells
    kinetic[0] = energy[0, 0]
    step = 0.5 * factor
    quarter = planes // 4
    for part, group in ((mine, shot), (other, flip(shot, 1))):
        for number, first in enumerate((first_plane(group, planes), first_plane(flip(group, 2), planes))):
            for j in range(quarter):
                at = (number * quarter + j) * rows
                out[first + j] = momentum[first + j] - step * part[at : at + rows]


def local(kernel, outs, *arrays):
    vmem = pl.BlockSpec(memory_space=pltpu.VMEM)
    shapes = [jax.ShapeDtypeStruct(shape, jnp.float32) for shape in outs]
    single = len(outs) == 1
    return pl.pallas_call(
        kernel,
        in_specs=[vmem] * len(arrays),
        out_specs=vmem if single else [vmem] * len(outs),
        out_shape=shapes[0] if single else shapes,
        compiler_params=pltpu.CompilerParams(vmem_limit_bytes=4 * 2**20),
        name=kernel.__name__,
    )(*arrays)


def exchange(value, bits):
    axes = ("shot", "chip", "core")
    return lax.ppermute(value, axes, [(i, i ^ bits) for i in range(lax.axis_size(axes))])


CORE, CHIP, Y, NEAR_Z, FAR_Z = 1, 2, 4, 8, 16


def whole_shards(
    courant_sq, momentum, fwd_prev, fwd_cur, adj_next, adj_cur, observed, src_cells, rec_cells, ckpt_step
):
    _, planes, rows_x, rows_y = fwd_cur.shape
    steps = observed.shape[1]
    planes_all = 4 * planes
    cells_all = planes_all * rows_x * rows_y
    vmem, smem = pl.BlockSpec(memory_space=pltpu.VMEM), pl.BlockSpec(memory_space=pltpu.SMEM)

    hbm = pl.BlockSpec(memory_space=pltpu.HBM)
    outgoing, c0, piece = pl.pallas_call(
        first_kernel,
        in_specs=[hbm] * 3,
        out_specs=[vmem] * 3,
        out_shape=[
            jax.ShapeDtypeStruct((2, planes, rows_x, rows_y), jnp.float32),
            jax.ShapeDtypeStruct(courant_sq.shape, jnp.float32),
            jax.ShapeDtypeStruct((planes // 2, rows_x, rows_y), jnp.float32),
        ],
        scratch_shapes=[
            pltpu.VMEM((2, planes, rows_x, rows_y), jnp.float32),
            pltpu.VMEM(courant_sq.shape, jnp.float32),
            pltpu.SemaphoreType.DMA((3,)),
        ],
        compiler_params=pltpu.CompilerParams(vmem_limit_bytes=63 * 2**20),
        name="first_to_cross",
    )(fwd_prev, fwd_cur, courant_sq)

    over = exchange(outgoing, CHIP)
    piece = exchange(piece, CHIP)

    placed, mark = scatter(rec_cells, observed, planes_all, rows_x, rows_y)
    placed = placed.reshape(steps + 1, planes_all, rows_x, rows_y)

    piece = after(mark, piece)
    adj_outgoing, adj_own, own = pick(
        (adj_next, adj_cur, True), (adj_next, adj_cur, False), (fwd_prev, fwd_cur, False), earlier=piece
    )
    mate = exchange(own, CORE)
    c2 = local(arrange_kernel, [courant_sq.shape], piece, exchange(piece, Y))
    c1, c3 = exchange(c0, CORE), exchange(c2, CORE)
    over = after(c2, over)
    far = exchange(over, CORE)
    adj_over = exchange(adj_outgoing, CHIP)
    adj_mate = exchange(adj_own, CORE)

    scratch = pltpu.VMEM((planes_all + 4, rows_x, rows_y), jnp.float32)
    y_scratch = pltpu.VMEM((BATCH * rows_x, rows_y), jnp.float32)
    step_scratch = [scratch, scratch, pltpu.VMEM((2 * rows_y, rows_y), jnp.bfloat16), y_scratch, y_scratch]
    params = pltpu.CompilerParams(vmem_limit_bytes=6 * 2**20)
    cost = pl.CostEstimate(flops=30 * steps * cells_all, bytes_accessed=16 * steps * cells_all, transcendentals=0)
    laps, history, cour, last = pl.pallas_call(
        forward_kernel,
        in_specs=[smem, smem] + [vmem] * 8,
        out_specs=[vmem] * 4,
        out_shape=[
            jax.ShapeDtypeStruct((steps, planes, 2, rows_x, rows_y), jnp.float32),
            jax.ShapeDtypeStruct((steps, planes_all, rows_x, rows_y), jnp.float32),
            jax.ShapeDtypeStruct((planes_all, rows_x, rows_y), jnp.float32),
            jax.ShapeDtypeStruct((2 * planes, rows_x, rows_y), jnp.float32),
        ],
        scratch_shapes=step_scratch
        + [
            pltpu.SemaphoreType.DMA((4,)),
            pltpu.SemaphoreType.DMA((4,)),
        ],
        compiler_params=pltpu.CompilerParams(vmem_limit_bytes=8 * 2**20),
        cost_estimate=pl.CostEstimate(flops=1000, bytes_accessed=1000, transcendentals=0),
        name="forward_steps",
    )(ckpt_step[None], src_cells, own, mate, over, far, c0, c1, c2, c3)

    adj_over = after(laps, adj_over)
    adj_far = exchange(adj_over, CORE)
    inject = pl.pallas_call(
        inject_kernel,
        in_specs=[vmem] * 2,
        out_specs=vmem,
        out_shape=jax.ShapeDtypeStruct(history.shape, jnp.float32),
        compiler_params=pltpu.CompilerParams(vmem_limit_bytes=4 * 2**20),
        name="inject",
    )(placed, history)
    slab = jax.ShapeDtypeStruct(courant_sq.shape, jnp.float32)
    half, quarter = (planes // 2, rows_x, rows_y), (planes // 4, rows_x, rows_y)
    keep, send_x, send_y, send_xy = pl.pallas_call(
        adjoint_kernel,
        in_specs=[vmem] * 8,
        out_specs=[vmem] * 4,
        out_shape=[jax.ShapeDtypeStruct(half, jnp.float32)] * 4,
        scratch_shapes=step_scratch[:2] + [pltpu.VMEM((2 * planes, rows_x, rows_y), jnp.float32)] + step_scratch[2:],
        compiler_params=params,
        cost_estimate=cost,
        name="adjoint_steps",
    )(adj_own, adj_mate, adj_over, adj_far, cour, laps, inject, last)

    by_xy, by_x, by_y = exchange(send_xy, CHIP + Y), exchange(send_x, CHIP), exchange(send_y, Y)
    keep, send = local(square_kernel, [quarter] * 2, keep, by_x, by_y, by_xy)
    part = local(add_kernel, [quarter], keep, exchange(send, NEAR_Z))
    rows, sums_shape = planes // 4 * rows_x, (8, rows_y)
    data, sums = local(sums_kernel, [(rows + 8, rows_y), sums_shape], part, exchange(part, FAR_Z), momentum)

    received = exchange(data, NEAR_Z)
    others = [exchange(sums, CORE), exchange(sums, NEAR_Z + CORE)]
    data, sums = local(join_kernel, [(2 * rows + 8, rows_y), sums_shape], data, received, sums, *others)
    received = exchange(data, Y)
    others = [exchange(sums, CHIP), exchange(sums, Y + CHIP)]
    momentum_half, kinetic = pl.pallas_call(
        finish_kernel,
        in_specs=[vmem] * 6,
        out_specs=[vmem, smem],
        out_shape=[jax.ShapeDtypeStruct(momentum.shape, jnp.float32), jax.ShapeDtypeStruct((1,), jnp.float32)],
        compiler_params=pltpu.CompilerParams(vmem_limit_bytes=4 * 2**20),
        name="finish",
    )(data, received, momentum, sums, *others)
    return momentum_half, kinetic[0]


def solution(mesh):
    shots, slabs = mesh.shape["shot"], mesh.shape["depth"]

    def placed(depth):
        field = P("shot", depth, None, None)
        slab = P(depth, None, None)
        inputs = (slab, slab, field, field, field, field, P("shot", None, None), P("shot"), P("shot", None), P())
        return dict(in_specs=inputs, out_specs=(slab, P()), check_vma=False)

    slab_plan = jax.shard_map(slab_shards, mesh=mesh, **placed("depth"))
    if slabs != 4 or shots != 8:
        return slab_plan
    chips = Mesh(mesh.devices.reshape(shots, 2, 2), ("shot", "chip", "core"))
    whole_plan = jax.shard_map(whole_shards, mesh=chips, **placed(("chip", "core")))

    def run(courant_sq, momentum, fwd_prev, *rest):
        total, planes, rows_x, rows_y = fwd_prev.shape
        steps = rest[3].shape[1]
        fits = total == 2 * shots and planes == 4 * shots and rows_y == 128 and rows_x % 16 == 0 and steps % 2 == 0
        plan = whole_plan if fits else slab_plan
        return plan(courant_sq, momentum, fwd_prev, *rest)

    return run
```

```python
import functools

import jax
import jax.numpy as jnp
from jax import lax
from jax.experimental import pallas as pl
from jax.experimental.pallas import tpu as pltpu
from jax.sharding import Mesh
from jax.sharding import PartitionSpec as P

CENTER = -2.5
NEAR = 4.0 / 3.0
FAR = -1.0 / 12.0
AMPLITUDE = 100.0
EPSILON = 1e-06


def with_halo(value, sides, width):
    for axis, dim in sides:
        size, length = (lax.axis_size(axis), value.shape[dim])
        up = [(i, (i + 1) % size) for i in range(size - 1)]
        down = [(j, i) for i, j in up]
        last = lax.slice_in_dim(value, length - width, length, axis=dim)
        leading = lax.slice_in_dim(value, 0, width, axis=dim)
        before = lax.ppermute(last, axis, up)
        after = lax.ppermute(leading, axis, down)
        value = jnp.concatenate([before, value, after], axis=dim)
    return value


def laplace(padded):
    lateral = jnp.pad(padded[:, 2:-2], ((0, 0), (0, 0), (2, 2), (2, 2)))
    center = padded[:, 2:-2]
    along_z = NEAR * (padded[:, 1:-3] + padded[:, 3:-1]) + FAR * (padded[:, :-4] + padded[:, 4:])
    along_x = NEAR * (lateral[:, :, 1:-3, 2:-2] + lateral[:, :, 3:-1, 2:-2]) + FAR * (
        lateral[:, :, :-4, 2:-2] + lateral[:, :, 4:, 2:-2]
    )
    along_y = NEAR * (lateral[:, :, 2:-2, 1:-3] + lateral[:, :, 2:-2, 3:-1]) + FAR * (
        lateral[:, :, 2:-2, :-4] + lateral[:, :, 2:-2, 4:]
    )
    return 3.0 * CENTER * center + along_z + along_x + along_y


def locate(field, cell_ids, first_plane):
    shot_count, planes, rows_x, rows_y = field.shape
    plane_cells = rows_x * rows_y
    local_index = cell_ids - first_plane * plane_cells
    inside = (local_index >= 0) & (local_index < planes * plane_cells)
    target = jnp.where(inside, local_index, 0)
    return (inside, target)


def inject(field, cell_ids, values, first_plane):
    shot_count = field.shape[0]
    inside, target = locate(field, cell_ids, first_plane)
    amount = jnp.where(inside, values, jnp.zeros_like(values))
    flattened = field.reshape(shot_count, -1)
    lanes = jnp.arange(shot_count)[:, None]
    flattened = flattened.at[lanes, target].add(amount)
    return flattened.reshape(field.shape)


def sample(field, cell_ids, first_plane):
    shot_count = field.shape[0]
    inside, target = locate(field, cell_ids, first_plane)
    values = jnp.take_along_axis(field.reshape(shot_count, -1), target, axis=1)
    return jnp.where(inside, values, jnp.zeros_like(values))


def wave_value(start, step):
    cycle = jnp.mod(start + jnp.int32(step), jnp.int32(48))
    phase = (cycle.astype(jnp.float32) - 24.0) / 12.0
    return AMPLITUDE * (1.0 - 2.0 * phase * phase) * jnp.exp(-phase * phase)


def statistics(scaled, moment, weight, cells_all):
    grand_total = lax.psum(jnp.sum(scaled * scaled), ("shot", "depth"))
    factor = lax.rsqrt(grand_total / cells_all + EPSILON)
    halfway = moment - 0.5 * factor * scaled
    energy = lax.psum(jnp.sum(weight * halfway * halfway), ("shot", "depth"))
    return (factor, 0.5 * energy / cells_all)


def slab_shards(
    courant_sq,
    momentum,
    fwd_prev,
    fwd_cur,
    adj_next,
    adj_cur,
    observed,
    src_cells,
    rec_cells,
    ckpt_step,
):
    shot_count, planes, rows_x, rows_y = fwd_cur.shape
    steps_all = observed.shape[1]
    first_plane = lax.axis_index("depth") * planes
    total_planes = planes * lax.axis_size("depth")
    cells_all = total_planes * rows_x * rows_y
    sources = src_cells[:, None]
    older, current = (fwd_prev, fwd_cur)
    laplacians = []
    misfits = []
    for step in range(steps_all):
        padded = with_halo(current, (("depth", 1),), 2)
        strength = jnp.full(sources.shape, wave_value(ckpt_step, step), jnp.float32)
        laplacian = inject(laplace(padded), sources, strength, first_plane)
        newer = 2.0 * current - older + courant_sq * laplacian
        misfits.append(sample(newer, rec_cells, first_plane) - observed[:, step, :])
        laplacians.append(laplacian)
        older, current = (current, newer)
    adj_later, adj_now = (adj_next, adj_cur)
    gradient = jnp.zeros((planes, rows_x, rows_y), jnp.float32)
    for step in reversed(range(steps_all)):
        padded = with_halo(courant_sq * adj_now, (("depth", 1),), 2)
        adj_new = 2.0 * adj_now - adj_later + laplace(padded)
        adj_new = inject(adj_new, rec_cells, misfits[step], first_plane)
        gradient = gradient + jnp.sum(adj_new * laplacians[step], axis=0)
        adj_later, adj_now = (adj_now, adj_new)
    depths = (first_plane + jnp.arange(planes)).astype(jnp.float32)
    weight = (1.0 + 2.0 * depths / (total_planes - 1))[:, None, None]
    share_rows = rows_x // lax.axis_size("shot")
    offset = lax.axis_index("shot") * share_rows
    moment_share = lax.dynamic_slice_in_dim(momentum, offset, share_rows, 1)
    gradient = lax.psum(gradient, "shot")
    scaled = weight * gradient
    scaled_share = lax.dynamic_slice_in_dim(scaled, offset, share_rows, 1)
    factor, kinetic = statistics(scaled_share, moment_share, weight, cells_all)
    momentum_half = momentum - 0.5 * factor * scaled
    return (momentum_half, kinetic)


def interleave(dst, slab, src, factor=None):
    planes, rows = src.shape[0], src.shape[1]
    groups = rows // 8

    @pl.loop(0, planes)
    def _(p):
        for i in range(groups):
            value = src[p, pl.ds(i, 8, stride=groups), :]
            if factor is not None:
                value = value * factor
            dst[(*slab, p, pl.ds(i * 8, 8), slice(None))] = value


def pick_kernel(across, *refs):
    count = len(across)
    fields, outs, (held, sems) = refs[: 2 * count], refs[2 * count : 3 * count], refs[3 * count :]
    chip = lax.axis_index("chip")
    copies = []
    for n in range(2 * count):
        shot = 1 - chip if across[n // 2] else chip
        copies.append(pltpu.make_async_copy(fields[n].at[shot], held.at[n], sems.at[n]))
        copies[-1].start()
    for n in range(2 * count):
        copies[n].wait()
        interleave(outs[n // 2], (n % 2,), held.at[n])


def pick(*pairs, earlier):
    plain = functools.partial(pick_kernel, tuple(pair[2] for pair in pairs))
    fields = [field for pair in pairs for field in pair[:2]]
    shape = fields[0].shape[1:]
    vmem, hbm = pl.BlockSpec(memory_space=pltpu.VMEM), pl.BlockSpec(memory_space=pltpu.HBM)
    return pl.pallas_call(
        lambda earlier, *refs: plain(*refs),
        in_specs=[pl.BlockSpec(memory_space=pl.ANY)] + [hbm] * len(fields),
        out_specs=[vmem] * len(pairs),
        out_shape=[jax.ShapeDtypeStruct((2, *shape), jnp.float32)] * len(pairs),
        scratch_shapes=[pltpu.VMEM((len(fields), *shape), jnp.float32), pltpu.SemaphoreType.DMA((len(fields),))],
        compiler_params=pltpu.CompilerParams(vmem_limit_bytes=4 * 2**20),
        name="pick",
    )(earlier, *fields)


def courant_kernel(first, second, courant, whole, piece):
    interleave(whole, (), courant, 1.0 / 12.0)
    count = piece.shape[0]
    piece[...] = whole[pl.ds(lax.axis_index("shot") % 2 * count, count)]


def band(lanes):
    near = jnp.abs(lax.broadcasted_iota(jnp.int32, (2 * lanes, lanes), 0) % lanes - lax.broadcasted_iota(jnp.int32, (2 * lanes, lanes), 1))
    return jnp.where(near == 0, -90.0, jnp.where(near == 1, 16.0, jnp.where(near == 2, -1.0, 0.0))).astype(jnp.bfloat16)


def along_y(field, z, banded, out):
    rows, lanes = field.shape[1:]
    whole = field[pl.ds(z + 2, BATCH)].reshape(BATCH * rows, lanes)
    high = whole.astype(jnp.bfloat16)
    low = (whole - high.astype(jnp.float32)).astype(jnp.bfloat16)
    out[...] = jnp.dot(jnp.concatenate([high, low], 1), banded[...], preferred_element_type=jnp.float32)


def laps12(field, z, y_part, fetch, finish):
    rows, lanes = field.shape[1:]
    groups = rows // 8
    sub = lax.broadcasted_iota(jnp.int32, (8, lanes), 0)

    def later(block):
        return jnp.where(sub < 7, pltpu.roll(block, 7, 0), 0.0)

    def earlier(block):
        return jnp.where(sub > 0, pltpu.roll(block, 1, 0), 0.0)

    for base in range(0, BATCH, PLANES):
        held = {}

        def tile(j, i):
            if (j, i) not in held:
                if i < 0:
                    held[j, i] = earlier(tile(j, i + groups))
                elif i >= groups:
                    held[j, i] = later(tile(j, i - groups))
                else:
                    held[j, i] = field[z + j + 2, i * 8 : (i + 1) * 8]
            return held[j, i]

        def load(i):
            found = []
            for j in range(base, base + PLANES):
                center = tile(j, i)
                near = (tile(j, i - 1), tile(j, i + 1), tile(j - 1, i), tile(j + 1, i))
                far = (tile(j, i - 2), tile(j, i + 2), tile(j - 2, i), tile(j + 2, i))
                at = (j * groups + i) * 8
                found.append((center, near, far, y_part[at : at + 8], fetch(j, slice(i * 8, i * 8 + 8))))
            return found

        ready = load(0)
        for i in range(groups):
            upcoming = load(i + 1) if i + 1 < groups else None
            for j, (center, near, far, part, extra) in enumerate(ready):
                near = (near[0] + near[1]) + (near[2] + near[3])
                far = (far[0] + far[1]) + (far[2] + far[3])
                finish(base + j, slice(i * 8, i * 8 + 8), center, 16.0 * near + (part - far), extra)
            ready = upcoming


def scatter_kernel(rows_x, cells_ref, observed_ref, out_ref, mark, row_ref, spread):
    _, steps, receivers = observed_ref.shape
    lanes = out_ref.shape[2]
    tile = out_ref.shape[1]
    groups = rows_x // 8

    @pl.when(pl.program_id(0) == 0)
    def _():
        chip = lax.axis_index("chip")
        cells = cells_ref[pl.ds(chip, 1)]
        x = cells // lanes % rows_x
        row_ref[...] = cells // (rows_x * lanes) * rows_x + x % groups * 8 + x // groups
        on_lanes = jnp.concatenate(
            [
                observed_ref[chip],
                jnp.broadcast_to((cells % lanes).astype(jnp.float32), (8, receivers)),
                jnp.zeros((lanes - steps - 8, receivers), jnp.float32),
            ],
            0,
        )
        columns = on_lanes.T
        lane = lax.broadcasted_iota(jnp.int32, (receivers, lanes), 1).astype(jnp.float32)
        at = lane == columns[:, steps : steps + 1]
        for k in range(steps):
            column = columns[:, k : k + 1]
            high = column.astype(jnp.bfloat16).astype(jnp.float32)
            low = column - high
            cols = pl.ds(k * lanes, lanes)
            spread[0:receivers, cols] = jnp.where(at, high, 0.0).astype(jnp.bfloat16)
            spread[receivers:, cols] = jnp.where(at, low, 0.0).astype(jnp.bfloat16)
        cols = pl.ds(steps * lanes, lanes)
        spread[0:receivers, cols] = jnp.where(at, 1.0, 0.0).astype(jnp.bfloat16)
        spread[receivers:, cols] = jnp.zeros((receivers, lanes), jnp.bfloat16)
        mark[...] = jnp.zeros(mark.shape, jnp.float32)

    ids = lax.broadcasted_iota(jnp.int32, (tile, receivers), 0) + pl.program_id(0) * tile
    chosen = jnp.where(ids == row_ref[...], 1.0, 0.0).astype(jnp.bfloat16)
    total = jnp.dot(jnp.concatenate([chosen, chosen], 1), spread[...], preferred_element_type=jnp.float32)
    for k in range(steps + 1):
        out_ref[k] = total[:, k * lanes : (k + 1) * lanes]


def scatter(rec_cells, observed, planes_all, rows_x, rows_y):
    _, steps, receivers = observed.shape
    rows_all = planes_all * rows_x
    tile = 512
    return pl.pallas_call(
        functools.partial(scatter_kernel, rows_x),
        grid=(rows_all // tile,),
        in_specs=[
            pl.BlockSpec((2, receivers), lambda t: (0, 0)),
            pl.BlockSpec((2, steps, receivers), lambda t: (0, 0, 0)),
        ],
        out_specs=[
            pl.BlockSpec((steps + 1, tile, rows_y), lambda t: (0, t, 0)),
            pl.BlockSpec((8, rows_y), lambda t: (0, 0)),
        ],
        out_shape=[
            jax.ShapeDtypeStruct((steps + 1, rows_all, rows_y), jnp.float32),
            jax.ShapeDtypeStruct((8, rows_y), jnp.float32),
        ],
        scratch_shapes=[
            pltpu.VMEM((1, receivers), jnp.int32),
            pltpu.VMEM((2 * receivers, (steps + 1) * rows_y), jnp.bfloat16),
        ],
        compiler_params=pltpu.CompilerParams(vmem_limit_bytes=56 * 2**20),
        cost_estimate=pl.CostEstimate(
            flops=4 * rows_all * receivers * (steps + 1) * rows_y,
            bytes_accessed=4 * (steps + 1) * rows_all * rows_y,
            transcendentals=0,
        ),
        name="receiver_scatter",
    )(rec_cells, observed)


def place(planes):
    chip, core = lax.axis_index("chip"), lax.axis_index("core")
    slabs = (2 * chip + core, 2 * chip + 1 - core, 2 * (1 - chip) + core, 2 * (1 - chip) + 1 - core)
    return chip, core, [slab * planes for slab in slabs]


def load_blocks(slabs, blocks, first, second, factor=None):
    ends, rows, lanes = first.shape
    planes = blocks[0].shape[1]
    for field in (first, second):
        for z in (0, 1, ends - 2, ends - 1):
            field[z] = jnp.zeros((rows, lanes), jnp.float32)
    for slab, block in zip(slabs, blocks):
        for p in range(planes):
            values = block[0, p], block[1, p]
            if factor is not None:
                speed = factor[slab + p]
                values = values[0] * speed, values[1] * speed
            first[slab + p + 2], second[slab + p + 2] = values


BATCH = 4
PLANES = 2


def sweep(core, planes, field, banded, y_first, y_second, work):
    order = [(chip, owned) for owned in (True, False) for chip in (0, 1)]
    parts = (y_first, y_second)

    def first(chip, owned):
        return (2 * chip + (core if owned else 1 - core)) * planes

    along_y(field, first(*order[0]), banded, y_first)
    for owned in (True, False):
        for chip in (0, 1):
            z = first(chip, owned)
            onward = first(1, owned) if chip == 0 else first(0, False)
            for n in range(planes // BATCH):
                last = n == planes // BATCH - 1
                if not last or chip == 0 or owned:
                    along_y(field, onward if last else z + (n + 1) * BATCH, banded, parts[(n + 1) % 2])
                work(z + n * BATCH, parts[n % 2], chip if owned else None, n * BATCH)


def forward_kernel(
    start, sources, own, mate, over, far, c0, c1, c2, c3, placed, laps, history, held, cour, last,
    even, odd, banded, y0, y1, sems, sems_even, sems_odd
):
    planes, rows, lanes = c0.shape
    steps = laps.shape[0]
    groups = rows // 8
    chip_here, core, slabs = place(planes)

    fetches = []
    for k in range(steps + 1):
        for n in range(4):
            at = pl.ds(n * planes, planes)
            fetches.append(pltpu.make_async_copy(placed.at[k, at], held.at[k, at], sems.at[k, n]))
            fetches[-1].start()

    def keep(k, field, done):
        for n in range(4):
            source = field.at[pl.ds(n * planes + 2, planes)]
            yield pltpu.make_async_copy(source, history.at[k, pl.ds(n * planes, planes)], done.at[n])

    banded[...] = band(lanes)
    load_blocks(slabs, (own, mate, over, far), odd, even)
    for slab, block in zip(slabs, (c0, c1, c2, c3)):
        for p in range(planes):
            cour[slab + p] = block[p]

    for index in range(2 * planes):
        z = (2 * (index // planes) + core) * planes + index % planes
        weight = 1.0 + 2.0 * jnp.full((rows, lanes), z, jnp.int32).astype(jnp.float32) / (4 * planes - 1)
        last[index] = weight / (12.0 * cour[z])

    cell = sources[chip_here]
    source_z, x, lane = cell // (rows * lanes), cell // lanes % rows, cell % lanes
    tile = pl.ds(pl.multiple_of(x % groups * 8, 8), 8)
    here = (lax.broadcasted_iota(jnp.int32, (8, lanes), 0) == x // groups) & (
        lax.broadcasted_iota(jnp.int32, (8, lanes), 1) == lane
    )
    source_slab, source_p = source_z // planes, lax.rem(source_z, planes)

    def advance(k, now, then, done):
        @pl.when(k >= 2)
        def _():
            for copy in keep(k - 2, then, done):
                copy.wait()

        def work(z, y_part, chip, p):
            def fetch(j, rows):
                return then[z + j + 2, rows], cour[z + j, rows]

            def finish(j, rows, center, lap, extra):
                old, speed = extra
                if chip is not None:
                    laps[k, p + j, chip, rows] = lap
                then[z + j + 2, rows] = 2.0 * center - old + speed * lap

            laps12(now, z, y_part, fetch, finish)

        cycle = (start[0] + k) % 48
        phase = (jnp.full((8, lanes), cycle, jnp.int32).astype(jnp.float32) - 24.0) / 12.0
        wave = AMPLITUDE * (1.0 - 2.0 * phase * phase) * jnp.exp(-phase * phase)
        strength = jnp.where(here, 12.0 * wave, 0.0)
        moved = cour[source_z, tile, :] * strength

        sweep(core, planes, now, banded, y0, y1, work)

        owned = jnp.where(lax.rem(source_slab, 2) == core, strength, 0.0)
        laps[k, source_p, source_slab // 2, tile, :] += owned
        then[source_z + 2, tile, :] += moved
        for copy in keep(k, then, done):
            copy.start()

    @pl.loop(0, steps // 2)
    def _(pair):
        advance(2 * pair, even, odd, sems_odd)
        advance(2 * pair + 1, odd, even, sems_even)

    for k, field, done in ((steps - 2, odd, sems_odd), (steps - 1, even, sems_even)):
        for copy in keep(k, field, done):
            copy.wait()
    for fetch in fetches:
        fetch.wait()


def inject_kernel(held, history, inject):
    steps, planes_all = history.shape[:2]

    @pl.loop(0, planes_all)
    def _(z):
        count = held[steps, z]
        for k in range(steps):
            inject[k, z] = held[k, z] - count * history[k, z]


def adjoint_kernel(own, mate, over, far, cour, laps, inject, last, keep, send_x, send_y, send_xy, even, odd, total, banded, y0, y1):
    planes, rows, lanes = own.shape[1:]
    steps = laps.shape[0]
    groups = rows // 8
    chip_here, core, slabs = place(planes)
    banded[...] = band(lanes)
    load_blocks(slabs, (own, mate, over, far), odd, even, factor=cour)

    total[...] = jnp.zeros(total.shape, jnp.float32)

    def advance(k, now, then):
        def work(z, y_part, chip, p):
            def fetch(j, rows):
                extra = (then[z + j + 2, rows], cour[z + j, rows], inject[k, z + j, rows])
                if chip is not None:
                    extra += (total[chip * planes + p + j, rows], laps[k, p + j, chip, rows])
                return extra

            def finish(j, rows, center, lap, extra):
                newer = 2.0 * center - extra[0] + extra[1] * (lap - extra[2])
                then[z + j + 2, rows] = newer
                if chip is not None:
                    total[chip * planes + p + j, rows] = extra[3] + newer * extra[4]

            laps12(now, z, y_part, fetch, finish)

        sweep(core, planes, now, banded, y0, y1, work)

    @pl.loop(0, steps // 2)
    def _(pair):
        advance(steps - 1 - 2 * pair, even, odd)
        advance(steps - 2 - 2 * pair, odd, even)

    count = keep.shape[0]
    mine, others = lax.axis_index("shot") % 2 * count, (1 - lax.axis_index("shot") % 2) * count
    here, there = chip_here, 1 - chip_here
    for ref, chip, start in ((keep, here, mine), (send_x, there, mine), (send_y, here, others), (send_xy, there, others)):

        @pl.loop(0, count)
        def _(n):
            p = start + n
            value = total[chip * planes + p] * last[chip * planes + p]
            for i in range(groups):
                ref[n, pl.ds(i, 8, stride=groups), :] = value[i * 8 : (i + 1) * 8]


def square_kernel(mine, by_xy, by_y, by_x, keep, send):
    half = lax.axis_index("shot") // 2 % 2
    count = keep.shape[0]
    for ref, part in ((keep, half), (send, 1 - half)):
        for p in range(count):
            at = part * count + p
            ref[p] = (mine[at] + by_x[at]) + (by_y[at] + by_xy[at])


def add_kernel(mine, other, out):
    out[...] = mine[...] + other[...]


def flip(index, bits):
    result = index
    for bit in (1, 2):
        if bits & bit:
            result = jnp.where(index // bit % 2 == 1, result - bit, result + bit)
    return result


def after_kernel(earlier, *refs):
    out = refs[-1]
    if len(refs) == 2:
        out[...] = refs[0][...]
    else:
        for n, value in enumerate(refs[:-1]):
            interleave(out, (n,), value)


def after(earlier, *values):
    vmem, anywhere = pl.BlockSpec(memory_space=pltpu.VMEM), pl.BlockSpec(memory_space=pl.ANY)
    shape = values[0].shape if len(values) == 1 else (len(values), *values[0].shape)
    return pl.pallas_call(
        after_kernel,
        in_specs=[anywhere] + [vmem] * len(values),
        out_specs=vmem,
        out_shape=jax.ShapeDtypeStruct(shape, jnp.float32),
        compiler_params=pltpu.CompilerParams(vmem_limit_bytes=4 * 2**20),
        name="after",
    )(earlier, *values)


def arrange_kernel(mine, other, out):
    y = lax.axis_index("shot") % 2
    count = mine.shape[0]
    out[pl.ds(y * count, count)] = mine[...]
    out[pl.ds((1 - y) * count, count)] = other[...]


def first_plane(shot, planes):
    return (shot % 2) * (planes // 2) + (shot // 2 % 2) * (planes // 4)


def sums_kernel(mine, other, momentum, data, sums):
    count, rows, lanes = mine.shape
    planes = momentum.shape[0]
    chip, core = lax.axis_index("chip"), lax.axis_index("core")
    first = first_plane(lax.axis_index("shot"), planes)
    parts = [jnp.zeros((rows, lanes), jnp.float32)] * 4
    for j in range(count):
        scaled = mine[j] + other[j]
        data[j * rows : (j + 1) * rows] = scaled
        z = (2 * chip + core) * planes + first + j
        weight = 1.0 + 2.0 * jnp.full((1, lanes), z, jnp.int32).astype(jnp.float32) / (4 * planes - 1)
        moment = momentum[first + j]
        square = scaled * scaled
        terms = (square, weight * moment * moment, weight * moment * scaled, weight * square)
        parts = [part + term for part, term in zip(parts, terms)]

    def total(value):
        by_lane = jnp.sum(value, axis=0, keepdims=True)
        return jnp.broadcast_to(jnp.sum(by_lane, axis=1, keepdims=True), (1, lanes))

    value = jnp.concatenate([total(part) for part in parts] + [jnp.zeros((4, lanes), jnp.float32)], 0)
    data[count * rows :] = value
    sums[...] = value


def join_kernel(mine, other, s0, s1, s2, data, sums):
    rows = mine.shape[0] - 8
    data[0:rows] = mine[0:rows]
    data[rows : 2 * rows] = other[0:rows]
    value = (s0[...] + s1[...]) + (other[rows:] + s2[...])
    data[2 * rows :] = value
    sums[...] = value


def finish_kernel(mine, other, momentum, s0, s1, s2, out, kinetic):
    planes, rows, lanes = momentum.shape
    cells = 4.0 * planes * rows * lanes
    shot = lax.axis_index("shot")
    sums = (s0[...] + s1[...]) + (other[planes // 2 * rows :] + s2[...])
    factor = lax.rsqrt(sums[0:1] / cells + EPSILON)
    energy = 0.5 * (sums[1:2] - factor * sums[2:3] + 0.25 * factor * factor * sums[3:4]) / cells
    kinetic[0] = energy[0, 0]
    step = 0.5 * factor
    quarter = planes // 4
    for part, group in ((mine, shot), (other, flip(shot, 1))):
        for number, first in enumerate((first_plane(group, planes), first_plane(flip(group, 2), planes))):
            for j in range(quarter):
                at = (number * quarter + j) * rows
                out[first + j] = momentum[first + j] - step * part[at : at + rows]


def local(kernel, outs, *arrays):
    vmem = pl.BlockSpec(memory_space=pltpu.VMEM)
    shapes = [jax.ShapeDtypeStruct(shape, jnp.float32) for shape in outs]
    single = len(outs) == 1
    return pl.pallas_call(
        kernel,
        in_specs=[vmem] * len(arrays),
        out_specs=vmem if single else [vmem] * len(outs),
        out_shape=shapes[0] if single else shapes,
        compiler_params=pltpu.CompilerParams(vmem_limit_bytes=4 * 2**20),
        name=kernel.__name__,
    )(*arrays)


def exchange(value, bits):
    axes = ("shot", "chip", "core")
    return lax.ppermute(value, axes, [(i, i ^ bits) for i in range(lax.axis_size(axes))])


CORE, CHIP, Y, NEAR_Z, FAR_Z = 1, 2, 4, 8, 16


def whole_shards(
    courant_sq, momentum, fwd_prev, fwd_cur, adj_next, adj_cur, observed, src_cells, rec_cells, ckpt_step
):
    _, planes, rows_x, rows_y = fwd_cur.shape
    steps = observed.shape[1]
    planes_all = 4 * planes
    cells_all = planes_all * rows_x * rows_y
    vmem, smem = pl.BlockSpec(memory_space=pltpu.VMEM), pl.BlockSpec(memory_space=pltpu.SMEM)

    across = 1 - lax.axis_index("chip")
    outgoing = [lax.dynamic_index_in_dim(field, across, 0, keepdims=False) for field in (fwd_prev, fwd_cur)]
    over = [exchange(field, CHIP) for field in outgoing]
    slab = jax.ShapeDtypeStruct(courant_sq.shape, jnp.float32)
    c0, piece = pl.pallas_call(
        courant_kernel,
        in_specs=[pl.BlockSpec(memory_space=pl.ANY)] * 2 + [vmem],
        out_specs=[vmem, vmem],
        out_shape=[slab, jax.ShapeDtypeStruct((planes // 2, rows_x, rows_y), jnp.float32)],
        compiler_params=pltpu.CompilerParams(vmem_limit_bytes=4 * 2**20),
        name="courant",
    )(*outgoing, courant_sq)
    piece = exchange(piece, CHIP)

    placed, mark = scatter(rec_cells, observed, planes_all, rows_x, rows_y)
    placed = placed.reshape(steps + 1, planes_all, rows_x, rows_y)

    piece = after(mark, piece)
    adj_outgoing, adj_own, own = pick(
        (adj_next, adj_cur, True), (adj_next, adj_cur, False), (fwd_prev, fwd_cur, False), earlier=piece
    )
    mate = exchange(own, CORE)
    c2 = local(arrange_kernel, [courant_sq.shape], piece, exchange(piece, Y))
    c1, c3 = exchange(c0, CORE), exchange(c2, CORE)
    over = after(c2, *over)
    far = exchange(over, CORE)
    adj_over = exchange(adj_outgoing, CHIP)
    adj_mate = exchange(adj_own, CORE)

    scratch = pltpu.VMEM((planes_all + 4, rows_x, rows_y), jnp.float32)
    y_scratch = pltpu.VMEM((BATCH * rows_x, rows_y), jnp.float32)
    step_scratch = [scratch, scratch, pltpu.VMEM((2 * rows_y, rows_y), jnp.bfloat16), y_scratch, y_scratch]
    params = pltpu.CompilerParams(vmem_limit_bytes=6 * 2**20)
    cost = pl.CostEstimate(flops=30 * steps * cells_all, bytes_accessed=16 * steps * cells_all, transcendentals=0)
    laps, history, held, cour, last = pl.pallas_call(
        forward_kernel,
        in_specs=[smem, smem] + [vmem] * 8 + [pl.BlockSpec(memory_space=pltpu.HBM)],
        out_specs=[vmem] * 5,
        out_shape=[
            jax.ShapeDtypeStruct((steps, planes, 2, rows_x, rows_y), jnp.float32),
            jax.ShapeDtypeStruct((steps, planes_all, rows_x, rows_y), jnp.float32),
            jax.ShapeDtypeStruct((steps + 1, planes_all, rows_x, rows_y), jnp.float32),
            jax.ShapeDtypeStruct((planes_all, rows_x, rows_y), jnp.float32),
            jax.ShapeDtypeStruct((2 * planes, rows_x, rows_y), jnp.float32),
        ],
        scratch_shapes=step_scratch
        + [
            pltpu.SemaphoreType.DMA((steps + 1, 4)),
            pltpu.SemaphoreType.DMA((4,)),
            pltpu.SemaphoreType.DMA((4,)),
        ],
        compiler_params=pltpu.CompilerParams(vmem_limit_bytes=25 * 2**20),
        cost_estimate=pl.CostEstimate(flops=1000, bytes_accessed=1000, transcendentals=0),
        name="forward_steps",
    )(ckpt_step[None], src_cells, own, mate, over, far, c0, c1, c2, c3, placed)

    adj_over = after(laps, adj_over)
    adj_far = exchange(adj_over, CORE)
    inject = pl.pallas_call(
        inject_kernel,
        in_specs=[vmem] * 2,
        out_specs=vmem,
        out_shape=jax.ShapeDtypeStruct(history.shape, jnp.float32),
        compiler_params=pltpu.CompilerParams(vmem_limit_bytes=4 * 2**20),
        name="inject",
    )(held, history)
    slab = jax.ShapeDtypeStruct(courant_sq.shape, jnp.float32)
    half, quarter = (planes // 2, rows_x, rows_y), (planes // 4, rows_x, rows_y)
    keep, send_x, send_y, send_xy = pl.pallas_call(
        adjoint_kernel,
        in_specs=[vmem] * 8,
        out_specs=[vmem] * 4,
        out_shape=[jax.ShapeDtypeStruct(half, jnp.float32)] * 4,
        scratch_shapes=step_scratch[:2] + [pltpu.VMEM((2 * planes, rows_x, rows_y), jnp.float32)] + step_scratch[2:],
        compiler_params=params,
        cost_estimate=cost,
        name="adjoint_steps",
    )(adj_own, adj_mate, adj_over, adj_far, cour, laps, inject, last)

    by_xy, by_x, by_y = exchange(send_xy, CHIP + Y), exchange(send_x, CHIP), exchange(send_y, Y)
    keep, send = local(square_kernel, [quarter] * 2, keep, by_xy, by_y, by_x)
    part = local(add_kernel, [quarter], keep, exchange(send, NEAR_Z))
    rows, sums_shape = planes // 4 * rows_x, (8, rows_y)
    data, sums = local(sums_kernel, [(rows + 8, rows_y), sums_shape], part, exchange(part, FAR_Z), momentum)

    received = exchange(data, NEAR_Z)
    others = [exchange(sums, CORE), exchange(sums, NEAR_Z + CORE)]
    data, sums = local(join_kernel, [(2 * rows + 8, rows_y), sums_shape], data, received, sums, *others)
    received = exchange(data, Y)
    others = [exchange(sums, CHIP), exchange(sums, Y + CHIP)]
    momentum_half, kinetic = pl.pallas_call(
        finish_kernel,
        in_specs=[vmem] * 6,
        out_specs=[vmem, smem],
        out_shape=[jax.ShapeDtypeStruct(momentum.shape, jnp.float32), jax.ShapeDtypeStruct((1,), jnp.float32)],
        compiler_params=pltpu.CompilerParams(vmem_limit_bytes=4 * 2**20),
        name="finish",
    )(data, received, momentum, sums, *others)
    return momentum_half, kinetic[0]


def solution(mesh):
    shots, slabs = mesh.shape["shot"], mesh.shape["depth"]

    def placed(depth):
        field = P("shot", depth, None, None)
        slab = P(depth, None, None)
        inputs = (slab, slab, field, field, field, field, P("shot", None, None), P("shot"), P("shot", None), P())
        return dict(in_specs=inputs, out_specs=(slab, P()), check_vma=False)

    slab_plan = jax.shard_map(slab_shards, mesh=mesh, **placed("depth"))
    if slabs != 4 or shots != 8:
        return slab_plan
    chips = Mesh(mesh.devices.reshape(shots, 2, 2), ("shot", "chip", "core"))
    whole_plan = jax.shard_map(whole_shards, mesh=chips, **placed(("chip", "core")))

    def run(courant_sq, momentum, fwd_prev, *rest):
        total, planes, rows_x, rows_y = fwd_prev.shape
        steps = rest[3].shape[1]
        fits = total == 2 * shots and planes == 4 * shots and rows_y == 128 and rows_x % 16 == 0 and steps % 2 == 0
        plan = whole_plan if fits else slab_plan
        return plan(courant_sq, momentum, fwd_prev, *rest)

    return run
```

```python
import functools

import jax
import jax.numpy as jnp
from jax import lax
from jax.experimental import pallas as pl
from jax.experimental.pallas import tpu as pltpu
from jax.sharding import Mesh
from jax.sharding import PartitionSpec as P

CENTER = -2.5
NEAR = 4.0 / 3.0
FAR = -1.0 / 12.0
AMPLITUDE = 100.0
EPSILON = 1e-06


def with_halo(value, sides, width):
    for axis, dim in sides:
        size, length = (lax.axis_size(axis), value.shape[dim])
        up = [(i, (i + 1) % size) for i in range(size - 1)]
        down = [(j, i) for i, j in up]
        last = lax.slice_in_dim(value, length - width, length, axis=dim)
        leading = lax.slice_in_dim(value, 0, width, axis=dim)
        before = lax.ppermute(last, axis, up)
        after = lax.ppermute(leading, axis, down)
        value = jnp.concatenate([before, value, after], axis=dim)
    return value


def laplace(padded):
    lateral = jnp.pad(padded[:, 2:-2], ((0, 0), (0, 0), (2, 2), (2, 2)))
    center = padded[:, 2:-2]
    along_z = NEAR * (padded[:, 1:-3] + padded[:, 3:-1]) + FAR * (padded[:, :-4] + padded[:, 4:])
    along_x = NEAR * (lateral[:, :, 1:-3, 2:-2] + lateral[:, :, 3:-1, 2:-2]) + FAR * (
        lateral[:, :, :-4, 2:-2] + lateral[:, :, 4:, 2:-2]
    )
    along_y = NEAR * (lateral[:, :, 2:-2, 1:-3] + lateral[:, :, 2:-2, 3:-1]) + FAR * (
        lateral[:, :, 2:-2, :-4] + lateral[:, :, 2:-2, 4:]
    )
    return 3.0 * CENTER * center + along_z + along_x + along_y


def locate(field, cell_ids, first_plane):
    shot_count, planes, rows_x, rows_y = field.shape
    plane_cells = rows_x * rows_y
    local_index = cell_ids - first_plane * plane_cells
    inside = (local_index >= 0) & (local_index < planes * plane_cells)
    target = jnp.where(inside, local_index, 0)
    return (inside, target)


def inject(field, cell_ids, values, first_plane):
    shot_count = field.shape[0]
    inside, target = locate(field, cell_ids, first_plane)
    amount = jnp.where(inside, values, jnp.zeros_like(values))
    flattened = field.reshape(shot_count, -1)
    lanes = jnp.arange(shot_count)[:, None]
    flattened = flattened.at[lanes, target].add(amount)
    return flattened.reshape(field.shape)


def sample(field, cell_ids, first_plane):
    shot_count = field.shape[0]
    inside, target = locate(field, cell_ids, first_plane)
    values = jnp.take_along_axis(field.reshape(shot_count, -1), target, axis=1)
    return jnp.where(inside, values, jnp.zeros_like(values))


def wave_value(start, step):
    cycle = jnp.mod(start + jnp.int32(step), jnp.int32(48))
    phase = (cycle.astype(jnp.float32) - 24.0) / 12.0
    return AMPLITUDE * (1.0 - 2.0 * phase * phase) * jnp.exp(-phase * phase)


def statistics(scaled, moment, weight, cells_all):
    grand_total = lax.psum(jnp.sum(scaled * scaled), ("shot", "depth"))
    factor = lax.rsqrt(grand_total / cells_all + EPSILON)
    halfway = moment - 0.5 * factor * scaled
    energy = lax.psum(jnp.sum(weight * halfway * halfway), ("shot", "depth"))
    return (factor, 0.5 * energy / cells_all)


def slab_shards(
    courant_sq,
    momentum,
    fwd_prev,
    fwd_cur,
    adj_next,
    adj_cur,
    observed,
    src_cells,
    rec_cells,
    ckpt_step,
):
    shot_count, planes, rows_x, rows_y = fwd_cur.shape
    steps_all = observed.shape[1]
    first_plane = lax.axis_index("depth") * planes
    total_planes = planes * lax.axis_size("depth")
    cells_all = total_planes * rows_x * rows_y
    sources = src_cells[:, None]
    older, current = (fwd_prev, fwd_cur)
    laplacians = []
    misfits = []
    for step in range(steps_all):
        padded = with_halo(current, (("depth", 1),), 2)
        strength = jnp.full(sources.shape, wave_value(ckpt_step, step), jnp.float32)
        laplacian = inject(laplace(padded), sources, strength, first_plane)
        newer = 2.0 * current - older + courant_sq * laplacian
        misfits.append(sample(newer, rec_cells, first_plane) - observed[:, step, :])
        laplacians.append(laplacian)
        older, current = (current, newer)
    adj_later, adj_now = (adj_next, adj_cur)
    gradient = jnp.zeros((planes, rows_x, rows_y), jnp.float32)
    for step in reversed(range(steps_all)):
        padded = with_halo(courant_sq * adj_now, (("depth", 1),), 2)
        adj_new = 2.0 * adj_now - adj_later + laplace(padded)
        adj_new = inject(adj_new, rec_cells, misfits[step], first_plane)
        gradient = gradient + jnp.sum(adj_new * laplacians[step], axis=0)
        adj_later, adj_now = (adj_now, adj_new)
    depths = (first_plane + jnp.arange(planes)).astype(jnp.float32)
    weight = (1.0 + 2.0 * depths / (total_planes - 1))[:, None, None]
    share_rows = rows_x // lax.axis_size("shot")
    offset = lax.axis_index("shot") * share_rows
    moment_share = lax.dynamic_slice_in_dim(momentum, offset, share_rows, 1)
    gradient = lax.psum(gradient, "shot")
    scaled = weight * gradient
    scaled_share = lax.dynamic_slice_in_dim(scaled, offset, share_rows, 1)
    factor, kinetic = statistics(scaled_share, moment_share, weight, cells_all)
    momentum_half = momentum - 0.5 * factor * scaled
    return (momentum_half, kinetic)


def interleave(dst, slab, src, factor=None):
    planes, rows = src.shape[0], src.shape[1]
    groups = rows // 8

    @pl.loop(0, planes)
    def _(p):
        for i in range(groups):
            value = src[p, pl.ds(i, 8, stride=groups), :]
            if factor is not None:
                value = value * factor
            dst[(*slab, p, pl.ds(i * 8, 8), slice(None))] = value


def pick_kernel(across, *refs):
    count = len(across)
    fields, outs, (held, sems) = refs[: 2 * count], refs[2 * count : 3 * count], refs[3 * count :]
    chip = lax.axis_index("chip")
    copies = []
    for n in range(2 * count):
        shot = 1 - chip if across[n // 2] else chip
        copies.append(pltpu.make_async_copy(fields[n].at[shot], held.at[n], sems.at[n]))
        copies[-1].start()
    for n in range(2 * count):
        copies[n].wait()
        interleave(outs[n // 2], (n % 2,), held.at[n])


def pick(*pairs, earlier):
    plain = functools.partial(pick_kernel, tuple(pair[2] for pair in pairs))
    fields = [field for pair in pairs for field in pair[:2]]
    shape = fields[0].shape[1:]
    vmem, hbm = pl.BlockSpec(memory_space=pltpu.VMEM), pl.BlockSpec(memory_space=pltpu.HBM)
    return pl.pallas_call(
        lambda earlier, *refs: plain(*refs),
        in_specs=[pl.BlockSpec(memory_space=pl.ANY)] + [hbm] * len(fields),
        out_specs=[vmem] * len(pairs),
        out_shape=[jax.ShapeDtypeStruct((2, *shape), jnp.float32)] * len(pairs),
        scratch_shapes=[pltpu.VMEM((len(fields), *shape), jnp.float32), pltpu.SemaphoreType.DMA((len(fields),))],
        compiler_params=pltpu.CompilerParams(vmem_limit_bytes=4 * 2**20),
        name="pick",
    )(earlier, *fields)


def first_kernel(first, second, courant, outgoing, whole, piece, held, held_courant, sems):
    shot = 1 - lax.axis_index("chip")
    copies = [
        pltpu.make_async_copy(first.at[shot], held.at[0], sems.at[0]),
        pltpu.make_async_copy(second.at[shot], held.at[1], sems.at[1]),
        pltpu.make_async_copy(courant, held_courant, sems.at[2]),
    ]
    for copy in copies:
        copy.start()
    for n in range(2):
        copies[n].wait()
        interleave(outgoing, (n,), held.at[n])
    copies[2].wait()
    interleave(whole, (), held_courant, 1.0 / 12.0)
    count = piece.shape[0]
    piece[...] = whole[pl.ds(lax.axis_index("shot") % 2 * count, count)]


def band(lanes):
    near = jnp.abs(lax.broadcasted_iota(jnp.int32, (2 * lanes, lanes), 0) % lanes - lax.broadcasted_iota(jnp.int32, (2 * lanes, lanes), 1))
    return jnp.where(near == 0, -90.0, jnp.where(near == 1, 16.0, jnp.where(near == 2, -1.0, 0.0))).astype(jnp.bfloat16)


def along_y(field, z, banded, out):
    rows, lanes = field.shape[1] - 8, field.shape[2]
    whole = field[pl.ds(z + 2, BATCH), 0:rows].reshape(BATCH * rows, lanes)
    high = whole.astype(jnp.bfloat16)
    low = (whole - high.astype(jnp.float32)).astype(jnp.bfloat16)
    out[...] = jnp.dot(jnp.concatenate([high, low], 1), banded[...], preferred_element_type=jnp.float32)


def laps12(field, z, y_part, fetch, finish):
    rows, lanes = field.shape[1] - 8, field.shape[2]
    groups = rows // 8
    sub = lax.broadcasted_iota(jnp.int32, (8, lanes), 0)

    def later(block):
        return jnp.where(sub < 7, pltpu.roll(block, 7, 0), 0.0)

    def earlier(block):
        return jnp.where(sub > 0, pltpu.roll(block, 1, 0), 0.0)

    for base in range(0, BATCH, PLANES):
        held = {}

        def tile(j, i):
            if (j, i) not in held:
                if i < 0:
                    held[j, i] = earlier(tile(j, i + groups))
                elif i >= groups:
                    held[j, i] = later(tile(j, i - groups))
                else:
                    held[j, i] = field[z + j + 2, i * 8 : (i + 1) * 8]
            return held[j, i]

        def load(i):
            found = []
            for j in range(base, base + PLANES):
                center = tile(j, i)
                near = (tile(j, i - 1), tile(j, i + 1), tile(j - 1, i), tile(j + 1, i))
                far = (tile(j, i - 2), tile(j, i + 2), tile(j - 2, i), tile(j + 2, i))
                at = (j * groups + i) * 8
                found.append((center, near, far, y_part[at : at + 8], fetch(j, slice(i * 8, i * 8 + 8))))
            return found

        ready = load(0)
        for i in range(groups):
            upcoming = load(i + 1) if i + 1 < groups else None
            for j, (center, near, far, part, extra) in enumerate(ready):
                near = (near[0] + near[1]) + (near[2] + near[3])
                far = (far[0] + far[1]) + (far[2] + far[3])
                finish(base + j, slice(i * 8, i * 8 + 8), center, 16.0 * near + (part - far), extra)
            ready = upcoming


def scatter_kernel(rows_x, cells_ref, observed_ref, out_ref, mark, row_ref, spread):
    _, steps, receivers = observed_ref.shape
    lanes = out_ref.shape[2]
    tile = out_ref.shape[1]
    groups = rows_x // 8

    @pl.when(pl.program_id(0) == 0)
    def _():
        chip = lax.axis_index("chip")
        cells = cells_ref[pl.ds(chip, 1)]
        x = cells // lanes % rows_x
        row_ref[...] = cells // (rows_x * lanes) * rows_x + x % groups * 8 + x // groups
        on_lanes = jnp.concatenate(
            [
                observed_ref[chip],
                jnp.broadcast_to((cells % lanes).astype(jnp.float32), (8, receivers)),
                jnp.zeros((lanes - steps - 8, receivers), jnp.float32),
            ],
            0,
        )
        columns = on_lanes.T
        lane = lax.broadcasted_iota(jnp.int32, (receivers, lanes), 1).astype(jnp.float32)
        at = lane == columns[:, steps : steps + 1]
        for k in range(steps):
            column = columns[:, k : k + 1]
            high = column.astype(jnp.bfloat16).astype(jnp.float32)
            low = column - high
            cols = pl.ds(k * lanes, lanes)
            spread[0:receivers, cols] = jnp.where(at, high, 0.0).astype(jnp.bfloat16)
            spread[receivers:, cols] = jnp.where(at, low, 0.0).astype(jnp.bfloat16)
        cols = pl.ds(steps * lanes, lanes)
        spread[0:receivers, cols] = jnp.where(at, 1.0, 0.0).astype(jnp.bfloat16)
        spread[receivers:, cols] = jnp.zeros((receivers, lanes), jnp.bfloat16)
        mark[...] = jnp.zeros(mark.shape, jnp.float32)

    ids = lax.broadcasted_iota(jnp.int32, (tile, receivers), 0) + pl.program_id(0) * tile
    chosen = jnp.where(ids == row_ref[...], 1.0, 0.0).astype(jnp.bfloat16)
    total = jnp.dot(jnp.concatenate([chosen, chosen], 1), spread[...], preferred_element_type=jnp.float32)
    for k in range(steps + 1):
        out_ref[k] = total[:, k * lanes : (k + 1) * lanes]


def scatter(rec_cells, observed, planes_all, rows_x, rows_y):
    _, steps, receivers = observed.shape
    rows_all = planes_all * rows_x
    tile = 512
    return pl.pallas_call(
        functools.partial(scatter_kernel, rows_x),
        grid=(rows_all // tile,),
        in_specs=[
            pl.BlockSpec((2, receivers), lambda t: (0, 0)),
            pl.BlockSpec((2, steps, receivers), lambda t: (0, 0, 0)),
        ],
        out_specs=[
            pl.BlockSpec((steps + 1, tile, rows_y), lambda t: (0, t, 0)),
            pl.BlockSpec((8, rows_y), lambda t: (0, 0)),
        ],
        out_shape=[
            jax.ShapeDtypeStruct((steps + 1, rows_all, rows_y), jnp.float32),
            jax.ShapeDtypeStruct((8, rows_y), jnp.float32),
        ],
        scratch_shapes=[
            pltpu.VMEM((1, receivers), jnp.int32),
            pltpu.VMEM((2 * receivers, (steps + 1) * rows_y), jnp.bfloat16),
        ],
        compiler_params=pltpu.CompilerParams(vmem_limit_bytes=56 * 2**20),
        cost_estimate=pl.CostEstimate(
            flops=4 * rows_all * receivers * (steps + 1) * rows_y,
            bytes_accessed=4 * (steps + 1) * rows_all * rows_y,
            transcendentals=0,
        ),
        name="receiver_scatter",
    )(rec_cells, observed)


def place(planes):
    chip, core = lax.axis_index("chip"), lax.axis_index("core")
    slabs = (2 * chip + core, 2 * chip + 1 - core, 2 * (1 - chip) + core, 2 * (1 - chip) + 1 - core)
    return chip, core, [slab * planes for slab in slabs]


def load_blocks(slabs, blocks, first, second, factor=None):
    ends, rows, lanes = first.shape[0], first.shape[1] - 8, first.shape[2]
    planes = (ends - 4) // 4
    for field in (first, second):
        for z in (0, 1, ends - 2, ends - 1):
            field[z, 0:rows] = jnp.zeros((rows, lanes), jnp.float32)
    for slab, block in zip(slabs, blocks):
        pair = block if isinstance(block, tuple) else (block.at[0], block.at[1])
        for p in range(planes):
            values = pair[0][p], pair[1][p]
            if factor is not None:
                speed = factor[slab + p]
                values = values[0] * speed, values[1] * speed
            first[slab + p + 2, 0:rows], second[slab + p + 2, 0:rows] = values


BATCH = 4
PLANES = 2


def sweep(core, planes, field, banded, y_first, y_second, work):
    order = [(chip, owned) for owned in (True, False) for chip in (0, 1)]
    parts = (y_first, y_second)

    def first(chip, owned):
        return (2 * chip + (core if owned else 1 - core)) * planes

    along_y(field, first(*order[0]), banded, y_first)
    for owned in (True, False):
        for chip in (0, 1):
            z = first(chip, owned)
            onward = first(1, owned) if chip == 0 else first(0, False)
            for n in range(planes // BATCH):
                last = n == planes // BATCH - 1
                if not last or chip == 0 or owned:
                    along_y(field, onward if last else z + (n + 1) * BATCH, banded, parts[(n + 1) % 2])
                work(z + n * BATCH, parts[n % 2], chip if owned else None, n * BATCH)


def forward_kernel(
    start, sources, own, mate, over0, over1, far0, far1, c0, c1, c2, c3, placed, laps, history, held, cour, last,
    even, odd, banded, y0, y1, sems, sems_even, sems_odd
):
    planes, rows, lanes = c0.shape
    steps = laps.shape[0]
    groups = rows // 8
    chip_here, core, slabs = place(planes)

    fetches = []
    for k in range(steps + 1):
        for n in range(4):
            at = pl.ds(n * planes, planes)
            fetches.append(pltpu.make_async_copy(placed.at[k, at], held.at[k, at], sems.at[k, n]))
            fetches[-1].start()

    def keep(k, field, done):
        for n in range(4):
            source = field.at[pl.ds(n * planes + 2, planes), pl.ds(0, rows)]
            yield pltpu.make_async_copy(source, history.at[k, pl.ds(n * planes, planes)], done.at[n])

    banded[...] = band(lanes)
    load_blocks(slabs, (own, mate, (over0, over1), (far0, far1)), odd, even)
    for slab, block in zip(slabs, (c0, c1, c2, c3)):
        for p in range(planes):
            cour[slab + p] = block[p]

    for index in range(2 * planes):
        z = (2 * (index // planes) + core) * planes + index % planes
        weight = 1.0 + 2.0 * jnp.full((rows, lanes), z, jnp.int32).astype(jnp.float32) / (4 * planes - 1)
        last[index] = weight / (12.0 * cour[z])

    cell = sources[chip_here]
    source_z, x, lane = cell // (rows * lanes), cell // lanes % rows, cell % lanes
    tile = pl.ds(pl.multiple_of(x % groups * 8, 8), 8)
    here = (lax.broadcasted_iota(jnp.int32, (8, lanes), 0) == x // groups) & (
        lax.broadcasted_iota(jnp.int32, (8, lanes), 1) == lane
    )
    source_slab, source_p = source_z // planes, lax.rem(source_z, planes)

    def advance(k, now, then, done):
        @pl.when(k >= 2)
        def _():
            for copy in keep(k - 2, then, done):
                copy.wait()

        def work(z, y_part, chip, p):
            def fetch(j, rows):
                return then[z + j + 2, rows], cour[z + j, rows]

            def finish(j, rows, center, lap, extra):
                old, speed = extra
                if chip is not None:
                    laps[k, p + j, chip, rows] = lap
                then[z + j + 2, rows] = 2.0 * center - old + speed * lap

            laps12(now, z, y_part, fetch, finish)

        cycle = (start[0] + k) % 48
        phase = (jnp.full((8, lanes), cycle, jnp.int32).astype(jnp.float32) - 24.0) / 12.0
        wave = AMPLITUDE * (1.0 - 2.0 * phase * phase) * jnp.exp(-phase * phase)
        strength = jnp.where(here, 12.0 * wave, 0.0)
        moved = cour[source_z, tile, :] * strength

        sweep(core, planes, now, banded, y0, y1, work)

        owned = jnp.where(lax.rem(source_slab, 2) == core, strength, 0.0)
        laps[k, source_p, source_slab // 2, tile, :] += owned
        then[source_z + 2, tile, :] += moved
        for copy in keep(k, then, done):
            copy.start()

    @pl.loop(0, steps // 2)
    def _(pair):
        advance(2 * pair, even, odd, sems_odd)
        advance(2 * pair + 1, odd, even, sems_even)

    for k, field, done in ((steps - 2, odd, sems_odd), (steps - 1, even, sems_even)):
        for copy in keep(k, field, done):
            copy.wait()
    for fetch in fetches:
        fetch.wait()


def inject_kernel(held, history, inject):
    steps, planes_all = history.shape[:2]

    @pl.loop(0, planes_all)
    def _(z):
        count = held[steps, z]
        for k in range(steps):
            inject[k, z] = held[k, z] - count * history[k, z]


def adjoint_kernel(own, mate, over, far, cour, laps, inject, last, keep, send_x, send_y, send_xy, even, odd, total, banded, y0, y1):
    planes, rows, lanes = own.shape[1:]
    steps = laps.shape[0]
    groups = rows // 8
    chip_here, core, slabs = place(planes)
    banded[...] = band(lanes)
    load_blocks(slabs, (own, mate, over, far), odd, even, factor=cour)

    total[...] = jnp.zeros(total.shape, jnp.float32)

    def advance(k, now, then):
        def work(z, y_part, chip, p):
            def fetch(j, rows):
                extra = (then[z + j + 2, rows], cour[z + j, rows], inject[k, z + j, rows])
                if chip is not None:
                    extra += (total[chip * planes + p + j, rows], laps[k, p + j, chip, rows])
                return extra

            def finish(j, rows, center, lap, extra):
                newer = 2.0 * center - extra[0] + extra[1] * (lap - extra[2])
                then[z + j + 2, rows] = newer
                if chip is not None:
                    total[chip * planes + p + j, rows] = extra[3] + newer * extra[4]

            laps12(now, z, y_part, fetch, finish)

        sweep(core, planes, now, banded, y0, y1, work)

    @pl.loop(0, steps // 2)
    def _(pair):
        advance(steps - 1 - 2 * pair, even, odd)
        advance(steps - 2 - 2 * pair, odd, even)

    count = keep.shape[0]
    mine, others = lax.axis_index("shot") % 2 * count, (1 - lax.axis_index("shot") % 2) * count
    here, there = chip_here, 1 - chip_here
    for ref, chip, start in ((keep, here, mine), (send_x, there, mine), (send_y, here, others), (send_xy, there, others)):

        @pl.loop(0, count)
        def _(n):
            p = start + n
            value = total[chip * planes + p] * last[chip * planes + p]
            for i in range(groups):
                ref[n, pl.ds(i, 8, stride=groups), :] = value[i * 8 : (i + 1) * 8]


def square_kernel(mine, by_xy, by_y, by_x, keep, send):
    half = lax.axis_index("shot") // 2 % 2
    count = keep.shape[0]
    for ref, part in ((keep, half), (send, 1 - half)):
        for p in range(count):
            at = part * count + p
            ref[p] = (mine[at] + by_x[at]) + (by_y[at] + by_xy[at])


def add_kernel(mine, other, out):
    out[...] = mine[...] + other[...]


def flip(index, bits):
    result = index
    for bit in (1, 2):
        if bits & bit:
            result = jnp.where(index // bit % 2 == 1, result - bit, result + bit)
    return result


def after_kernel(earlier, value, *outs):
    if len(outs) == 1:
        outs[0][...] = value[...]
    else:
        for n, out in enumerate(outs):
            out[...] = value[n]


def after(earlier, value, parts=1):
    vmem, anywhere = pl.BlockSpec(memory_space=pltpu.VMEM), pl.BlockSpec(memory_space=pl.ANY)
    shape = value.shape if parts == 1 else value.shape[1:]
    results = pl.pallas_call(
        after_kernel,
        in_specs=[anywhere, vmem],
        out_specs=[vmem] * parts,
        out_shape=[jax.ShapeDtypeStruct(shape, jnp.float32)] * parts,
        compiler_params=pltpu.CompilerParams(vmem_limit_bytes=4 * 2**20),
        name="after",
    )(earlier, value)
    return results[0] if parts == 1 else results


def arrange_kernel(mine, other, out):
    y = lax.axis_index("shot") % 2
    count = mine.shape[0]
    out[pl.ds(y * count, count)] = mine[...]
    out[pl.ds((1 - y) * count, count)] = other[...]


def first_plane(shot, planes):
    return (shot % 2) * (planes // 2) + (shot // 2 % 2) * (planes // 4)


def sums_kernel(mine, other, momentum, data, sums):
    count, rows, lanes = mine.shape
    planes = momentum.shape[0]
    chip, core = lax.axis_index("chip"), lax.axis_index("core")
    first = first_plane(lax.axis_index("shot"), planes)
    parts = [jnp.zeros((rows, lanes), jnp.float32)] * 4
    for j in range(count):
        scaled = mine[j] + other[j]
        data[j * rows : (j + 1) * rows] = scaled
        z = (2 * chip + core) * planes + first + j
        weight = 1.0 + 2.0 * jnp.full((1, lanes), z, jnp.int32).astype(jnp.float32) / (4 * planes - 1)
        moment = momentum[first + j]
        square = scaled * scaled
        terms = (square, weight * moment * moment, weight * moment * scaled, weight * square)
        parts = [part + term for part, term in zip(parts, terms)]

    def total(value):
        by_lane = jnp.sum(value, axis=0, keepdims=True)
        return jnp.broadcast_to(jnp.sum(by_lane, axis=1, keepdims=True), (1, lanes))

    value = jnp.concatenate([total(part) for part in parts] + [jnp.zeros((4, lanes), jnp.float32)], 0)
    data[count * rows :] = value
    sums[...] = value


def join_kernel(mine, other, s0, s1, s2, data, sums):
    rows = mine.shape[0] - 8
    data[0:rows] = mine[0:rows]
    data[rows : 2 * rows] = other[0:rows]
    value = (s0[...] + s1[...]) + (other[rows:] + s2[...])
    data[2 * rows :] = value
    sums[...] = value


def finish_kernel(mine, other, momentum, s0, s1, s2, out, kinetic):
    planes, rows, lanes = momentum.shape
    cells = 4.0 * planes * rows * lanes
    shot = lax.axis_index("shot")
    sums = (s0[...] + s1[...]) + (other[planes // 2 * rows :] + s2[...])
    factor = lax.rsqrt(sums[0:1] / cells + EPSILON)
    energy = 0.5 * (sums[1:2] - factor * sums[2:3] + 0.25 * factor * factor * sums[3:4]) / cells
    kinetic[0] = energy[0, 0]
    step = 0.5 * factor
    quarter = planes // 4
    for part, group in ((mine, shot), (other, flip(shot, 1))):
        for number, first in enumerate((first_plane(group, planes), first_plane(flip(group, 2), planes))):
            for j in range(quarter):
                at = (number * quarter + j) * rows
                out[first + j] = momentum[first + j] - step * part[at : at + rows]


def local(kernel, outs, *arrays):
    vmem = pl.BlockSpec(memory_space=pltpu.VMEM)
    shapes = [jax.ShapeDtypeStruct(shape, jnp.float32) for shape in outs]
    single = len(outs) == 1
    return pl.pallas_call(
        kernel,
        in_specs=[vmem] * len(arrays),
        out_specs=vmem if single else [vmem] * len(outs),
        out_shape=shapes[0] if single else shapes,
        compiler_params=pltpu.CompilerParams(vmem_limit_bytes=4 * 2**20),
        name=kernel.__name__,
    )(*arrays)


def exchange(value, bits):
    axes = ("shot", "chip", "core")
    return lax.ppermute(value, axes, [(i, i ^ bits) for i in range(lax.axis_size(axes))])


CORE, CHIP, Y, NEAR_Z, FAR_Z = 1, 2, 4, 8, 16


def whole_shards(
    courant_sq, momentum, fwd_prev, fwd_cur, adj_next, adj_cur, observed, src_cells, rec_cells, ckpt_step
):
    _, planes, rows_x, rows_y = fwd_cur.shape
    steps = observed.shape[1]
    planes_all = 4 * planes
    cells_all = planes_all * rows_x * rows_y
    vmem, smem = pl.BlockSpec(memory_space=pltpu.VMEM), pl.BlockSpec(memory_space=pltpu.SMEM)

    hbm = pl.BlockSpec(memory_space=pltpu.HBM)
    outgoing, c0, piece = pl.pallas_call(
        first_kernel,
        in_specs=[hbm] * 3,
        out_specs=[vmem] * 3,
        out_shape=[
            jax.ShapeDtypeStruct((2, planes, rows_x, rows_y), jnp.float32),
            jax.ShapeDtypeStruct(courant_sq.shape, jnp.float32),
            jax.ShapeDtypeStruct((planes // 2, rows_x, rows_y), jnp.float32),
        ],
        scratch_shapes=[
            pltpu.VMEM((2, planes, rows_x, rows_y), jnp.float32),
            pltpu.VMEM(courant_sq.shape, jnp.float32),
            pltpu.SemaphoreType.DMA((3,)),
        ],
        compiler_params=pltpu.CompilerParams(vmem_limit_bytes=63 * 2**20),
        name="first_to_cross",
    )(fwd_prev, fwd_cur, courant_sq)

    over = exchange(outgoing, CHIP)
    piece = exchange(piece, CHIP)

    placed, mark = scatter(rec_cells, observed, planes_all, rows_x, rows_y)
    placed = placed.reshape(steps + 1, planes_all, rows_x, rows_y)

    piece = after(mark, piece)
    adj_outgoing, adj_own, own = pick(
        (adj_next, adj_cur, True), (adj_next, adj_cur, False), (fwd_prev, fwd_cur, False), earlier=piece
    )
    mate = exchange(own, CORE)
    c2 = local(arrange_kernel, [courant_sq.shape], piece, exchange(piece, Y))
    c1, c3 = exchange(c0, CORE), exchange(c2, CORE)
    over = after(c2, over, parts=2)
    far = [exchange(field, CORE) for field in over]
    adj_over = exchange(adj_outgoing, CHIP)
    adj_mate = exchange(adj_own, CORE)

    scratch = pltpu.VMEM((planes_all + 4, rows_x + 8, rows_y), jnp.float32)
    y_scratch = pltpu.VMEM((BATCH * rows_x, rows_y), jnp.float32)
    step_scratch = [scratch, scratch, pltpu.VMEM((2 * rows_y, rows_y), jnp.bfloat16), y_scratch, y_scratch]
    params = pltpu.CompilerParams(vmem_limit_bytes=6 * 2**20)
    cost = pl.CostEstimate(flops=30 * steps * cells_all, bytes_accessed=16 * steps * cells_all, transcendentals=0)
    laps, history, held, cour, last = pl.pallas_call(
        forward_kernel,
        in_specs=[smem, smem] + [vmem] * 10 + [pl.BlockSpec(memory_space=pltpu.HBM)],
        out_specs=[vmem] * 5,
        out_shape=[
            jax.ShapeDtypeStruct((steps, planes, 2, rows_x, rows_y), jnp.float32),
            jax.ShapeDtypeStruct((steps, planes_all, rows_x, rows_y), jnp.float32),
            jax.ShapeDtypeStruct((steps + 1, planes_all, rows_x, rows_y), jnp.float32),
            jax.ShapeDtypeStruct((planes_all, rows_x, rows_y), jnp.float32),
            jax.ShapeDtypeStruct((2 * planes, rows_x, rows_y), jnp.float32),
        ],
        scratch_shapes=step_scratch
        + [
            pltpu.SemaphoreType.DMA((steps + 1, 4)),
            pltpu.SemaphoreType.DMA((4,)),
            pltpu.SemaphoreType.DMA((4,)),
        ],
        compiler_params=pltpu.CompilerParams(vmem_limit_bytes=25 * 2**20),
        cost_estimate=pl.CostEstimate(flops=1000, bytes_accessed=1000, transcendentals=0),
        name="forward_steps",
    )(ckpt_step[None], src_cells, own, mate, *over, *far, c0, c1, c2, c3, placed)

    adj_over = after(laps, adj_over)
    adj_far = exchange(adj_over, CORE)
    inject = pl.pallas_call(
        inject_kernel,
        in_specs=[vmem] * 2,
        out_specs=vmem,
        out_shape=jax.ShapeDtypeStruct(history.shape, jnp.float32),
        compiler_params=pltpu.CompilerParams(vmem_limit_bytes=4 * 2**20),
        name="inject",
    )(held, history)
    slab = jax.ShapeDtypeStruct(courant_sq.shape, jnp.float32)
    half, quarter = (planes // 2, rows_x, rows_y), (planes // 4, rows_x, rows_y)
    keep, send_x, send_y, send_xy = pl.pallas_call(
        adjoint_kernel,
        in_specs=[vmem] * 8,
        out_specs=[vmem] * 4,
        out_shape=[jax.ShapeDtypeStruct(half, jnp.float32)] * 4,
        scratch_shapes=step_scratch[:2] + [pltpu.VMEM((2 * planes, rows_x, rows_y), jnp.float32)] + step_scratch[2:],
        compiler_params=params,
        cost_estimate=cost,
        name="adjoint_steps",
    )(adj_own, adj_mate, adj_over, adj_far, cour, laps, inject, last)

    by_xy, by_x, by_y = exchange(send_xy, CHIP + Y), exchange(send_x, CHIP), exchange(send_y, Y)
    keep, send = local(square_kernel, [quarter] * 2, keep, by_xy, by_y, by_x)
    part = local(add_kernel, [quarter], keep, exchange(send, NEAR_Z))
    rows, sums_shape = planes // 4 * rows_x, (8, rows_y)
    data, sums = local(sums_kernel, [(rows + 8, rows_y), sums_shape], part, exchange(part, FAR_Z), momentum)

    received = exchange(data, NEAR_Z)
    others = [exchange(sums, CORE), exchange(sums, NEAR_Z + CORE)]
    data, sums = local(join_kernel, [(2 * rows + 8, rows_y), sums_shape], data, received, sums, *others)
    received = exchange(data, Y)
    others = [exchange(sums, CHIP), exchange(sums, Y + CHIP)]
    momentum_half, kinetic = pl.pallas_call(
        finish_kernel,
        in_specs=[vmem] * 6,
        out_specs=[vmem, smem],
        out_shape=[jax.ShapeDtypeStruct(momentum.shape, jnp.float32), jax.ShapeDtypeStruct((1,), jnp.float32)],
        compiler_params=pltpu.CompilerParams(vmem_limit_bytes=4 * 2**20),
        name="finish",
    )(data, received, momentum, sums, *others)
    return momentum_half, kinetic[0]


def solution(mesh):
    shots, slabs = mesh.shape["shot"], mesh.shape["depth"]

    def placed(depth):
        field = P("shot", depth, None, None)
        slab = P(depth, None, None)
        inputs = (slab, slab, field, field, field, field, P("shot", None, None), P("shot"), P("shot", None), P())
        return dict(in_specs=inputs, out_specs=(slab, P()), check_vma=False)

    slab_plan = jax.shard_map(slab_shards, mesh=mesh, **placed("depth"))
    if slabs != 4 or shots != 8:
        return slab_plan
    chips = Mesh(mesh.devices.reshape(shots, 2, 2), ("shot", "chip", "core"))
    whole_plan = jax.shard_map(whole_shards, mesh=chips, **placed(("chip", "core")))

    def run(courant_sq, momentum, fwd_prev, *rest):
        total, planes, rows_x, rows_y = fwd_prev.shape
        steps = rest[3].shape[1]
        fits = total == 2 * shots and planes == 4 * shots and rows_y == 128 and rows_x % 16 == 0 and steps % 2 == 0
        plan = whole_plan if fits else slab_plan
        return plan(courant_sq, momentum, fwd_prev, *rest)

    return run
```

```python
import functools

import jax
import jax.numpy as jnp
from jax import lax
from jax.experimental import pallas as pl
from jax.experimental.pallas import tpu as pltpu
from jax.sharding import Mesh
from jax.sharding import PartitionSpec as P

CENTER = -2.5
NEAR = 4.0 / 3.0
FAR = -1.0 / 12.0
AMPLITUDE = 100.0
EPSILON = 1e-06


def with_halo(value, sides, width):
    for axis, dim in sides:
        size, length = (lax.axis_size(axis), value.shape[dim])
        up = [(i, (i + 1) % size) for i in range(size - 1)]
        down = [(j, i) for i, j in up]
        last = lax.slice_in_dim(value, length - width, length, axis=dim)
        leading = lax.slice_in_dim(value, 0, width, axis=dim)
        before = lax.ppermute(last, axis, up)
        after = lax.ppermute(leading, axis, down)
        value = jnp.concatenate([before, value, after], axis=dim)
    return value


def laplace(padded):
    lateral = jnp.pad(padded[:, 2:-2], ((0, 0), (0, 0), (2, 2), (2, 2)))
    center = padded[:, 2:-2]
    along_z = NEAR * (padded[:, 1:-3] + padded[:, 3:-1]) + FAR * (padded[:, :-4] + padded[:, 4:])
    along_x = NEAR * (lateral[:, :, 1:-3, 2:-2] + lateral[:, :, 3:-1, 2:-2]) + FAR * (
        lateral[:, :, :-4, 2:-2] + lateral[:, :, 4:, 2:-2]
    )
    along_y = NEAR * (lateral[:, :, 2:-2, 1:-3] + lateral[:, :, 2:-2, 3:-1]) + FAR * (
        lateral[:, :, 2:-2, :-4] + lateral[:, :, 2:-2, 4:]
    )
    return 3.0 * CENTER * center + along_z + along_x + along_y


def locate(field, cell_ids, first_plane):
    shot_count, planes, rows_x, rows_y = field.shape
    plane_cells = rows_x * rows_y
    local_index = cell_ids - first_plane * plane_cells
    inside = (local_index >= 0) & (local_index < planes * plane_cells)
    target = jnp.where(inside, local_index, 0)
    return (inside, target)


def inject(field, cell_ids, values, first_plane):
    shot_count = field.shape[0]
    inside, target = locate(field, cell_ids, first_plane)
    amount = jnp.where(inside, values, jnp.zeros_like(values))
    flattened = field.reshape(shot_count, -1)
    lanes = jnp.arange(shot_count)[:, None]
    flattened = flattened.at[lanes, target].add(amount)
    return flattened.reshape(field.shape)


def sample(field, cell_ids, first_plane):
    shot_count = field.shape[0]
    inside, target = locate(field, cell_ids, first_plane)
    values = jnp.take_along_axis(field.reshape(shot_count, -1), target, axis=1)
    return jnp.where(inside, values, jnp.zeros_like(values))


def wave_value(start, step):
    cycle = jnp.mod(start + jnp.int32(step), jnp.int32(48))
    phase = (cycle.astype(jnp.float32) - 24.0) / 12.0
    return AMPLITUDE * (1.0 - 2.0 * phase * phase) * jnp.exp(-phase * phase)


def statistics(scaled, moment, weight, cells_all):
    grand_total = lax.psum(jnp.sum(scaled * scaled), ("shot", "depth"))
    factor = lax.rsqrt(grand_total / cells_all + EPSILON)
    halfway = moment - 0.5 * factor * scaled
    energy = lax.psum(jnp.sum(weight * halfway * halfway), ("shot", "depth"))
    return (factor, 0.5 * energy / cells_all)


def slab_shards(
    courant_sq,
    momentum,
    fwd_prev,
    fwd_cur,
    adj_next,
    adj_cur,
    observed,
    src_cells,
    rec_cells,
    ckpt_step,
):
    shot_count, planes, rows_x, rows_y = fwd_cur.shape
    steps_all = observed.shape[1]
    first_plane = lax.axis_index("depth") * planes
    total_planes = planes * lax.axis_size("depth")
    cells_all = total_planes * rows_x * rows_y
    sources = src_cells[:, None]
    older, current = (fwd_prev, fwd_cur)
    laplacians = []
    misfits = []
    for step in range(steps_all):
        padded = with_halo(current, (("depth", 1),), 2)
        strength = jnp.full(sources.shape, wave_value(ckpt_step, step), jnp.float32)
        laplacian = inject(laplace(padded), sources, strength, first_plane)
        newer = 2.0 * current - older + courant_sq * laplacian
        misfits.append(sample(newer, rec_cells, first_plane) - observed[:, step, :])
        laplacians.append(laplacian)
        older, current = (current, newer)
    adj_later, adj_now = (adj_next, adj_cur)
    gradient = jnp.zeros((planes, rows_x, rows_y), jnp.float32)
    for step in reversed(range(steps_all)):
        padded = with_halo(courant_sq * adj_now, (("depth", 1),), 2)
        adj_new = 2.0 * adj_now - adj_later + laplace(padded)
        adj_new = inject(adj_new, rec_cells, misfits[step], first_plane)
        gradient = gradient + jnp.sum(adj_new * laplacians[step], axis=0)
        adj_later, adj_now = (adj_now, adj_new)
    depths = (first_plane + jnp.arange(planes)).astype(jnp.float32)
    weight = (1.0 + 2.0 * depths / (total_planes - 1))[:, None, None]
    share_rows = rows_x // lax.axis_size("shot")
    offset = lax.axis_index("shot") * share_rows
    moment_share = lax.dynamic_slice_in_dim(momentum, offset, share_rows, 1)
    gradient = lax.psum(gradient, "shot")
    scaled = weight * gradient
    scaled_share = lax.dynamic_slice_in_dim(scaled, offset, share_rows, 1)
    factor, kinetic = statistics(scaled_share, moment_share, weight, cells_all)
    momentum_half = momentum - 0.5 * factor * scaled
    return (momentum_half, kinetic)


def interleave(dst, slab, src, factor=None):
    planes, rows = src.shape[0], src.shape[1]
    groups = rows // 8

    @pl.loop(0, planes)
    def _(p):
        for i in range(groups):
            value = src[p, pl.ds(i, 8, stride=groups), :]
            if factor is not None:
                value = value * factor
            dst[(*slab, p, pl.ds(i * 8, 8), slice(None))] = value


def pick_kernel(across, *refs):
    count = len(across)
    fields, outs, (held, sems) = refs[: 2 * count], refs[2 * count : 3 * count], refs[3 * count :]
    chip = lax.axis_index("chip")
    copies = []
    for n in range(2 * count):
        shot = 1 - chip if across[n // 2] else chip
        copies.append(pltpu.make_async_copy(fields[n].at[shot], held.at[n], sems.at[n]))
        copies[-1].start()
    for n in range(2 * count):
        copies[n].wait()
        interleave(outs[n // 2], (n % 2,), held.at[n])


def pick(*pairs, earlier):
    plain = functools.partial(pick_kernel, tuple(pair[2] for pair in pairs))
    fields = [field for pair in pairs for field in pair[:2]]
    shape = fields[0].shape[1:]
    vmem, hbm = pl.BlockSpec(memory_space=pltpu.VMEM), pl.BlockSpec(memory_space=pltpu.HBM)
    return pl.pallas_call(
        lambda earlier, *refs: plain(*refs),
        in_specs=[pl.BlockSpec(memory_space=pl.ANY)] + [hbm] * len(fields),
        out_specs=[vmem] * len(pairs),
        out_shape=[jax.ShapeDtypeStruct((2, *shape), jnp.float32)] * len(pairs),
        scratch_shapes=[pltpu.VMEM((len(fields), *shape), jnp.float32), pltpu.SemaphoreType.DMA((len(fields),))],
        compiler_params=pltpu.CompilerParams(vmem_limit_bytes=4 * 2**20),
        name="pick",
    )(earlier, *fields)


def first_kernel(first, second, courant, outgoing, whole, piece, held, held_courant, sems):
    shot = 1 - lax.axis_index("chip")
    copies = [
        pltpu.make_async_copy(first.at[shot], held.at[0], sems.at[0]),
        pltpu.make_async_copy(second.at[shot], held.at[1], sems.at[1]),
        pltpu.make_async_copy(courant, held_courant, sems.at[2]),
    ]
    for copy in copies:
        copy.start()
    for n in range(2):
        copies[n].wait()
        interleave(outgoing, (n,), held.at[n])
    copies[2].wait()
    interleave(whole, (), held_courant, 1.0 / 12.0)
    count = piece.shape[0]
    piece[...] = whole[pl.ds(lax.axis_index("shot") % 2 * count, count)]


def band(lanes):
    near = jnp.abs(lax.broadcasted_iota(jnp.int32, (2 * lanes, lanes), 0) % lanes - lax.broadcasted_iota(jnp.int32, (2 * lanes, lanes), 1))
    return jnp.where(near == 0, -90.0, jnp.where(near == 1, 16.0, jnp.where(near == 2, -1.0, 0.0))).astype(jnp.bfloat16)


def along_y(field, z, banded, out):
    rows, lanes = field.shape[1] - 8, field.shape[2]
    whole = field[pl.ds(z + 2, BATCH), 0:rows].reshape(BATCH * rows, lanes)
    high = whole.astype(jnp.bfloat16)
    low = (whole - high.astype(jnp.float32)).astype(jnp.bfloat16)
    out[...] = jnp.dot(jnp.concatenate([high, low], 1), banded[...], preferred_element_type=jnp.float32)


def laps12(field, z, y_part, fetch, finish):
    rows, lanes = field.shape[1] - 8, field.shape[2]
    groups = rows // 8
    sub = lax.broadcasted_iota(jnp.int32, (8, lanes), 0)

    def later(block):
        return jnp.where(sub < 7, pltpu.roll(block, 7, 0), 0.0)

    def earlier(block):
        return jnp.where(sub > 0, pltpu.roll(block, 1, 0), 0.0)

    for base in range(0, BATCH, PLANES):
        held = {}

        def tile(j, i):
            if (j, i) not in held:
                if i < 0:
                    held[j, i] = earlier(tile(j, i + groups))
                elif i >= groups:
                    held[j, i] = later(tile(j, i - groups))
                else:
                    held[j, i] = field[z + j + 2, i * 8 : (i + 1) * 8]
            return held[j, i]

        def load(i):
            found = []
            for j in range(base, base + PLANES):
                center = tile(j, i)
                near = (tile(j, i - 1), tile(j, i + 1), tile(j - 1, i), tile(j + 1, i))
                far = (tile(j, i - 2), tile(j, i + 2), tile(j - 2, i), tile(j + 2, i))
                at = (j * groups + i) * 8
                found.append((center, near, far, y_part[at : at + 8], fetch(j, slice(i * 8, i * 8 + 8))))
            return found

        ready = load(0)
        for i in range(groups):
            upcoming = load(i + 1) if i + 1 < groups else None
            for j, (center, near, far, part, extra) in enumerate(ready):
                near = (near[0] + near[1]) + (near[2] + near[3])
                far = (far[0] + far[1]) + (far[2] + far[3])
                finish(base + j, slice(i * 8, i * 8 + 8), center, 16.0 * near + (part - far), extra)
            ready = upcoming


def scatter_kernel(rows_x, cells_ref, observed_ref, out_ref, mark, row_ref, spread):
    _, steps, receivers = observed_ref.shape
    lanes = out_ref.shape[2]
    tile = out_ref.shape[1]
    groups = rows_x // 8

    @pl.when(pl.program_id(0) == 0)
    def _():
        chip = lax.axis_index("chip")
        cells = cells_ref[pl.ds(chip, 1)]
        x = cells // lanes % rows_x
        row_ref[...] = cells // (rows_x * lanes) * rows_x + x % groups * 8 + x // groups
        on_lanes = jnp.concatenate(
            [
                observed_ref[chip],
                jnp.broadcast_to((cells % lanes).astype(jnp.float32), (8, receivers)),
                jnp.zeros((lanes - steps - 8, receivers), jnp.float32),
            ],
            0,
        )
        columns = on_lanes.T
        lane = lax.broadcasted_iota(jnp.int32, (receivers, lanes), 1).astype(jnp.float32)
        at = lane == columns[:, steps : steps + 1]
        for k in range(steps):
            column = columns[:, k : k + 1]
            high = column.astype(jnp.bfloat16).astype(jnp.float32)
            low = column - high
            cols = pl.ds(k * lanes, lanes)
            spread[0:receivers, cols] = jnp.where(at, high, 0.0).astype(jnp.bfloat16)
            spread[receivers:, cols] = jnp.where(at, low, 0.0).astype(jnp.bfloat16)
        cols = pl.ds(steps * lanes, lanes)
        spread[0:receivers, cols] = jnp.where(at, 1.0, 0.0).astype(jnp.bfloat16)
        spread[receivers:, cols] = jnp.zeros((receivers, lanes), jnp.bfloat16)
        mark[...] = jnp.zeros(mark.shape, jnp.float32)

    ids = lax.broadcasted_iota(jnp.int32, (tile, receivers), 0) + pl.program_id(0) * tile
    chosen = jnp.where(ids == row_ref[...], 1.0, 0.0).astype(jnp.bfloat16)
    total = jnp.dot(jnp.concatenate([chosen, chosen], 1), spread[...], preferred_element_type=jnp.float32)
    for k in range(steps + 1):
        out_ref[k] = total[:, k * lanes : (k + 1) * lanes]


def scatter(rec_cells, observed, planes_all, rows_x, rows_y):
    _, steps, receivers = observed.shape
    rows_all = planes_all * rows_x
    tile = 512
    return pl.pallas_call(
        functools.partial(scatter_kernel, rows_x),
        grid=(rows_all // tile,),
        in_specs=[
            pl.BlockSpec((2, receivers), lambda t: (0, 0)),
            pl.BlockSpec((2, steps, receivers), lambda t: (0, 0, 0)),
        ],
        out_specs=[
            pl.BlockSpec((steps + 1, tile, rows_y), lambda t: (0, t, 0)),
            pl.BlockSpec((8, rows_y), lambda t: (0, 0)),
        ],
        out_shape=[
            jax.ShapeDtypeStruct((steps + 1, rows_all, rows_y), jnp.float32),
            jax.ShapeDtypeStruct((8, rows_y), jnp.float32),
        ],
        scratch_shapes=[
            pltpu.VMEM((1, receivers), jnp.int32),
            pltpu.VMEM((2 * receivers, (steps + 1) * rows_y), jnp.bfloat16),
        ],
        compiler_params=pltpu.CompilerParams(vmem_limit_bytes=56 * 2**20),
        cost_estimate=pl.CostEstimate(
            flops=4 * rows_all * receivers * (steps + 1) * rows_y,
            bytes_accessed=4 * (steps + 1) * rows_all * rows_y,
            transcendentals=0,
        ),
        name="receiver_scatter",
    )(rec_cells, observed)


def place(planes):
    chip, core = lax.axis_index("chip"), lax.axis_index("core")
    slabs = (2 * chip + core, 2 * chip + 1 - core, 2 * (1 - chip) + core, 2 * (1 - chip) + 1 - core)
    return chip, core, [slab * planes for slab in slabs]


def load_blocks(slabs, blocks, first, second, factor=None):
    ends, rows, lanes = first.shape[0], first.shape[1] - 8, first.shape[2]
    planes = (ends - 4) // 4
    for field in (first, second):
        for z in (0, 1, ends - 2, ends - 1):
            field[z, 0:rows] = jnp.zeros((rows, lanes), jnp.float32)
    for slab, block in zip(slabs, blocks):
        pair = block if isinstance(block, tuple) else (block.at[0], block.at[1])
        for p in range(planes):
            values = pair[0][p], pair[1][p]
            if factor is not None:
                speed = factor[slab + p]
                values = values[0] * speed, values[1] * speed
            first[slab + p + 2, 0:rows], second[slab + p + 2, 0:rows] = values


BATCH = 4
PLANES = 2


def sweep(core, planes, field, banded, y_first, y_second, work):
    order = [(chip, owned) for owned in (True, False) for chip in (0, 1)]
    parts = (y_first, y_second)

    def first(chip, owned):
        return (2 * chip + (core if owned else 1 - core)) * planes

    along_y(field, first(*order[0]), banded, y_first)
    for owned in (True, False):
        for chip in (0, 1):
            z = first(chip, owned)
            onward = first(1, owned) if chip == 0 else first(0, False)
            for n in range(planes // BATCH):
                last = n == planes // BATCH - 1
                if not last or chip == 0 or owned:
                    along_y(field, onward if last else z + (n + 1) * BATCH, banded, parts[(n + 1) % 2])
                work(z + n * BATCH, parts[n % 2], chip if owned else None, n * BATCH)


def forward_kernel(
    start, sources, own, mate, over0, over1, far0, far1, large, small, large_mate, small_mate, placed, laps, history, held, cour, last,
    even, odd, banded, y0, y1, sems, sems_even, sems_odd
):
    planes, rows, lanes = own.shape[1:]
    steps = laps.shape[0]
    groups = rows // 8
    chip_here, core, slabs = place(planes)

    fetches = []
    for k in range(steps + 1):
        for n in range(4):
            at = pl.ds(n * planes, planes)
            fetches.append(pltpu.make_async_copy(placed.at[k, at], held.at[k, at], sems.at[k, n]))
            fetches[-1].start()

    def keep(k, field, done):
        for n in range(4):
            source = field.at[pl.ds(n * planes + 2, planes), pl.ds(0, rows)]
            yield pltpu.make_async_copy(source, history.at[k, pl.ds(n * planes, planes)], done.at[n])

    banded[...] = band(lanes)
    load_blocks(slabs, (own, mate, (over0, over1), (far0, far1)), odd, even)
    head = large.shape[0] - planes
    for here, across, first, rest in ((slabs[0], slabs[2], large, small), (slabs[1], slabs[3], large_mate, small_mate)):
        for p in range(planes):
            cour[across + p] = first[p]
            cour[here + p] = first[planes + p] if p < head else rest[p - head]

    for index in range(2 * planes):
        z = (2 * (index // planes) + core) * planes + index % planes
        weight = 1.0 + 2.0 * jnp.full((rows, lanes), z, jnp.int32).astype(jnp.float32) / (4 * planes - 1)
        last[index] = weight / (12.0 * cour[z])

    cell = sources[chip_here]
    source_z, x, lane = cell // (rows * lanes), cell // lanes % rows, cell % lanes
    tile = pl.ds(pl.multiple_of(x % groups * 8, 8), 8)
    here = (lax.broadcasted_iota(jnp.int32, (8, lanes), 0) == x // groups) & (
        lax.broadcasted_iota(jnp.int32, (8, lanes), 1) == lane
    )
    source_slab, source_p = source_z // planes, lax.rem(source_z, planes)

    def advance(k, now, then, done):
        @pl.when(k >= 2)
        def _():
            for copy in keep(k - 2, then, done):
                copy.wait()

        def work(z, y_part, chip, p):
            def fetch(j, rows):
                return then[z + j + 2, rows], cour[z + j, rows]

            def finish(j, rows, center, lap, extra):
                old, speed = extra
                if chip is not None:
                    laps[k, p + j, chip, rows] = lap
                then[z + j + 2, rows] = 2.0 * center - old + speed * lap

            laps12(now, z, y_part, fetch, finish)

        cycle = (start[0] + k) % 48
        phase = (jnp.full((8, lanes), cycle, jnp.int32).astype(jnp.float32) - 24.0) / 12.0
        wave = AMPLITUDE * (1.0 - 2.0 * phase * phase) * jnp.exp(-phase * phase)
        strength = jnp.where(here, 12.0 * wave, 0.0)
        moved = cour[source_z, tile, :] * strength

        sweep(core, planes, now, banded, y0, y1, work)

        owned = jnp.where(lax.rem(source_slab, 2) == core, strength, 0.0)
        laps[k, source_p, source_slab // 2, tile, :] += owned
        then[source_z + 2, tile, :] += moved
        for copy in keep(k, then, done):
            copy.start()

    @pl.loop(0, steps // 2)
    def _(pair):
        advance(2 * pair, even, odd, sems_odd)
        advance(2 * pair + 1, odd, even, sems_even)

    for k, field, done in ((steps - 2, odd, sems_odd), (steps - 1, even, sems_even)):
        for copy in keep(k, field, done):
            copy.wait()
    for fetch in fetches:
        fetch.wait()


def inject_kernel(held, history, inject):
    steps, planes_all = history.shape[:2]

    @pl.loop(0, planes_all)
    def _(z):
        count = held[steps, z]
        for k in range(steps):
            inject[k, z] = held[k, z] - count * history[k, z]


def adjoint_kernel(own, mate, over, far, cour, laps, inject, last, keep, send_x, send_y, send_xy, even, odd, total, banded, y0, y1):
    planes, rows, lanes = own.shape[1:]
    steps = laps.shape[0]
    groups = rows // 8
    chip_here, core, slabs = place(planes)
    banded[...] = band(lanes)
    load_blocks(slabs, (own, mate, over, far), odd, even, factor=cour)

    total[...] = jnp.zeros(total.shape, jnp.float32)

    def advance(k, now, then):
        def work(z, y_part, chip, p):
            def fetch(j, rows):
                extra = (then[z + j + 2, rows], cour[z + j, rows], inject[k, z + j, rows])
                if chip is not None:
                    extra += (total[chip * planes + p + j, rows], laps[k, p + j, chip, rows])
                return extra

            def finish(j, rows, center, lap, extra):
                newer = 2.0 * center - extra[0] + extra[1] * (lap - extra[2])
                then[z + j + 2, rows] = newer
                if chip is not None:
                    total[chip * planes + p + j, rows] = extra[3] + newer * extra[4]

            laps12(now, z, y_part, fetch, finish)

        sweep(core, planes, now, banded, y0, y1, work)

    @pl.loop(0, steps // 2)
    def _(pair):
        advance(steps - 1 - 2 * pair, even, odd)
        advance(steps - 2 - 2 * pair, odd, even)

    count = keep.shape[0]
    mine, others = lax.axis_index("shot") % 2 * count, (1 - lax.axis_index("shot") % 2) * count
    here, there = chip_here, 1 - chip_here
    for ref, chip, start in ((keep, here, mine), (send_x, there, mine), (send_y, here, others), (send_xy, there, others)):

        @pl.loop(0, count)
        def _(n):
            p = start + n
            value = total[chip * planes + p] * last[chip * planes + p]
            for i in range(groups):
                ref[n, pl.ds(i, 8, stride=groups), :] = value[i * 8 : (i + 1) * 8]


def square_kernel(mine, by_xy, by_y, by_x, keep, send):
    half = lax.axis_index("shot") // 2 % 2
    count = keep.shape[0]
    for ref, part in ((keep, half), (send, 1 - half)):
        for p in range(count):
            at = part * count + p
            ref[p] = (mine[at] + by_x[at]) + (by_y[at] + by_xy[at])


def add_kernel(mine, other, out):
    out[...] = mine[...] + other[...]


def flip(index, bits):
    result = index
    for bit in (1, 2):
        if bits & bit:
            result = jnp.where(index // bit % 2 == 1, result - bit, result + bit)
    return result


def after_kernel(earlier, value, *outs):
    if len(outs) == 1:
        outs[0][...] = value[...]
    else:
        for n, out in enumerate(outs):
            out[...] = value[n]


def after(earlier, value, parts=1):
    vmem, anywhere = pl.BlockSpec(memory_space=pltpu.VMEM), pl.BlockSpec(memory_space=pl.ANY)
    shape = value.shape if parts == 1 else value.shape[1:]
    results = pl.pallas_call(
        after_kernel,
        in_specs=[anywhere, vmem],
        out_specs=[vmem] * parts,
        out_shape=[jax.ShapeDtypeStruct(shape, jnp.float32)] * parts,
        compiler_params=pltpu.CompilerParams(vmem_limit_bytes=4 * 2**20),
        name="after",
    )(earlier, value)
    return results[0] if parts == 1 else results


def arrange_kernel(own, mine, other, large, small):
    y = lax.axis_index("shot") % 2
    count, planes = mine.shape[0], own.shape[0]
    head = planes - small.shape[0]
    large[pl.ds(y * count, count)] = mine[...]
    large[pl.ds((1 - y) * count, count)] = other[...]
    large[planes:] = own[0:head]
    small[...] = own[head:]


def first_plane(shot, planes):
    return (shot % 2) * (planes // 2) + (shot // 2 % 2) * (planes // 4)


def sums_kernel(mine, other, momentum, data, sums):
    count, rows, lanes = mine.shape
    planes = momentum.shape[0]
    chip, core = lax.axis_index("chip"), lax.axis_index("core")
    first = first_plane(lax.axis_index("shot"), planes)
    parts = [jnp.zeros((rows, lanes), jnp.float32)] * 4
    for j in range(count):
        scaled = mine[j] + other[j]
        data[j * rows : (j + 1) * rows] = scaled
        z = (2 * chip + core) * planes + first + j
        weight = 1.0 + 2.0 * jnp.full((1, lanes), z, jnp.int32).astype(jnp.float32) / (4 * planes - 1)
        moment = momentum[first + j]
        square = scaled * scaled
        terms = (square, weight * moment * moment, weight * moment * scaled, weight * square)
        parts = [part + term for part, term in zip(parts, terms)]

    def total(value):
        by_lane = jnp.sum(value, axis=0, keepdims=True)
        return jnp.broadcast_to(jnp.sum(by_lane, axis=1, keepdims=True), (1, lanes))

    value = jnp.concatenate([total(part) for part in parts] + [jnp.zeros((4, lanes), jnp.float32)], 0)
    data[count * rows :] = value
    sums[...] = value


def join_kernel(mine, other, s0, s1, s2, data, sums):
    rows = mine.shape[0] - 8
    data[0:rows] = mine[0:rows]
    data[rows : 2 * rows] = other[0:rows]
    value = (s0[...] + s1[...]) + (other[rows:] + s2[...])
    data[2 * rows :] = value
    sums[...] = value


def finish_kernel(mine, other, momentum, s0, s1, s2, out, kinetic):
    planes, rows, lanes = momentum.shape
    cells = 4.0 * planes * rows * lanes
    shot = lax.axis_index("shot")
    sums = (s0[...] + s1[...]) + (other[planes // 2 * rows :] + s2[...])
    factor = lax.rsqrt(sums[0:1] / cells + EPSILON)
    energy = 0.5 * (sums[1:2] - factor * sums[2:3] + 0.25 * factor * factor * sums[3:4]) / cells
    kinetic[0] = energy[0, 0]
    step = 0.5 * factor
    quarter = planes // 4
    for part, group in ((mine, shot), (other, flip(shot, 1))):
        for number, first in enumerate((first_plane(group, planes), first_plane(flip(group, 2), planes))):
            for j in range(quarter):
                at = (number * quarter + j) * rows
                out[first + j] = momentum[first + j] - step * part[at : at + rows]


def local(kernel, outs, *arrays):
    vmem = pl.BlockSpec(memory_space=pltpu.VMEM)
    shapes = [jax.ShapeDtypeStruct(shape, jnp.float32) for shape in outs]
    single = len(outs) == 1
    return pl.pallas_call(
        kernel,
        in_specs=[vmem] * len(arrays),
        out_specs=vmem if single else [vmem] * len(outs),
        out_shape=shapes[0] if single else shapes,
        compiler_params=pltpu.CompilerParams(vmem_limit_bytes=4 * 2**20),
        name=kernel.__name__,
    )(*arrays)


def exchange(value, bits):
    axes = ("shot", "chip", "core")
    return lax.ppermute(value, axes, [(i, i ^ bits) for i in range(lax.axis_size(axes))])


CORE, CHIP, Y, NEAR_Z, FAR_Z = 1, 2, 4, 8, 16


def whole_shards(
    courant_sq, momentum, fwd_prev, fwd_cur, adj_next, adj_cur, observed, src_cells, rec_cells, ckpt_step
):
    _, planes, rows_x, rows_y = fwd_cur.shape
    steps = observed.shape[1]
    planes_all = 4 * planes
    cells_all = planes_all * rows_x * rows_y
    vmem, smem = pl.BlockSpec(memory_space=pltpu.VMEM), pl.BlockSpec(memory_space=pltpu.SMEM)

    hbm = pl.BlockSpec(memory_space=pltpu.HBM)
    outgoing, c0, piece = pl.pallas_call(
        first_kernel,
        in_specs=[hbm] * 3,
        out_specs=[vmem] * 3,
        out_shape=[
            jax.ShapeDtypeStruct((2, planes, rows_x, rows_y), jnp.float32),
            jax.ShapeDtypeStruct(courant_sq.shape, jnp.float32),
            jax.ShapeDtypeStruct((planes // 2, rows_x, rows_y), jnp.float32),
        ],
        scratch_shapes=[
            pltpu.VMEM((2, planes, rows_x, rows_y), jnp.float32),
            pltpu.VMEM(courant_sq.shape, jnp.float32),
            pltpu.SemaphoreType.DMA((3,)),
        ],
        compiler_params=pltpu.CompilerParams(vmem_limit_bytes=63 * 2**20),
        name="first_to_cross",
    )(fwd_prev, fwd_cur, courant_sq)

    over = exchange(outgoing, CHIP)
    piece = exchange(piece, CHIP)

    placed, mark = scatter(rec_cells, observed, planes_all, rows_x, rows_y)
    placed = placed.reshape(steps + 1, planes_all, rows_x, rows_y)

    piece = after(mark, piece)
    adj_outgoing, adj_own, own = pick(
        (adj_next, adj_cur, True), (adj_next, adj_cur, False), (fwd_prev, fwd_cur, False), earlier=piece
    )
    mate = exchange(own, CORE)
    head = planes * 5 // 8
    large, small = local(
        arrange_kernel,
        [(planes + head, rows_x, rows_y), (planes - head, rows_x, rows_y)],
        c0,
        piece,
        exchange(piece, Y),
    )
    speeds = [large, small, exchange(large, CORE), exchange(small, CORE)]
    over = after(large, over, parts=2)
    far = [exchange(field, CORE) for field in over]
    adj_over = exchange(adj_outgoing, CHIP)
    adj_mate = exchange(adj_own, CORE)

    scratch = pltpu.VMEM((planes_all + 4, rows_x + 8, rows_y), jnp.float32)
    y_scratch = pltpu.VMEM((BATCH * rows_x, rows_y), jnp.float32)
    step_scratch = [scratch, scratch, pltpu.VMEM((2 * rows_y, rows_y), jnp.bfloat16), y_scratch, y_scratch]
    params = pltpu.CompilerParams(vmem_limit_bytes=6 * 2**20)
    cost = pl.CostEstimate(flops=30 * steps * cells_all, bytes_accessed=16 * steps * cells_all, transcendentals=0)
    laps, history, held, cour, last = pl.pallas_call(
        forward_kernel,
        in_specs=[smem, smem] + [vmem] * 10 + [pl.BlockSpec(memory_space=pltpu.HBM)],
        out_specs=[vmem] * 5,
        out_shape=[
            jax.ShapeDtypeStruct((steps, planes, 2, rows_x, rows_y), jnp.float32),
            jax.ShapeDtypeStruct((steps, planes_all, rows_x, rows_y), jnp.float32),
            jax.ShapeDtypeStruct((steps + 1, planes_all, rows_x, rows_y), jnp.float32),
            jax.ShapeDtypeStruct((planes_all, rows_x, rows_y), jnp.float32),
            jax.ShapeDtypeStruct((2 * planes, rows_x, rows_y), jnp.float32),
        ],
        scratch_shapes=step_scratch
        + [
            pltpu.SemaphoreType.DMA((steps + 1, 4)),
            pltpu.SemaphoreType.DMA((4,)),
            pltpu.SemaphoreType.DMA((4,)),
        ],
        compiler_params=pltpu.CompilerParams(vmem_limit_bytes=25 * 2**20),
        cost_estimate=pl.CostEstimate(flops=1000, bytes_accessed=1000, transcendentals=0),
        name="forward_steps",
    )(ckpt_step[None], src_cells, own, mate, *over, *far, *speeds, placed)

    adj_over = after(laps, adj_over)
    adj_far = exchange(adj_over, CORE)
    inject = pl.pallas_call(
        inject_kernel,
        in_specs=[vmem] * 2,
        out_specs=vmem,
        out_shape=jax.ShapeDtypeStruct(history.shape, jnp.float32),
        compiler_params=pltpu.CompilerParams(vmem_limit_bytes=4 * 2**20),
        name="inject",
    )(held, history)
    slab = jax.ShapeDtypeStruct(courant_sq.shape, jnp.float32)
    half, quarter = (planes // 2, rows_x, rows_y), (planes // 4, rows_x, rows_y)
    keep, send_x, send_y, send_xy = pl.pallas_call(
        adjoint_kernel,
        in_specs=[vmem] * 8,
        out_specs=[vmem] * 4,
        out_shape=[jax.ShapeDtypeStruct(half, jnp.float32)] * 4,
        scratch_shapes=step_scratch[:2] + [pltpu.VMEM((2 * planes, rows_x, rows_y), jnp.float32)] + step_scratch[2:],
        compiler_params=params,
        cost_estimate=cost,
        name="adjoint_steps",
    )(adj_own, adj_mate, adj_over, adj_far, cour, laps, inject, last)

    by_xy, by_x, by_y = exchange(send_xy, CHIP + Y), exchange(send_x, CHIP), exchange(send_y, Y)
    keep, send = local(square_kernel, [quarter] * 2, keep, by_xy, by_y, by_x)
    part = local(add_kernel, [quarter], keep, exchange(send, NEAR_Z))
    rows, sums_shape = planes // 4 * rows_x, (8, rows_y)
    data, sums = local(sums_kernel, [(rows + 8, rows_y), sums_shape], part, exchange(part, FAR_Z), momentum)

    received = exchange(data, NEAR_Z)
    others = [exchange(sums, CORE), exchange(sums, NEAR_Z + CORE)]
    data, sums = local(join_kernel, [(2 * rows + 8, rows_y), sums_shape], data, received, sums, *others)
    received = exchange(data, Y)
    others = [exchange(sums, CHIP), exchange(sums, Y + CHIP)]
    momentum_half, kinetic = pl.pallas_call(
        finish_kernel,
        in_specs=[vmem] * 6,
        out_specs=[vmem, smem],
        out_shape=[jax.ShapeDtypeStruct(momentum.shape, jnp.float32), jax.ShapeDtypeStruct((1,), jnp.float32)],
        compiler_params=pltpu.CompilerParams(vmem_limit_bytes=4 * 2**20),
        name="finish",
    )(data, received, momentum, sums, *others)
    return momentum_half, kinetic[0]


def solution(mesh):
    shots, slabs = mesh.shape["shot"], mesh.shape["depth"]

    def placed(depth):
        field = P("shot", depth, None, None)
        slab = P(depth, None, None)
        inputs = (slab, slab, field, field, field, field, P("shot", None, None), P("shot"), P("shot", None), P())
        return dict(in_specs=inputs, out_specs=(slab, P()), check_vma=False)

    slab_plan = jax.shard_map(slab_shards, mesh=mesh, **placed("depth"))
    if slabs != 4 or shots != 8:
        return slab_plan
    chips = Mesh(mesh.devices.reshape(shots, 2, 2), ("shot", "chip", "core"))
    whole_plan = jax.shard_map(whole_shards, mesh=chips, **placed(("chip", "core")))

    def run(courant_sq, momentum, fwd_prev, *rest):
        total, planes, rows_x, rows_y = fwd_prev.shape
        steps = rest[3].shape[1]
        fits = total == 2 * shots and planes == 4 * shots and rows_y == 128 and rows_x % 16 == 0 and steps % 2 == 0
        plan = whole_plan if fits else slab_plan
        return plan(courant_sq, momentum, fwd_prev, *rest)

    return run
```

```python
import functools

import jax
import jax.numpy as jnp
from jax import lax
from jax.experimental import pallas as pl
from jax.experimental.pallas import tpu as pltpu
from jax.sharding import Mesh
from jax.sharding import PartitionSpec as P

CENTER = -2.5
NEAR = 4.0 / 3.0
FAR = -1.0 / 12.0
AMPLITUDE = 100.0
EPSILON = 1e-06


def with_halo(value, sides, width):
    for axis, dim in sides:
        size, length = (lax.axis_size(axis), value.shape[dim])
        up = [(i, (i + 1) % size) for i in range(size - 1)]
        down = [(j, i) for i, j in up]
        last = lax.slice_in_dim(value, length - width, length, axis=dim)
        leading = lax.slice_in_dim(value, 0, width, axis=dim)
        before = lax.ppermute(last, axis, up)
        after = lax.ppermute(leading, axis, down)
        value = jnp.concatenate([before, value, after], axis=dim)
    return value


def laplace(padded):
    lateral = jnp.pad(padded[:, 2:-2], ((0, 0), (0, 0), (2, 2), (2, 2)))
    center = padded[:, 2:-2]
    along_z = NEAR * (padded[:, 1:-3] + padded[:, 3:-1]) + FAR * (padded[:, :-4] + padded[:, 4:])
    along_x = NEAR * (lateral[:, :, 1:-3, 2:-2] + lateral[:, :, 3:-1, 2:-2]) + FAR * (
        lateral[:, :, :-4, 2:-2] + lateral[:, :, 4:, 2:-2]
    )
    along_y = NEAR * (lateral[:, :, 2:-2, 1:-3] + lateral[:, :, 2:-2, 3:-1]) + FAR * (
        lateral[:, :, 2:-2, :-4] + lateral[:, :, 2:-2, 4:]
    )
    return 3.0 * CENTER * center + along_z + along_x + along_y


def locate(field, cell_ids, first_plane):
    shot_count, planes, rows_x, rows_y = field.shape
    plane_cells = rows_x * rows_y
    local_index = cell_ids - first_plane * plane_cells
    inside = (local_index >= 0) & (local_index < planes * plane_cells)
    target = jnp.where(inside, local_index, 0)
    return (inside, target)


def inject(field, cell_ids, values, first_plane):
    shot_count = field.shape[0]
    inside, target = locate(field, cell_ids, first_plane)
    amount = jnp.where(inside, values, jnp.zeros_like(values))
    flattened = field.reshape(shot_count, -1)
    lanes = jnp.arange(shot_count)[:, None]
    flattened = flattened.at[lanes, target].add(amount)
    return flattened.reshape(field.shape)


def sample(field, cell_ids, first_plane):
    shot_count = field.shape[0]
    inside, target = locate(field, cell_ids, first_plane)
    values = jnp.take_along_axis(field.reshape(shot_count, -1), target, axis=1)
    return jnp.where(inside, values, jnp.zeros_like(values))


def wave_value(start, step):
    cycle = jnp.mod(start + jnp.int32(step), jnp.int32(48))
    phase = (cycle.astype(jnp.float32) - 24.0) / 12.0
    return AMPLITUDE * (1.0 - 2.0 * phase * phase) * jnp.exp(-phase * phase)


def statistics(scaled, moment, weight, cells_all):
    grand_total = lax.psum(jnp.sum(scaled * scaled), ("shot", "depth"))
    factor = lax.rsqrt(grand_total / cells_all + EPSILON)
    halfway = moment - 0.5 * factor * scaled
    energy = lax.psum(jnp.sum(weight * halfway * halfway), ("shot", "depth"))
    return (factor, 0.5 * energy / cells_all)


def slab_shards(
    courant_sq,
    momentum,
    fwd_prev,
    fwd_cur,
    adj_next,
    adj_cur,
    observed,
    src_cells,
    rec_cells,
    ckpt_step,
):
    shot_count, planes, rows_x, rows_y = fwd_cur.shape
    steps_all = observed.shape[1]
    first_plane = lax.axis_index("depth") * planes
    total_planes = planes * lax.axis_size("depth")
    cells_all = total_planes * rows_x * rows_y
    sources = src_cells[:, None]
    older, current = (fwd_prev, fwd_cur)
    laplacians = []
    misfits = []
    for step in range(steps_all):
        padded = with_halo(current, (("depth", 1),), 2)
        strength = jnp.full(sources.shape, wave_value(ckpt_step, step), jnp.float32)
        laplacian = inject(laplace(padded), sources, strength, first_plane)
        newer = 2.0 * current - older + courant_sq * laplacian
        misfits.append(sample(newer, rec_cells, first_plane) - observed[:, step, :])
        laplacians.append(laplacian)
        older, current = (current, newer)
    adj_later, adj_now = (adj_next, adj_cur)
    gradient = jnp.zeros((planes, rows_x, rows_y), jnp.float32)
    for step in reversed(range(steps_all)):
        padded = with_halo(courant_sq * adj_now, (("depth", 1),), 2)
        adj_new = 2.0 * adj_now - adj_later + laplace(padded)
        adj_new = inject(adj_new, rec_cells, misfits[step], first_plane)
        gradient = gradient + jnp.sum(adj_new * laplacians[step], axis=0)
        adj_later, adj_now = (adj_now, adj_new)
    depths = (first_plane + jnp.arange(planes)).astype(jnp.float32)
    weight = (1.0 + 2.0 * depths / (total_planes - 1))[:, None, None]
    share_rows = rows_x // lax.axis_size("shot")
    offset = lax.axis_index("shot") * share_rows
    moment_share = lax.dynamic_slice_in_dim(momentum, offset, share_rows, 1)
    gradient = lax.psum(gradient, "shot")
    scaled = weight * gradient
    scaled_share = lax.dynamic_slice_in_dim(scaled, offset, share_rows, 1)
    factor, kinetic = statistics(scaled_share, moment_share, weight, cells_all)
    momentum_half = momentum - 0.5 * factor * scaled
    return (momentum_half, kinetic)


def interleave(dst, slab, src, factor=None):
    planes, rows = src.shape[0], src.shape[1]
    groups = rows // 8

    @pl.loop(0, planes)
    def _(p):
        for i in range(groups):
            value = src[p, pl.ds(i, 8, stride=groups), :]
            if factor is not None:
                value = value * factor
            dst[(*slab, p, pl.ds(i * 8, 8), slice(None))] = value


def pick_kernel(across, *refs):
    count = len(across)
    fields, outs, (held, sems) = refs[: 2 * count], refs[2 * count : 3 * count], refs[3 * count :]
    chip = lax.axis_index("chip")
    copies = []
    for n in range(2 * count):
        shot = 1 - chip if across[n // 2] else chip
        copies.append(pltpu.make_async_copy(fields[n].at[shot], held.at[n], sems.at[n]))
        copies[-1].start()
    for n in range(2 * count):
        copies[n].wait()
        interleave(outs[n // 2], (n % 2,), held.at[n])


def pick(*pairs, earlier):
    plain = functools.partial(pick_kernel, tuple(pair[2] for pair in pairs))
    fields = [field for pair in pairs for field in pair[:2]]
    shape = fields[0].shape[1:]
    vmem, hbm = pl.BlockSpec(memory_space=pltpu.VMEM), pl.BlockSpec(memory_space=pltpu.HBM)
    return pl.pallas_call(
        lambda earlier, *refs: plain(*refs),
        in_specs=[pl.BlockSpec(memory_space=pl.ANY)] + [hbm] * len(fields),
        out_specs=[vmem] * len(pairs),
        out_shape=[jax.ShapeDtypeStruct((2, *shape), jnp.float32)] * len(pairs),
        scratch_shapes=[pltpu.VMEM((len(fields), *shape), jnp.float32), pltpu.SemaphoreType.DMA((len(fields),))],
        compiler_params=pltpu.CompilerParams(vmem_limit_bytes=4 * 2**20),
        name="pick",
    )(earlier, *fields)


def first_kernel(first, second, courant, outgoing, whole, piece, held, held_courant, sems):
    shot = 1 - lax.axis_index("chip")
    copies = [
        pltpu.make_async_copy(first.at[shot], held.at[0], sems.at[0]),
        pltpu.make_async_copy(second.at[shot], held.at[1], sems.at[1]),
        pltpu.make_async_copy(courant, held_courant, sems.at[2]),
    ]
    for copy in copies:
        copy.start()
    for n in range(2):
        copies[n].wait()
        interleave(outgoing, (n,), held.at[n])
    copies[2].wait()
    interleave(whole, (), held_courant, 1.0 / 12.0)
    count = piece.shape[0]
    piece[...] = whole[pl.ds(lax.axis_index("shot") % 2 * count, count)]


def band(lanes):
    near = jnp.abs(lax.broadcasted_iota(jnp.int32, (2 * lanes, lanes), 0) % lanes - lax.broadcasted_iota(jnp.int32, (2 * lanes, lanes), 1))
    return jnp.where(near == 0, -90.0, jnp.where(near == 1, 16.0, jnp.where(near == 2, -1.0, 0.0))).astype(jnp.bfloat16)


def along_y(field, z, banded, out):
    rows, lanes = field.shape[1] - 8, field.shape[2]
    whole = field[pl.ds(z + 2, BATCH), 0:rows].reshape(BATCH * rows, lanes)
    high = whole.astype(jnp.bfloat16)
    low = (whole - high.astype(jnp.float32)).astype(jnp.bfloat16)
    out[...] = jnp.dot(jnp.concatenate([high, low], 1), banded[...], preferred_element_type=jnp.float32)


def laps12(field, z, y_part, fetch, finish):
    rows, lanes = field.shape[1] - 8, field.shape[2]
    groups = rows // 8
    sub = lax.broadcasted_iota(jnp.int32, (8, lanes), 0)

    def later(block):
        return jnp.where(sub < 7, pltpu.roll(block, 7, 0), 0.0)

    def earlier(block):
        return jnp.where(sub > 0, pltpu.roll(block, 1, 0), 0.0)

    for base in range(0, BATCH, PLANES):
        held = {}

        def tile(j, i):
            if (j, i) not in held:
                if i < 0:
                    held[j, i] = earlier(tile(j, i + groups))
                elif i >= groups:
                    held[j, i] = later(tile(j, i - groups))
                else:
                    held[j, i] = field[z + j + 2, i * 8 : (i + 1) * 8]
            return held[j, i]

        def load(i):
            found = []
            for j in range(base, base + PLANES):
                center = tile(j, i)
                near = (tile(j, i - 1), tile(j, i + 1), tile(j - 1, i), tile(j + 1, i))
                far = (tile(j, i - 2), tile(j, i + 2), tile(j - 2, i), tile(j + 2, i))
                at = (j * groups + i) * 8
                found.append((center, near, far, y_part[at : at + 8], fetch(j, slice(i * 8, i * 8 + 8))))
            return found

        ready = load(0)
        for i in range(groups):
            upcoming = load(i + 1) if i + 1 < groups else None
            for j, (center, near, far, part, extra) in enumerate(ready):
                near = (near[0] + near[1]) + (near[2] + near[3])
                far = (far[0] + far[1]) + (far[2] + far[3])
                finish(base + j, slice(i * 8, i * 8 + 8), center, 16.0 * near + (part - far), extra)
            ready = upcoming


def scatter_kernel(rows_x, cells_ref, observed_ref, out_ref, mark, row_ref, spread):
    _, steps, receivers = observed_ref.shape
    lanes = out_ref.shape[2]
    tile = out_ref.shape[1]
    groups = rows_x // 8

    @pl.when(pl.program_id(0) == 0)
    def _():
        chip = lax.axis_index("chip")
        cells = cells_ref[pl.ds(chip, 1)]
        x = cells // lanes % rows_x
        row_ref[...] = cells // (rows_x * lanes) * rows_x + x % groups * 8 + x // groups
        on_lanes = jnp.concatenate(
            [
                observed_ref[chip],
                jnp.broadcast_to((cells % lanes).astype(jnp.float32), (8, receivers)),
                jnp.zeros((lanes - steps - 8, receivers), jnp.float32),
            ],
            0,
        )
        columns = on_lanes.T
        lane = lax.broadcasted_iota(jnp.int32, (receivers, lanes), 1).astype(jnp.float32)
        at = lane == columns[:, steps : steps + 1]
        for k in range(steps):
            column = columns[:, k : k + 1]
            high = column.astype(jnp.bfloat16).astype(jnp.float32)
            low = column - high
            cols = pl.ds(k * lanes, lanes)
            spread[0:receivers, cols] = jnp.where(at, high, 0.0).astype(jnp.bfloat16)
            spread[receivers:, cols] = jnp.where(at, low, 0.0).astype(jnp.bfloat16)
        cols = pl.ds(steps * lanes, lanes)
        spread[0:receivers, cols] = jnp.where(at, 1.0, 0.0).astype(jnp.bfloat16)
        spread[receivers:, cols] = jnp.zeros((receivers, lanes), jnp.bfloat16)
        mark[...] = jnp.zeros(mark.shape, jnp.float32)

    ids = lax.broadcasted_iota(jnp.int32, (tile, receivers), 0) + pl.program_id(0) * tile
    chosen = jnp.where(ids == row_ref[...], 1.0, 0.0).astype(jnp.bfloat16)
    total = jnp.dot(jnp.concatenate([chosen, chosen], 1), spread[...], preferred_element_type=jnp.float32)
    for k in range(steps + 1):
        out_ref[k] = total[:, k * lanes : (k + 1) * lanes]


def scatter(rec_cells, observed, planes_all, rows_x, rows_y):
    _, steps, receivers = observed.shape
    rows_all = planes_all * rows_x
    tile = 512
    return pl.pallas_call(
        functools.partial(scatter_kernel, rows_x),
        grid=(rows_all // tile,),
        in_specs=[
            pl.BlockSpec((2, receivers), lambda t: (0, 0)),
            pl.BlockSpec((2, steps, receivers), lambda t: (0, 0, 0)),
        ],
        out_specs=[
            pl.BlockSpec((steps + 1, tile, rows_y), lambda t: (0, t, 0)),
            pl.BlockSpec((8, rows_y), lambda t: (0, 0)),
        ],
        out_shape=[
            jax.ShapeDtypeStruct((steps + 1, rows_all, rows_y), jnp.float32),
            jax.ShapeDtypeStruct((8, rows_y), jnp.float32),
        ],
        scratch_shapes=[
            pltpu.VMEM((1, receivers), jnp.int32),
            pltpu.VMEM((2 * receivers, (steps + 1) * rows_y), jnp.bfloat16),
        ],
        compiler_params=pltpu.CompilerParams(vmem_limit_bytes=56 * 2**20),
        cost_estimate=pl.CostEstimate(
            flops=4 * rows_all * receivers * (steps + 1) * rows_y,
            bytes_accessed=4 * (steps + 1) * rows_all * rows_y,
            transcendentals=0,
        ),
        name="receiver_scatter",
    )(rec_cells, observed)


def place(planes):
    chip, core = lax.axis_index("chip"), lax.axis_index("core")
    slabs = (2 * chip + core, 2 * chip + 1 - core, 2 * (1 - chip) + core, 2 * (1 - chip) + 1 - core)
    return chip, core, [slab * planes for slab in slabs]


def load_blocks(slabs, blocks, first, second, factor=None):
    ends, rows, lanes = first.shape[0], first.shape[1] - 8, first.shape[2]
    planes = (ends - 4) // 4
    for field in (first, second):
        for z in (0, 1, ends - 2, ends - 1):
            field[z, 0:rows] = jnp.zeros((rows, lanes), jnp.float32)
    for slab, block in zip(slabs, blocks):
        pair = block if isinstance(block, tuple) else (block.at[0], block.at[1])
        for p in range(planes):
            values = pair[0][p], pair[1][p]
            if factor is not None:
                speed = factor[slab + p]
                values = values[0] * speed, values[1] * speed
            first[slab + p + 2, 0:rows], second[slab + p + 2, 0:rows] = values


BATCH = 4
PLANES = 2


def sweep(core, planes, field, banded, y_first, y_second, work):
    order = [(chip, owned) for owned in (True, False) for chip in (0, 1)]
    parts = (y_first, y_second)

    def first(chip, owned):
        return (2 * chip + (core if owned else 1 - core)) * planes

    along_y(field, first(*order[0]), banded, y_first)
    for owned in (True, False):
        for chip in (0, 1):
            z = first(chip, owned)
            onward = first(1, owned) if chip == 0 else first(0, False)
            for n in range(planes // BATCH):
                last = n == planes // BATCH - 1
                if not last or chip == 0 or owned:
                    along_y(field, onward if last else z + (n + 1) * BATCH, banded, parts[(n + 1) % 2])
                work(z + n * BATCH, parts[n % 2], chip if owned else None, n * BATCH)


def forward_kernel(
    start, sources, own, mate, over0, over1, far0, far1, large, small, large_mate, small_mate, placed, laps, history, held, cour, last,
    even, odd, banded, y0, y1, sems, sems_even, sems_odd
):
    planes, rows, lanes = own.shape[1:]
    steps = laps.shape[0]
    groups = rows // 8
    chip_here, core, slabs = place(planes)

    fetches = []
    for k in range(steps + 1):
        for n in range(4):
            at = pl.ds(n * planes, planes)
            fetches.append(pltpu.make_async_copy(placed.at[k, at], held.at[k, at], sems.at[k, n]))
            fetches[-1].start()

    def keep(k, field, done):
        for n in range(4):
            source = field.at[pl.ds(n * planes + 2, planes), pl.ds(0, rows)]
            yield pltpu.make_async_copy(source, history.at[k, pl.ds(n * planes, planes)], done.at[n])

    banded[...] = band(lanes)
    load_blocks(slabs, (own, mate, (over0, over1), (far0, far1)), odd, even)
    head = large.shape[0] - planes
    for here, across, first, rest in ((slabs[0], slabs[2], large, small), (slabs[1], slabs[3], large_mate, small_mate)):
        for p in range(planes):
            cour[across + p] = first[p]
            cour[here + p] = first[planes + p] if p < head else rest[p - head]

    for index in range(2 * planes):
        z = (2 * (index // planes) + core) * planes + index % planes
        weight = 1.0 + 2.0 * jnp.full((rows, lanes), z, jnp.int32).astype(jnp.float32) / (4 * planes - 1)
        last[index] = weight / (12.0 * cour[z])

    cell = sources[chip_here]
    source_z, x, lane = cell // (rows * lanes), cell // lanes % rows, cell % lanes
    tile = pl.ds(pl.multiple_of(x % groups * 8, 8), 8)
    here = (lax.broadcasted_iota(jnp.int32, (8, lanes), 0) == x // groups) & (
        lax.broadcasted_iota(jnp.int32, (8, lanes), 1) == lane
    )
    source_slab, source_p = source_z // planes, lax.rem(source_z, planes)

    def advance(k, now, then, done):
        @pl.when(k >= 2)
        def _():
            for copy in keep(k - 2, then, done):
                copy.wait()

        def work(z, y_part, chip, p):
            def fetch(j, rows):
                return then[z + j + 2, rows], cour[z + j, rows]

            def finish(j, rows, center, lap, extra):
                old, speed = extra
                if chip is not None:
                    laps[k, p + j, chip, rows] = lap
                then[z + j + 2, rows] = 2.0 * center - old + speed * lap

            laps12(now, z, y_part, fetch, finish)

        cycle = (start[0] + k) % 48
        phase = (jnp.full((8, lanes), cycle, jnp.int32).astype(jnp.float32) - 24.0) / 12.0
        wave = AMPLITUDE * (1.0 - 2.0 * phase * phase) * jnp.exp(-phase * phase)
        strength = jnp.where(here, 12.0 * wave, 0.0)
        moved = cour[source_z, tile, :] * strength

        sweep(core, planes, now, banded, y0, y1, work)

        owned = jnp.where(lax.rem(source_slab, 2) == core, strength, 0.0)
        laps[k, source_p, source_slab // 2, tile, :] += owned
        then[source_z + 2, tile, :] += moved
        for copy in keep(k, then, done):
            copy.start()

    @pl.loop(0, steps // 2)
    def _(pair):
        advance(2 * pair, even, odd, sems_odd)
        advance(2 * pair + 1, odd, even, sems_even)

    for k, field, done in ((steps - 2, odd, sems_odd), (steps - 1, even, sems_even)):
        for copy in keep(k, field, done):
            copy.wait()
    for fetch in fetches:
        fetch.wait()


def inject_kernel(held, history, inject):
    steps, planes_all = history.shape[:2]

    @pl.loop(0, planes_all)
    def _(z):
        count = held[steps, z]
        for k in range(steps):
            inject[k, z] = held[k, z] - count * history[k, z]


def adjoint_kernel(own, mate, over, far, cour, laps, inject, last, keep, send_x, send_y, send_xy, even, odd, total, banded, y0, y1):
    planes, rows, lanes = own.shape[1:]
    steps = laps.shape[0]
    groups = rows // 8
    chip_here, core, slabs = place(planes)
    banded[...] = band(lanes)
    load_blocks(slabs, (own, mate, over, far), odd, even, factor=cour)

    total[...] = jnp.zeros(total.shape, jnp.float32)

    def advance(k, now, then):
        def work(z, y_part, chip, p):
            def fetch(j, rows):
                extra = (then[z + j + 2, rows], cour[z + j, rows], inject[k, z + j, rows])
                if chip is not None:
                    extra += (total[chip * planes + p + j, rows], laps[k, p + j, chip, rows])
                return extra

            def finish(j, rows, center, lap, extra):
                newer = 2.0 * center - extra[0] + extra[1] * (lap - extra[2])
                then[z + j + 2, rows] = newer
                if chip is not None:
                    total[chip * planes + p + j, rows] = extra[3] + newer * extra[4]

            laps12(now, z, y_part, fetch, finish)

        sweep(core, planes, now, banded, y0, y1, work)

    @pl.loop(0, steps // 2)
    def _(pair):
        advance(steps - 1 - 2 * pair, even, odd)
        advance(steps - 2 - 2 * pair, odd, even)

    count = keep.shape[0]
    mine, others = lax.axis_index("shot") % 2 * count, (1 - lax.axis_index("shot") % 2) * count
    here, there = chip_here, 1 - chip_here
    for ref, chip, start in ((keep, here, mine), (send_x, there, mine), (send_y, here, others), (send_xy, there, others)):

        @pl.loop(0, count)
        def _(n):
            p = start + n
            value = total[chip * planes + p] * last[chip * planes + p]
            for i in range(groups):
                ref[n, pl.ds(i, 8, stride=groups), :] = value[i * 8 : (i + 1) * 8]


def square_kernel(mine, by_xy, by_y, by_x, keep, send):
    half = lax.axis_index("shot") // 2 % 2
    count = keep.shape[0]
    for ref, part in ((keep, half), (send, 1 - half)):
        for p in range(count):
            at = part * count + p
            ref[p] = (mine[at] + by_x[at]) + (by_y[at] + by_xy[at])


def add_kernel(mine, other, out):
    out[...] = mine[...] + other[...]


def flip(index, bits):
    result = index
    for bit in (1, 2):
        if bits & bit:
            result = jnp.where(index // bit % 2 == 1, result - bit, result + bit)
    return result


def after_kernel(earlier, value, *outs):
    if len(outs) == 1:
        outs[0][...] = value[...]
    else:
        for n, out in enumerate(outs):
            out[...] = value[n]


def after(earlier, value, parts=1):
    vmem, anywhere = pl.BlockSpec(memory_space=pltpu.VMEM), pl.BlockSpec(memory_space=pl.ANY)
    shape = value.shape if parts == 1 else value.shape[1:]
    results = pl.pallas_call(
        after_kernel,
        in_specs=[anywhere, vmem],
        out_specs=[vmem] * parts,
        out_shape=[jax.ShapeDtypeStruct(shape, jnp.float32)] * parts,
        compiler_params=pltpu.CompilerParams(vmem_limit_bytes=4 * 2**20),
        name="after",
    )(earlier, value)
    return results[0] if parts == 1 else results


def arrange_kernel(own, mine, other, large, small):
    y = lax.axis_index("shot") % 2
    count, planes = mine.shape[0], own.shape[0]
    head = planes - small.shape[0]
    large[pl.ds(y * count, count)] = mine[...]
    large[pl.ds((1 - y) * count, count)] = other[...]
    large[planes:] = own[0:head]
    small[...] = own[head:]


def first_plane(shot, planes):
    return (shot % 2) * (planes // 2) + (shot // 2 % 2) * (planes // 4)


def sums_kernel(mine, other, momentum, data, sums):
    count, rows, lanes = mine.shape
    planes = momentum.shape[0]
    chip, core = lax.axis_index("chip"), lax.axis_index("core")
    first = first_plane(lax.axis_index("shot"), planes)
    parts = [jnp.zeros((rows, lanes), jnp.float32)] * 4
    for j in range(count):
        scaled = mine[j] + other[j]
        data[j * rows : (j + 1) * rows] = scaled
        z = (2 * chip + core) * planes + first + j
        weight = 1.0 + 2.0 * jnp.full((1, lanes), z, jnp.int32).astype(jnp.float32) / (4 * planes - 1)
        moment = momentum[first + j]
        square = scaled * scaled
        terms = (square, weight * moment * moment, weight * moment * scaled, weight * square)
        parts = [part + term for part, term in zip(parts, terms)]

    def total(value):
        by_lane = jnp.sum(value, axis=0, keepdims=True)
        return jnp.broadcast_to(jnp.sum(by_lane, axis=1, keepdims=True), (1, lanes))

    value = jnp.concatenate([total(part) for part in parts] + [jnp.zeros((4, lanes), jnp.float32)], 0)
    data[count * rows :] = value
    sums[...] = value


def join_kernel(mine, other, s0, s1, s2, data, sums):
    rows = mine.shape[0] - 8
    data[0:rows] = mine[0:rows]
    data[rows : 2 * rows] = other[0:rows]
    value = (s0[...] + s1[...]) + (other[rows:] + s2[...])
    data[2 * rows :] = value
    sums[...] = value


def finish_kernel(mine, other, momentum, s0, s1, s2, out, kinetic):
    planes, rows, lanes = momentum.shape
    cells = 4.0 * planes * rows * lanes
    shot = lax.axis_index("shot")
    sums = (s0[...] + s1[...]) + (other[planes // 2 * rows :] + s2[...])
    factor = lax.rsqrt(sums[0:1] / cells + EPSILON)
    energy = 0.5 * (sums[1:2] - factor * sums[2:3] + 0.25 * factor * factor * sums[3:4]) / cells
    kinetic[0] = energy[0, 0]
    step = 0.5 * factor
    quarter = planes // 4
    for part, group in ((mine, shot), (other, flip(shot, 1))):
        for number, first in enumerate((first_plane(group, planes), first_plane(flip(group, 2), planes))):
            for j in range(quarter):
                at = (number * quarter + j) * rows
                out[first + j] = momentum[first + j] - step * part[at : at + rows]


def local(kernel, outs, *arrays):
    vmem = pl.BlockSpec(memory_space=pltpu.VMEM)
    shapes = [jax.ShapeDtypeStruct(shape, jnp.float32) for shape in outs]
    single = len(outs) == 1
    return pl.pallas_call(
        kernel,
        in_specs=[vmem] * len(arrays),
        out_specs=vmem if single else [vmem] * len(outs),
        out_shape=shapes[0] if single else shapes,
        compiler_params=pltpu.CompilerParams(vmem_limit_bytes=4 * 2**20),
        name=kernel.__name__,
    )(*arrays)


def exchange(value, bits):
    axes = ("shot", "chip", "core")
    return lax.ppermute(value, axes, [(i, i ^ bits) for i in range(lax.axis_size(axes))])


CORE, CHIP, Y, NEAR_Z, FAR_Z = 1, 2, 4, 8, 16


def whole_shards(
    courant_sq, momentum, fwd_prev, fwd_cur, adj_next, adj_cur, observed, src_cells, rec_cells, ckpt_step
):
    _, planes, rows_x, rows_y = fwd_cur.shape
    steps = observed.shape[1]
    planes_all = 4 * planes
    cells_all = planes_all * rows_x * rows_y
    vmem, smem = pl.BlockSpec(memory_space=pltpu.VMEM), pl.BlockSpec(memory_space=pltpu.SMEM)

    hbm = pl.BlockSpec(memory_space=pltpu.HBM)
    outgoing, c0, piece = pl.pallas_call(
        first_kernel,
        in_specs=[hbm] * 3,
        out_specs=[vmem] * 3,
        out_shape=[
            jax.ShapeDtypeStruct((2, planes, rows_x, rows_y), jnp.float32),
            jax.ShapeDtypeStruct(courant_sq.shape, jnp.float32),
            jax.ShapeDtypeStruct((planes // 2, rows_x, rows_y), jnp.float32),
        ],
        scratch_shapes=[
            pltpu.VMEM((2, planes, rows_x, rows_y), jnp.float32),
            pltpu.VMEM(courant_sq.shape, jnp.float32),
            pltpu.SemaphoreType.DMA((3,)),
        ],
        compiler_params=pltpu.CompilerParams(vmem_limit_bytes=63 * 2**20),
        name="first_to_cross",
    )(fwd_prev, fwd_cur, courant_sq)

    over = exchange(outgoing, CHIP)
    piece = exchange(piece, CHIP)

    placed, mark = scatter(rec_cells, observed, planes_all, rows_x, rows_y)
    placed = placed.reshape(steps + 1, planes_all, rows_x, rows_y)

    piece = after(mark, piece)
    adj_outgoing, adj_own, own = pick(
        (adj_next, adj_cur, True), (adj_next, adj_cur, False), (fwd_prev, fwd_cur, False), earlier=piece
    )
    mate = exchange(own, CORE)
    head = planes * 5 // 8
    large, small = local(
        arrange_kernel,
        [(planes + head, rows_x, rows_y), (planes - head, rows_x, rows_y)],
        c0,
        piece,
        exchange(piece, Y),
    )
    speeds = [large, small, exchange(large, CORE), exchange(small, CORE)]
    over = after(large, over, parts=2)
    far = [exchange(field, CORE) for field in over]
    adj_over = exchange(adj_outgoing, CHIP)
    adj_mate = exchange(adj_own, CORE)

    scratch = pltpu.VMEM((planes_all + 4, rows_x + 8, rows_y), jnp.float32)
    y_scratch = pltpu.VMEM((BATCH * rows_x, rows_y), jnp.float32)
    step_scratch = [scratch, scratch, pltpu.VMEM((2 * rows_y, rows_y), jnp.bfloat16), y_scratch, y_scratch]
    params = pltpu.CompilerParams(vmem_limit_bytes=6 * 2**20)
    cost = pl.CostEstimate(flops=30 * steps * cells_all, bytes_accessed=16 * steps * cells_all, transcendentals=0)
    laps, history, held, cour, last = pl.pallas_call(
        forward_kernel,
        in_specs=[smem, smem] + [vmem] * 10 + [pl.BlockSpec(memory_space=pltpu.HBM)],
        out_specs=[vmem] * 5,
        out_shape=[
            jax.ShapeDtypeStruct((steps, planes, 2, rows_x, rows_y), jnp.float32),
            jax.ShapeDtypeStruct((steps, planes_all, rows_x, rows_y), jnp.float32),
            jax.ShapeDtypeStruct((steps + 1, planes_all, rows_x, rows_y), jnp.float32),
            jax.ShapeDtypeStruct((planes_all, rows_x, rows_y), jnp.float32),
            jax.ShapeDtypeStruct((2 * planes, rows_x, rows_y), jnp.float32),
        ],
        scratch_shapes=step_scratch
        + [
            pltpu.SemaphoreType.DMA((steps + 1, 4)),
            pltpu.SemaphoreType.DMA((4,)),
            pltpu.SemaphoreType.DMA((4,)),
        ],
        compiler_params=pltpu.CompilerParams(vmem_limit_bytes=21 * 2**20),
        cost_estimate=pl.CostEstimate(flops=1000, bytes_accessed=1000, transcendentals=0),
        name="forward_steps",
    )(ckpt_step[None], src_cells, own, mate, *over, *far, *speeds, placed)

    adj_over = after(laps, adj_over)
    adj_far = exchange(adj_over, CORE)
    inject = pl.pallas_call(
        inject_kernel,
        in_specs=[vmem] * 2,
        out_specs=vmem,
        out_shape=jax.ShapeDtypeStruct(history.shape, jnp.float32),
        compiler_params=pltpu.CompilerParams(vmem_limit_bytes=4 * 2**20),
        name="inject",
    )(held, history)
    slab = jax.ShapeDtypeStruct(courant_sq.shape, jnp.float32)
    half, quarter = (planes // 2, rows_x, rows_y), (planes // 4, rows_x, rows_y)
    keep, send_x, send_y, send_xy = pl.pallas_call(
        adjoint_kernel,
        in_specs=[vmem] * 8,
        out_specs=[vmem] * 4,
        out_shape=[jax.ShapeDtypeStruct(half, jnp.float32)] * 4,
        scratch_shapes=step_scratch[:2] + [pltpu.VMEM((2 * planes, rows_x, rows_y), jnp.float32)] + step_scratch[2:],
        compiler_params=params,
        cost_estimate=cost,
        name="adjoint_steps",
    )(adj_own, adj_mate, adj_over, adj_far, cour, laps, inject, last)

    by_xy, by_x, by_y = exchange(send_xy, CHIP + Y), exchange(send_x, CHIP), exchange(send_y, Y)
    keep, send = local(square_kernel, [quarter] * 2, keep, by_xy, by_y, by_x)
    part = local(add_kernel, [quarter], keep, exchange(send, NEAR_Z))
    rows, sums_shape = planes // 4 * rows_x, (8, rows_y)
    data, sums = local(sums_kernel, [(rows + 8, rows_y), sums_shape], part, exchange(part, FAR_Z), momentum)

    received = exchange(data, NEAR_Z)
    others = [exchange(sums, CORE), exchange(sums, NEAR_Z + CORE)]
    data, sums = local(join_kernel, [(2 * rows + 8, rows_y), sums_shape], data, received, sums, *others)
    received = exchange(data, Y)
    others = [exchange(sums, CHIP), exchange(sums, Y + CHIP)]
    momentum_half, kinetic = pl.pallas_call(
        finish_kernel,
        in_specs=[vmem] * 6,
        out_specs=[vmem, smem],
        out_shape=[jax.ShapeDtypeStruct(momentum.shape, jnp.float32), jax.ShapeDtypeStruct((1,), jnp.float32)],
        compiler_params=pltpu.CompilerParams(vmem_limit_bytes=4 * 2**20),
        name="finish",
    )(data, received, momentum, sums, *others)
    return momentum_half, kinetic[0]


def solution(mesh):
    shots, slabs = mesh.shape["shot"], mesh.shape["depth"]

    def placed(depth):
        field = P("shot", depth, None, None)
        slab = P(depth, None, None)
        inputs = (slab, slab, field, field, field, field, P("shot", None, None), P("shot"), P("shot", None), P())
        return dict(in_specs=inputs, out_specs=(slab, P()), check_vma=False)

    slab_plan = jax.shard_map(slab_shards, mesh=mesh, **placed("depth"))
    if slabs != 4 or shots != 8:
        return slab_plan
    chips = Mesh(mesh.devices.reshape(shots, 2, 2), ("shot", "chip", "core"))
    whole_plan = jax.shard_map(whole_shards, mesh=chips, **placed(("chip", "core")))

    def run(courant_sq, momentum, fwd_prev, *rest):
        total, planes, rows_x, rows_y = fwd_prev.shape
        steps = rest[3].shape[1]
        fits = total == 2 * shots and planes == 4 * shots and rows_y == 128 and rows_x % 16 == 0 and steps % 2 == 0
        plan = whole_plan if fits else slab_plan
        return plan(courant_sq, momentum, fwd_prev, *rest)

    return run
```

```python
import functools

import jax
import jax.numpy as jnp
from jax import lax
from jax.experimental import pallas as pl
from jax.experimental.pallas import tpu as pltpu
from jax.sharding import Mesh
from jax.sharding import PartitionSpec as P

CENTER = -2.5
NEAR = 4.0 / 3.0
FAR = -1.0 / 12.0
AMPLITUDE = 100.0
EPSILON = 1e-06


def with_halo(value, sides, width):
    for axis, dim in sides:
        size, length = (lax.axis_size(axis), value.shape[dim])
        up = [(i, (i + 1) % size) for i in range(size - 1)]
        down = [(j, i) for i, j in up]
        last = lax.slice_in_dim(value, length - width, length, axis=dim)
        leading = lax.slice_in_dim(value, 0, width, axis=dim)
        before = lax.ppermute(last, axis, up)
        after = lax.ppermute(leading, axis, down)
        value = jnp.concatenate([before, value, after], axis=dim)
    return value


def laplace(padded):
    lateral = jnp.pad(padded[:, 2:-2], ((0, 0), (0, 0), (2, 2), (2, 2)))
    center = padded[:, 2:-2]
    along_z = NEAR * (padded[:, 1:-3] + padded[:, 3:-1]) + FAR * (padded[:, :-4] + padded[:, 4:])
    along_x = NEAR * (lateral[:, :, 1:-3, 2:-2] + lateral[:, :, 3:-1, 2:-2]) + FAR * (
        lateral[:, :, :-4, 2:-2] + lateral[:, :, 4:, 2:-2]
    )
    along_y = NEAR * (lateral[:, :, 2:-2, 1:-3] + lateral[:, :, 2:-2, 3:-1]) + FAR * (
        lateral[:, :, 2:-2, :-4] + lateral[:, :, 2:-2, 4:]
    )
    return 3.0 * CENTER * center + along_z + along_x + along_y


def locate(field, cell_ids, first_plane):
    shot_count, planes, rows_x, rows_y = field.shape
    plane_cells = rows_x * rows_y
    local_index = cell_ids - first_plane * plane_cells
    inside = (local_index >= 0) & (local_index < planes * plane_cells)
    target = jnp.where(inside, local_index, 0)
    return (inside, target)


def inject(field, cell_ids, values, first_plane):
    shot_count = field.shape[0]
    inside, target = locate(field, cell_ids, first_plane)
    amount = jnp.where(inside, values, jnp.zeros_like(values))
    flattened = field.reshape(shot_count, -1)
    lanes = jnp.arange(shot_count)[:, None]
    flattened = flattened.at[lanes, target].add(amount)
    return flattened.reshape(field.shape)


def sample(field, cell_ids, first_plane):
    shot_count = field.shape[0]
    inside, target = locate(field, cell_ids, first_plane)
    values = jnp.take_along_axis(field.reshape(shot_count, -1), target, axis=1)
    return jnp.where(inside, values, jnp.zeros_like(values))


def wave_value(start, step):
    cycle = jnp.mod(start + jnp.int32(step), jnp.int32(48))
    phase = (cycle.astype(jnp.float32) - 24.0) / 12.0
    return AMPLITUDE * (1.0 - 2.0 * phase * phase) * jnp.exp(-phase * phase)


def statistics(scaled, moment, weight, cells_all):
    grand_total = lax.psum(jnp.sum(scaled * scaled), ("shot", "depth"))
    factor = lax.rsqrt(grand_total / cells_all + EPSILON)
    halfway = moment - 0.5 * factor * scaled
    energy = lax.psum(jnp.sum(weight * halfway * halfway), ("shot", "depth"))
    return (factor, 0.5 * energy / cells_all)


def slab_shards(
    courant_sq,
    momentum,
    fwd_prev,
    fwd_cur,
    adj_next,
    adj_cur,
    observed,
    src_cells,
    rec_cells,
    ckpt_step,
):
    shot_count, planes, rows_x, rows_y = fwd_cur.shape
    steps_all = observed.shape[1]
    first_plane = lax.axis_index("depth") * planes
    total_planes = planes * lax.axis_size("depth")
    cells_all = total_planes * rows_x * rows_y
    sources = src_cells[:, None]
    older, current = (fwd_prev, fwd_cur)
    laplacians = []
    misfits = []
    for step in range(steps_all):
        padded = with_halo(current, (("depth", 1),), 2)
        strength = jnp.full(sources.shape, wave_value(ckpt_step, step), jnp.float32)
        laplacian = inject(laplace(padded), sources, strength, first_plane)
        newer = 2.0 * current - older + courant_sq * laplacian
        misfits.append(sample(newer, rec_cells, first_plane) - observed[:, step, :])
        laplacians.append(laplacian)
        older, current = (current, newer)
    adj_later, adj_now = (adj_next, adj_cur)
    gradient = jnp.zeros((planes, rows_x, rows_y), jnp.float32)
    for step in reversed(range(steps_all)):
        padded = with_halo(courant_sq * adj_now, (("depth", 1),), 2)
        adj_new = 2.0 * adj_now - adj_later + laplace(padded)
        adj_new = inject(adj_new, rec_cells, misfits[step], first_plane)
        gradient = gradient + jnp.sum(adj_new * laplacians[step], axis=0)
        adj_later, adj_now = (adj_now, adj_new)
    depths = (first_plane + jnp.arange(planes)).astype(jnp.float32)
    weight = (1.0 + 2.0 * depths / (total_planes - 1))[:, None, None]
    share_rows = rows_x // lax.axis_size("shot")
    offset = lax.axis_index("shot") * share_rows
    moment_share = lax.dynamic_slice_in_dim(momentum, offset, share_rows, 1)
    gradient = lax.psum(gradient, "shot")
    scaled = weight * gradient
    scaled_share = lax.dynamic_slice_in_dim(scaled, offset, share_rows, 1)
    factor, kinetic = statistics(scaled_share, moment_share, weight, cells_all)
    momentum_half = momentum - 0.5 * factor * scaled
    return (momentum_half, kinetic)


def interleave(dst, slab, src, factor=None):
    planes, rows = src.shape[0], src.shape[1]
    groups = rows // 8

    @pl.loop(0, planes)
    def _(p):
        for i in range(groups):
            value = src[p, pl.ds(i, 8, stride=groups), :]
            if factor is not None:
                value = value * factor
            dst[(*slab, p, pl.ds(i * 8, 8), slice(None))] = value


def pick_kernel(earlier, adj_next, adj_cur, fwd_prev, fwd_cur, speed, adj_out, adj_own, prev_own, cur_own, held, sems):
    chip = lax.axis_index("chip")
    planes = adj_own.shape[1]
    wanted = (
        (adj_next, 1 - chip, adj_out, (0,)),
        (adj_cur, 1 - chip, adj_out, (1,)),
        (adj_next, chip, adj_own, (0,)),
        (adj_cur, chip, adj_own, (1,)),
        (fwd_prev, chip, prev_own, ()),
        (fwd_cur, chip, cur_own, ()),
    )
    copies = []
    for n, (field, shot, _, _) in enumerate(wanted):
        copies.append(pltpu.make_async_copy(field.at[shot], held.at[n], sems.at[n]))
        copies[-1].start()
    for n, (_, _, out, slab) in enumerate(wanted):
        copies[n].wait()
        interleave(out, slab, held.at[n])
    tail = cur_own.shape[0] - planes
    cur_own[planes:] = speed[planes - tail :]


def pick(adj_next, adj_cur, fwd_prev, fwd_cur, speed, tail, earlier):
    planes, *plane = fwd_cur.shape[1:]
    vmem, hbm = pl.BlockSpec(memory_space=pltpu.VMEM), pl.BlockSpec(memory_space=pltpu.HBM)
    shapes = [(2, planes, *plane), (2, planes, *plane), (planes, *plane), (planes + tail, *plane)]
    return pl.pallas_call(
        pick_kernel,
        in_specs=[pl.BlockSpec(memory_space=pl.ANY)] + [hbm] * 4 + [vmem],
        out_specs=[vmem] * 4,
        out_shape=[jax.ShapeDtypeStruct(shape, jnp.float32) for shape in shapes],
        scratch_shapes=[pltpu.VMEM((6, planes, *plane), jnp.float32), pltpu.SemaphoreType.DMA((6,))],
        compiler_params=pltpu.CompilerParams(vmem_limit_bytes=4 * 2**20),
        name="pick",
    )(earlier, adj_next, adj_cur, fwd_prev, fwd_cur, speed)


def first_kernel(first, second, courant, outgoing, whole, piece, held, held_courant, sems):
    shot = 1 - lax.axis_index("chip")
    copies = [
        pltpu.make_async_copy(first.at[shot], held.at[0], sems.at[0]),
        pltpu.make_async_copy(second.at[shot], held.at[1], sems.at[1]),
        pltpu.make_async_copy(courant, held_courant, sems.at[2]),
    ]
    for copy in copies:
        copy.start()
    for n in range(2):
        copies[n].wait()
        interleave(outgoing, (n,), held.at[n])
    copies[2].wait()
    interleave(whole, (), held_courant, 1.0 / 12.0)
    count = piece.shape[0]
    piece[...] = whole[pl.ds(lax.axis_index("shot") % 2 * count, count)]


def band(lanes):
    near = jnp.abs(lax.broadcasted_iota(jnp.int32, (2 * lanes, lanes), 0) % lanes - lax.broadcasted_iota(jnp.int32, (2 * lanes, lanes), 1))
    return jnp.where(near == 0, -90.0, jnp.where(near == 1, 16.0, jnp.where(near == 2, -1.0, 0.0))).astype(jnp.bfloat16)


def along_y(field, z, banded, out):
    rows, lanes = field.shape[1] - 8, field.shape[2]
    whole = field[pl.ds(z + 2, BATCH), 0:rows].reshape(BATCH * rows, lanes)
    high = whole.astype(jnp.bfloat16)
    low = (whole - high.astype(jnp.float32)).astype(jnp.bfloat16)
    out[...] = jnp.dot(jnp.concatenate([high, low], 1), banded[...], preferred_element_type=jnp.float32)


def laps12(field, z, y_part, fetch, finish):
    rows, lanes = field.shape[1] - 8, field.shape[2]
    groups = rows // 8
    sub = lax.broadcasted_iota(jnp.int32, (8, lanes), 0)

    def later(block):
        return jnp.where(sub < 7, pltpu.roll(block, 7, 0), 0.0)

    def earlier(block):
        return jnp.where(sub > 0, pltpu.roll(block, 1, 0), 0.0)

    for base in range(0, BATCH, PLANES):
        held = {}

        def tile(j, i):
            if (j, i) not in held:
                if i < 0:
                    held[j, i] = earlier(tile(j, i + groups))
                elif i >= groups:
                    held[j, i] = later(tile(j, i - groups))
                else:
                    held[j, i] = field[z + j + 2, i * 8 : (i + 1) * 8]
            return held[j, i]

        def load(i):
            found = []
            for j in range(base, base + PLANES):
                center = tile(j, i)
                near = (tile(j, i - 1), tile(j, i + 1), tile(j - 1, i), tile(j + 1, i))
                far = (tile(j, i - 2), tile(j, i + 2), tile(j - 2, i), tile(j + 2, i))
                at = (j * groups + i) * 8
                found.append((center, near, far, y_part[at : at + 8], fetch(j, slice(i * 8, i * 8 + 8))))
            return found

        ready = load(0)
        for i in range(groups):
            upcoming = load(i + 1) if i + 1 < groups else None
            for j, (center, near, far, part, extra) in enumerate(ready):
                near = (near[0] + near[1]) + (near[2] + near[3])
                far = (far[0] + far[1]) + (far[2] + far[3])
                finish(base + j, slice(i * 8, i * 8 + 8), center, 16.0 * near + (part - far), extra)
            ready = upcoming


def scatter_kernel(rows_x, cells_ref, observed_ref, out_ref, mark, row_ref, spread):
    _, steps, receivers = observed_ref.shape
    lanes = out_ref.shape[2]
    tile = out_ref.shape[1]
    groups = rows_x // 8

    @pl.when(pl.program_id(0) == 0)
    def _():
        chip = lax.axis_index("chip")
        cells = cells_ref[pl.ds(chip, 1)]
        x = cells // lanes % rows_x
        row_ref[...] = cells // (rows_x * lanes) * rows_x + x % groups * 8 + x // groups
        on_lanes = jnp.concatenate(
            [
                observed_ref[chip],
                jnp.broadcast_to((cells % lanes).astype(jnp.float32), (8, receivers)),
                jnp.zeros((lanes - steps - 8, receivers), jnp.float32),
            ],
            0,
        )
        columns = on_lanes.T
        lane = lax.broadcasted_iota(jnp.int32, (receivers, lanes), 1).astype(jnp.float32)
        at = lane == columns[:, steps : steps + 1]
        for k in range(steps):
            column = columns[:, k : k + 1]
            high = column.astype(jnp.bfloat16).astype(jnp.float32)
            low = column - high
            cols = pl.ds(k * lanes, lanes)
            spread[0:receivers, cols] = jnp.where(at, high, 0.0).astype(jnp.bfloat16)
            spread[receivers:, cols] = jnp.where(at, low, 0.0).astype(jnp.bfloat16)
        cols = pl.ds(steps * lanes, lanes)
        spread[0:receivers, cols] = jnp.where(at, 1.0, 0.0).astype(jnp.bfloat16)
        spread[receivers:, cols] = jnp.zeros((receivers, lanes), jnp.bfloat16)
        mark[...] = jnp.zeros(mark.shape, jnp.float32)

    ids = lax.broadcasted_iota(jnp.int32, (tile, receivers), 0) + pl.program_id(0) * tile
    chosen = jnp.where(ids == row_ref[...], 1.0, 0.0).astype(jnp.bfloat16)
    total = jnp.dot(jnp.concatenate([chosen, chosen], 1), spread[...], preferred_element_type=jnp.float32)
    for k in range(steps + 1):
        out_ref[k] = total[:, k * lanes : (k + 1) * lanes]


def scatter(rec_cells, observed, planes_all, rows_x, rows_y):
    _, steps, receivers = observed.shape
    rows_all = planes_all * rows_x
    tile = 512
    return pl.pallas_call(
        functools.partial(scatter_kernel, rows_x),
        grid=(rows_all // tile,),
        in_specs=[
            pl.BlockSpec((2, receivers), lambda t: (0, 0)),
            pl.BlockSpec((2, steps, receivers), lambda t: (0, 0, 0)),
        ],
        out_specs=[
            pl.BlockSpec((steps + 1, tile, rows_y), lambda t: (0, t, 0)),
            pl.BlockSpec((8, rows_y), lambda t: (0, 0)),
        ],
        out_shape=[
            jax.ShapeDtypeStruct((steps + 1, rows_all, rows_y), jnp.float32),
            jax.ShapeDtypeStruct((8, rows_y), jnp.float32),
        ],
        scratch_shapes=[
            pltpu.VMEM((1, receivers), jnp.int32),
            pltpu.VMEM((2 * receivers, (steps + 1) * rows_y), jnp.bfloat16),
        ],
        compiler_params=pltpu.CompilerParams(vmem_limit_bytes=56 * 2**20),
        cost_estimate=pl.CostEstimate(
            flops=4 * rows_all * receivers * (steps + 1) * rows_y,
            bytes_accessed=4 * (steps + 1) * rows_all * rows_y,
            transcendentals=0,
        ),
        name="receiver_scatter",
    )(rec_cells, observed)


def place(planes):
    chip, core = lax.axis_index("chip"), lax.axis_index("core")
    slabs = (2 * chip + core, 2 * chip + 1 - core, 2 * (1 - chip) + core, 2 * (1 - chip) + 1 - core)
    return chip, core, [slab * planes for slab in slabs]


def load_blocks(slabs, blocks, first, second, factor=None):
    ends, rows, lanes = first.shape[0], first.shape[1] - 8, first.shape[2]
    planes = (ends - 4) // 4
    for field in (first, second):
        for z in (0, 1, ends - 2, ends - 1):
            field[z, 0:rows] = jnp.zeros((rows, lanes), jnp.float32)
    for slab, block in zip(slabs, blocks):
        pair = block if isinstance(block, tuple) else (block.at[0], block.at[1])
        for p in range(planes):
            values = pair[0][p], pair[1][p]
            if factor is not None:
                speed = factor[slab + p]
                values = values[0] * speed, values[1] * speed
            first[slab + p + 2, 0:rows], second[slab + p + 2, 0:rows] = values


BATCH = 4
PLANES = 2


def sweep(core, planes, field, banded, y_first, y_second, work):
    order = [(chip, owned) for owned in (True, False) for chip in (0, 1)]
    parts = (y_first, y_second)

    def first(chip, owned):
        return (2 * chip + (core if owned else 1 - core)) * planes

    along_y(field, first(*order[0]), banded, y_first)
    for owned in (True, False):
        for chip in (0, 1):
            z = first(chip, owned)
            onward = first(1, owned) if chip == 0 else first(0, False)
            for n in range(planes // BATCH):
                last = n == planes // BATCH - 1
                if not last or chip == 0 or owned:
                    along_y(field, onward if last else z + (n + 1) * BATCH, banded, parts[(n + 1) % 2])
                work(z + n * BATCH, parts[n % 2], chip if owned else None, n * BATCH)


def forward_kernel(
    start, sources, own0, own1, mate0, mate1, over0, over1, far0, far1, speed, speed_mate, placed, laps, history, held, cour, last,
    even, odd, banded, y0, y1, sems, sems_even, sems_odd
):
    planes, rows, lanes = own0.shape
    steps = laps.shape[0]
    groups = rows // 8
    chip_here, core, slabs = place(planes)

    fetches = []
    for k in range(steps + 1):
        for n in range(4):
            at = pl.ds(n * planes, planes)
            fetches.append(pltpu.make_async_copy(placed.at[k, at], held.at[k, at], sems.at[k, n]))
            fetches[-1].start()

    def keep(k, field, done):
        for n in range(4):
            source = field.at[pl.ds(n * planes + 2, planes), pl.ds(0, rows)]
            yield pltpu.make_async_copy(source, history.at[k, pl.ds(n * planes, planes)], done.at[n])

    banded[...] = band(lanes)
    load_blocks(slabs, ((own0, own1), (mate0, mate1), (over0, over1), (far0, far1)), odd, even)
    head = speed.shape[0] - planes
    for here, across, first, rest in ((slabs[0], slabs[2], speed, own1), (slabs[1], slabs[3], speed_mate, mate1)):
        for p in range(planes):
            cour[across + p] = first[p]
            cour[here + p] = first[planes + p] if p < head else rest[planes + p - head]

    for index in range(2 * planes):
        z = (2 * (index // planes) + core) * planes + index % planes
        weight = 1.0 + 2.0 * jnp.full((rows, lanes), z, jnp.int32).astype(jnp.float32) / (4 * planes - 1)
        last[index] = weight / (12.0 * cour[z])

    cell = sources[chip_here]
    source_z, x, lane = cell // (rows * lanes), cell // lanes % rows, cell % lanes
    tile = pl.ds(pl.multiple_of(x % groups * 8, 8), 8)
    here = (lax.broadcasted_iota(jnp.int32, (8, lanes), 0) == x // groups) & (
        lax.broadcasted_iota(jnp.int32, (8, lanes), 1) == lane
    )
    source_slab, source_p = source_z // planes, lax.rem(source_z, planes)

    def advance(k, now, then, done):
        @pl.when(k >= 2)
        def _():
            for copy in keep(k - 2, then, done):
                copy.wait()

        def work(z, y_part, chip, p):
            def fetch(j, rows):
                return then[z + j + 2, rows], cour[z + j, rows]

            def finish(j, rows, center, lap, extra):
                old, speed = extra
                if chip is not None:
                    laps[k, p + j, chip, rows] = lap
                then[z + j + 2, rows] = 2.0 * center - old + speed * lap

            laps12(now, z, y_part, fetch, finish)

        cycle = (start[0] + k) % 48
        phase = (jnp.full((8, lanes), cycle, jnp.int32).astype(jnp.float32) - 24.0) / 12.0
        wave = AMPLITUDE * (1.0 - 2.0 * phase * phase) * jnp.exp(-phase * phase)
        strength = jnp.where(here, 12.0 * wave, 0.0)
        moved = cour[source_z, tile, :] * strength

        sweep(core, planes, now, banded, y0, y1, work)

        owned = jnp.where(lax.rem(source_slab, 2) == core, strength, 0.0)
        laps[k, source_p, source_slab // 2, tile, :] += owned
        then[source_z + 2, tile, :] += moved
        for copy in keep(k, then, done):
            copy.start()

    @pl.loop(0, steps // 2)
    def _(pair):
        advance(2 * pair, even, odd, sems_odd)
        advance(2 * pair + 1, odd, even, sems_even)

    for k, field, done in ((steps - 2, odd, sems_odd), (steps - 1, even, sems_even)):
        for copy in keep(k, field, done):
            copy.wait()
    for fetch in fetches:
        fetch.wait()


def inject_kernel(held, history, inject):
    steps, planes_all = history.shape[:2]

    @pl.loop(0, planes_all)
    def _(z):
        count = held[steps, z]
        for k in range(steps):
            inject[k, z] = held[k, z] - count * history[k, z]


def adjoint_kernel(own, mate, over, far, cour, laps, inject, last, keep, send_x, send_y, send_xy, even, odd, total, banded, y0, y1):
    planes, rows, lanes = own.shape[1:]
    steps = laps.shape[0]
    groups = rows // 8
    chip_here, core, slabs = place(planes)
    banded[...] = band(lanes)
    load_blocks(slabs, (own, mate, over, far), odd, even, factor=cour)

    total[...] = jnp.zeros(total.shape, jnp.float32)

    def advance(k, now, then):
        def work(z, y_part, chip, p):
            def fetch(j, rows):
                extra = (then[z + j + 2, rows], cour[z + j, rows], inject[k, z + j, rows])
                if chip is not None:
                    extra += (total[chip * planes + p + j, rows], laps[k, p + j, chip, rows])
                return extra

            def finish(j, rows, center, lap, extra):
                newer = 2.0 * center - extra[0] + extra[1] * (lap - extra[2])
                then[z + j + 2, rows] = newer
                if chip is not None:
                    total[chip * planes + p + j, rows] = extra[3] + newer * extra[4]

            laps12(now, z, y_part, fetch, finish)

        sweep(core, planes, now, banded, y0, y1, work)

    @pl.loop(0, steps // 2)
    def _(pair):
        advance(steps - 1 - 2 * pair, even, odd)
        advance(steps - 2 - 2 * pair, odd, even)

    count = keep.shape[0]
    mine, others = lax.axis_index("shot") % 2 * count, (1 - lax.axis_index("shot") % 2) * count
    here, there = chip_here, 1 - chip_here
    for ref, chip, start in ((keep, here, mine), (send_x, there, mine), (send_y, here, others), (send_xy, there, others)):

        @pl.loop(0, count)
        def _(n):
            p = start + n
            value = total[chip * planes + p] * last[chip * planes + p]
            for i in range(groups):
                ref[n, pl.ds(i, 8, stride=groups), :] = value[i * 8 : (i + 1) * 8]


def square_kernel(mine, by_xy, by_y, by_x, keep, send):
    half = lax.axis_index("shot") // 2 % 2
    count = keep.shape[0]
    for ref, part in ((keep, half), (send, 1 - half)):
        for p in range(count):
            at = part * count + p
            ref[p] = (mine[at] + by_x[at]) + (by_y[at] + by_xy[at])


def add_kernel(mine, other, out):
    out[...] = mine[...] + other[...]


def flip(index, bits):
    result = index
    for bit in (1, 2):
        if bits & bit:
            result = jnp.where(index // bit % 2 == 1, result - bit, result + bit)
    return result


def after_kernel(earlier, value, *outs):
    if len(outs) == 1:
        outs[0][...] = value[...]
    else:
        for n, out in enumerate(outs):
            out[...] = value[n]


def after(earlier, value, parts=1):
    vmem, anywhere = pl.BlockSpec(memory_space=pltpu.VMEM), pl.BlockSpec(memory_space=pl.ANY)
    shape = value.shape if parts == 1 else value.shape[1:]
    results = pl.pallas_call(
        after_kernel,
        in_specs=[anywhere, vmem],
        out_specs=[vmem] * parts,
        out_shape=[jax.ShapeDtypeStruct(shape, jnp.float32)] * parts,
        compiler_params=pltpu.CompilerParams(vmem_limit_bytes=4 * 2**20),
        name="after",
    )(earlier, value)
    return results[0] if parts == 1 else results


def arrange_kernel(own, mine, other, out):
    y = lax.axis_index("shot") % 2
    count, planes = mine.shape[0], own.shape[0]
    out[pl.ds(y * count, count)] = mine[...]
    out[pl.ds((1 - y) * count, count)] = other[...]
    out[planes:] = own[0 : out.shape[0] - planes]


def first_plane(shot, planes):
    return (shot % 2) * (planes // 2) + (shot // 2 % 2) * (planes // 4)


def sums_kernel(mine, other, momentum, data, sums):
    count, rows, lanes = mine.shape
    planes = momentum.shape[0]
    chip, core = lax.axis_index("chip"), lax.axis_index("core")
    first = first_plane(lax.axis_index("shot"), planes)
    parts = [jnp.zeros((rows, lanes), jnp.float32)] * 4
    for j in range(count):
        scaled = mine[j] + other[j]
        data[j * rows : (j + 1) * rows] = scaled
        z = (2 * chip + core) * planes + first + j
        weight = 1.0 + 2.0 * jnp.full((1, lanes), z, jnp.int32).astype(jnp.float32) / (4 * planes - 1)
        moment = momentum[first + j]
        square = scaled * scaled
        terms = (square, weight * moment * moment, weight * moment * scaled, weight * square)
        parts = [part + term for part, term in zip(parts, terms)]

    def total(value):
        by_lane = jnp.sum(value, axis=0, keepdims=True)
        return jnp.broadcast_to(jnp.sum(by_lane, axis=1, keepdims=True), (1, lanes))

    value = jnp.concatenate([total(part) for part in parts] + [jnp.zeros((4, lanes), jnp.float32)], 0)
    data[count * rows :] = value
    sums[...] = value


def join_kernel(mine, other, s0, s1, s2, data, sums):
    rows = mine.shape[0] - 8
    data[0:rows] = mine[0:rows]
    data[rows : 2 * rows] = other[0:rows]
    value = (s0[...] + s1[...]) + (other[rows:] + s2[...])
    data[2 * rows :] = value
    sums[...] = value


def finish_kernel(mine, other, momentum, s0, s1, s2, out, kinetic):
    planes, rows, lanes = momentum.shape
    cells = 4.0 * planes * rows * lanes
    shot = lax.axis_index("shot")
    sums = (s0[...] + s1[...]) + (other[planes // 2 * rows :] + s2[...])
    factor = lax.rsqrt(sums[0:1] / cells + EPSILON)
    energy = 0.5 * (sums[1:2] - factor * sums[2:3] + 0.25 * factor * factor * sums[3:4]) / cells
    kinetic[0] = energy[0, 0]
    step = 0.5 * factor
    quarter = planes // 4
    for part, group in ((mine, shot), (other, flip(shot, 1))):
        for number, first in enumerate((first_plane(group, planes), first_plane(flip(group, 2), planes))):
            for j in range(quarter):
                at = (number * quarter + j) * rows
                out[first + j] = momentum[first + j] - step * part[at : at + rows]


def local(kernel, outs, *arrays):
    vmem = pl.BlockSpec(memory_space=pltpu.VMEM)
    shapes = [jax.ShapeDtypeStruct(shape, jnp.float32) for shape in outs]
    single = len(outs) == 1
    return pl.pallas_call(
        kernel,
        in_specs=[vmem] * len(arrays),
        out_specs=vmem if single else [vmem] * len(outs),
        out_shape=shapes[0] if single else shapes,
        compiler_params=pltpu.CompilerParams(vmem_limit_bytes=4 * 2**20),
        name=kernel.__name__,
    )(*arrays)


def exchange(value, bits):
    axes = ("shot", "chip", "core")
    return lax.ppermute(value, axes, [(i, i ^ bits) for i in range(lax.axis_size(axes))])


CORE, CHIP, Y, NEAR_Z, FAR_Z = 1, 2, 4, 8, 16


def whole_shards(
    courant_sq, momentum, fwd_prev, fwd_cur, adj_next, adj_cur, observed, src_cells, rec_cells, ckpt_step
):
    _, planes, rows_x, rows_y = fwd_cur.shape
    steps = observed.shape[1]
    planes_all = 4 * planes
    cells_all = planes_all * rows_x * rows_y
    vmem, smem = pl.BlockSpec(memory_space=pltpu.VMEM), pl.BlockSpec(memory_space=pltpu.SMEM)

    hbm = pl.BlockSpec(memory_space=pltpu.HBM)
    outgoing, c0, piece = pl.pallas_call(
        first_kernel,
        in_specs=[hbm] * 3,
        out_specs=[vmem] * 3,
        out_shape=[
            jax.ShapeDtypeStruct((2, planes, rows_x, rows_y), jnp.float32),
            jax.ShapeDtypeStruct(courant_sq.shape, jnp.float32),
            jax.ShapeDtypeStruct((planes // 2, rows_x, rows_y), jnp.float32),
        ],
        scratch_shapes=[
            pltpu.VMEM((2, planes, rows_x, rows_y), jnp.float32),
            pltpu.VMEM(courant_sq.shape, jnp.float32),
            pltpu.SemaphoreType.DMA((3,)),
        ],
        compiler_params=pltpu.CompilerParams(vmem_limit_bytes=63 * 2**20),
        name="first_to_cross",
    )(fwd_prev, fwd_cur, courant_sq)

    over = exchange(outgoing, CHIP)
    piece = exchange(piece, CHIP)

    placed, mark = scatter(rec_cells, observed, planes_all, rows_x, rows_y)
    placed = placed.reshape(steps + 1, planes_all, rows_x, rows_y)

    piece = after(mark, piece)
    head = planes * 5 // 8
    adj_outgoing, adj_own, *own = pick(adj_next, adj_cur, fwd_prev, fwd_cur, c0, planes - head, piece)
    mate = [exchange(field, CORE) for field in own]
    speed = local(arrange_kernel, [(planes + head, rows_x, rows_y)], c0, piece, exchange(piece, Y))
    speed_mate = exchange(speed, CORE)
    over = after(speed, over, parts=2)
    far = [exchange(field, CORE) for field in over]
    adj_over = exchange(adj_outgoing, CHIP)
    adj_mate = exchange(adj_own, CORE)

    scratch = pltpu.VMEM((planes_all + 4, rows_x + 8, rows_y), jnp.float32)
    y_scratch = pltpu.VMEM((BATCH * rows_x, rows_y), jnp.float32)
    step_scratch = [scratch, scratch, pltpu.VMEM((2 * rows_y, rows_y), jnp.bfloat16), y_scratch, y_scratch]
    params = pltpu.CompilerParams(vmem_limit_bytes=6 * 2**20)
    cost = pl.CostEstimate(flops=30 * steps * cells_all, bytes_accessed=16 * steps * cells_all, transcendentals=0)
    laps, history, held, cour, last = pl.pallas_call(
        forward_kernel,
        in_specs=[smem, smem] + [vmem] * 10 + [pl.BlockSpec(memory_space=pltpu.HBM)],
        out_specs=[vmem] * 5,
        out_shape=[
            jax.ShapeDtypeStruct((steps, planes, 2, rows_x, rows_y), jnp.float32),
            jax.ShapeDtypeStruct((steps, planes_all, rows_x, rows_y), jnp.float32),
            jax.ShapeDtypeStruct((steps + 1, planes_all, rows_x, rows_y), jnp.float32),
            jax.ShapeDtypeStruct((planes_all, rows_x, rows_y), jnp.float32),
            jax.ShapeDtypeStruct((2 * planes, rows_x, rows_y), jnp.float32),
        ],
        scratch_shapes=step_scratch
        + [
            pltpu.SemaphoreType.DMA((steps + 1, 4)),
            pltpu.SemaphoreType.DMA((4,)),
            pltpu.SemaphoreType.DMA((4,)),
        ],
        compiler_params=pltpu.CompilerParams(vmem_limit_bytes=21 * 2**20),
        cost_estimate=pl.CostEstimate(flops=1000, bytes_accessed=1000, transcendentals=0),
        name="forward_steps",
    )(ckpt_step[None], src_cells, *own, *mate, *over, *far, speed, speed_mate, placed)

    adj_over = after(laps, adj_over)
    adj_far = exchange(adj_over, CORE)
    inject = pl.pallas_call(
        inject_kernel,
        in_specs=[vmem] * 2,
        out_specs=vmem,
        out_shape=jax.ShapeDtypeStruct(history.shape, jnp.float32),
        compiler_params=pltpu.CompilerParams(vmem_limit_bytes=4 * 2**20),
        name="inject",
    )(held, history)
    slab = jax.ShapeDtypeStruct(courant_sq.shape, jnp.float32)
    half, quarter = (planes // 2, rows_x, rows_y), (planes // 4, rows_x, rows_y)
    keep, send_x, send_y, send_xy = pl.pallas_call(
        adjoint_kernel,
        in_specs=[vmem] * 8,
        out_specs=[vmem] * 4,
        out_shape=[jax.ShapeDtypeStruct(half, jnp.float32)] * 4,
        scratch_shapes=step_scratch[:2] + [pltpu.VMEM((2 * planes, rows_x, rows_y), jnp.float32)] + step_scratch[2:],
        compiler_params=params,
        cost_estimate=cost,
        name="adjoint_steps",
    )(adj_own, adj_mate, adj_over, adj_far, cour, laps, inject, last)

    by_xy, by_x, by_y = exchange(send_xy, CHIP + Y), exchange(send_x, CHIP), exchange(send_y, Y)
    keep, send = local(square_kernel, [quarter] * 2, keep, by_xy, by_y, by_x)
    part = local(add_kernel, [quarter], keep, exchange(send, NEAR_Z))
    rows, sums_shape = planes // 4 * rows_x, (8, rows_y)
    data, sums = local(sums_kernel, [(rows + 8, rows_y), sums_shape], part, exchange(part, FAR_Z), momentum)

    received = exchange(data, NEAR_Z)
    others = [exchange(sums, CORE), exchange(sums, NEAR_Z + CORE)]
    data, sums = local(join_kernel, [(2 * rows + 8, rows_y), sums_shape], data, received, sums, *others)
    received = exchange(data, Y)
    others = [exchange(sums, CHIP), exchange(sums, Y + CHIP)]
    momentum_half, kinetic = pl.pallas_call(
        finish_kernel,
        in_specs=[vmem] * 6,
        out_specs=[vmem, smem],
        out_shape=[jax.ShapeDtypeStruct(momentum.shape, jnp.float32), jax.ShapeDtypeStruct((1,), jnp.float32)],
        compiler_params=pltpu.CompilerParams(vmem_limit_bytes=4 * 2**20),
        name="finish",
    )(data, received, momentum, sums, *others)
    return momentum_half, kinetic[0]


def solution(mesh):
    shots, slabs = mesh.shape["shot"], mesh.shape["depth"]

    def placed(depth):
        field = P("shot", depth, None, None)
        slab = P(depth, None, None)
        inputs = (slab, slab, field, field, field, field, P("shot", None, None), P("shot"), P("shot", None), P())
        return dict(in_specs=inputs, out_specs=(slab, P()), check_vma=False)

    slab_plan = jax.shard_map(slab_shards, mesh=mesh, **placed("depth"))
    if slabs != 4 or shots != 8:
        return slab_plan
    chips = Mesh(mesh.devices.reshape(shots, 2, 2), ("shot", "chip", "core"))
    whole_plan = jax.shard_map(whole_shards, mesh=chips, **placed(("chip", "core")))

    def run(courant_sq, momentum, fwd_prev, *rest):
        total, planes, rows_x, rows_y = fwd_prev.shape
        steps = rest[3].shape[1]
        fits = total == 2 * shots and planes == 4 * shots and rows_y == 128 and rows_x % 16 == 0 and steps % 2 == 0
        plan = whole_plan if fits else slab_plan
        return plan(courant_sq, momentum, fwd_prev, *rest)

    return run
```

```python
import functools

import jax
import jax.numpy as jnp
from jax import lax
from jax.experimental import pallas as pl
from jax.experimental.pallas import tpu as pltpu
from jax.sharding import Mesh
from jax.sharding import PartitionSpec as P

CENTER = -2.5
NEAR = 4.0 / 3.0
FAR = -1.0 / 12.0
AMPLITUDE = 100.0
EPSILON = 1e-06


def with_halo(value, sides, width):
    for axis, dim in sides:
        size, length = (lax.axis_size(axis), value.shape[dim])
        up = [(i, (i + 1) % size) for i in range(size - 1)]
        down = [(j, i) for i, j in up]
        last = lax.slice_in_dim(value, length - width, length, axis=dim)
        leading = lax.slice_in_dim(value, 0, width, axis=dim)
        before = lax.ppermute(last, axis, up)
        after = lax.ppermute(leading, axis, down)
        value = jnp.concatenate([before, value, after], axis=dim)
    return value


def laplace(padded):
    lateral = jnp.pad(padded[:, 2:-2], ((0, 0), (0, 0), (2, 2), (2, 2)))
    center = padded[:, 2:-2]
    along_z = NEAR * (padded[:, 1:-3] + padded[:, 3:-1]) + FAR * (padded[:, :-4] + padded[:, 4:])
    along_x = NEAR * (lateral[:, :, 1:-3, 2:-2] + lateral[:, :, 3:-1, 2:-2]) + FAR * (
        lateral[:, :, :-4, 2:-2] + lateral[:, :, 4:, 2:-2]
    )
    along_y = NEAR * (lateral[:, :, 2:-2, 1:-3] + lateral[:, :, 2:-2, 3:-1]) + FAR * (
        lateral[:, :, 2:-2, :-4] + lateral[:, :, 2:-2, 4:]
    )
    return 3.0 * CENTER * center + along_z + along_x + along_y


def locate(field, cell_ids, first_plane):
    shot_count, planes, rows_x, rows_y = field.shape
    plane_cells = rows_x * rows_y
    local_index = cell_ids - first_plane * plane_cells
    inside = (local_index >= 0) & (local_index < planes * plane_cells)
    target = jnp.where(inside, local_index, 0)
    return (inside, target)


def inject(field, cell_ids, values, first_plane):
    shot_count = field.shape[0]
    inside, target = locate(field, cell_ids, first_plane)
    amount = jnp.where(inside, values, jnp.zeros_like(values))
    flattened = field.reshape(shot_count, -1)
    lanes = jnp.arange(shot_count)[:, None]
    flattened = flattened.at[lanes, target].add(amount)
    return flattened.reshape(field.shape)


def sample(field, cell_ids, first_plane):
    shot_count = field.shape[0]
    inside, target = locate(field, cell_ids, first_plane)
    values = jnp.take_along_axis(field.reshape(shot_count, -1), target, axis=1)
    return jnp.where(inside, values, jnp.zeros_like(values))


def wave_value(start, step):
    cycle = jnp.mod(start + jnp.int32(step), jnp.int32(48))
    phase = (cycle.astype(jnp.float32) - 24.0) / 12.0
    return AMPLITUDE * (1.0 - 2.0 * phase * phase) * jnp.exp(-phase * phase)


def statistics(scaled, moment, weight, cells_all):
    grand_total = lax.psum(jnp.sum(scaled * scaled), ("shot", "depth"))
    factor = lax.rsqrt(grand_total / cells_all + EPSILON)
    halfway = moment - 0.5 * factor * scaled
    energy = lax.psum(jnp.sum(weight * halfway * halfway), ("shot", "depth"))
    return (factor, 0.5 * energy / cells_all)


def slab_shards(
    courant_sq,
    momentum,
    fwd_prev,
    fwd_cur,
    adj_next,
    adj_cur,
    observed,
    src_cells,
    rec_cells,
    ckpt_step,
):
    shot_count, planes, rows_x, rows_y = fwd_cur.shape
    steps_all = observed.shape[1]
    first_plane = lax.axis_index("depth") * planes
    total_planes = planes * lax.axis_size("depth")
    cells_all = total_planes * rows_x * rows_y
    sources = src_cells[:, None]
    older, current = (fwd_prev, fwd_cur)
    laplacians = []
    misfits = []
    for step in range(steps_all):
        padded = with_halo(current, (("depth", 1),), 2)
        strength = jnp.full(sources.shape, wave_value(ckpt_step, step), jnp.float32)
        laplacian = inject(laplace(padded), sources, strength, first_plane)
        newer = 2.0 * current - older + courant_sq * laplacian
        misfits.append(sample(newer, rec_cells, first_plane) - observed[:, step, :])
        laplacians.append(laplacian)
        older, current = (current, newer)
    adj_later, adj_now = (adj_next, adj_cur)
    gradient = jnp.zeros((planes, rows_x, rows_y), jnp.float32)
    for step in reversed(range(steps_all)):
        padded = with_halo(courant_sq * adj_now, (("depth", 1),), 2)
        adj_new = 2.0 * adj_now - adj_later + laplace(padded)
        adj_new = inject(adj_new, rec_cells, misfits[step], first_plane)
        gradient = gradient + jnp.sum(adj_new * laplacians[step], axis=0)
        adj_later, adj_now = (adj_now, adj_new)
    depths = (first_plane + jnp.arange(planes)).astype(jnp.float32)
    weight = (1.0 + 2.0 * depths / (total_planes - 1))[:, None, None]
    share_rows = rows_x // lax.axis_size("shot")
    offset = lax.axis_index("shot") * share_rows
    moment_share = lax.dynamic_slice_in_dim(momentum, offset, share_rows, 1)
    gradient = lax.psum(gradient, "shot")
    scaled = weight * gradient
    scaled_share = lax.dynamic_slice_in_dim(scaled, offset, share_rows, 1)
    factor, kinetic = statistics(scaled_share, moment_share, weight, cells_all)
    momentum_half = momentum - 0.5 * factor * scaled
    return (momentum_half, kinetic)


def interleave(dst, slab, src, factor=None):
    planes, rows = src.shape[0], src.shape[1]
    groups = rows // 8

    @pl.loop(0, planes)
    def _(p):
        for i in range(groups):
            value = src[p, pl.ds(i, 8, stride=groups), :]
            if factor is not None:
                value = value * factor
            dst[(*slab, p, pl.ds(i * 8, 8), slice(None))] = value


def pick_kernel(earlier, adj_next, adj_cur, fwd_prev, fwd_cur, speed, adj_out, adj_own, prev_own, cur_own, held, sems):
    chip = lax.axis_index("chip")
    planes = adj_own.shape[1]
    wanted = (
        (adj_next, 1 - chip, adj_out, (0,)),
        (adj_cur, 1 - chip, adj_out, (1,)),
        (adj_next, chip, adj_own, (0,)),
        (adj_cur, chip, adj_own, (1,)),
        (fwd_prev, chip, prev_own, ()),
        (fwd_cur, chip, cur_own, ()),
    )
    copies = []
    for n, (field, shot, _, _) in enumerate(wanted):
        copies.append(pltpu.make_async_copy(field.at[shot], held.at[n], sems.at[n]))
        copies[-1].start()
    for n, (_, _, out, slab) in enumerate(wanted):
        copies[n].wait()
        interleave(out, slab, held.at[n])
    tail = cur_own.shape[0] - planes
    cur_own[planes:] = speed[planes - tail :]


def pick(adj_next, adj_cur, fwd_prev, fwd_cur, speed, tail, earlier):
    planes, *plane = fwd_cur.shape[1:]
    vmem, hbm = pl.BlockSpec(memory_space=pltpu.VMEM), pl.BlockSpec(memory_space=pltpu.HBM)
    shapes = [(2, planes, *plane), (2, planes, *plane), (planes, *plane), (planes + tail, *plane)]
    return pl.pallas_call(
        pick_kernel,
        in_specs=[pl.BlockSpec(memory_space=pl.ANY)] + [hbm] * 4 + [vmem],
        out_specs=[vmem] * 4,
        out_shape=[jax.ShapeDtypeStruct(shape, jnp.float32) for shape in shapes],
        scratch_shapes=[pltpu.VMEM((6, planes, *plane), jnp.float32), pltpu.SemaphoreType.DMA((6,))],
        compiler_params=pltpu.CompilerParams(vmem_limit_bytes=4 * 2**20),
        name="pick",
    )(earlier, adj_next, adj_cur, fwd_prev, fwd_cur, speed)


def first_kernel(first, second, courant, outgoing, whole, piece, held, held_courant, sems):
    shot = 1 - lax.axis_index("chip")
    copies = [
        pltpu.make_async_copy(first.at[shot], held.at[0], sems.at[0]),
        pltpu.make_async_copy(second.at[shot], held.at[1], sems.at[1]),
        pltpu.make_async_copy(courant, held_courant, sems.at[2]),
    ]
    for copy in copies:
        copy.start()
    for n in range(2):
        copies[n].wait()
        interleave(outgoing, (n,), held.at[n])
    copies[2].wait()
    interleave(whole, (), held_courant, 1.0 / 12.0)
    count = piece.shape[0]
    piece[...] = whole[pl.ds(lax.axis_index("shot") % 2 * count, count)]


def band(lanes):
    near = jnp.abs(lax.broadcasted_iota(jnp.int32, (2 * lanes, lanes), 0) % lanes - lax.broadcasted_iota(jnp.int32, (2 * lanes, lanes), 1))
    return jnp.where(near == 0, -90.0, jnp.where(near == 1, 16.0, jnp.where(near == 2, -1.0, 0.0))).astype(jnp.bfloat16)


def along_y(field, z, banded, out):
    rows, lanes = field.shape[1] - 8, field.shape[2]
    whole = field[pl.ds(z + 2, BATCH), 0:rows].reshape(BATCH * rows, lanes)
    high = whole.astype(jnp.bfloat16)
    low = (whole - high.astype(jnp.float32)).astype(jnp.bfloat16)
    out[...] = jnp.dot(jnp.concatenate([high, low], 1), banded[...], preferred_element_type=jnp.float32)


def laps12(field, z, y_part, fetch, finish):
    rows, lanes = field.shape[1] - 8, field.shape[2]
    groups = rows // 8
    sub = lax.broadcasted_iota(jnp.int32, (8, lanes), 0)

    def later(block):
        return jnp.where(sub < 7, pltpu.roll(block, 7, 0), 0.0)

    def earlier(block):
        return jnp.where(sub > 0, pltpu.roll(block, 1, 0), 0.0)

    for base in range(0, BATCH, PLANES):
        held = {}

        def tile(j, i):
            if (j, i) not in held:
                if i < 0:
                    held[j, i] = earlier(tile(j, i + groups))
                elif i >= groups:
                    held[j, i] = later(tile(j, i - groups))
                else:
                    held[j, i] = field[z + j + 2, i * 8 : (i + 1) * 8]
            return held[j, i]

        def load(i):
            found = []
            for j in range(base, base + PLANES):
                center = tile(j, i)
                near = (tile(j, i - 1), tile(j, i + 1), tile(j - 1, i), tile(j + 1, i))
                far = (tile(j, i - 2), tile(j, i + 2), tile(j - 2, i), tile(j + 2, i))
                at = (j * groups + i) * 8
                found.append((center, near, far, y_part[at : at + 8], fetch(j, slice(i * 8, i * 8 + 8))))
            return found

        ready = load(0)
        for i in range(groups):
            upcoming = load(i + 1) if i + 1 < groups else None
            for j, (center, near, far, part, extra) in enumerate(ready):
                near = (near[0] + near[1]) + (near[2] + near[3])
                far = (far[0] + far[1]) + (far[2] + far[3])
                finish(base + j, slice(i * 8, i * 8 + 8), center, 16.0 * near + (part - far), extra)
            ready = upcoming


def scatter_kernel(rows_x, cells_ref, observed_ref, out_ref, mark, row_ref, spread):
    _, steps, receivers = observed_ref.shape
    lanes = out_ref.shape[2]
    tile = out_ref.shape[1]
    groups = rows_x // 8

    @pl.when(pl.program_id(0) == 0)
    def _():
        chip = lax.axis_index("chip")
        cells = cells_ref[pl.ds(chip, 1)]
        x = cells // lanes % rows_x
        row_ref[...] = cells // (rows_x * lanes) * rows_x + x % groups * 8 + x // groups
        on_lanes = jnp.concatenate(
            [
                observed_ref[chip],
                jnp.broadcast_to((cells % lanes).astype(jnp.float32), (8, receivers)),
                jnp.zeros((lanes - steps - 8, receivers), jnp.float32),
            ],
            0,
        )
        columns = on_lanes.T
        lane = lax.broadcasted_iota(jnp.int32, (receivers, lanes), 1).astype(jnp.float32)
        at = lane == columns[:, steps : steps + 1]
        for k in range(steps):
            column = columns[:, k : k + 1]
            high = column.astype(jnp.bfloat16).astype(jnp.float32)
            low = column - high
            cols = pl.ds(k * lanes, lanes)
            spread[0:receivers, cols] = jnp.where(at, high, 0.0).astype(jnp.bfloat16)
            spread[receivers:, cols] = jnp.where(at, low, 0.0).astype(jnp.bfloat16)
        cols = pl.ds(steps * lanes, lanes)
        spread[0:receivers, cols] = jnp.where(at, 1.0, 0.0).astype(jnp.bfloat16)
        spread[receivers:, cols] = jnp.zeros((receivers, lanes), jnp.bfloat16)
        mark[...] = jnp.zeros(mark.shape, jnp.float32)

    ids = lax.broadcasted_iota(jnp.int32, (tile, receivers), 0) + pl.program_id(0) * tile
    chosen = jnp.where(ids == row_ref[...], 1.0, 0.0).astype(jnp.bfloat16)
    total = jnp.dot(jnp.concatenate([chosen, chosen], 1), spread[...], preferred_element_type=jnp.float32)
    for k in range(steps + 1):
        out_ref[k] = total[:, k * lanes : (k + 1) * lanes]


def scatter(rec_cells, observed, planes_all, rows_x, rows_y):
    _, steps, receivers = observed.shape
    rows_all = planes_all * rows_x
    tile = 512
    return pl.pallas_call(
        functools.partial(scatter_kernel, rows_x),
        grid=(rows_all // tile,),
        in_specs=[
            pl.BlockSpec((2, receivers), lambda t: (0, 0)),
            pl.BlockSpec((2, steps, receivers), lambda t: (0, 0, 0)),
        ],
        out_specs=[
            pl.BlockSpec((steps + 1, tile, rows_y), lambda t: (0, t, 0)),
            pl.BlockSpec((8, rows_y), lambda t: (0, 0)),
        ],
        out_shape=[
            jax.ShapeDtypeStruct((steps + 1, rows_all, rows_y), jnp.float32),
            jax.ShapeDtypeStruct((8, rows_y), jnp.float32),
        ],
        scratch_shapes=[
            pltpu.VMEM((1, receivers), jnp.int32),
            pltpu.VMEM((2 * receivers, (steps + 1) * rows_y), jnp.bfloat16),
        ],
        compiler_params=pltpu.CompilerParams(vmem_limit_bytes=56 * 2**20),
        cost_estimate=pl.CostEstimate(
            flops=4 * rows_all * receivers * (steps + 1) * rows_y,
            bytes_accessed=4 * (steps + 1) * rows_all * rows_y,
            transcendentals=0,
        ),
        name="receiver_scatter",
    )(rec_cells, observed)


def place(planes):
    chip, core = lax.axis_index("chip"), lax.axis_index("core")
    slabs = (2 * chip + core, 2 * chip + 1 - core, 2 * (1 - chip) + core, 2 * (1 - chip) + 1 - core)
    return chip, core, [slab * planes for slab in slabs]


def load_blocks(slabs, blocks, first, second, factor=None):
    ends, rows, lanes = first.shape[0], first.shape[1] - 8, first.shape[2]
    planes = (ends - 4) // 4
    for field in (first, second):
        for z in (0, 1, ends - 2, ends - 1):
            field[z, 0:rows] = jnp.zeros((rows, lanes), jnp.float32)
    for slab, block in zip(slabs, blocks):
        pair = block if isinstance(block, tuple) else (block.at[0], block.at[1])
        for p in range(planes):
            values = pair[0][p], pair[1][p]
            if factor is not None:
                speed = factor[slab + p]
                values = values[0] * speed, values[1] * speed
            first[slab + p + 2, 0:rows], second[slab + p + 2, 0:rows] = values


BATCH = 4
PLANES = 2


def sweep(core, planes, field, banded, y_first, y_second, work):
    order = [(chip, owned) for owned in (True, False) for chip in (0, 1)]
    parts = (y_first, y_second)

    def first(chip, owned):
        return (2 * chip + (core if owned else 1 - core)) * planes

    along_y(field, first(*order[0]), banded, y_first)
    for owned in (True, False):
        for chip in (0, 1):
            z = first(chip, owned)
            onward = first(1, owned) if chip == 0 else first(0, False)
            for n in range(planes // BATCH):
                last = n == planes // BATCH - 1
                if not last or chip == 0 or owned:
                    along_y(field, onward if last else z + (n + 1) * BATCH, banded, parts[(n + 1) % 2])
                work(z + n * BATCH, parts[n % 2], chip if owned else None, n * BATCH)


def forward_kernel(
    start, sources, own0, own1, mate0, mate1, over0, over1, far0, far1, speed, speed_mate, placed, laps, history, held, cour, last,
    even, odd, banded, y0, y1, sems, sems_even, sems_odd
):
    planes, rows, lanes = own0.shape
    steps = laps.shape[0]
    groups = rows // 8
    chip_here, core, slabs = place(planes)

    fetch_all = pltpu.make_async_copy(placed, held, sems.at[0])
    fetch_all.start()

    def keep(k, field, done):
        source = field.at[pl.ds(2, 4 * planes), pl.ds(0, rows)]
        return pltpu.make_async_copy(source, history.at[k], done.at[0])

    banded[...] = band(lanes)
    load_blocks(slabs, ((own0, own1), (mate0, mate1), (over0, over1), (far0, far1)), odd, even)
    head = speed.shape[0] - planes
    for here, across, first, rest in ((slabs[0], slabs[2], speed, own1), (slabs[1], slabs[3], speed_mate, mate1)):
        for p in range(planes):
            cour[across + p] = first[p]
            cour[here + p] = first[planes + p] if p < head else rest[planes + p - head]

    for index in range(2 * planes):
        z = (2 * (index // planes) + core) * planes + index % planes
        weight = 1.0 + 2.0 * jnp.full((rows, lanes), z, jnp.int32).astype(jnp.float32) / (4 * planes - 1)
        last[index] = weight / (12.0 * cour[z])

    cell = sources[chip_here]
    source_z, x, lane = cell // (rows * lanes), cell // lanes % rows, cell % lanes
    tile = pl.ds(pl.multiple_of(x % groups * 8, 8), 8)
    here = (lax.broadcasted_iota(jnp.int32, (8, lanes), 0) == x // groups) & (
        lax.broadcasted_iota(jnp.int32, (8, lanes), 1) == lane
    )
    source_slab, source_p = source_z // planes, lax.rem(source_z, planes)

    def advance(k, now, then, done):
        @pl.when(k >= 2)
        def _():
            keep(k - 2, then, done).wait()

        def work(z, y_part, chip, p):
            def fetch(j, rows):
                return then[z + j + 2, rows], cour[z + j, rows]

            def finish(j, rows, center, lap, extra):
                old, speed = extra
                if chip is not None:
                    laps[k, p + j, chip, rows] = lap
                then[z + j + 2, rows] = 2.0 * center - old + speed * lap

            laps12(now, z, y_part, fetch, finish)

        cycle = (start[0] + k) % 48
        phase = (jnp.full((8, lanes), cycle, jnp.int32).astype(jnp.float32) - 24.0) / 12.0
        wave = AMPLITUDE * (1.0 - 2.0 * phase * phase) * jnp.exp(-phase * phase)
        strength = jnp.where(here, 12.0 * wave, 0.0)
        moved = cour[source_z, tile, :] * strength

        sweep(core, planes, now, banded, y0, y1, work)

        owned = jnp.where(lax.rem(source_slab, 2) == core, strength, 0.0)
        laps[k, source_p, source_slab // 2, tile, :] += owned
        then[source_z + 2, tile, :] += moved
        keep(k, then, done).start()

    @pl.loop(0, steps // 2)
    def _(pair):
        advance(2 * pair, even, odd, sems_odd)
        advance(2 * pair + 1, odd, even, sems_even)

    for k, field, done in ((steps - 2, odd, sems_odd), (steps - 1, even, sems_even)):
        keep(k, field, done).wait()
    fetch_all.wait()


def inject_kernel(held, history, inject):
    steps, planes_all = history.shape[:2]

    @pl.loop(0, planes_all)
    def _(z):
        count = held[steps, z]
        for k in range(steps):
            inject[k, z] = held[k, z] - count * history[k, z]


def adjoint_kernel(own, mate, over, far, cour, laps, inject, last, keep, send_x, send_y, send_xy, even, odd, total, banded, y0, y1):
    planes, rows, lanes = own.shape[1:]
    steps = laps.shape[0]
    groups = rows // 8
    chip_here, core, slabs = place(planes)
    banded[...] = band(lanes)
    load_blocks(slabs, (own, mate, over, far), odd, even, factor=cour)

    total[...] = jnp.zeros(total.shape, jnp.float32)

    def advance(k, now, then):
        def work(z, y_part, chip, p):
            def fetch(j, rows):
                extra = (then[z + j + 2, rows], cour[z + j, rows], inject[k, z + j, rows])
                if chip is not None:
                    extra += (total[chip * planes + p + j, rows], laps[k, p + j, chip, rows])
                return extra

            def finish(j, rows, center, lap, extra):
                newer = 2.0 * center - extra[0] + extra[1] * (lap - extra[2])
                then[z + j + 2, rows] = newer
                if chip is not None:
                    total[chip * planes + p + j, rows] = extra[3] + newer * extra[4]

            laps12(now, z, y_part, fetch, finish)

        sweep(core, planes, now, banded, y0, y1, work)

    @pl.loop(0, steps // 2)
    def _(pair):
        advance(steps - 1 - 2 * pair, even, odd)
        advance(steps - 2 - 2 * pair, odd, even)

    count = keep.shape[0]
    mine, others = lax.axis_index("shot") % 2 * count, (1 - lax.axis_index("shot") % 2) * count
    here, there = chip_here, 1 - chip_here
    for ref, chip, start in ((keep, here, mine), (send_x, there, mine), (send_y, here, others), (send_xy, there, others)):

        @pl.loop(0, count)
        def _(n):
            p = start + n
            value = total[chip * planes + p] * last[chip * planes + p]
            for i in range(groups):
                ref[n, pl.ds(i, 8, stride=groups), :] = value[i * 8 : (i + 1) * 8]


def square_kernel(mine, by_xy, by_y, by_x, keep, send):
    half = lax.axis_index("shot") // 2 % 2
    count = keep.shape[0]
    for ref, part in ((keep, half), (send, 1 - half)):
        for p in range(count):
            at = part * count + p
            ref[p] = (mine[at] + by_x[at]) + (by_y[at] + by_xy[at])


def add_kernel(mine, other, out):
    out[...] = mine[...] + other[...]


def flip(index, bits):
    result = index
    for bit in (1, 2):
        if bits & bit:
            result = jnp.where(index // bit % 2 == 1, result - bit, result + bit)
    return result


def after_kernel(earlier, value, *outs):
    if len(outs) == 1:
        outs[0][...] = value[...]
    else:
        for n, out in enumerate(outs):
            out[...] = value[n]


def after(earlier, value, parts=1):
    vmem, anywhere = pl.BlockSpec(memory_space=pltpu.VMEM), pl.BlockSpec(memory_space=pl.ANY)
    shape = value.shape if parts == 1 else value.shape[1:]
    results = pl.pallas_call(
        after_kernel,
        in_specs=[anywhere, vmem],
        out_specs=[vmem] * parts,
        out_shape=[jax.ShapeDtypeStruct(shape, jnp.float32)] * parts,
        compiler_params=pltpu.CompilerParams(vmem_limit_bytes=4 * 2**20),
        name="after",
    )(earlier, value)
    return results[0] if parts == 1 else results


def arrange_kernel(own, mine, other, out):
    y = lax.axis_index("shot") % 2
    count, planes = mine.shape[0], own.shape[0]
    out[pl.ds(y * count, count)] = mine[...]
    out[pl.ds((1 - y) * count, count)] = other[...]
    out[planes:] = own[0 : out.shape[0] - planes]


def first_plane(shot, planes):
    return (shot % 2) * (planes // 2) + (shot // 2 % 2) * (planes // 4)


def sums_kernel(mine, other, momentum, data, sums):
    count, rows, lanes = mine.shape
    planes = momentum.shape[0]
    chip, core = lax.axis_index("chip"), lax.axis_index("core")
    first = first_plane(lax.axis_index("shot"), planes)
    parts = [jnp.zeros((rows, lanes), jnp.float32)] * 4
    for j in range(count):
        scaled = mine[j] + other[j]
        data[j * rows : (j + 1) * rows] = scaled
        z = (2 * chip + core) * planes + first + j
        weight = 1.0 + 2.0 * jnp.full((1, lanes), z, jnp.int32).astype(jnp.float32) / (4 * planes - 1)
        moment = momentum[first + j]
        square = scaled * scaled
        terms = (square, weight * moment * moment, weight * moment * scaled, weight * square)
        parts = [part + term for part, term in zip(parts, terms)]

    def total(value):
        by_lane = jnp.sum(value, axis=0, keepdims=True)
        return jnp.broadcast_to(jnp.sum(by_lane, axis=1, keepdims=True), (1, lanes))

    value = jnp.concatenate([total(part) for part in parts] + [jnp.zeros((4, lanes), jnp.float32)], 0)
    data[count * rows :] = value
    sums[...] = value


def join_kernel(mine, other, s0, s1, s2, data, sums):
    rows = mine.shape[0] - 8
    data[0:rows] = mine[0:rows]
    data[rows : 2 * rows] = other[0:rows]
    value = (s0[...] + s1[...]) + (other[rows:] + s2[...])
    data[2 * rows :] = value
    sums[...] = value


def finish_kernel(mine, other, momentum, s0, s1, s2, out, kinetic):
    planes, rows, lanes = momentum.shape
    cells = 4.0 * planes * rows * lanes
    shot = lax.axis_index("shot")
    sums = (s0[...] + s1[...]) + (other[planes // 2 * rows :] + s2[...])
    factor = lax.rsqrt(sums[0:1] / cells + EPSILON)
    energy = 0.5 * (sums[1:2] - factor * sums[2:3] + 0.25 * factor * factor * sums[3:4]) / cells
    kinetic[0] = energy[0, 0]
    step = 0.5 * factor
    quarter = planes // 4
    for part, group in ((mine, shot), (other, flip(shot, 1))):
        for number, first in enumerate((first_plane(group, planes), first_plane(flip(group, 2), planes))):
            for j in range(quarter):
                at = (number * quarter + j) * rows
                out[first + j] = momentum[first + j] - step * part[at : at + rows]


def local(kernel, outs, *arrays):
    vmem = pl.BlockSpec(memory_space=pltpu.VMEM)
    shapes = [jax.ShapeDtypeStruct(shape, jnp.float32) for shape in outs]
    single = len(outs) == 1
    return pl.pallas_call(
        kernel,
        in_specs=[vmem] * len(arrays),
        out_specs=vmem if single else [vmem] * len(outs),
        out_shape=shapes[0] if single else shapes,
        compiler_params=pltpu.CompilerParams(vmem_limit_bytes=4 * 2**20),
        name=kernel.__name__,
    )(*arrays)


def exchange(value, bits):
    axes = ("shot", "chip", "core")
    return lax.ppermute(value, axes, [(i, i ^ bits) for i in range(lax.axis_size(axes))])


CORE, CHIP, Y, NEAR_Z, FAR_Z = 1, 2, 4, 8, 16


def whole_shards(
    courant_sq, momentum, fwd_prev, fwd_cur, adj_next, adj_cur, observed, src_cells, rec_cells, ckpt_step
):
    _, planes, rows_x, rows_y = fwd_cur.shape
    steps = observed.shape[1]
    planes_all = 4 * planes
    cells_all = planes_all * rows_x * rows_y
    vmem, smem = pl.BlockSpec(memory_space=pltpu.VMEM), pl.BlockSpec(memory_space=pltpu.SMEM)

    hbm = pl.BlockSpec(memory_space=pltpu.HBM)
    outgoing, c0, piece = pl.pallas_call(
        first_kernel,
        in_specs=[hbm] * 3,
        out_specs=[vmem] * 3,
        out_shape=[
            jax.ShapeDtypeStruct((2, planes, rows_x, rows_y), jnp.float32),
            jax.ShapeDtypeStruct(courant_sq.shape, jnp.float32),
            jax.ShapeDtypeStruct((planes // 2, rows_x, rows_y), jnp.float32),
        ],
        scratch_shapes=[
            pltpu.VMEM((2, planes, rows_x, rows_y), jnp.float32),
            pltpu.VMEM(courant_sq.shape, jnp.float32),
            pltpu.SemaphoreType.DMA((3,)),
        ],
        compiler_params=pltpu.CompilerParams(vmem_limit_bytes=63 * 2**20),
        name="first_to_cross",
    )(fwd_prev, fwd_cur, courant_sq)

    over = exchange(outgoing, CHIP)
    piece = exchange(piece, CHIP)

    placed, mark = scatter(rec_cells, observed, planes_all, rows_x, rows_y)
    placed = placed.reshape(steps + 1, planes_all, rows_x, rows_y)

    piece = after(mark, piece)
    head = planes * 5 // 8
    adj_outgoing, adj_own, *own = pick(adj_next, adj_cur, fwd_prev, fwd_cur, c0, planes - head, piece)
    mate = [exchange(field, CORE) for field in own]
    speed = local(arrange_kernel, [(planes + head, rows_x, rows_y)], c0, piece, exchange(piece, Y))
    speed_mate = exchange(speed, CORE)
    over = after(speed, over, parts=2)
    far = [exchange(field, CORE) for field in over]
    adj_over = exchange(adj_outgoing, CHIP)
    adj_mate = exchange(adj_own, CORE)

    scratch = pltpu.VMEM((planes_all + 4, rows_x + 8, rows_y), jnp.float32)
    y_scratch = pltpu.VMEM((BATCH * rows_x, rows_y), jnp.float32)
    step_scratch = [scratch, scratch, pltpu.VMEM((2 * rows_y, rows_y), jnp.bfloat16), y_scratch, y_scratch]
    params = pltpu.CompilerParams(vmem_limit_bytes=6 * 2**20)
    cost = pl.CostEstimate(flops=30 * steps * cells_all, bytes_accessed=16 * steps * cells_all, transcendentals=0)
    laps, history, held, cour, last = pl.pallas_call(
        forward_kernel,
        in_specs=[smem, smem] + [vmem] * 10 + [pl.BlockSpec(memory_space=pltpu.HBM)],
        out_specs=[vmem] * 5,
        out_shape=[
            jax.ShapeDtypeStruct((steps, planes, 2, rows_x, rows_y), jnp.float32),
            jax.ShapeDtypeStruct((steps, planes_all, rows_x, rows_y), jnp.float32),
            jax.ShapeDtypeStruct((steps + 1, planes_all, rows_x, rows_y), jnp.float32),
            jax.ShapeDtypeStruct((planes_all, rows_x, rows_y), jnp.float32),
            jax.ShapeDtypeStruct((2 * planes, rows_x, rows_y), jnp.float32),
        ],
        scratch_shapes=step_scratch
        + [
            pltpu.SemaphoreType.DMA((1,)),
            pltpu.SemaphoreType.DMA((1,)),
            pltpu.SemaphoreType.DMA((1,)),
        ],
        compiler_params=pltpu.CompilerParams(vmem_limit_bytes=21 * 2**20),
        cost_estimate=pl.CostEstimate(flops=1000, bytes_accessed=1000, transcendentals=0),
        name="forward_steps",
    )(ckpt_step[None], src_cells, *own, *mate, *over, *far, speed, speed_mate, placed)

    adj_over = after(laps, adj_over)
    adj_far = exchange(adj_over, CORE)
    inject = pl.pallas_call(
        inject_kernel,
        in_specs=[vmem] * 2,
        out_specs=vmem,
        out_shape=jax.ShapeDtypeStruct(history.shape, jnp.float32),
        compiler_params=pltpu.CompilerParams(vmem_limit_bytes=4 * 2**20),
        name="inject",
    )(held, history)
    slab = jax.ShapeDtypeStruct(courant_sq.shape, jnp.float32)
    half, quarter = (planes // 2, rows_x, rows_y), (planes // 4, rows_x, rows_y)
    keep, send_x, send_y, send_xy = pl.pallas_call(
        adjoint_kernel,
        in_specs=[vmem] * 8,
        out_specs=[vmem] * 4,
        out_shape=[jax.ShapeDtypeStruct(half, jnp.float32)] * 4,
        scratch_shapes=step_scratch[:2] + [pltpu.VMEM((2 * planes, rows_x, rows_y), jnp.float32)] + step_scratch[2:],
        compiler_params=params,
        cost_estimate=cost,
        name="adjoint_steps",
    )(adj_own, adj_mate, adj_over, adj_far, cour, laps, inject, last)

    by_xy, by_x, by_y = exchange(send_xy, CHIP + Y), exchange(send_x, CHIP), exchange(send_y, Y)
    keep, send = local(square_kernel, [quarter] * 2, keep, by_xy, by_y, by_x)
    part = local(add_kernel, [quarter], keep, exchange(send, NEAR_Z))
    rows, sums_shape = planes // 4 * rows_x, (8, rows_y)
    data, sums = local(sums_kernel, [(rows + 8, rows_y), sums_shape], part, exchange(part, FAR_Z), momentum)

    received = exchange(data, NEAR_Z)
    others = [exchange(sums, CORE), exchange(sums, NEAR_Z + CORE)]
    data, sums = local(join_kernel, [(2 * rows + 8, rows_y), sums_shape], data, received, sums, *others)
    received = exchange(data, Y)
    others = [exchange(sums, CHIP), exchange(sums, Y + CHIP)]
    momentum_half, kinetic = pl.pallas_call(
        finish_kernel,
        in_specs=[vmem] * 6,
        out_specs=[vmem, smem],
        out_shape=[jax.ShapeDtypeStruct(momentum.shape, jnp.float32), jax.ShapeDtypeStruct((1,), jnp.float32)],
        compiler_params=pltpu.CompilerParams(vmem_limit_bytes=4 * 2**20),
        name="finish",
    )(data, received, momentum, sums, *others)
    return momentum_half, kinetic[0]


def solution(mesh):
    shots, slabs = mesh.shape["shot"], mesh.shape["depth"]

    def placed(depth):
        field = P("shot", depth, None, None)
        slab = P(depth, None, None)
        inputs = (slab, slab, field, field, field, field, P("shot", None, None), P("shot"), P("shot", None), P())
        return dict(in_specs=inputs, out_specs=(slab, P()), check_vma=False)

    slab_plan = jax.shard_map(slab_shards, mesh=mesh, **placed("depth"))
    if slabs != 4 or shots != 8:
        return slab_plan
    chips = Mesh(mesh.devices.reshape(shots, 2, 2), ("shot", "chip", "core"))
    whole_plan = jax.shard_map(whole_shards, mesh=chips, **placed(("chip", "core")))

    def run(courant_sq, momentum, fwd_prev, *rest):
        total, planes, rows_x, rows_y = fwd_prev.shape
        steps = rest[3].shape[1]
        fits = total == 2 * shots and planes == 4 * shots and rows_y == 128 and rows_x % 16 == 0 and steps % 2 == 0
        plan = whole_plan if fits else slab_plan
        return plan(courant_sq, momentum, fwd_prev, *rest)

    return run
```

```python
import functools

import jax
import jax.numpy as jnp
from jax import lax
from jax.experimental import pallas as pl
from jax.experimental.pallas import tpu as pltpu
from jax.sharding import Mesh
from jax.sharding import PartitionSpec as P

CENTER = -2.5
NEAR = 4.0 / 3.0
FAR = -1.0 / 12.0
AMPLITUDE = 100.0
EPSILON = 1e-06


def with_halo(value, sides, width):
    for axis, dim in sides:
        size, length = (lax.axis_size(axis), value.shape[dim])
        up = [(i, (i + 1) % size) for i in range(size - 1)]
        down = [(j, i) for i, j in up]
        last = lax.slice_in_dim(value, length - width, length, axis=dim)
        leading = lax.slice_in_dim(value, 0, width, axis=dim)
        before = lax.ppermute(last, axis, up)
        after = lax.ppermute(leading, axis, down)
        value = jnp.concatenate([before, value, after], axis=dim)
    return value


def laplace(padded):
    lateral = jnp.pad(padded[:, 2:-2], ((0, 0), (0, 0), (2, 2), (2, 2)))
    center = padded[:, 2:-2]
    along_z = NEAR * (padded[:, 1:-3] + padded[:, 3:-1]) + FAR * (padded[:, :-4] + padded[:, 4:])
    along_x = NEAR * (lateral[:, :, 1:-3, 2:-2] + lateral[:, :, 3:-1, 2:-2]) + FAR * (
        lateral[:, :, :-4, 2:-2] + lateral[:, :, 4:, 2:-2]
    )
    along_y = NEAR * (lateral[:, :, 2:-2, 1:-3] + lateral[:, :, 2:-2, 3:-1]) + FAR * (
        lateral[:, :, 2:-2, :-4] + lateral[:, :, 2:-2, 4:]
    )
    return 3.0 * CENTER * center + along_z + along_x + along_y


def locate(field, cell_ids, first_plane):
    shot_count, planes, rows_x, rows_y = field.shape
    plane_cells = rows_x * rows_y
    local_index = cell_ids - first_plane * plane_cells
    inside = (local_index >= 0) & (local_index < planes * plane_cells)
    target = jnp.where(inside, local_index, 0)
    return (inside, target)


def inject(field, cell_ids, values, first_plane):
    shot_count = field.shape[0]
    inside, target = locate(field, cell_ids, first_plane)
    amount = jnp.where(inside, values, jnp.zeros_like(values))
    flattened = field.reshape(shot_count, -1)
    lanes = jnp.arange(shot_count)[:, None]
    flattened = flattened.at[lanes, target].add(amount)
    return flattened.reshape(field.shape)


def sample(field, cell_ids, first_plane):
    shot_count = field.shape[0]
    inside, target = locate(field, cell_ids, first_plane)
    values = jnp.take_along_axis(field.reshape(shot_count, -1), target, axis=1)
    return jnp.where(inside, values, jnp.zeros_like(values))


def wave_value(start, step):
    cycle = jnp.mod(start + jnp.int32(step), jnp.int32(48))
    phase = (cycle.astype(jnp.float32) - 24.0) / 12.0
    return AMPLITUDE * (1.0 - 2.0 * phase * phase) * jnp.exp(-phase * phase)


def statistics(scaled, moment, weight, cells_all):
    grand_total = lax.psum(jnp.sum(scaled * scaled), ("shot", "depth"))
    factor = lax.rsqrt(grand_total / cells_all + EPSILON)
    halfway = moment - 0.5 * factor * scaled
    energy = lax.psum(jnp.sum(weight * halfway * halfway), ("shot", "depth"))
    return (factor, 0.5 * energy / cells_all)


def slab_shards(
    courant_sq,
    momentum,
    fwd_prev,
    fwd_cur,
    adj_next,
    adj_cur,
    observed,
    src_cells,
    rec_cells,
    ckpt_step,
):
    shot_count, planes, rows_x, rows_y = fwd_cur.shape
    steps_all = observed.shape[1]
    first_plane = lax.axis_index("depth") * planes
    total_planes = planes * lax.axis_size("depth")
    cells_all = total_planes * rows_x * rows_y
    sources = src_cells[:, None]
    older, current = (fwd_prev, fwd_cur)
    laplacians = []
    misfits = []
    for step in range(steps_all):
        padded = with_halo(current, (("depth", 1),), 2)
        strength = jnp.full(sources.shape, wave_value(ckpt_step, step), jnp.float32)
        laplacian = inject(laplace(padded), sources, strength, first_plane)
        newer = 2.0 * current - older + courant_sq * laplacian
        misfits.append(sample(newer, rec_cells, first_plane) - observed[:, step, :])
        laplacians.append(laplacian)
        older, current = (current, newer)
    adj_later, adj_now = (adj_next, adj_cur)
    gradient = jnp.zeros((planes, rows_x, rows_y), jnp.float32)
    for step in reversed(range(steps_all)):
        padded = with_halo(courant_sq * adj_now, (("depth", 1),), 2)
        adj_new = 2.0 * adj_now - adj_later + laplace(padded)
        adj_new = inject(adj_new, rec_cells, misfits[step], first_plane)
        gradient = gradient + jnp.sum(adj_new * laplacians[step], axis=0)
        adj_later, adj_now = (adj_now, adj_new)
    depths = (first_plane + jnp.arange(planes)).astype(jnp.float32)
    weight = (1.0 + 2.0 * depths / (total_planes - 1))[:, None, None]
    share_rows = rows_x // lax.axis_size("shot")
    offset = lax.axis_index("shot") * share_rows
    moment_share = lax.dynamic_slice_in_dim(momentum, offset, share_rows, 1)
    gradient = lax.psum(gradient, "shot")
    scaled = weight * gradient
    scaled_share = lax.dynamic_slice_in_dim(scaled, offset, share_rows, 1)
    factor, kinetic = statistics(scaled_share, moment_share, weight, cells_all)
    momentum_half = momentum - 0.5 * factor * scaled
    return (momentum_half, kinetic)


def interleave(dst, slab, src, factor=None):
    planes, rows = src.shape[0], src.shape[1]
    groups = rows // 8

    @pl.loop(0, planes)
    def _(p):
        for i in range(groups):
            value = src[p, pl.ds(i, 8, stride=groups), :]
            if factor is not None:
                value = value * factor
            dst[(*slab, p, pl.ds(i * 8, 8), slice(None))] = value


def pick_kernel(earlier, adj_next, adj_cur, fwd_prev, fwd_cur, speed, adj_out, adj_own, prev_own, cur_own, held, sems):
    chip = lax.axis_index("chip")
    planes = adj_own.shape[1]
    wanted = (
        (adj_next, 1 - chip, adj_out, (0,)),
        (adj_cur, 1 - chip, adj_out, (1,)),
        (adj_next, chip, adj_own, (0,)),
        (adj_cur, chip, adj_own, (1,)),
        (fwd_prev, chip, prev_own, ()),
        (fwd_cur, chip, cur_own, ()),
    )
    copies = []
    for n, (field, shot, _, _) in enumerate(wanted):
        copies.append(pltpu.make_async_copy(field.at[shot], held.at[n], sems.at[n]))
        copies[-1].start()
    for n, (_, _, out, slab) in enumerate(wanted):
        copies[n].wait()
        interleave(out, slab, held.at[n])
    tail = cur_own.shape[0] - planes
    cur_own[planes:] = speed[planes - tail :]


def pick(adj_next, adj_cur, fwd_prev, fwd_cur, speed, tail, earlier):
    planes, *plane = fwd_cur.shape[1:]
    vmem, hbm = pl.BlockSpec(memory_space=pltpu.VMEM), pl.BlockSpec(memory_space=pltpu.HBM)
    shapes = [(2, planes, *plane), (2, planes, *plane), (planes, *plane), (planes + tail, *plane)]
    return pl.pallas_call(
        pick_kernel,
        in_specs=[pl.BlockSpec(memory_space=pl.ANY)] + [hbm] * 4 + [vmem],
        out_specs=[vmem] * 4,
        out_shape=[jax.ShapeDtypeStruct(shape, jnp.float32) for shape in shapes],
        scratch_shapes=[pltpu.VMEM((6, planes, *plane), jnp.float32), pltpu.SemaphoreType.DMA((6,))],
        compiler_params=pltpu.CompilerParams(vmem_limit_bytes=4 * 2**20),
        name="pick",
    )(earlier, adj_next, adj_cur, fwd_prev, fwd_cur, speed)


def first_kernel(first, second, courant, outgoing, whole, piece, held, held_courant, sems):
    shot = 1 - lax.axis_index("chip")
    copies = [
        pltpu.make_async_copy(first.at[shot], held.at[0], sems.at[0]),
        pltpu.make_async_copy(second.at[shot], held.at[1], sems.at[1]),
        pltpu.make_async_copy(courant, held_courant, sems.at[2]),
    ]
    for copy in copies:
        copy.start()
    for n in range(2):
        copies[n].wait()
        interleave(outgoing, (n,), held.at[n])
    copies[2].wait()
    interleave(whole, (), held_courant, 1.0 / 12.0)
    count = piece.shape[0]
    piece[...] = whole[pl.ds(lax.axis_index("shot") % 2 * count, count)]


def band(lanes):
    near = jnp.abs(lax.broadcasted_iota(jnp.int32, (2 * lanes, lanes), 0) % lanes - lax.broadcasted_iota(jnp.int32, (2 * lanes, lanes), 1))
    return jnp.where(near == 0, -90.0, jnp.where(near == 1, 16.0, jnp.where(near == 2, -1.0, 0.0))).astype(jnp.bfloat16)


def along_y(field, z, banded, out):
    rows, lanes = field.shape[1] - 8, field.shape[2]
    whole = field[pl.ds(z + 2, BATCH), 0:rows].reshape(BATCH * rows, lanes)
    high = whole.astype(jnp.bfloat16)
    low = (whole - high.astype(jnp.float32)).astype(jnp.bfloat16)
    out[...] = jnp.dot(jnp.concatenate([high, low], 1), banded[...], preferred_element_type=jnp.float32)


def laps12(field, z, y_part, fetch, finish):
    rows, lanes = field.shape[1] - 8, field.shape[2]
    groups = rows // 8
    sub = lax.broadcasted_iota(jnp.int32, (8, lanes), 0)

    def later(block):
        return jnp.where(sub < 7, pltpu.roll(block, 7, 0), 0.0)

    def earlier(block):
        return jnp.where(sub > 0, pltpu.roll(block, 1, 0), 0.0)

    for base in range(0, BATCH, PLANES):
        held = {}

        def tile(j, i):
            if (j, i) not in held:
                if i < 0:
                    held[j, i] = earlier(tile(j, i + groups))
                elif i >= groups:
                    held[j, i] = later(tile(j, i - groups))
                else:
                    held[j, i] = field[z + j + 2, i * 8 : (i + 1) * 8]
            return held[j, i]

        def load(i):
            found = []
            for j in range(base, base + PLANES):
                center = tile(j, i)
                near = (tile(j, i - 1), tile(j, i + 1), tile(j - 1, i), tile(j + 1, i))
                far = (tile(j, i - 2), tile(j, i + 2), tile(j - 2, i), tile(j + 2, i))
                at = (j * groups + i) * 8
                found.append((center, near, far, y_part[at : at + 8], fetch(j, slice(i * 8, i * 8 + 8))))
            return found

        ready = load(0)
        for i in range(groups):
            upcoming = load(i + 1) if i + 1 < groups else None
            for j, (center, near, far, part, extra) in enumerate(ready):
                near = (near[0] + near[1]) + (near[2] + near[3])
                far = (far[0] + far[1]) + (far[2] + far[3])
                finish(base + j, slice(i * 8, i * 8 + 8), center, 16.0 * near + (part - far), extra)
            ready = upcoming


def scatter_kernel(rows_x, cells_ref, observed_ref, out_ref, mark, row_ref, spread):
    _, steps, receivers = observed_ref.shape
    lanes = out_ref.shape[2]
    tile = out_ref.shape[1]
    groups = rows_x // 8

    @pl.when(pl.program_id(0) == 0)
    def _():
        chip = lax.axis_index("chip")
        cells = cells_ref[pl.ds(chip, 1)]
        x = cells // lanes % rows_x
        row_ref[...] = cells // (rows_x * lanes) * rows_x + x % groups * 8 + x // groups
        on_lanes = jnp.concatenate(
            [
                observed_ref[chip],
                jnp.broadcast_to((cells % lanes).astype(jnp.float32), (8, receivers)),
                jnp.zeros((lanes - steps - 8, receivers), jnp.float32),
            ],
            0,
        )
        columns = on_lanes.T
        lane = lax.broadcasted_iota(jnp.int32, (receivers, lanes), 1).astype(jnp.float32)
        at = lane == columns[:, steps : steps + 1]
        for k in range(steps):
            column = columns[:, k : k + 1]
            high = column.astype(jnp.bfloat16).astype(jnp.float32)
            low = column - high
            cols = pl.ds(k * lanes, lanes)
            spread[0:receivers, cols] = jnp.where(at, high, 0.0).astype(jnp.bfloat16)
            spread[receivers:, cols] = jnp.where(at, low, 0.0).astype(jnp.bfloat16)
        cols = pl.ds(steps * lanes, lanes)
        spread[0:receivers, cols] = jnp.where(at, 1.0, 0.0).astype(jnp.bfloat16)
        spread[receivers:, cols] = jnp.zeros((receivers, lanes), jnp.bfloat16)
        mark[...] = jnp.zeros(mark.shape, jnp.float32)

    ids = lax.broadcasted_iota(jnp.int32, (tile, receivers), 0) + pl.program_id(0) * tile
    chosen = jnp.where(ids == row_ref[...], 1.0, 0.0).astype(jnp.bfloat16)
    total = jnp.dot(jnp.concatenate([chosen, chosen], 1), spread[...], preferred_element_type=jnp.float32)
    for k in range(steps + 1):
        out_ref[k] = total[:, k * lanes : (k + 1) * lanes]


def scatter(rec_cells, observed, planes_all, rows_x, rows_y):
    _, steps, receivers = observed.shape
    rows_all = planes_all * rows_x
    tile = 512
    return pl.pallas_call(
        functools.partial(scatter_kernel, rows_x),
        grid=(rows_all // tile,),
        in_specs=[
            pl.BlockSpec((2, receivers), lambda t: (0, 0)),
            pl.BlockSpec((2, steps, receivers), lambda t: (0, 0, 0)),
        ],
        out_specs=[
            pl.BlockSpec((steps + 1, tile, rows_y), lambda t: (0, t, 0)),
            pl.BlockSpec((8, rows_y), lambda t: (0, 0)),
        ],
        out_shape=[
            jax.ShapeDtypeStruct((steps + 1, rows_all, rows_y), jnp.float32),
            jax.ShapeDtypeStruct((8, rows_y), jnp.float32),
        ],
        scratch_shapes=[
            pltpu.VMEM((1, receivers), jnp.int32),
            pltpu.VMEM((2 * receivers, (steps + 1) * rows_y), jnp.bfloat16),
        ],
        compiler_params=pltpu.CompilerParams(vmem_limit_bytes=56 * 2**20),
        cost_estimate=pl.CostEstimate(
            flops=4 * rows_all * receivers * (steps + 1) * rows_y,
            bytes_accessed=4 * (steps + 1) * rows_all * rows_y,
            transcendentals=0,
        ),
        name="receiver_scatter",
    )(rec_cells, observed)


def place(planes):
    chip, core = lax.axis_index("chip"), lax.axis_index("core")
    slabs = (2 * chip + core, 2 * chip + 1 - core, 2 * (1 - chip) + core, 2 * (1 - chip) + 1 - core)
    return chip, core, [slab * planes for slab in slabs]


def load_blocks(slabs, blocks, first, second, factor=None):
    ends, rows, lanes = first.shape[0], first.shape[1] - 8, first.shape[2]
    planes = (ends - 4) // 4
    for field in (first, second):
        for z in (0, 1, ends - 2, ends - 1):
            field[z, 0:rows] = jnp.zeros((rows, lanes), jnp.float32)
    for slab, block in zip(slabs, blocks):
        pair = block if isinstance(block, tuple) else (block.at[0], block.at[1])
        for p in range(planes):
            values = pair[0][p], pair[1][p]
            if factor is not None:
                speed = factor[slab + p]
                values = values[0] * speed, values[1] * speed
            first[slab + p + 2, 0:rows], second[slab + p + 2, 0:rows] = values


BATCH = 4
PLANES = 2


def sweep(core, planes, field, banded, y_first, y_second, work):
    order = [(chip, owned) for owned in (True, False) for chip in (0, 1)]
    parts = (y_first, y_second)

    def first(chip, owned):
        return (2 * chip + (core if owned else 1 - core)) * planes

    along_y(field, first(*order[0]), banded, y_first)
    for owned in (True, False):
        for chip in (0, 1):
            z = first(chip, owned)
            onward = first(1, owned) if chip == 0 else first(0, False)
            for n in range(planes // BATCH):
                last = n == planes // BATCH - 1
                if not last or chip == 0 or owned:
                    along_y(field, onward if last else z + (n + 1) * BATCH, banded, parts[(n + 1) % 2])
                work(z + n * BATCH, parts[n % 2], chip if owned else None, n * BATCH)


def forward_kernel(
    start, sources, own0, own1, mate0, mate1, over0, over1, far0, far1, speed, speed_mate, placed, laps, history, held, cour, last,
    even, odd, banded, y0, y1, sems, sems_even, sems_odd
):
    planes, rows, lanes = own0.shape
    steps = laps.shape[0]
    groups = rows // 8
    chip_here, core, slabs = place(planes)

    fetch_all = pltpu.make_async_copy(placed, held, sems.at[0])
    fetch_all.start()

    def keep(k, field, done):
        source = field.at[pl.ds(2, 4 * planes), pl.ds(0, rows)]
        return pltpu.make_async_copy(source, history.at[k], done.at[0])

    banded[...] = band(lanes)
    load_blocks(slabs, ((own0, own1), (mate0, mate1), (over0, over1), (far0, far1)), odd, even)
    head = speed.shape[0] - planes
    for here, across, first, rest in ((slabs[0], slabs[2], speed, own1), (slabs[1], slabs[3], speed_mate, mate1)):
        for p in range(planes):
            cour[across + p] = first[p]
            cour[here + p] = first[planes + p] if p < head else rest[planes + p - head]

    for index in range(2 * planes):
        z = (2 * (index // planes) + core) * planes + index % planes
        weight = 1.0 + 2.0 * jnp.full((rows, lanes), z, jnp.int32).astype(jnp.float32) / (4 * planes - 1)
        last[index] = weight / (12.0 * cour[z])

    cell = sources[chip_here]
    source_z, x, lane = cell // (rows * lanes), cell // lanes % rows, cell % lanes
    tile = pl.ds(pl.multiple_of(x % groups * 8, 8), 8)
    here = (lax.broadcasted_iota(jnp.int32, (8, lanes), 0) == x // groups) & (
        lax.broadcasted_iota(jnp.int32, (8, lanes), 1) == lane
    )
    source_slab, source_p = source_z // planes, lax.rem(source_z, planes)

    def advance(k, now, then, done):
        @pl.when(k >= 2)
        def _():
            keep(k - 2, then, done).wait()

        def work(z, y_part, chip, p):
            def fetch(j, rows):
                return then[z + j + 2, rows], cour[z + j, rows]

            def finish(j, rows, center, lap, extra):
                old, speed = extra
                if chip is not None:
                    laps[k, p + j, chip, rows] = lap
                then[z + j + 2, rows] = 2.0 * center - old + speed * lap

            laps12(now, z, y_part, fetch, finish)

        cycle = (start[0] + k) % 48
        phase = (jnp.full((8, lanes), cycle, jnp.int32).astype(jnp.float32) - 24.0) / 12.0
        wave = AMPLITUDE * (1.0 - 2.0 * phase * phase) * jnp.exp(-phase * phase)
        strength = jnp.where(here, 12.0 * wave, 0.0)
        moved = cour[source_z, tile, :] * strength

        sweep(core, planes, now, banded, y0, y1, work)

        owned = jnp.where(lax.rem(source_slab, 2) == core, strength, 0.0)
        laps[k, source_p, source_slab // 2, tile, :] += owned
        then[source_z + 2, tile, :] += moved
        keep(k, then, done).start()

    @pl.loop(0, steps // 2)
    def _(pair):
        advance(2 * pair, even, odd, sems_odd)
        advance(2 * pair + 1, odd, even, sems_even)

    for k, field, done in ((steps - 2, odd, sems_odd), (steps - 1, even, sems_even)):
        keep(k, field, done).wait()
    fetch_all.wait()


def inject_kernel(held, history, inject):
    steps, planes_all = history.shape[:2]

    @pl.loop(0, planes_all)
    def _(z):
        count = held[steps, z]
        for k in range(steps):
            inject[k, z] = held[k, z] - count * history[k, z]


def adjoint_kernel(own, mate, over, far, cour, laps, inject, last, keep, send_x, send_y, send_xy, even, odd, total, banded, y0, y1):
    planes, rows, lanes = own.shape[1:]
    steps = laps.shape[0]
    groups = rows // 8
    chip_here, core, slabs = place(planes)
    banded[...] = band(lanes)
    load_blocks(slabs, (own, mate, over, far), odd, even, factor=cour)

    total[...] = jnp.zeros(total.shape, jnp.float32)

    def advance(k, now, then):
        def work(z, y_part, chip, p):
            def fetch(j, rows):
                extra = (then[z + j + 2, rows], cour[z + j, rows], inject[k, z + j, rows])
                if chip is not None:
                    extra += (total[chip * planes + p + j, rows], laps[k, p + j, chip, rows])
                return extra

            def finish(j, rows, center, lap, extra):
                newer = 2.0 * center - extra[0] + extra[1] * (lap - extra[2])
                then[z + j + 2, rows] = newer
                if chip is not None:
                    total[chip * planes + p + j, rows] = extra[3] + newer * extra[4]

            laps12(now, z, y_part, fetch, finish)

        sweep(core, planes, now, banded, y0, y1, work)

    @pl.loop(0, steps // 2)
    def _(pair):
        advance(steps - 1 - 2 * pair, even, odd)
        advance(steps - 2 - 2 * pair, odd, even)

    count = keep.shape[0]
    mine, others = lax.axis_index("shot") % 2 * count, (1 - lax.axis_index("shot") % 2) * count
    here, there = chip_here, 1 - chip_here
    for ref, chip, start in ((keep, here, mine), (send_x, there, mine), (send_y, here, others), (send_xy, there, others)):

        @pl.loop(0, count)
        def _(n):
            p = start + n
            value = total[chip * planes + p] * last[chip * planes + p]
            for i in range(groups):
                ref[n, pl.ds(i, 8, stride=groups), :] = value[i * 8 : (i + 1) * 8]


def square_kernel(mine, by_xy, by_y, by_x, keep, send):
    half = lax.axis_index("shot") // 2 % 2
    count = keep.shape[0]
    for ref, part in ((keep, half), (send, 1 - half)):
        for p in range(count):
            at = part * count + p
            ref[p] = (mine[at] + by_x[at]) + (by_y[at] + by_xy[at])


def add_kernel(mine, other, out):
    out[...] = mine[...] + other[...]


def flip(index, bits):
    result = index
    for bit in (1, 2):
        if bits & bit:
            result = jnp.where(index // bit % 2 == 1, result - bit, result + bit)
    return result


def after_kernel(earlier, value, *outs):
    if len(outs) == 1:
        outs[0][...] = value[...]
    else:
        for n, out in enumerate(outs):
            out[...] = value[n]


def after(earlier, value, parts=1):
    vmem, anywhere = pl.BlockSpec(memory_space=pltpu.VMEM), pl.BlockSpec(memory_space=pl.ANY)
    shape = value.shape if parts == 1 else value.shape[1:]
    results = pl.pallas_call(
        after_kernel,
        in_specs=[anywhere, vmem],
        out_specs=[vmem] * parts,
        out_shape=[jax.ShapeDtypeStruct(shape, jnp.float32)] * parts,
        compiler_params=pltpu.CompilerParams(vmem_limit_bytes=4 * 2**20),
        name="after",
    )(earlier, value)
    return results[0] if parts == 1 else results


def arrange_kernel(own, mine, other, out):
    y = lax.axis_index("shot") % 2
    count, planes = mine.shape[0], own.shape[0]
    out[pl.ds(y * count, count)] = mine[...]
    out[pl.ds((1 - y) * count, count)] = other[...]
    out[planes:] = own[0 : out.shape[0] - planes]


def first_plane(shot, planes):
    return (shot % 2) * (planes // 2) + (shot // 2 % 2) * (planes // 4)


def sums_kernel(mine, other, momentum, data, sums):
    count, rows, lanes = mine.shape
    planes = momentum.shape[0]
    chip, core = lax.axis_index("chip"), lax.axis_index("core")
    first = first_plane(lax.axis_index("shot"), planes)
    parts = [jnp.zeros((rows, lanes), jnp.float32)] * 4
    for j in range(count):
        scaled = mine[j] + other[j]
        data[j * rows : (j + 1) * rows] = scaled
        z = (2 * chip + core) * planes + first + j
        weight = 1.0 + 2.0 * jnp.full((1, lanes), z, jnp.int32).astype(jnp.float32) / (4 * planes - 1)
        moment = momentum[first + j]
        square = scaled * scaled
        terms = (square, weight * moment * moment, weight * moment * scaled, weight * square)
        parts = [part + term for part, term in zip(parts, terms)]

    def total(value):
        by_lane = jnp.sum(value, axis=0, keepdims=True)
        return jnp.broadcast_to(jnp.sum(by_lane, axis=1, keepdims=True), (1, lanes))

    value = jnp.concatenate([total(part) for part in parts] + [jnp.zeros((4, lanes), jnp.float32)], 0)
    data[count * rows :] = value
    sums[...] = value


def join_kernel(mine, other, s0, s1, s2, data, sums):
    rows = mine.shape[0] - 8
    data[0:rows] = mine[0:rows]
    data[rows : 2 * rows] = other[0:rows]
    value = (s0[...] + s1[...]) + (other[rows:] + s2[...])
    data[2 * rows :] = value
    sums[...] = value


def finish_kernel(s2, other, s1, mine, momentum, s0, out, kinetic):
    planes, rows, lanes = momentum.shape
    cells = 4.0 * planes * rows * lanes
    shot = lax.axis_index("shot")
    sums = (s0[...] + s1[...]) + (other[planes // 2 * rows :] + s2[...])
    factor = lax.rsqrt(sums[0:1] / cells + EPSILON)
    energy = 0.5 * (sums[1:2] - factor * sums[2:3] + 0.25 * factor * factor * sums[3:4]) / cells
    kinetic[0] = energy[0, 0]
    step = 0.5 * factor
    quarter = planes // 4
    for part, group in ((mine, shot), (other, flip(shot, 1))):
        for number, first in enumerate((first_plane(group, planes), first_plane(flip(group, 2), planes))):
            for j in range(quarter):
                at = (number * quarter + j) * rows
                out[first + j] = momentum[first + j] - step * part[at : at + rows]


def local(kernel, outs, *arrays):
    vmem = pl.BlockSpec(memory_space=pltpu.VMEM)
    shapes = [jax.ShapeDtypeStruct(shape, jnp.float32) for shape in outs]
    single = len(outs) == 1
    return pl.pallas_call(
        kernel,
        in_specs=[vmem] * len(arrays),
        out_specs=vmem if single else [vmem] * len(outs),
        out_shape=shapes[0] if single else shapes,
        compiler_params=pltpu.CompilerParams(vmem_limit_bytes=4 * 2**20),
        name=kernel.__name__,
    )(*arrays)


def exchange(value, bits):
    axes = ("shot", "chip", "core")
    return lax.ppermute(value, axes, [(i, i ^ bits) for i in range(lax.axis_size(axes))])


CORE, CHIP, Y, NEAR_Z, FAR_Z = 1, 2, 4, 8, 16


def whole_shards(
    courant_sq, momentum, fwd_prev, fwd_cur, adj_next, adj_cur, observed, src_cells, rec_cells, ckpt_step
):
    _, planes, rows_x, rows_y = fwd_cur.shape
    steps = observed.shape[1]
    planes_all = 4 * planes
    cells_all = planes_all * rows_x * rows_y
    vmem, smem = pl.BlockSpec(memory_space=pltpu.VMEM), pl.BlockSpec(memory_space=pltpu.SMEM)

    hbm = pl.BlockSpec(memory_space=pltpu.HBM)
    outgoing, c0, piece = pl.pallas_call(
        first_kernel,
        in_specs=[hbm] * 3,
        out_specs=[vmem] * 3,
        out_shape=[
            jax.ShapeDtypeStruct((2, planes, rows_x, rows_y), jnp.float32),
            jax.ShapeDtypeStruct(courant_sq.shape, jnp.float32),
            jax.ShapeDtypeStruct((planes // 2, rows_x, rows_y), jnp.float32),
        ],
        scratch_shapes=[
            pltpu.VMEM((2, planes, rows_x, rows_y), jnp.float32),
            pltpu.VMEM(courant_sq.shape, jnp.float32),
            pltpu.SemaphoreType.DMA((3,)),
        ],
        compiler_params=pltpu.CompilerParams(vmem_limit_bytes=63 * 2**20),
        name="first_to_cross",
    )(fwd_prev, fwd_cur, courant_sq)

    over = exchange(outgoing, CHIP)
    piece = exchange(piece, CHIP)

    placed, mark = scatter(rec_cells, observed, planes_all, rows_x, rows_y)
    placed = placed.reshape(steps + 1, planes_all, rows_x, rows_y)

    piece = after(mark, piece)
    head = planes * 5 // 8
    adj_outgoing, adj_own, *own = pick(adj_next, adj_cur, fwd_prev, fwd_cur, c0, planes - head, piece)
    mate = [exchange(field, CORE) for field in own]
    speed = local(arrange_kernel, [(planes + head, rows_x, rows_y)], c0, piece, exchange(piece, Y))
    speed_mate = exchange(speed, CORE)
    over = after(speed, over, parts=2)
    far = [exchange(field, CORE) for field in over]
    adj_over = exchange(adj_outgoing, CHIP)
    adj_mate = exchange(adj_own, CORE)

    scratch = pltpu.VMEM((planes_all + 4, rows_x + 8, rows_y), jnp.float32)
    y_scratch = pltpu.VMEM((BATCH * rows_x, rows_y), jnp.float32)
    step_scratch = [scratch, scratch, pltpu.VMEM((2 * rows_y, rows_y), jnp.bfloat16), y_scratch, y_scratch]
    params = pltpu.CompilerParams(vmem_limit_bytes=6 * 2**20)
    cost = pl.CostEstimate(flops=30 * steps * cells_all, bytes_accessed=16 * steps * cells_all, transcendentals=0)
    laps, history, held, cour, last = pl.pallas_call(
        forward_kernel,
        in_specs=[smem, smem] + [vmem] * 10 + [pl.BlockSpec(memory_space=pltpu.HBM)],
        out_specs=[vmem] * 5,
        out_shape=[
            jax.ShapeDtypeStruct((steps, planes, 2, rows_x, rows_y), jnp.float32),
            jax.ShapeDtypeStruct((steps, planes_all, rows_x, rows_y), jnp.float32),
            jax.ShapeDtypeStruct((steps + 1, planes_all, rows_x, rows_y), jnp.float32),
            jax.ShapeDtypeStruct((planes_all, rows_x, rows_y), jnp.float32),
            jax.ShapeDtypeStruct((2 * planes, rows_x, rows_y), jnp.float32),
        ],
        scratch_shapes=step_scratch
        + [
            pltpu.SemaphoreType.DMA((1,)),
            pltpu.SemaphoreType.DMA((1,)),
            pltpu.SemaphoreType.DMA((1,)),
        ],
        compiler_params=pltpu.CompilerParams(vmem_limit_bytes=21 * 2**20),
        cost_estimate=pl.CostEstimate(flops=1000, bytes_accessed=1000, transcendentals=0),
        name="forward_steps",
    )(ckpt_step[None], src_cells, *own, *mate, *over, *far, speed, speed_mate, placed)

    adj_over = after(laps, adj_over)
    adj_far = exchange(adj_over, CORE)
    inject = pl.pallas_call(
        inject_kernel,
        in_specs=[vmem] * 2,
        out_specs=vmem,
        out_shape=jax.ShapeDtypeStruct(history.shape, jnp.float32),
        compiler_params=pltpu.CompilerParams(vmem_limit_bytes=4 * 2**20),
        name="inject",
    )(held, history)
    slab = jax.ShapeDtypeStruct(courant_sq.shape, jnp.float32)
    half, quarter = (planes // 2, rows_x, rows_y), (planes // 4, rows_x, rows_y)
    keep, send_x, send_y, send_xy = pl.pallas_call(
        adjoint_kernel,
        in_specs=[vmem] * 8,
        out_specs=[vmem] * 4,
        out_shape=[jax.ShapeDtypeStruct(half, jnp.float32)] * 4,
        scratch_shapes=step_scratch[:2] + [pltpu.VMEM((2 * planes, rows_x, rows_y), jnp.float32)] + step_scratch[2:],
        compiler_params=params,
        cost_estimate=cost,
        name="adjoint_steps",
    )(adj_own, adj_mate, adj_over, adj_far, cour, laps, inject, last)

    by_xy, by_x, by_y = exchange(send_xy, CHIP + Y), exchange(send_x, CHIP), exchange(send_y, Y)
    keep, send = local(square_kernel, [quarter] * 2, keep, by_xy, by_y, by_x)
    part = local(add_kernel, [quarter], keep, exchange(send, NEAR_Z))
    rows, sums_shape = planes // 4 * rows_x, (8, rows_y)
    data, sums = local(sums_kernel, [(rows + 8, rows_y), sums_shape], part, exchange(part, FAR_Z), momentum)

    received = exchange(data, NEAR_Z)
    others = [exchange(sums, CORE), exchange(sums, NEAR_Z + CORE)]
    data, sums = local(join_kernel, [(2 * rows + 8, rows_y), sums_shape], data, received, sums, *others)
    received = exchange(data, Y)
    others = [exchange(sums, CHIP), exchange(sums, Y + CHIP)]
    momentum_half, kinetic = pl.pallas_call(
        finish_kernel,
        in_specs=[vmem] * 6,
        out_specs=[vmem, smem],
        out_shape=[jax.ShapeDtypeStruct(momentum.shape, jnp.float32), jax.ShapeDtypeStruct((1,), jnp.float32)],
        compiler_params=pltpu.CompilerParams(vmem_limit_bytes=4 * 2**20),
        name="finish",
    )(others[1], received, others[0], data, momentum, sums)
    return momentum_half, kinetic[0]


def solution(mesh):
    shots, slabs = mesh.shape["shot"], mesh.shape["depth"]

    def placed(depth):
        field = P("shot", depth, None, None)
        slab = P(depth, None, None)
        inputs = (slab, slab, field, field, field, field, P("shot", None, None), P("shot"), P("shot", None), P())
        return dict(in_specs=inputs, out_specs=(slab, P()), check_vma=False)

    slab_plan = jax.shard_map(slab_shards, mesh=mesh, **placed("depth"))
    if slabs != 4 or shots != 8:
        return slab_plan
    chips = Mesh(mesh.devices.reshape(shots, 2, 2), ("shot", "chip", "core"))
    whole_plan = jax.shard_map(whole_shards, mesh=chips, **placed(("chip", "core")))

    def run(courant_sq, momentum, fwd_prev, *rest):
        total, planes, rows_x, rows_y = fwd_prev.shape
        steps = rest[3].shape[1]
        fits = total == 2 * shots and planes == 4 * shots and rows_y == 128 and rows_x % 16 == 0 and steps % 2 == 0
        plan = whole_plan if fits else slab_plan
        return plan(courant_sq, momentum, fwd_prev, *rest)

    return run
```

```python
import functools

import jax
import jax.numpy as jnp
from jax import lax
from jax.experimental import pallas as pl
from jax.experimental.pallas import tpu as pltpu
from jax.sharding import Mesh
from jax.sharding import PartitionSpec as P

CENTER = -2.5
NEAR = 4.0 / 3.0
FAR = -1.0 / 12.0
AMPLITUDE = 100.0
EPSILON = 1e-06


def with_halo(value, sides, width):
    for axis, dim in sides:
        size, length = (lax.axis_size(axis), value.shape[dim])
        up = [(i, (i + 1) % size) for i in range(size - 1)]
        down = [(j, i) for i, j in up]
        last = lax.slice_in_dim(value, length - width, length, axis=dim)
        leading = lax.slice_in_dim(value, 0, width, axis=dim)
        before = lax.ppermute(last, axis, up)
        after = lax.ppermute(leading, axis, down)
        value = jnp.concatenate([before, value, after], axis=dim)
    return value


def laplace(padded):
    lateral = jnp.pad(padded[:, 2:-2], ((0, 0), (0, 0), (2, 2), (2, 2)))
    center = padded[:, 2:-2]
    along_z = NEAR * (padded[:, 1:-3] + padded[:, 3:-1]) + FAR * (padded[:, :-4] + padded[:, 4:])
    along_x = NEAR * (lateral[:, :, 1:-3, 2:-2] + lateral[:, :, 3:-1, 2:-2]) + FAR * (
        lateral[:, :, :-4, 2:-2] + lateral[:, :, 4:, 2:-2]
    )
    along_y = NEAR * (lateral[:, :, 2:-2, 1:-3] + lateral[:, :, 2:-2, 3:-1]) + FAR * (
        lateral[:, :, 2:-2, :-4] + lateral[:, :, 2:-2, 4:]
    )
    return 3.0 * CENTER * center + along_z + along_x + along_y


def locate(field, cell_ids, first_plane):
    shot_count, planes, rows_x, rows_y = field.shape
    plane_cells = rows_x * rows_y
    local_index = cell_ids - first_plane * plane_cells
    inside = (local_index >= 0) & (local_index < planes * plane_cells)
    target = jnp.where(inside, local_index, 0)
    return (inside, target)


def inject(field, cell_ids, values, first_plane):
    shot_count = field.shape[0]
    inside, target = locate(field, cell_ids, first_plane)
    amount = jnp.where(inside, values, jnp.zeros_like(values))
    flattened = field.reshape(shot_count, -1)
    lanes = jnp.arange(shot_count)[:, None]
    flattened = flattened.at[lanes, target].add(amount)
    return flattened.reshape(field.shape)


def sample(field, cell_ids, first_plane):
    shot_count = field.shape[0]
    inside, target = locate(field, cell_ids, first_plane)
    values = jnp.take_along_axis(field.reshape(shot_count, -1), target, axis=1)
    return jnp.where(inside, values, jnp.zeros_like(values))


def wave_value(start, step):
    cycle = jnp.mod(start + jnp.int32(step), jnp.int32(48))
    phase = (cycle.astype(jnp.float32) - 24.0) / 12.0
    return AMPLITUDE * (1.0 - 2.0 * phase * phase) * jnp.exp(-phase * phase)


def statistics(scaled, moment, weight, cells_all):
    grand_total = lax.psum(jnp.sum(scaled * scaled), ("shot", "depth"))
    factor = lax.rsqrt(grand_total / cells_all + EPSILON)
    halfway = moment - 0.5 * factor * scaled
    energy = lax.psum(jnp.sum(weight * halfway * halfway), ("shot", "depth"))
    return (factor, 0.5 * energy / cells_all)


def slab_shards(
    courant_sq,
    momentum,
    fwd_prev,
    fwd_cur,
    adj_next,
    adj_cur,
    observed,
    src_cells,
    rec_cells,
    ckpt_step,
):
    shot_count, planes, rows_x, rows_y = fwd_cur.shape
    steps_all = observed.shape[1]
    first_plane = lax.axis_index("depth") * planes
    total_planes = planes * lax.axis_size("depth")
    cells_all = total_planes * rows_x * rows_y
    sources = src_cells[:, None]
    older, current = (fwd_prev, fwd_cur)
    laplacians = []
    misfits = []
    for step in range(steps_all):
        padded = with_halo(current, (("depth", 1),), 2)
        strength = jnp.full(sources.shape, wave_value(ckpt_step, step), jnp.float32)
        laplacian = inject(laplace(padded), sources, strength, first_plane)
        newer = 2.0 * current - older + courant_sq * laplacian
        misfits.append(sample(newer, rec_cells, first_plane) - observed[:, step, :])
        laplacians.append(laplacian)
        older, current = (current, newer)
    adj_later, adj_now = (adj_next, adj_cur)
    gradient = jnp.zeros((planes, rows_x, rows_y), jnp.float32)
    for step in reversed(range(steps_all)):
        padded = with_halo(courant_sq * adj_now, (("depth", 1),), 2)
        adj_new = 2.0 * adj_now - adj_later + laplace(padded)
        adj_new = inject(adj_new, rec_cells, misfits[step], first_plane)
        gradient = gradient + jnp.sum(adj_new * laplacians[step], axis=0)
        adj_later, adj_now = (adj_now, adj_new)
    depths = (first_plane + jnp.arange(planes)).astype(jnp.float32)
    weight = (1.0 + 2.0 * depths / (total_planes - 1))[:, None, None]
    share_rows = rows_x // lax.axis_size("shot")
    offset = lax.axis_index("shot") * share_rows
    moment_share = lax.dynamic_slice_in_dim(momentum, offset, share_rows, 1)
    gradient = lax.psum(gradient, "shot")
    scaled = weight * gradient
    scaled_share = lax.dynamic_slice_in_dim(scaled, offset, share_rows, 1)
    factor, kinetic = statistics(scaled_share, moment_share, weight, cells_all)
    momentum_half = momentum - 0.5 * factor * scaled
    return (momentum_half, kinetic)


def interleave(dst, slab, src, factor=None):
    planes, rows = src.shape[0], src.shape[1]
    groups = rows // 8

    @pl.loop(0, planes)
    def _(p):
        for i in range(groups):
            value = src[p, pl.ds(i, 8, stride=groups), :]
            if factor is not None:
                value = value * factor
            dst[(*slab, p, pl.ds(i * 8, 8), slice(None))] = value


def pick_kernel(earlier, adj_next, adj_cur, fwd_prev, fwd_cur, speed, adj_out, adj_own, prev_own, cur_own, held, sems):
    chip = lax.axis_index("chip")
    planes = adj_own.shape[1]
    wanted = (
        (adj_next, 1 - chip, adj_out, (0,)),
        (adj_cur, 1 - chip, adj_out, (1,)),
        (adj_next, chip, adj_own, (0,)),
        (adj_cur, chip, adj_own, (1,)),
        (fwd_prev, chip, prev_own, ()),
        (fwd_cur, chip, cur_own, ()),
    )
    copies = []
    for n, (field, shot, _, _) in enumerate(wanted):
        copies.append(pltpu.make_async_copy(field.at[shot], held.at[n], sems.at[n]))
        copies[-1].start()
    for n, (_, _, out, slab) in enumerate(wanted):
        copies[n].wait()
        interleave(out, slab, held.at[n])
    tail = cur_own.shape[0] - planes
    cur_own[planes:] = speed[planes - tail :]


def pick(adj_next, adj_cur, fwd_prev, fwd_cur, speed, tail, earlier):
    planes, *plane = fwd_cur.shape[1:]
    vmem, hbm = pl.BlockSpec(memory_space=pltpu.VMEM), pl.BlockSpec(memory_space=pltpu.HBM)
    shapes = [(2, planes, *plane), (2, planes, *plane), (planes, *plane), (planes + tail, *plane)]
    return pl.pallas_call(
        pick_kernel,
        in_specs=[pl.BlockSpec(memory_space=pl.ANY)] + [hbm] * 4 + [vmem],
        out_specs=[vmem] * 4,
        out_shape=[jax.ShapeDtypeStruct(shape, jnp.float32) for shape in shapes],
        scratch_shapes=[pltpu.VMEM((6, planes, *plane), jnp.float32), pltpu.SemaphoreType.DMA((6,))],
        compiler_params=pltpu.CompilerParams(vmem_limit_bytes=4 * 2**20),
        name="pick",
    )(earlier, adj_next, adj_cur, fwd_prev, fwd_cur, speed)


def first_kernel(first, second, courant, outgoing, whole, piece, held, held_courant, sems):
    shot = 1 - lax.axis_index("chip")
    copies = [
        pltpu.make_async_copy(first.at[shot], held.at[0], sems.at[0]),
        pltpu.make_async_copy(second.at[shot], held.at[1], sems.at[1]),
        pltpu.make_async_copy(courant, held_courant, sems.at[2]),
    ]
    for copy in copies:
        copy.start()
    for n in range(2):
        copies[n].wait()
        interleave(outgoing, (n,), held.at[n])
    copies[2].wait()
    interleave(whole, (), held_courant, 1.0 / 12.0)
    count = piece.shape[0]
    piece[...] = whole[pl.ds(lax.axis_index("shot") % 2 * count, count)]


def band(lanes):
    near = jnp.abs(lax.broadcasted_iota(jnp.int32, (2 * lanes, lanes), 0) % lanes - lax.broadcasted_iota(jnp.int32, (2 * lanes, lanes), 1))
    return jnp.where(near == 0, -90.0, jnp.where(near == 1, 16.0, jnp.where(near == 2, -1.0, 0.0))).astype(jnp.bfloat16)


def along_y(field, z, banded, out):
    rows, lanes = field.shape[1] - 8, field.shape[2]
    whole = field[pl.ds(z + 2, BATCH), 0:rows].reshape(BATCH * rows, lanes)
    high = whole.astype(jnp.bfloat16)
    low = (whole - high.astype(jnp.float32)).astype(jnp.bfloat16)
    out[...] = jnp.dot(jnp.concatenate([high, low], 1), banded[...], preferred_element_type=jnp.float32)


def laps12(field, z, y_part, fetch, finish):
    rows, lanes = field.shape[1] - 8, field.shape[2]
    groups = rows // 8
    sub = lax.broadcasted_iota(jnp.int32, (8, lanes), 0)

    def later(block):
        return jnp.where(sub < 7, pltpu.roll(block, 7, 0), 0.0)

    def earlier(block):
        return jnp.where(sub > 0, pltpu.roll(block, 1, 0), 0.0)

    for base in range(0, BATCH, PLANES):
        held = {}

        def tile(j, i):
            if (j, i) not in held:
                if i < 0:
                    held[j, i] = earlier(tile(j, i + groups))
                elif i >= groups:
                    held[j, i] = later(tile(j, i - groups))
                else:
                    held[j, i] = field[z + j + 2, i * 8 : (i + 1) * 8]
            return held[j, i]

        def load(i):
            found = []
            for j in range(base, base + PLANES):
                center = tile(j, i)
                near = (tile(j, i - 1), tile(j, i + 1), tile(j - 1, i), tile(j + 1, i))
                far = (tile(j, i - 2), tile(j, i + 2), tile(j - 2, i), tile(j + 2, i))
                at = (j * groups + i) * 8
                found.append((center, near, far, y_part[at : at + 8], fetch(j, slice(i * 8, i * 8 + 8))))
            return found

        ready = load(0)
        for i in range(groups):
            upcoming = load(i + 1) if i + 1 < groups else None
            for j, (center, near, far, part, extra) in enumerate(ready):
                near = (near[0] + near[1]) + (near[2] + near[3])
                far = (far[0] + far[1]) + (far[2] + far[3])
                finish(base + j, slice(i * 8, i * 8 + 8), center, 16.0 * near + (part - far), extra)
            ready = upcoming


def scatter_kernel(rows_x, cells_ref, observed_ref, out_ref, mark, row_ref, spread):
    _, steps, receivers = observed_ref.shape
    lanes = out_ref.shape[2]
    tile = out_ref.shape[1]
    groups = rows_x // 8

    @pl.when(pl.program_id(0) == 0)
    def _():
        chip = lax.axis_index("chip")
        cells = cells_ref[pl.ds(chip, 1)]
        x = cells // lanes % rows_x
        row_ref[...] = cells // (rows_x * lanes) * rows_x + x % groups * 8 + x // groups
        on_lanes = jnp.concatenate(
            [
                observed_ref[chip],
                jnp.broadcast_to((cells % lanes).astype(jnp.float32), (8, receivers)),
                jnp.zeros((lanes - steps - 8, receivers), jnp.float32),
            ],
            0,
        )
        columns = on_lanes.T
        lane = lax.broadcasted_iota(jnp.int32, (receivers, lanes), 1).astype(jnp.float32)
        at = lane == columns[:, steps : steps + 1]
        for k in range(steps):
            column = columns[:, k : k + 1]
            high = column.astype(jnp.bfloat16).astype(jnp.float32)
            low = column - high
            cols = pl.ds(k * lanes, lanes)
            spread[0:receivers, cols] = jnp.where(at, high, 0.0).astype(jnp.bfloat16)
            spread[receivers:, cols] = jnp.where(at, low, 0.0).astype(jnp.bfloat16)
        cols = pl.ds(steps * lanes, lanes)
        spread[0:receivers, cols] = jnp.where(at, 1.0, 0.0).astype(jnp.bfloat16)
        spread[receivers:, cols] = jnp.zeros((receivers, lanes), jnp.bfloat16)
        mark[...] = jnp.zeros(mark.shape, jnp.float32)

    ids = lax.broadcasted_iota(jnp.int32, (tile, receivers), 0) + pl.program_id(0) * tile
    chosen = jnp.where(ids == row_ref[...], 1.0, 0.0).astype(jnp.bfloat16)
    total = jnp.dot(jnp.concatenate([chosen, chosen], 1), spread[...], preferred_element_type=jnp.float32)
    for k in range(steps + 1):
        out_ref[k] = total[:, k * lanes : (k + 1) * lanes]


def scatter(rec_cells, observed, planes_all, rows_x, rows_y):
    _, steps, receivers = observed.shape
    rows_all = planes_all * rows_x
    tile = 512
    return pl.pallas_call(
        functools.partial(scatter_kernel, rows_x),
        grid=(rows_all // tile,),
        in_specs=[
            pl.BlockSpec((2, receivers), lambda t: (0, 0)),
            pl.BlockSpec((2, steps, receivers), lambda t: (0, 0, 0)),
        ],
        out_specs=[
            pl.BlockSpec((steps + 1, tile, rows_y), lambda t: (0, t, 0)),
            pl.BlockSpec((8, rows_y), lambda t: (0, 0)),
        ],
        out_shape=[
            jax.ShapeDtypeStruct((steps + 1, rows_all, rows_y), jnp.float32),
            jax.ShapeDtypeStruct((8, rows_y), jnp.float32),
        ],
        scratch_shapes=[
            pltpu.VMEM((1, receivers), jnp.int32),
            pltpu.VMEM((2 * receivers, (steps + 1) * rows_y), jnp.bfloat16),
        ],
        compiler_params=pltpu.CompilerParams(vmem_limit_bytes=56 * 2**20),
        cost_estimate=pl.CostEstimate(
            flops=4 * rows_all * receivers * (steps + 1) * rows_y,
            bytes_accessed=4 * (steps + 1) * rows_all * rows_y,
            transcendentals=0,
        ),
        name="receiver_scatter",
    )(rec_cells, observed)


def place(planes):
    chip, core = lax.axis_index("chip"), lax.axis_index("core")
    slabs = (2 * chip + core, 2 * chip + 1 - core, 2 * (1 - chip) + core, 2 * (1 - chip) + 1 - core)
    return chip, core, [slab * planes for slab in slabs]


def load_blocks(slabs, blocks, first, second, factor=None):
    ends, rows, lanes = first.shape[0], first.shape[1] - 8, first.shape[2]
    planes = (ends - 4) // 4
    for field in (first, second):
        for z in (0, 1, ends - 2, ends - 1):
            field[z, 0:rows] = jnp.zeros((rows, lanes), jnp.float32)
    for slab, block in zip(slabs, blocks):
        pair = block if isinstance(block, tuple) else (block.at[0], block.at[1])
        for p in range(planes):
            values = pair[0][p], pair[1][p]
            if factor is not None:
                speed = factor[slab + p]
                values = values[0] * speed, values[1] * speed
            first[slab + p + 2, 0:rows], second[slab + p + 2, 0:rows] = values


BATCH = 4
PLANES = 2


def sweep(core, planes, field, banded, y_first, y_second, work, newer=None):
    order = [(chip, owned) for owned in (True, False) for chip in (0, 1)]
    parts = (y_first, y_second)

    def first(chip, owned):
        return (2 * chip + (core if owned else 1 - core)) * planes

    if newer is None:
        along_y(field, first(*order[0]), banded, y_first)
    for owned in (True, False):
        for chip in (0, 1):
            z = first(chip, owned)
            onward = first(1, owned) if chip == 0 else first(0, False)
            for n in range(planes // BATCH):
                last = n == planes // BATCH - 1
                if not last or chip == 0 or owned:
                    along_y(field, onward if last else z + (n + 1) * BATCH, banded, parts[(n + 1) % 2])
                elif newer is not None:
                    along_y(newer, first(*order[0]), banded, y_first)
                work(z + n * BATCH, parts[n % 2], chip if owned else None, n * BATCH)


def forward_kernel(
    start, sources, own0, own1, mate0, mate1, over0, over1, far0, far1, speed, speed_mate, placed, laps, history, held, cour, last,
    even, odd, banded, y0, y1, sems, sems_even, sems_odd
):
    planes, rows, lanes = own0.shape
    steps = laps.shape[0]
    groups = rows // 8
    chip_here, core, slabs = place(planes)

    fetch_all = pltpu.make_async_copy(placed, held, sems.at[0])
    fetch_all.start()

    def keep(k, field, done):
        source = field.at[pl.ds(2, 4 * planes), pl.ds(0, rows)]
        return pltpu.make_async_copy(source, history.at[k], done.at[0])

    banded[...] = band(lanes)
    load_blocks(slabs, ((own0, own1), (mate0, mate1), (over0, over1), (far0, far1)), odd, even)
    head = speed.shape[0] - planes
    for here, across, first, rest in ((slabs[0], slabs[2], speed, own1), (slabs[1], slabs[3], speed_mate, mate1)):
        for p in range(planes):
            cour[across + p] = first[p]
            cour[here + p] = first[planes + p] if p < head else rest[planes + p - head]

    for index in range(2 * planes):
        z = (2 * (index // planes) + core) * planes + index % planes
        weight = 1.0 + 2.0 * jnp.full((rows, lanes), z, jnp.int32).astype(jnp.float32) / (4 * planes - 1)
        last[index] = weight / (12.0 * cour[z])

    cell = sources[chip_here]
    source_z, x, lane = cell // (rows * lanes), cell // lanes % rows, cell % lanes
    tile = pl.ds(pl.multiple_of(x % groups * 8, 8), 8)
    here = (lax.broadcasted_iota(jnp.int32, (8, lanes), 0) == x // groups) & (
        lax.broadcasted_iota(jnp.int32, (8, lanes), 1) == lane
    )
    source_slab, source_p = source_z // planes, lax.rem(source_z, planes)

    def advance(k, now, then, done):
        @pl.when(k >= 2)
        def _():
            keep(k - 2, then, done).wait()

        def work(z, y_part, chip, p):
            def fetch(j, rows):
                return then[z + j + 2, rows], cour[z + j, rows]

            def finish(j, rows, center, lap, extra):
                old, speed = extra
                if chip is not None:
                    laps[k, p + j, chip, rows] = lap
                then[z + j + 2, rows] = 2.0 * center - old + speed * lap

            laps12(now, z, y_part, fetch, finish)

        cycle = (start[0] + k) % 48
        phase = (jnp.full((8, lanes), cycle, jnp.int32).astype(jnp.float32) - 24.0) / 12.0
        wave = AMPLITUDE * (1.0 - 2.0 * phase * phase) * jnp.exp(-phase * phase)
        strength = jnp.where(here, 12.0 * wave, 0.0)
        moved = cour[source_z, tile, :] * strength

        sweep(core, planes, now, banded, y0, y1, work)

        owned = jnp.where(lax.rem(source_slab, 2) == core, strength, 0.0)
        laps[k, source_p, source_slab // 2, tile, :] += owned
        then[source_z + 2, tile, :] += moved
        keep(k, then, done).start()

    @pl.loop(0, steps // 2)
    def _(pair):
        advance(2 * pair, even, odd, sems_odd)
        advance(2 * pair + 1, odd, even, sems_even)

    for k, field, done in ((steps - 2, odd, sems_odd), (steps - 1, even, sems_even)):
        keep(k, field, done).wait()
    fetch_all.wait()


def inject_kernel(held, history, inject):
    steps, planes_all = history.shape[:2]

    @pl.loop(0, planes_all)
    def _(z):
        count = held[steps, z]
        for k in range(steps):
            inject[k, z] = held[k, z] - count * history[k, z]


def adjoint_kernel(own, mate, over, far, cour, laps, inject, last, keep, send_x, send_y, send_xy, even, odd, total, banded, y0, y1):
    planes, rows, lanes = own.shape[1:]
    steps = laps.shape[0]
    groups = rows // 8
    chip_here, core, slabs = place(planes)
    banded[...] = band(lanes)
    load_blocks(slabs, (own, mate, over, far), odd, even, factor=cour)

    total[...] = jnp.zeros(total.shape, jnp.float32)

    def advance(k, now, then):
        def work(z, y_part, chip, p):
            def fetch(j, rows):
                extra = (then[z + j + 2, rows], cour[z + j, rows], inject[k, z + j, rows])
                if chip is not None:
                    extra += (total[chip * planes + p + j, rows], laps[k, p + j, chip, rows])
                return extra

            def finish(j, rows, center, lap, extra):
                newer = 2.0 * center - extra[0] + extra[1] * (lap - extra[2])
                then[z + j + 2, rows] = newer
                if chip is not None:
                    total[chip * planes + p + j, rows] = extra[3] + newer * extra[4]

            laps12(now, z, y_part, fetch, finish)

        sweep(core, planes, now, banded, y0, y1, work, then)

    along_y(even, core * planes, banded, y0)

    @pl.loop(0, steps // 2)
    def _(pair):
        advance(steps - 1 - 2 * pair, even, odd)
        advance(steps - 2 - 2 * pair, odd, even)

    count = keep.shape[0]
    mine, others = lax.axis_index("shot") % 2 * count, (1 - lax.axis_index("shot") % 2) * count
    here, there = chip_here, 1 - chip_here
    for ref, chip, start in ((keep, here, mine), (send_x, there, mine), (send_y, here, others), (send_xy, there, others)):

        @pl.loop(0, count)
        def _(n):
            p = start + n
            value = total[chip * planes + p] * last[chip * planes + p]
            for i in range(groups):
                ref[n, pl.ds(i, 8, stride=groups), :] = value[i * 8 : (i + 1) * 8]


def square_kernel(mine, by_xy, by_y, by_x, keep, send):
    half = lax.axis_index("shot") // 2 % 2
    count = keep.shape[0]
    for ref, part in ((keep, half), (send, 1 - half)):
        for p in range(count):
            at = part * count + p
            ref[p] = (mine[at] + by_x[at]) + (by_y[at] + by_xy[at])


def add_kernel(mine, other, out):
    out[...] = mine[...] + other[...]


def flip(index, bits):
    result = index
    for bit in (1, 2):
        if bits & bit:
            result = jnp.where(index // bit % 2 == 1, result - bit, result + bit)
    return result


def after_kernel(earlier, value, *outs):
    if len(outs) == 1:
        outs[0][...] = value[...]
    else:
        for n, out in enumerate(outs):
            out[...] = value[n]


def after(earlier, value, parts=1):
    vmem, anywhere = pl.BlockSpec(memory_space=pltpu.VMEM), pl.BlockSpec(memory_space=pl.ANY)
    shape = value.shape if parts == 1 else value.shape[1:]
    results = pl.pallas_call(
        after_kernel,
        in_specs=[anywhere, vmem],
        out_specs=[vmem] * parts,
        out_shape=[jax.ShapeDtypeStruct(shape, jnp.float32)] * parts,
        compiler_params=pltpu.CompilerParams(vmem_limit_bytes=4 * 2**20),
        name="after",
    )(earlier, value)
    return results[0] if parts == 1 else results


def arrange_kernel(own, mine, other, out):
    y = lax.axis_index("shot") % 2
    count, planes = mine.shape[0], own.shape[0]
    out[pl.ds(y * count, count)] = mine[...]
    out[pl.ds((1 - y) * count, count)] = other[...]
    out[planes:] = own[0 : out.shape[0] - planes]


def first_plane(shot, planes):
    return (shot % 2) * (planes // 2) + (shot // 2 % 2) * (planes // 4)


def sums_kernel(mine, other, momentum, data, sums):
    count, rows, lanes = mine.shape
    planes = momentum.shape[0]
    chip, core = lax.axis_index("chip"), lax.axis_index("core")
    first = first_plane(lax.axis_index("shot"), planes)
    parts = [jnp.zeros((rows, lanes), jnp.float32)] * 4
    for j in range(count):
        scaled = mine[j] + other[j]
        data[j * rows : (j + 1) * rows] = scaled
        z = (2 * chip + core) * planes + first + j
        weight = 1.0 + 2.0 * jnp.full((1, lanes), z, jnp.int32).astype(jnp.float32) / (4 * planes - 1)
        moment = momentum[first + j]
        square = scaled * scaled
        terms = (square, weight * moment * moment, weight * moment * scaled, weight * square)
        parts = [part + term for part, term in zip(parts, terms)]

    def total(value):
        by_lane = jnp.sum(value, axis=0, keepdims=True)
        return jnp.broadcast_to(jnp.sum(by_lane, axis=1, keepdims=True), (1, lanes))

    value = jnp.concatenate([total(part) for part in parts] + [jnp.zeros((4, lanes), jnp.float32)], 0)
    data[count * rows :] = value
    sums[...] = value


def join_kernel(mine, other, s0, s1, s2, data, sums):
    rows = mine.shape[0] - 8
    data[0:rows] = mine[0:rows]
    data[rows : 2 * rows] = other[0:rows]
    value = (s0[...] + s1[...]) + (other[rows:] + s2[...])
    data[2 * rows :] = value
    sums[...] = value


def finish_kernel(mine, other, momentum, s0, s1, s2, out, kinetic):
    planes, rows, lanes = momentum.shape
    cells = 4.0 * planes * rows * lanes
    shot = lax.axis_index("shot")
    sums = (s0[...] + s1[...]) + (other[planes // 2 * rows :] + s2[...])
    factor = lax.rsqrt(sums[0:1] / cells + EPSILON)
    energy = 0.5 * (sums[1:2] - factor * sums[2:3] + 0.25 * factor * factor * sums[3:4]) / cells
    kinetic[0] = energy[0, 0]
    step = 0.5 * factor
    quarter = planes // 4
    for part, group in ((mine, shot), (other, flip(shot, 1))):
        for number, first in enumerate((first_plane(group, planes), first_plane(flip(group, 2), planes))):
            for j in range(quarter):
                at = (number * quarter + j) * rows
                out[first + j] = momentum[first + j] - step * part[at : at + rows]


def local(kernel, outs, *arrays):
    vmem = pl.BlockSpec(memory_space=pltpu.VMEM)
    shapes = [jax.ShapeDtypeStruct(shape, jnp.float32) for shape in outs]
    single = len(outs) == 1
    return pl.pallas_call(
        kernel,
        in_specs=[vmem] * len(arrays),
        out_specs=vmem if single else [vmem] * len(outs),
        out_shape=shapes[0] if single else shapes,
        compiler_params=pltpu.CompilerParams(vmem_limit_bytes=4 * 2**20),
        name=kernel.__name__,
    )(*arrays)


def exchange(value, bits):
    axes = ("shot", "chip", "core")
    return lax.ppermute(value, axes, [(i, i ^ bits) for i in range(lax.axis_size(axes))])


CORE, CHIP, Y, NEAR_Z, FAR_Z = 1, 2, 4, 8, 16


def whole_shards(
    courant_sq, momentum, fwd_prev, fwd_cur, adj_next, adj_cur, observed, src_cells, rec_cells, ckpt_step
):
    _, planes, rows_x, rows_y = fwd_cur.shape
    steps = observed.shape[1]
    planes_all = 4 * planes
    cells_all = planes_all * rows_x * rows_y
    vmem, smem = pl.BlockSpec(memory_space=pltpu.VMEM), pl.BlockSpec(memory_space=pltpu.SMEM)

    hbm = pl.BlockSpec(memory_space=pltpu.HBM)
    outgoing, c0, piece = pl.pallas_call(
        first_kernel,
        in_specs=[hbm] * 3,
        out_specs=[vmem] * 3,
        out_shape=[
            jax.ShapeDtypeStruct((2, planes, rows_x, rows_y), jnp.float32),
            jax.ShapeDtypeStruct(courant_sq.shape, jnp.float32),
            jax.ShapeDtypeStruct((planes // 2, rows_x, rows_y), jnp.float32),
        ],
        scratch_shapes=[
            pltpu.VMEM((2, planes, rows_x, rows_y), jnp.float32),
            pltpu.VMEM(courant_sq.shape, jnp.float32),
            pltpu.SemaphoreType.DMA((3,)),
        ],
        compiler_params=pltpu.CompilerParams(vmem_limit_bytes=63 * 2**20),
        name="first_to_cross",
    )(fwd_prev, fwd_cur, courant_sq)

    over = exchange(outgoing, CHIP)
    piece = exchange(piece, CHIP)

    placed, mark = scatter(rec_cells, observed, planes_all, rows_x, rows_y)
    placed = placed.reshape(steps + 1, planes_all, rows_x, rows_y)

    piece = after(mark, piece)
    head = planes * 5 // 8
    adj_outgoing, adj_own, *own = pick(adj_next, adj_cur, fwd_prev, fwd_cur, c0, planes - head, piece)
    mate = [exchange(field, CORE) for field in own]
    speed = local(arrange_kernel, [(planes + head, rows_x, rows_y)], c0, piece, exchange(piece, Y))
    speed_mate = exchange(speed, CORE)
    over = after(speed, over, parts=2)
    far = [exchange(field, CORE) for field in over]
    adj_over = exchange(adj_outgoing, CHIP)
    adj_mate = exchange(adj_own, CORE)

    scratch = pltpu.VMEM((planes_all + 4, rows_x + 8, rows_y), jnp.float32)
    y_scratch = pltpu.VMEM((BATCH * rows_x, rows_y), jnp.float32)
    step_scratch = [scratch, scratch, pltpu.VMEM((2 * rows_y, rows_y), jnp.bfloat16), y_scratch, y_scratch]
    params = pltpu.CompilerParams(vmem_limit_bytes=6 * 2**20)
    cost = pl.CostEstimate(flops=30 * steps * cells_all, bytes_accessed=16 * steps * cells_all, transcendentals=0)
    laps, history, held, cour, last = pl.pallas_call(
        forward_kernel,
        in_specs=[smem, smem] + [vmem] * 10 + [pl.BlockSpec(memory_space=pltpu.HBM)],
        out_specs=[vmem] * 5,
        out_shape=[
            jax.ShapeDtypeStruct((steps, planes, 2, rows_x, rows_y), jnp.float32),
            jax.ShapeDtypeStruct((steps, planes_all, rows_x, rows_y), jnp.float32),
            jax.ShapeDtypeStruct((steps + 1, planes_all, rows_x, rows_y), jnp.float32),
            jax.ShapeDtypeStruct((planes_all, rows_x, rows_y), jnp.float32),
            jax.ShapeDtypeStruct((2 * planes, rows_x, rows_y), jnp.float32),
        ],
        scratch_shapes=step_scratch
        + [
            pltpu.SemaphoreType.DMA((1,)),
            pltpu.SemaphoreType.DMA((1,)),
            pltpu.SemaphoreType.DMA((1,)),
        ],
        compiler_params=pltpu.CompilerParams(vmem_limit_bytes=21 * 2**20),
        cost_estimate=pl.CostEstimate(flops=1000, bytes_accessed=1000, transcendentals=0),
        name="forward_steps",
    )(ckpt_step[None], src_cells, *own, *mate, *over, *far, speed, speed_mate, placed)

    adj_over = after(laps, adj_over)
    adj_far = exchange(adj_over, CORE)
    inject = pl.pallas_call(
        inject_kernel,
        in_specs=[vmem] * 2,
        out_specs=vmem,
        out_shape=jax.ShapeDtypeStruct(history.shape, jnp.float32),
        compiler_params=pltpu.CompilerParams(vmem_limit_bytes=4 * 2**20),
        name="inject",
    )(held, history)
    slab = jax.ShapeDtypeStruct(courant_sq.shape, jnp.float32)
    half, quarter = (planes // 2, rows_x, rows_y), (planes // 4, rows_x, rows_y)
    keep, send_x, send_y, send_xy = pl.pallas_call(
        adjoint_kernel,
        in_specs=[vmem] * 8,
        out_specs=[vmem] * 4,
        out_shape=[jax.ShapeDtypeStruct(half, jnp.float32)] * 4,
        scratch_shapes=step_scratch[:2] + [pltpu.VMEM((2 * planes, rows_x, rows_y), jnp.float32)] + step_scratch[2:],
        compiler_params=params,
        cost_estimate=cost,
        name="adjoint_steps",
    )(adj_own, adj_mate, adj_over, adj_far, cour, laps, inject, last)

    by_xy, by_x, by_y = exchange(send_xy, CHIP + Y), exchange(send_x, CHIP), exchange(send_y, Y)
    keep, send = local(square_kernel, [quarter] * 2, keep, by_xy, by_y, by_x)
    part = local(add_kernel, [quarter], keep, exchange(send, NEAR_Z))
    rows, sums_shape = planes // 4 * rows_x, (8, rows_y)
    data, sums = local(sums_kernel, [(rows + 8, rows_y), sums_shape], part, exchange(part, FAR_Z), momentum)

    received = exchange(data, NEAR_Z)
    others = [exchange(sums, CORE), exchange(sums, NEAR_Z + CORE)]
    data, sums = local(join_kernel, [(2 * rows + 8, rows_y), sums_shape], data, received, sums, *others)
    received = exchange(data, Y)
    others = [exchange(sums, CHIP), exchange(sums, Y + CHIP)]
    momentum_half, kinetic = pl.pallas_call(
        finish_kernel,
        in_specs=[vmem] * 6,
        out_specs=[vmem, smem],
        out_shape=[jax.ShapeDtypeStruct(momentum.shape, jnp.float32), jax.ShapeDtypeStruct((1,), jnp.float32)],
        compiler_params=pltpu.CompilerParams(vmem_limit_bytes=4 * 2**20),
        name="finish",
    )(data, received, momentum, sums, *others)
    return momentum_half, kinetic[0]


def solution(mesh):
    shots, slabs = mesh.shape["shot"], mesh.shape["depth"]

    def placed(depth):
        field = P("shot", depth, None, None)
        slab = P(depth, None, None)
        inputs = (slab, slab, field, field, field, field, P("shot", None, None), P("shot"), P("shot", None), P())
        return dict(in_specs=inputs, out_specs=(slab, P()), check_vma=False)

    slab_plan = jax.shard_map(slab_shards, mesh=mesh, **placed("depth"))
    if slabs != 4 or shots != 8:
        return slab_plan
    chips = Mesh(mesh.devices.reshape(shots, 2, 2), ("shot", "chip", "core"))
    whole_plan = jax.shard_map(whole_shards, mesh=chips, **placed(("chip", "core")))

    def run(courant_sq, momentum, fwd_prev, *rest):
        total, planes, rows_x, rows_y = fwd_prev.shape
        steps = rest[3].shape[1]
        fits = total == 2 * shots and planes == 4 * shots and rows_y == 128 and rows_x % 16 == 0 and steps % 2 == 0
        plan = whole_plan if fits else slab_plan
        return plan(courant_sq, momentum, fwd_prev, *rest)

    return run
```

```python
import functools

import jax
import jax.numpy as jnp
from jax import lax
from jax.experimental import pallas as pl
from jax.experimental.pallas import tpu as pltpu
from jax.sharding import Mesh
from jax.sharding import PartitionSpec as P

CENTER = -2.5
NEAR = 4.0 / 3.0
FAR = -1.0 / 12.0
AMPLITUDE = 100.0
EPSILON = 1e-06


def with_halo(value, sides, width):
    for axis, dim in sides:
        size, length = (lax.axis_size(axis), value.shape[dim])
        up = [(i, (i + 1) % size) for i in range(size - 1)]
        down = [(j, i) for i, j in up]
        last = lax.slice_in_dim(value, length - width, length, axis=dim)
        leading = lax.slice_in_dim(value, 0, width, axis=dim)
        before = lax.ppermute(last, axis, up)
        after = lax.ppermute(leading, axis, down)
        value = jnp.concatenate([before, value, after], axis=dim)
    return value


def laplace(padded):
    lateral = jnp.pad(padded[:, 2:-2], ((0, 0), (0, 0), (2, 2), (2, 2)))
    center = padded[:, 2:-2]
    along_z = NEAR * (padded[:, 1:-3] + padded[:, 3:-1]) + FAR * (padded[:, :-4] + padded[:, 4:])
    along_x = NEAR * (lateral[:, :, 1:-3, 2:-2] + lateral[:, :, 3:-1, 2:-2]) + FAR * (
        lateral[:, :, :-4, 2:-2] + lateral[:, :, 4:, 2:-2]
    )
    along_y = NEAR * (lateral[:, :, 2:-2, 1:-3] + lateral[:, :, 2:-2, 3:-1]) + FAR * (
        lateral[:, :, 2:-2, :-4] + lateral[:, :, 2:-2, 4:]
    )
    return 3.0 * CENTER * center + along_z + along_x + along_y


def locate(field, cell_ids, first_plane):
    shot_count, planes, rows_x, rows_y = field.shape
    plane_cells = rows_x * rows_y
    local_index = cell_ids - first_plane * plane_cells
    inside = (local_index >= 0) & (local_index < planes * plane_cells)
    target = jnp.where(inside, local_index, 0)
    return (inside, target)


def inject(field, cell_ids, values, first_plane):
    shot_count = field.shape[0]
    inside, target = locate(field, cell_ids, first_plane)
    amount = jnp.where(inside, values, jnp.zeros_like(values))
    flattened = field.reshape(shot_count, -1)
    lanes = jnp.arange(shot_count)[:, None]
    flattened = flattened.at[lanes, target].add(amount)
    return flattened.reshape(field.shape)


def sample(field, cell_ids, first_plane):
    shot_count = field.shape[0]
    inside, target = locate(field, cell_ids, first_plane)
    values = jnp.take_along_axis(field.reshape(shot_count, -1), target, axis=1)
    return jnp.where(inside, values, jnp.zeros_like(values))


def wave_value(start, step):
    cycle = jnp.mod(start + jnp.int32(step), jnp.int32(48))
    phase = (cycle.astype(jnp.float32) - 24.0) / 12.0
    return AMPLITUDE * (1.0 - 2.0 * phase * phase) * jnp.exp(-phase * phase)


def statistics(scaled, moment, weight, cells_all):
    grand_total = lax.psum(jnp.sum(scaled * scaled), ("shot", "depth"))
    factor = lax.rsqrt(grand_total / cells_all + EPSILON)
    halfway = moment - 0.5 * factor * scaled
    energy = lax.psum(jnp.sum(weight * halfway * halfway), ("shot", "depth"))
    return (factor, 0.5 * energy / cells_all)


def slab_shards(
    courant_sq,
    momentum,
    fwd_prev,
    fwd_cur,
    adj_next,
    adj_cur,
    observed,
    src_cells,
    rec_cells,
    ckpt_step,
):
    shot_count, planes, rows_x, rows_y = fwd_cur.shape
    steps_all = observed.shape[1]
    first_plane = lax.axis_index("depth") * planes
    total_planes = planes * lax.axis_size("depth")
    cells_all = total_planes * rows_x * rows_y
    sources = src_cells[:, None]
    older, current = (fwd_prev, fwd_cur)
    laplacians = []
    misfits = []
    for step in range(steps_all):
        padded = with_halo(current, (("depth", 1),), 2)
        strength = jnp.full(sources.shape, wave_value(ckpt_step, step), jnp.float32)
        laplacian = inject(laplace(padded), sources, strength, first_plane)
        newer = 2.0 * current - older + courant_sq * laplacian
        misfits.append(sample(newer, rec_cells, first_plane) - observed[:, step, :])
        laplacians.append(laplacian)
        older, current = (current, newer)
    adj_later, adj_now = (adj_next, adj_cur)
    gradient = jnp.zeros((planes, rows_x, rows_y), jnp.float32)
    for step in reversed(range(steps_all)):
        padded = with_halo(courant_sq * adj_now, (("depth", 1),), 2)
        adj_new = 2.0 * adj_now - adj_later + laplace(padded)
        adj_new = inject(adj_new, rec_cells, misfits[step], first_plane)
        gradient = gradient + jnp.sum(adj_new * laplacians[step], axis=0)
        adj_later, adj_now = (adj_now, adj_new)
    depths = (first_plane + jnp.arange(planes)).astype(jnp.float32)
    weight = (1.0 + 2.0 * depths / (total_planes - 1))[:, None, None]
    share_rows = rows_x // lax.axis_size("shot")
    offset = lax.axis_index("shot") * share_rows
    moment_share = lax.dynamic_slice_in_dim(momentum, offset, share_rows, 1)
    gradient = lax.psum(gradient, "shot")
    scaled = weight * gradient
    scaled_share = lax.dynamic_slice_in_dim(scaled, offset, share_rows, 1)
    factor, kinetic = statistics(scaled_share, moment_share, weight, cells_all)
    momentum_half = momentum - 0.5 * factor * scaled
    return (momentum_half, kinetic)


def interleave(dst, slab, src, factor=None):
    planes, rows = src.shape[0], src.shape[1]
    groups = rows // 8

    @pl.loop(0, planes)
    def _(p):
        for i in range(groups):
            value = src[p, pl.ds(i, 8, stride=groups), :]
            if factor is not None:
                value = value * factor
            dst[(*slab, p, pl.ds(i * 8, 8), slice(None))] = value


def pick_kernel(earlier, adj_next, adj_cur, fwd_prev, fwd_cur, speed, adj_out, adj_own, prev_own, cur_own, held, sems):
    chip = lax.axis_index("chip")
    planes = adj_own.shape[1]
    wanted = (
        (adj_next, 1 - chip, adj_out, (0,)),
        (adj_cur, 1 - chip, adj_out, (1,)),
        (adj_next, chip, adj_own, (0,)),
        (adj_cur, chip, adj_own, (1,)),
        (fwd_prev, chip, prev_own, ()),
        (fwd_cur, chip, cur_own, ()),
    )
    copies = []
    for n, (field, shot, _, _) in enumerate(wanted):
        copies.append(pltpu.make_async_copy(field.at[shot], held.at[n], sems.at[n]))
        copies[-1].start()
    for n, (_, _, out, slab) in enumerate(wanted):
        copies[n].wait()
        interleave(out, slab, held.at[n])
    tail = cur_own.shape[0] - planes
    cur_own[planes:] = speed[planes - tail :]


def pick(adj_next, adj_cur, fwd_prev, fwd_cur, speed, tail, earlier):
    planes, *plane = fwd_cur.shape[1:]
    vmem, hbm = pl.BlockSpec(memory_space=pltpu.VMEM), pl.BlockSpec(memory_space=pltpu.HBM)
    shapes = [(2, planes, *plane), (2, planes, *plane), (planes, *plane), (planes + tail, *plane)]
    return pl.pallas_call(
        pick_kernel,
        in_specs=[pl.BlockSpec(memory_space=pl.ANY)] + [hbm] * 4 + [vmem],
        out_specs=[vmem] * 4,
        out_shape=[jax.ShapeDtypeStruct(shape, jnp.float32) for shape in shapes],
        scratch_shapes=[pltpu.VMEM((6, planes, *plane), jnp.float32), pltpu.SemaphoreType.DMA((6,))],
        compiler_params=pltpu.CompilerParams(vmem_limit_bytes=4 * 2**20),
        name="pick",
    )(earlier, adj_next, adj_cur, fwd_prev, fwd_cur, speed)


def first_kernel(first, second, courant, outgoing, whole, piece, held, held_courant, sems):
    shot = 1 - lax.axis_index("chip")
    copies = [
        pltpu.make_async_copy(first.at[shot], held.at[0], sems.at[0]),
        pltpu.make_async_copy(second.at[shot], held.at[1], sems.at[1]),
        pltpu.make_async_copy(courant, held_courant, sems.at[2]),
    ]
    for copy in copies:
        copy.start()
    for n in range(2):
        copies[n].wait()
        interleave(outgoing, (n,), held.at[n])
    copies[2].wait()
    interleave(whole, (), held_courant, 1.0 / 12.0)
    count = piece.shape[0]
    piece[...] = whole[pl.ds(lax.axis_index("shot") % 2 * count, count)]


def band(lanes):
    near = jnp.abs(lax.broadcasted_iota(jnp.int32, (2 * lanes, lanes), 0) % lanes - lax.broadcasted_iota(jnp.int32, (2 * lanes, lanes), 1))
    return jnp.where(near == 0, -90.0, jnp.where(near == 1, 16.0, jnp.where(near == 2, -1.0, 0.0))).astype(jnp.bfloat16)


def along_y(field, z, banded, out):
    rows, lanes = field.shape[1] - 8, field.shape[2]
    whole = field[pl.ds(z + 2, BATCH), 0:rows].reshape(BATCH * rows, lanes)
    high = whole.astype(jnp.bfloat16)
    low = (whole - high.astype(jnp.float32)).astype(jnp.bfloat16)
    out[...] = jnp.dot(jnp.concatenate([high, low], 1), banded[...], preferred_element_type=jnp.float32)


def laps12(field, z, y_part, fetch, finish):
    rows, lanes = field.shape[1] - 8, field.shape[2]
    groups = rows // 8
    sub = lax.broadcasted_iota(jnp.int32, (8, lanes), 0)

    def later(block):
        return jnp.where(sub < 7, pltpu.roll(block, 7, 0), 0.0)

    def earlier(block):
        return jnp.where(sub > 0, pltpu.roll(block, 1, 0), 0.0)

    for base in range(0, BATCH, PLANES):
        held = {}

        def tile(j, i):
            if (j, i) not in held:
                if i < 0:
                    held[j, i] = earlier(tile(j, i + groups))
                elif i >= groups:
                    held[j, i] = later(tile(j, i - groups))
                else:
                    held[j, i] = field[z + j + 2, i * 8 : (i + 1) * 8]
            return held[j, i]

        def load(i):
            found = []
            for j in range(base, base + PLANES):
                center = tile(j, i)
                near = (tile(j, i - 1), tile(j, i + 1), tile(j - 1, i), tile(j + 1, i))
                far = (tile(j, i - 2), tile(j, i + 2), tile(j - 2, i), tile(j + 2, i))
                at = (j * groups + i) * 8
                found.append((center, near, far, y_part[at : at + 8], fetch(j, slice(i * 8, i * 8 + 8))))
            return found

        ready = load(0)
        for i in range(groups):
            upcoming = load(i + 1) if i + 1 < groups else None
            for j, (center, near, far, part, extra) in enumerate(ready):
                near = (near[0] + near[1]) + (near[2] + near[3])
                far = (far[0] + far[1]) + (far[2] + far[3])
                finish(base + j, slice(i * 8, i * 8 + 8), center, 16.0 * near + (part - far), extra)
            ready = upcoming


def scatter_kernel(rows_x, cells_ref, observed_ref, out_ref, mark, row_ref, spread):
    _, steps, receivers = observed_ref.shape
    lanes = out_ref.shape[2]
    tile = out_ref.shape[1]
    groups = rows_x // 8

    @pl.when(pl.program_id(0) == 0)
    def _():
        chip = lax.axis_index("chip")
        cells = cells_ref[pl.ds(chip, 1)]
        x = cells // lanes % rows_x
        row_ref[...] = cells // (rows_x * lanes) * rows_x + x % groups * 8 + x // groups
        on_lanes = jnp.concatenate(
            [
                observed_ref[chip],
                jnp.broadcast_to((cells % lanes).astype(jnp.float32), (8, receivers)),
                jnp.zeros((lanes - steps - 8, receivers), jnp.float32),
            ],
            0,
        )
        columns = on_lanes.T
        lane = lax.broadcasted_iota(jnp.int32, (receivers, lanes), 1).astype(jnp.float32)
        at = lane == columns[:, steps : steps + 1]
        for k in range(steps):
            column = columns[:, k : k + 1]
            high = column.astype(jnp.bfloat16).astype(jnp.float32)
            low = column - high
            cols = pl.ds(k * lanes, lanes)
            spread[0:receivers, cols] = jnp.where(at, high, 0.0).astype(jnp.bfloat16)
            spread[receivers:, cols] = jnp.where(at, low, 0.0).astype(jnp.bfloat16)
        cols = pl.ds(steps * lanes, lanes)
        spread[0:receivers, cols] = jnp.where(at, 1.0, 0.0).astype(jnp.bfloat16)
        spread[receivers:, cols] = jnp.zeros((receivers, lanes), jnp.bfloat16)
        mark[...] = jnp.zeros(mark.shape, jnp.float32)

    ids = lax.broadcasted_iota(jnp.int32, (tile, receivers), 0) + pl.program_id(0) * tile
    chosen = jnp.where(ids == row_ref[...], 1.0, 0.0).astype(jnp.bfloat16)
    total = jnp.dot(jnp.concatenate([chosen, chosen], 1), spread[...], preferred_element_type=jnp.float32)
    for k in range(steps + 1):
        out_ref[k] = total[:, k * lanes : (k + 1) * lanes]


def scatter(rec_cells, observed, planes_all, rows_x, rows_y):
    _, steps, receivers = observed.shape
    rows_all = planes_all * rows_x
    tile = 512
    return pl.pallas_call(
        functools.partial(scatter_kernel, rows_x),
        grid=(rows_all // tile,),
        in_specs=[
            pl.BlockSpec((2, receivers), lambda t: (0, 0)),
            pl.BlockSpec((2, steps, receivers), lambda t: (0, 0, 0)),
        ],
        out_specs=[
            pl.BlockSpec((steps + 1, tile, rows_y), lambda t: (0, t, 0)),
            pl.BlockSpec((8, rows_y), lambda t: (0, 0)),
        ],
        out_shape=[
            jax.ShapeDtypeStruct((steps + 1, rows_all, rows_y), jnp.float32),
            jax.ShapeDtypeStruct((8, rows_y), jnp.float32),
        ],
        scratch_shapes=[
            pltpu.VMEM((1, receivers), jnp.int32),
            pltpu.VMEM((2 * receivers, (steps + 1) * rows_y), jnp.bfloat16),
        ],
        compiler_params=pltpu.CompilerParams(vmem_limit_bytes=56 * 2**20),
        cost_estimate=pl.CostEstimate(
            flops=4 * rows_all * receivers * (steps + 1) * rows_y,
            bytes_accessed=4 * (steps + 1) * rows_all * rows_y,
            transcendentals=0,
        ),
        name="receiver_scatter",
    )(rec_cells, observed)


def place(planes):
    chip, core = lax.axis_index("chip"), lax.axis_index("core")
    slabs = (2 * chip + core, 2 * chip + 1 - core, 2 * (1 - chip) + core, 2 * (1 - chip) + 1 - core)
    return chip, core, [slab * planes for slab in slabs]


def load_blocks(slabs, blocks, first, second, factor=None):
    ends, rows, lanes = first.shape[0], first.shape[1] - 8, first.shape[2]
    planes = (ends - 4) // 4
    for field in (first, second):
        for z in (0, 1, ends - 2, ends - 1):
            field[z, 0:rows] = jnp.zeros((rows, lanes), jnp.float32)
    for slab, block in zip(slabs, blocks):
        pair = block if isinstance(block, tuple) else (block.at[0], block.at[1])
        for p in range(planes):
            values = pair[0][p], pair[1][p]
            if factor is not None:
                speed = factor[slab + p]
                values = values[0] * speed, values[1] * speed
            first[slab + p + 2, 0:rows], second[slab + p + 2, 0:rows] = values


BATCH = 4
PLANES = 4


def sweep(core, planes, field, banded, y_first, y_second, work):
    order = [(chip, owned) for owned in (True, False) for chip in (0, 1)]
    parts = (y_first, y_second)

    def first(chip, owned):
        return (2 * chip + (core if owned else 1 - core)) * planes

    along_y(field, first(*order[0]), banded, y_first)
    for owned in (True, False):
        for chip in (0, 1):
            z = first(chip, owned)
            onward = first(1, owned) if chip == 0 else first(0, False)
            for n in range(planes // BATCH):
                last = n == planes // BATCH - 1
                if not last or chip == 0 or owned:
                    along_y(field, onward if last else z + (n + 1) * BATCH, banded, parts[(n + 1) % 2])
                work(z + n * BATCH, parts[n % 2], chip if owned else None, n * BATCH)


def forward_kernel(
    start, sources, own0, own1, mate0, mate1, over0, over1, far0, far1, speed, speed_mate, placed, laps, history, held, cour, last,
    even, odd, banded, y0, y1, sems, sems_even, sems_odd
):
    planes, rows, lanes = own0.shape
    steps = laps.shape[0]
    groups = rows // 8
    chip_here, core, slabs = place(planes)

    fetch_all = pltpu.make_async_copy(placed, held, sems.at[0])
    fetch_all.start()

    def keep(k, field, done):
        source = field.at[pl.ds(2, 4 * planes), pl.ds(0, rows)]
        return pltpu.make_async_copy(source, history.at[k], done.at[0])

    banded[...] = band(lanes)
    load_blocks(slabs, ((own0, own1), (mate0, mate1), (over0, over1), (far0, far1)), odd, even)
    head = speed.shape[0] - planes
    for here, across, first, rest in ((slabs[0], slabs[2], speed, own1), (slabs[1], slabs[3], speed_mate, mate1)):
        for p in range(planes):
            cour[across + p] = first[p]
            cour[here + p] = first[planes + p] if p < head else rest[planes + p - head]

    for index in range(2 * planes):
        z = (2 * (index // planes) + core) * planes + index % planes
        weight = 1.0 + 2.0 * jnp.full((rows, lanes), z, jnp.int32).astype(jnp.float32) / (4 * planes - 1)
        last[index] = weight / (12.0 * cour[z])

    cell = sources[chip_here]
    source_z, x, lane = cell // (rows * lanes), cell // lanes % rows, cell % lanes
    tile = pl.ds(pl.multiple_of(x % groups * 8, 8), 8)
    here = (lax.broadcasted_iota(jnp.int32, (8, lanes), 0) == x // groups) & (
        lax.broadcasted_iota(jnp.int32, (8, lanes), 1) == lane
    )
    source_slab, source_p = source_z // planes, lax.rem(source_z, planes)

    def advance(k, now, then, done):
        @pl.when(k >= 2)
        def _():
            keep(k - 2, then, done).wait()

        def work(z, y_part, chip, p):
            def fetch(j, rows):
                return then[z + j + 2, rows], cour[z + j, rows]

            def finish(j, rows, center, lap, extra):
                old, speed = extra
                if chip is not None:
                    laps[k, p + j, chip, rows] = lap
                then[z + j + 2, rows] = 2.0 * center - old + speed * lap

            laps12(now, z, y_part, fetch, finish)

        cycle = (start[0] + k) % 48
        phase = (jnp.full((8, lanes), cycle, jnp.int32).astype(jnp.float32) - 24.0) / 12.0
        wave = AMPLITUDE * (1.0 - 2.0 * phase * phase) * jnp.exp(-phase * phase)
        strength = jnp.where(here, 12.0 * wave, 0.0)
        moved = cour[source_z, tile, :] * strength

        sweep(core, planes, now, banded, y0, y1, work)

        owned = jnp.where(lax.rem(source_slab, 2) == core, strength, 0.0)
        laps[k, source_p, source_slab // 2, tile, :] += owned
        then[source_z + 2, tile, :] += moved
        keep(k, then, done).start()

    @pl.loop(0, steps // 2)
    def _(pair):
        advance(2 * pair, even, odd, sems_odd)
        advance(2 * pair + 1, odd, even, sems_even)

    for k, field, done in ((steps - 2, odd, sems_odd), (steps - 1, even, sems_even)):
        keep(k, field, done).wait()
    fetch_all.wait()


def inject_kernel(held, history, inject):
    steps, planes_all = history.shape[:2]

    @pl.loop(0, planes_all)
    def _(z):
        count = held[steps, z]
        for k in range(steps):
            inject[k, z] = held[k, z] - count * history[k, z]


def adjoint_kernel(own, mate, over, far, cour, laps, inject, last, keep, send_x, send_y, send_xy, even, odd, total, banded, y0, y1):
    planes, rows, lanes = own.shape[1:]
    steps = laps.shape[0]
    groups = rows // 8
    chip_here, core, slabs = place(planes)
    banded[...] = band(lanes)
    load_blocks(slabs, (own, mate, over, far), odd, even, factor=cour)

    total[...] = jnp.zeros(total.shape, jnp.float32)

    def advance(k, now, then):
        def work(z, y_part, chip, p):
            def fetch(j, rows):
                extra = (then[z + j + 2, rows], cour[z + j, rows], inject[k, z + j, rows])
                if chip is not None:
                    extra += (total[chip * planes + p + j, rows], laps[k, p + j, chip, rows])
                return extra

            def finish(j, rows, center, lap, extra):
                newer = 2.0 * center - extra[0] + extra[1] * (lap - extra[2])
                then[z + j + 2, rows] = newer
                if chip is not None:
                    total[chip * planes + p + j, rows] = extra[3] + newer * extra[4]

            laps12(now, z, y_part, fetch, finish)

        sweep(core, planes, now, banded, y0, y1, work)

    @pl.loop(0, steps // 2)
    def _(pair):
        advance(steps - 1 - 2 * pair, even, odd)
        advance(steps - 2 - 2 * pair, odd, even)

    count = keep.shape[0]
    mine, others = lax.axis_index("shot") % 2 * count, (1 - lax.axis_index("shot") % 2) * count
    here, there = chip_here, 1 - chip_here
    for ref, chip, start in ((keep, here, mine), (send_x, there, mine), (send_y, here, others), (send_xy, there, others)):

        @pl.loop(0, count)
        def _(n):
            p = start + n
            value = total[chip * planes + p] * last[chip * planes + p]
            for i in range(groups):
                ref[n, pl.ds(i, 8, stride=groups), :] = value[i * 8 : (i + 1) * 8]


def square_kernel(mine, by_xy, by_y, by_x, keep, send):
    half = lax.axis_index("shot") // 2 % 2
    count = keep.shape[0]
    for ref, part in ((keep, half), (send, 1 - half)):
        for p in range(count):
            at = part * count + p
            ref[p] = (mine[at] + by_x[at]) + (by_y[at] + by_xy[at])


def add_kernel(mine, other, out):
    out[...] = mine[...] + other[...]


def flip(index, bits):
    result = index
    for bit in (1, 2):
        if bits & bit:
            result = jnp.where(index // bit % 2 == 1, result - bit, result + bit)
    return result


def after_kernel(earlier, value, *outs):
    if len(outs) == 1:
        outs[0][...] = value[...]
    else:
        for n, out in enumerate(outs):
            out[...] = value[n]


def after(earlier, value, parts=1):
    vmem, anywhere = pl.BlockSpec(memory_space=pltpu.VMEM), pl.BlockSpec(memory_space=pl.ANY)
    shape = value.shape if parts == 1 else value.shape[1:]
    results = pl.pallas_call(
        after_kernel,
        in_specs=[anywhere, vmem],
        out_specs=[vmem] * parts,
        out_shape=[jax.ShapeDtypeStruct(shape, jnp.float32)] * parts,
        compiler_params=pltpu.CompilerParams(vmem_limit_bytes=4 * 2**20),
        name="after",
    )(earlier, value)
    return results[0] if parts == 1 else results


def arrange_kernel(own, mine, other, out):
    y = lax.axis_index("shot") % 2
    count, planes = mine.shape[0], own.shape[0]
    out[pl.ds(y * count, count)] = mine[...]
    out[pl.ds((1 - y) * count, count)] = other[...]
    out[planes:] = own[0 : out.shape[0] - planes]


def first_plane(shot, planes):
    return (shot % 2) * (planes // 2) + (shot // 2 % 2) * (planes // 4)


def sums_kernel(mine, other, momentum, data, sums):
    count, rows, lanes = mine.shape
    planes = momentum.shape[0]
    chip, core = lax.axis_index("chip"), lax.axis_index("core")
    first = first_plane(lax.axis_index("shot"), planes)
    parts = [jnp.zeros((rows, lanes), jnp.float32)] * 4
    for j in range(count):
        scaled = mine[j] + other[j]
        data[j * rows : (j + 1) * rows] = scaled
        z = (2 * chip + core) * planes + first + j
        weight = 1.0 + 2.0 * jnp.full((1, lanes), z, jnp.int32).astype(jnp.float32) / (4 * planes - 1)
        moment = momentum[first + j]
        square = scaled * scaled
        terms = (square, weight * moment * moment, weight * moment * scaled, weight * square)
        parts = [part + term for part, term in zip(parts, terms)]

    def total(value):
        by_lane = jnp.sum(value, axis=0, keepdims=True)
        return jnp.broadcast_to(jnp.sum(by_lane, axis=1, keepdims=True), (1, lanes))

    value = jnp.concatenate([total(part) for part in parts] + [jnp.zeros((4, lanes), jnp.float32)], 0)
    data[count * rows :] = value
    sums[...] = value


def join_kernel(mine, other, s0, s1, s2, data, sums):
    rows = mine.shape[0] - 8
    data[0:rows] = mine[0:rows]
    data[rows : 2 * rows] = other[0:rows]
    value = (s0[...] + s1[...]) + (other[rows:] + s2[...])
    data[2 * rows :] = value
    sums[...] = value


def finish_kernel(mine, other, momentum, s0, s1, s2, out, kinetic):
    planes, rows, lanes = momentum.shape
    cells = 4.0 * planes * rows * lanes
    shot = lax.axis_index("shot")
    sums = (s0[...] + s1[...]) + (other[planes // 2 * rows :] + s2[...])
    factor = lax.rsqrt(sums[0:1] / cells + EPSILON)
    energy = 0.5 * (sums[1:2] - factor * sums[2:3] + 0.25 * factor * factor * sums[3:4]) / cells
    kinetic[0] = energy[0, 0]
    step = 0.5 * factor
    quarter = planes // 4
    for part, group in ((mine, shot), (other, flip(shot, 1))):
        for number, first in enumerate((first_plane(group, planes), first_plane(flip(group, 2), planes))):
            for j in range(quarter):
                at = (number * quarter + j) * rows
                out[first + j] = momentum[first + j] - step * part[at : at + rows]


def local(kernel, outs, *arrays):
    vmem = pl.BlockSpec(memory_space=pltpu.VMEM)
    shapes = [jax.ShapeDtypeStruct(shape, jnp.float32) for shape in outs]
    single = len(outs) == 1
    return pl.pallas_call(
        kernel,
        in_specs=[vmem] * len(arrays),
        out_specs=vmem if single else [vmem] * len(outs),
        out_shape=shapes[0] if single else shapes,
        compiler_params=pltpu.CompilerParams(vmem_limit_bytes=4 * 2**20),
        name=kernel.__name__,
    )(*arrays)


def exchange(value, bits):
    axes = ("shot", "chip", "core")
    return lax.ppermute(value, axes, [(i, i ^ bits) for i in range(lax.axis_size(axes))])


CORE, CHIP, Y, NEAR_Z, FAR_Z = 1, 2, 4, 8, 16


def whole_shards(
    courant_sq, momentum, fwd_prev, fwd_cur, adj_next, adj_cur, observed, src_cells, rec_cells, ckpt_step
):
    _, planes, rows_x, rows_y = fwd_cur.shape
    steps = observed.shape[1]
    planes_all = 4 * planes
    cells_all = planes_all * rows_x * rows_y
    vmem, smem = pl.BlockSpec(memory_space=pltpu.VMEM), pl.BlockSpec(memory_space=pltpu.SMEM)

    hbm = pl.BlockSpec(memory_space=pltpu.HBM)
    outgoing, c0, piece = pl.pallas_call(
        first_kernel,
        in_specs=[hbm] * 3,
        out_specs=[vmem] * 3,
        out_shape=[
            jax.ShapeDtypeStruct((2, planes, rows_x, rows_y), jnp.float32),
            jax.ShapeDtypeStruct(courant_sq.shape, jnp.float32),
            jax.ShapeDtypeStruct((planes // 2, rows_x, rows_y), jnp.float32),
        ],
        scratch_shapes=[
            pltpu.VMEM((2, planes, rows_x, rows_y), jnp.float32),
            pltpu.VMEM(courant_sq.shape, jnp.float32),
            pltpu.SemaphoreType.DMA((3,)),
        ],
        compiler_params=pltpu.CompilerParams(vmem_limit_bytes=63 * 2**20),
        name="first_to_cross",
    )(fwd_prev, fwd_cur, courant_sq)

    over = exchange(outgoing, CHIP)
    piece = exchange(piece, CHIP)

    placed, mark = scatter(rec_cells, observed, planes_all, rows_x, rows_y)
    placed = placed.reshape(steps + 1, planes_all, rows_x, rows_y)

    piece = after(mark, piece)
    head = planes * 5 // 8
    adj_outgoing, adj_own, *own = pick(adj_next, adj_cur, fwd_prev, fwd_cur, c0, planes - head, piece)
    mate = [exchange(field, CORE) for field in own]
    speed = local(arrange_kernel, [(planes + head, rows_x, rows_y)], c0, piece, exchange(piece, Y))
    speed_mate = exchange(speed, CORE)
    over = after(speed, over, parts=2)
    far = [exchange(field, CORE) for field in over]
    adj_over = exchange(adj_outgoing, CHIP)
    adj_mate = exchange(adj_own, CORE)

    scratch = pltpu.VMEM((planes_all + 4, rows_x + 8, rows_y), jnp.float32)
    y_scratch = pltpu.VMEM((BATCH * rows_x, rows_y), jnp.float32)
    step_scratch = [scratch, scratch, pltpu.VMEM((2 * rows_y, rows_y), jnp.bfloat16), y_scratch, y_scratch]
    params = pltpu.CompilerParams(vmem_limit_bytes=6 * 2**20)
    cost = pl.CostEstimate(flops=30 * steps * cells_all, bytes_accessed=16 * steps * cells_all, transcendentals=0)
    laps, history, held, cour, last = pl.pallas_call(
        forward_kernel,
        in_specs=[smem, smem] + [vmem] * 10 + [pl.BlockSpec(memory_space=pltpu.HBM)],
        out_specs=[vmem] * 5,
        out_shape=[
            jax.ShapeDtypeStruct((steps, planes, 2, rows_x, rows_y), jnp.float32),
            jax.ShapeDtypeStruct((steps, planes_all, rows_x, rows_y), jnp.float32),
            jax.ShapeDtypeStruct((steps + 1, planes_all, rows_x, rows_y), jnp.float32),
            jax.ShapeDtypeStruct((planes_all, rows_x, rows_y), jnp.float32),
            jax.ShapeDtypeStruct((2 * planes, rows_x, rows_y), jnp.float32),
        ],
        scratch_shapes=step_scratch
        + [
            pltpu.SemaphoreType.DMA((1,)),
            pltpu.SemaphoreType.DMA((1,)),
            pltpu.SemaphoreType.DMA((1,)),
        ],
        compiler_params=pltpu.CompilerParams(vmem_limit_bytes=21 * 2**20),
        cost_estimate=pl.CostEstimate(flops=1000, bytes_accessed=1000, transcendentals=0),
        name="forward_steps",
    )(ckpt_step[None], src_cells, *own, *mate, *over, *far, speed, speed_mate, placed)

    adj_over = after(laps, adj_over)
    adj_far = exchange(adj_over, CORE)
    inject = pl.pallas_call(
        inject_kernel,
        in_specs=[vmem] * 2,
        out_specs=vmem,
        out_shape=jax.ShapeDtypeStruct(history.shape, jnp.float32),
        compiler_params=pltpu.CompilerParams(vmem_limit_bytes=4 * 2**20),
        name="inject",
    )(held, history)
    slab = jax.ShapeDtypeStruct(courant_sq.shape, jnp.float32)
    half, quarter = (planes // 2, rows_x, rows_y), (planes // 4, rows_x, rows_y)
    keep, send_x, send_y, send_xy = pl.pallas_call(
        adjoint_kernel,
        in_specs=[vmem] * 8,
        out_specs=[vmem] * 4,
        out_shape=[jax.ShapeDtypeStruct(half, jnp.float32)] * 4,
        scratch_shapes=step_scratch[:2] + [pltpu.VMEM((2 * planes, rows_x, rows_y), jnp.float32)] + step_scratch[2:],
        compiler_params=params,
        cost_estimate=cost,
        name="adjoint_steps",
    )(adj_own, adj_mate, adj_over, adj_far, cour, laps, inject, last)

    by_xy, by_x, by_y = exchange(send_xy, CHIP + Y), exchange(send_x, CHIP), exchange(send_y, Y)
    keep, send = local(square_kernel, [quarter] * 2, keep, by_xy, by_y, by_x)
    part = local(add_kernel, [quarter], keep, exchange(send, NEAR_Z))
    rows, sums_shape = planes // 4 * rows_x, (8, rows_y)
    data, sums = local(sums_kernel, [(rows + 8, rows_y), sums_shape], part, exchange(part, FAR_Z), momentum)

    received = exchange(data, NEAR_Z)
    others = [exchange(sums, CORE), exchange(sums, NEAR_Z + CORE)]
    data, sums = local(join_kernel, [(2 * rows + 8, rows_y), sums_shape], data, received, sums, *others)
    received = exchange(data, Y)
    others = [exchange(sums, CHIP), exchange(sums, Y + CHIP)]
    momentum_half, kinetic = pl.pallas_call(
        finish_kernel,
        in_specs=[vmem] * 6,
        out_specs=[vmem, smem],
        out_shape=[jax.ShapeDtypeStruct(momentum.shape, jnp.float32), jax.ShapeDtypeStruct((1,), jnp.float32)],
        compiler_params=pltpu.CompilerParams(vmem_limit_bytes=4 * 2**20),
        name="finish",
    )(data, received, momentum, sums, *others)
    return momentum_half, kinetic[0]


def solution(mesh):
    shots, slabs = mesh.shape["shot"], mesh.shape["depth"]

    def placed(depth):
        field = P("shot", depth, None, None)
        slab = P(depth, None, None)
        inputs = (slab, slab, field, field, field, field, P("shot", None, None), P("shot"), P("shot", None), P())
        return dict(in_specs=inputs, out_specs=(slab, P()), check_vma=False)

    slab_plan = jax.shard_map(slab_shards, mesh=mesh, **placed("depth"))
    if slabs != 4 or shots != 8:
        return slab_plan
    chips = Mesh(mesh.devices.reshape(shots, 2, 2), ("shot", "chip", "core"))
    whole_plan = jax.shard_map(whole_shards, mesh=chips, **placed(("chip", "core")))

    def run(courant_sq, momentum, fwd_prev, *rest):
        total, planes, rows_x, rows_y = fwd_prev.shape
        steps = rest[3].shape[1]
        fits = total == 2 * shots and planes == 4 * shots and rows_y == 128 and rows_x % 16 == 0 and steps % 2 == 0
        plan = whole_plan if fits else slab_plan
        return plan(courant_sq, momentum, fwd_prev, *rest)

    return run
```
